32 devices in a mesh: dp: 4 (over y, x), fsdp: 8 (over z, core).
Axes of the slice: x: 2, y: 2, z: 4, core: 2. Of those that a mesh axis runs over, the one named last changes fastest.
Arguments:
- inputs: bfloat16 [2, 16384, 512], P(None, ('dp', 'fsdp')), may hold values from -6 to 6
- memory: bfloat16 [2, 16384, 512], P(None, ('dp', 'fsdp')), may hold values from -6 to 6
- cotangent: bfloat16 [2, 16384, 512], P(None, ('dp', 'fsdp')), may hold values from -6 to 6
- lengths: int32 [2, 32, 2, 32], P(None, ('dp', 'fsdp')), may hold values from 0 to 512, as said below
- stacked_weights: float32 [8, 512, 512], P(None, 'fsdp')
- expand_weights: float32 [512, 2048], P('fsdp'), may hold values from -0.25 to 0.25
- contract_weights: float32 [2048, 512], P('fsdp'), may hold values from -0.125 to 0.125
- scale_vectors: float32 [9, 512], P(None, 'fsdp'), as said below
- stacked_first: float32 [8, 512, 512], P(None, 'fsdp'), may hold values from -434.4464 to 434.4464
- stacked_second: float32 [8, 512, 512], P(None, 'fsdp'), may hold values from 655.36 to 32768
- expand_first: float32 [512, 2048], P('fsdp'), may hold values from -434.4464 to 434.4464
- expand_second: float32 [512, 2048], P('fsdp'), may hold values from 655.36 to 32768
- contract_first: float32 [2048, 512], P('fsdp'), may hold values from -434.4464 to 434.4464
- contract_second: float32 [2048, 512], P('fsdp'), may hold values from 655.36 to 32768
- vector_first: float32 [9, 512], P(None, 'fsdp'), may hold values from -434.4464 to 434.4464
- vector_second: float32 [9, 512], P(None, 'fsdp'), may hold values from 655.36 to 32768
Outputs:
- output: bfloat16 [2, 16384, 512], P(None, ('dp', 'fsdp'))
- input_grad: float32 [2, 16384, 512], P(None, ('dp', 'fsdp'))
- memory_grad: float32 [2, 16384, 512], P(None, ('dp', 'fsdp'))
- stacked_next: float32 [8, 512, 512], P(None, 'fsdp')
- expand_next: float32 [512, 2048], P('fsdp')
- contract_next: float32 [2048, 512], P('fsdp')
- vector_next: float32 [9, 512], P(None, 'fsdp')
- stacked_first_next: float32 [8, 512, 512], P(None, 'fsdp')
- stacked_second_next: float32 [8, 512, 512], P(None, 'fsdp')
- expand_first_next: float32 [512, 2048], P('fsdp')
- expand_second_next: float32 [512, 2048], P('fsdp')
- contract_first_next: float32 [2048, 512], P('fsdp')
- contract_second_next: float32 [2048, 512], P('fsdp')
- vector_first_next: float32 [9, 512], P(None, 'fsdp')
- vector_second_next: float32 [9, 512], P(None, 'fsdp')
The draws below stay inside these ranges and needn't reach their ends.
Inputs may be any that keep to these rules, and one draw needn't show every extreme that they name: In every micro-batch exactly half of the slabs, drawn from the seed, hold one document pair: entry 0 of both sides is 512, the others 0. In the other slabs the target entries are sentence lengths of 16 to 63, except the last nonzero one, which may be shorter, and the memory side holds the same nonzero lengths in reverse order. Each side of each slab sums to 512. `scale_vectors`: rows 6 to 8 are positive.
All inputs are finite; a program needn't handle non-finite values.
Results may differ from the reference program's by a relative error of at most 0.02.
Values may be sent and summed in bfloat16 or wider, within the bound.
No kernel may reach another device: no remote copies, remote signals or barrier semaphores. Data moves between devices by JAX's collectives and lax.ppermute only.
A program may use at most 192 MiB of HBM per device.

```python
import math
import jax
import jax.numpy as jnp
from jax import lax

D = 512
FF = 2048
HEADS = 8
HEAD = 64
SLAB = 512
MICRO = 2
STEP = 3
SENT = 64
CMAX = 32
SLABS = 32
TOKENS = 16384


def draw_lengths(key, part):
    key = jax.random.fold_in(key, 7)
    piece_key, kind_key = jax.random.split(key)
    shortest = SENT // 4
    pieces = shortest + jax.random.randint(piece_key, (MICRO, SLABS, CMAX), 0, SENT - shortest, dtype=jnp.int32)
    closing = jnp.cumsum(pieces, axis=-1).astype(jnp.int32)
    starts = closing - pieces
    target = jnp.minimum(jnp.maximum(SLAB - starts, 0), pieces).astype(jnp.int32)
    filled = jnp.sum((target > 0).astype(jnp.int32), axis=-1, keepdims=True, dtype=jnp.int32)
    places = jnp.arange(CMAX, dtype=jnp.int32)
    mirrored = jnp.where(places < filled, filled - 1 - places, places).astype(jnp.int32)
    source = jnp.take_along_axis(target, mirrored, axis=-1)
    single = jnp.where(places == 0, SLAB, 0).astype(jnp.int32)
    shuffled = jnp.stack([jax.random.permutation(jax.random.fold_in(kind_key, micro_index), SLABS) for micro_index in range(MICRO)])
    document_slab = (shuffled < SLABS // 2)[:, :, None]
    target = jnp.where(document_slab, single, target)
    source = jnp.where(document_slab, single, source)
    return jnp.stack([target, source], axis=2).astype(jnp.int32)


def draw_stacked_weights(key, part):
    key = jax.random.fold_in(key, 3)
    scales = jnp.array([1.0, 1.0, 1.0, 4.0, 1.0, 1.0, 1.0, 4.0], jnp.float32) * D ** (-0.5)
    return jax.random.normal(key, (8, D, D), jnp.float32) * scales[:, None, None]


def draw_scale_vectors(key, part):
    key = jax.random.fold_in(key, 5)
    gain_key, shift_key, omega_key = jax.random.split(key, 3)
    gains = 1.0 + 0.3 * jax.random.uniform(gain_key, (3, D), jnp.float32, -1.0, 1.0)
    shifts = 0.3 * jax.random.normal(shift_key, (3, D), jnp.float32)
    omegas = jnp.exp(jax.random.uniform(omega_key, (3, D), jnp.float32, math.log(0.7), math.log(2.5)))
    return jnp.concatenate([gains, shifts, omegas], axis=0)


def levels(stream_key, extent, shards, low, top_value):
    level = 1.0
    for dim, blocks in shards:
        steps = jax.random.uniform(jax.random.fold_in(jax.random.fold_in(stream_key, 6), dim), (blocks,), jnp.float32, low / len(shards), top_value / len(shards))
        level = level * jnp.repeat(jnp.exp(steps), extent[dim] // blocks).reshape((-1,) + (1,) * (len(extent) - 1 - dim))
    return level


def bell_draw(stream_key, shape, scale, bound, shards=(), kind=jnp.bfloat16):
    values = jax.random.normal(stream_key, shape, jnp.float32) * scale
    if len(shards) > 0:
        values = levels(stream_key, shape, shards, -0.22, 0.18) * values
    return jnp.clip(values, min=-bound, max=bound).astype(kind)


def setup_inputs(seed: int = 0) -> dict:
    splits = jax.random.split(jax.random.key(seed), 17)
    inputs = bell_draw(splits[0], (MICRO, TOKENS, D), 1.0, 6.0, ((1, 32),))
    memory = bell_draw(splits[1], (MICRO, TOKENS, D), 1.0, 6.0, ((1, 32),))
    cotangent = bell_draw(splits[2], (MICRO, TOKENS, D), 1.0, 6.0, ((1, 32),))
    lengths = draw_lengths(jax.random.fold_in(splits[16], 71), 0)
    stacked_weights = draw_stacked_weights(jax.random.fold_in(splits[16], 71), 0)
    expand_weights = bell_draw(splits[5], (D, FF), D ** -0.5, 0.25, ((0, 8),), jnp.float32)
    contract_weights = bell_draw(splits[6], (FF, D), FF ** -0.5, 0.125, ((0, 8),), jnp.float32)
    scale_vectors = draw_scale_vectors(jax.random.fold_in(splits[16], 71), 0)
    stacked_first = bell_draw(splits[8], (8, D, D), (0.4 * (MICRO * TOKENS) ** 0.5), 434.4464, ((1, 8),), jnp.float32)
    stacked_second = jnp.clip(jnp.exp(math.log(32768.0) - 3.912023 * jax.random.uniform(splits[9], (8, D, D), jnp.float32) ** levels(splits[9], (8, D, D), ((1, 8),), -0.2, 0.2)), 655.36, 32768.0)
    expand_first = bell_draw(splits[10], (D, FF), (0.4 * (MICRO * TOKENS) ** 0.5), 434.4464, ((0, 8),), jnp.float32)
    expand_second = jnp.clip(jnp.exp(math.log(32768.0) - 3.912023 * jax.random.uniform(splits[11], (D, FF), jnp.float32) ** levels(splits[11], (D, FF), ((0, 8),), -0.2, 0.2)), 655.36, 32768.0)
    contract_first = bell_draw(splits[12], (FF, D), (0.4 * (MICRO * TOKENS) ** 0.5), 434.4464, ((0, 8),), jnp.float32)
    contract_second = jnp.clip(jnp.exp(math.log(32768.0) - 3.912023 * jax.random.uniform(splits[13], (FF, D), jnp.float32) ** levels(splits[13], (FF, D), ((0, 8),), -0.2, 0.2)), 655.36, 32768.0)
    vector_first = bell_draw(splits[14], (9, D), (0.4 * (MICRO * TOKENS) ** 0.5), 434.4464, ((1, 8),), jnp.float32)
    vector_second = jnp.clip(jnp.exp(math.log(32768.0) - 3.912023 * jax.random.uniform(splits[15], (9, D), jnp.float32) ** levels(splits[15], (9, D), ((1, 8),), -0.2, 0.2)), 655.36, 32768.0)
    return {"inputs": inputs, "memory": memory, "cotangent": cotangent, "lengths": lengths, "stacked_weights": stacked_weights, "expand_weights": expand_weights, "contract_weights": contract_weights, "scale_vectors": scale_vectors, "stacked_first": stacked_first, "stacked_second": stacked_second, "expand_first": expand_first, "expand_second": expand_second, "contract_first": contract_first, "contract_second": contract_second, "vector_first": vector_first, "vector_second": vector_second}


@jax.custom_vjp
def low(v):
    return lax.optimization_barrier(v.astype(jnp.bfloat16)).astype(jnp.float32)

@jax.custom_vjp
def low_back(v):
    return v

def low_keep(v):
    return (low(v), None)

def low_pass(kept, grad):
    return (grad,)

def back_keep(v):
    return (v, None)

def back_low(kept, grad):
    return (low(grad),)
low.defvjp(low_keep, low_pass)
low_back.defvjp(back_keep, back_low)
NORM_EPS = 1e-05
ADAM_EPS = 1e-08
LEARN_RATE = 0.2
FAR_BELOW = -1e+30
HIGHEST = lax.Precision.HIGHEST

def matmul_high(left_side, right_side):
    return jnp.dot(left_side, right_side, precision=HIGHEST)

def normalize(residual, gain_row, shift_row):
    centred = residual - lax.optimization_barrier(jnp.mean(residual, axis=-1, keepdims=True))
    spread = lax.optimization_barrier(jnp.mean(centred * centred, axis=-1, keepdims=True))
    return centred * lax.rsqrt(spread + NORM_EPS) * gain_row + shift_row

def segments(piece_lengths, row_count):
    closing = jnp.cumsum(piece_lengths, axis=-1).astype(jnp.int32)
    places = jnp.arange(row_count, dtype=jnp.int32)
    return lax.optimization_barrier(jnp.sum((closing[:, None, :] <= places[None, :, None]).astype(jnp.int32), axis=-1, dtype=jnp.int32))

def attention(queries, key_rows, value_rows, allowed):
    row_count = queries.shape[0]
    query_heads = queries.reshape(row_count, HEADS, HEAD)
    key_heads = key_rows.reshape(key_rows.shape[0], HEADS, HEAD)
    value_heads = value_rows.reshape(value_rows.shape[0], HEADS, HEAD)
    scores = jnp.einsum('qhd,khd->hqk', query_heads, key_heads, precision=HIGHEST) * HEAD ** (-0.5)
    scores = jnp.where(allowed[None], low_back(scores), FAR_BELOW)
    exponent = jnp.exp(scores - lax.optimization_barrier(jnp.max(scores, axis=-1, keepdims=True)))
    probabilities = exponent / lax.optimization_barrier(jnp.sum(exponent, axis=-1, keepdims=True))
    mixture = jnp.einsum('hqk,khd->qhd', low(probabilities), value_heads, precision=HIGHEST)
    return mixture.reshape(row_count, HEADS * HEAD)

def slab_layer(weights, tokens, memory_rows, piece_lengths):
    stacked, expand, contract, vector_rows = weights
    row_count = tokens.shape[0]
    labels = segments(piece_lengths, row_count)
    places = jnp.arange(row_count, dtype=jnp.int32)
    self_allowed = (labels[0][:, None] == labels[0][None, :]) & (places[None, :] <= places[:, None])
    cross_allowed = labels[0][:, None] == labels[1][None, :]
    queries = low(low_back(matmul_high(tokens, stacked[0])))
    key_rows = low(low_back(matmul_high(tokens, stacked[1])))
    value_rows = low(low_back(matmul_high(tokens, stacked[2])))
    first_mix = low(low_back(attention(queries, key_rows, value_rows, self_allowed)))
    first_branch = low_back(matmul_high(first_mix, stacked[3]))
    first_state = normalize(vector_rows[6] * tokens + first_branch, vector_rows[0], vector_rows[3])
    cross_queries = low(low_back(matmul_high(low(first_state), stacked[4])))
    cross_keys = low(low_back(matmul_high(memory_rows, stacked[5])))
    cross_values = low(low_back(matmul_high(memory_rows, stacked[6])))
    second_mix = low(low_back(attention(cross_queries, cross_keys, cross_values, cross_allowed)))
    second_branch = low_back(matmul_high(second_mix, stacked[7]))
    second_state = normalize(vector_rows[7] * first_state + second_branch, vector_rows[1], vector_rows[4])
    hidden = low_back(matmul_high(low(second_state), expand))
    activated = low(jax.nn.gelu(hidden, approximate=True))
    ffn_branch = low_back(matmul_high(activated, contract))
    return normalize(vector_rows[8] * second_state + ffn_branch, vector_rows[2], vector_rows[5])

def group_layer(weights, tokens, memory_rows, piece_lengths):
    return jax.vmap(slab_layer, in_axes=(None, 0, 0, 0))(weights, tokens, memory_rows, piece_lengths)

def forward(params, inputs, memory, lengths):
    weights = (low(params[0]), low(params[1]), low(params[2]), low(params[3]))
    group_size = math.gcd(SLABS, max(1, 4096 // SLAB))
    blocks = SLABS // group_size
    checked = jax.checkpoint(group_layer)

    def one_block(block_items):
        return checked(weights, block_items[0], block_items[1], block_items[2])
    results = []
    for micro_index in range(MICRO):
        block_tokens = inputs[micro_index].reshape(blocks, group_size, SLAB, D)
        block_memory = memory[micro_index].reshape(blocks, group_size, SLAB, D)
        block_lengths = lengths[micro_index].reshape(blocks, group_size, 2, CMAX)
        result_now = lax.map(one_block, (block_tokens, block_memory, block_lengths))
        results.append(result_now.reshape(TOKENS, D))
    return jnp.stack(results)

def adam_update(weight, first_moment, second_moment, gradient, correction):
    first_next = 0.5 * first_moment + 0.5 * gradient
    second_next = 0.5 * second_moment + 0.5 * gradient * gradient
    weight_next = weight - LEARN_RATE * (first_next / correction) / (jnp.sqrt(second_next / correction) + ADAM_EPS)
    return (weight_next, first_next, second_next)

def reference(inputs, memory, cotangent, lengths, stacked_weights, expand_weights, contract_weights, scale_vectors, stacked_first, stacked_second, expand_first, expand_second, contract_first, contract_second, vector_first, vector_second):
    params = (stacked_weights, expand_weights, contract_weights, scale_vectors)

    def traced(params_now, inputs_now, memory_now):
        return forward(params_now, inputs_now, memory_now, lengths)
    output_full, pullback = jax.vjp(traced, params, inputs.astype(jnp.float32), memory.astype(jnp.float32))
    gradients, input_grad, memory_grad = pullback(cotangent.astype(jnp.float32))
    correction = 1.0 - 0.5 ** STEP
    firsts = (stacked_first, expand_first, contract_first, vector_first)
    seconds = (stacked_second, expand_second, contract_second, vector_second)
    updates = [adam_update(params[position], firsts[position], seconds[position], gradients[position], correction) for position in range(4)]
    return (output_full.astype(jnp.bfloat16), input_grad, memory_grad, updates[0][0], updates[1][0], updates[2][0], updates[3][0], updates[0][1], updates[0][2], updates[1][1], updates[1][2], updates[2][1], updates[2][2], updates[3][1], updates[3][2])
```

```python
import math

import jax
import jax.numpy as jnp
from jax import lax
from jax.experimental import pallas as pl
from jax.experimental.pallas import tpu as pltpu
from jax.sharding import PartitionSpec as P

HEADS = 8
HEAD = 64
SLAB = 512
WIDTH = 512
PAIR = 2 * HEAD
STEP = 3
NORM_EPS = 1e-05
ADAM_EPS = 1e-08
LEARN_RATE = 0.2
FAR = -1e30
LOG2E = math.log2(math.e)
QSCALE = HEAD**-0.5 * LOG2E
TILE = 256
BF = jnp.bfloat16
F32 = jnp.float32
MIB = 1 << 20


def nn(a, b):
    return jnp.dot(a, b, preferred_element_type=F32)


def nt(a, b):
    return lax.dot_general(a, b, (((1,), (1,)), ((), ())), preferred_element_type=F32)


def tn(a, b):
    return lax.dot_general(a, b, (((0,), (0,)), ((), ())), preferred_element_type=F32)


def norm_forward(residual, eps=NORM_EPS):
    centred = residual - jnp.mean(residual, axis=-1, keepdims=True)
    spread = jnp.mean(centred * centred, axis=-1, keepdims=True)
    scale = lax.rsqrt(spread + eps)
    return centred * scale, scale


def norm_backward(upstream, unit, scale, gain):
    inner = upstream * gain
    first = jnp.mean(inner, axis=-1, keepdims=True)
    second = jnp.mean(inner * unit, axis=-1, keepdims=True)
    return scale * (inner - first - unit * second)


def rows_sum(values):
    return jnp.sum(values, axis=0, keepdims=True)


def attend_forward(k_ref, qt, vt, u, wt, e_ref, o_ref, r_ref, causal):
    lane = lax.broadcasted_iota(jnp.int32, (SLAB, PAIR), 1)
    low_half = lane < HEAD
    if causal:
        key_at = lax.broadcasted_iota(jnp.int32, (TILE, TILE), 0)
        query_at = lax.broadcasted_iota(jnp.int32, (TILE, TILE), 1)
        bias = jnp.where(key_at <= query_at, 0.0, FAR).astype(F32)
    for head in range(HEADS):
        pair = head // 2
        keys = k_ref[:, pair * PAIR : (pair + 1) * PAIR]
        query = qt[head * HEAD : (head + 1) * HEAD]
        value = vt[head * HEAD : (head + 1) * HEAD]
        if head % 2 == 0:
            left = jnp.where(low_half, keys, u)
            right = jnp.concatenate([query, wt], axis=0)
        else:
            left = jnp.where(low_half, u, keys)
            right = jnp.concatenate([wt, query], axis=0)
        for tile in range(SLAB // TILE):
            cols = slice(tile * TILE, (tile + 1) * TILE)
            depth = (tile + 1) * TILE if causal else SLAB
            scores = nn(left[:depth], right[:, cols])
            if causal:
                last = scores[tile * TILE :] + bias
                scores = last if tile == 0 else jnp.concatenate([scores[: tile * TILE], last], axis=0)
            top = jnp.max(scores, axis=0, keepdims=True)
            power = jnp.exp2(scores - top)
            inverse = 1.0 / jnp.sum(power, axis=0, keepdims=True)
            power = power.astype(BF)
            e_ref[head, :depth, cols] = power
            mix = nn(value[:, :depth], power) * inverse
            o_ref[head * HEAD : (head + 1) * HEAD, cols] = mix.astype(BF)
            r_ref[head : head + 1, cols] = inverse


def attend_backward(e_ref, r_ref, o_ref, qt_ref, kt_ref, v_ref, dmt, dqt_ref, dk_ref, dv_ref, causal):
    zero = jnp.zeros((HEAD, SLAB), BF)
    for pair in range(HEADS // 2):
        values = v_ref[:, pair * PAIR : (pair + 1) * PAIR]
        dk = [None] * (SLAB // TILE)
        dv = [None] * (SLAB // TILE)
        for side in range(2):
            head = 2 * pair + side
            rows = slice(head * HEAD, (head + 1) * HEAD)
            mixed = dmt[rows] * r_ref[head : head + 1, :]
            mixed = mixed.astype(BF)
            centre = jnp.sum(mixed.astype(F32) * o_ref[rows, :].astype(F32), axis=0, keepdims=True)
            query = qt_ref[rows, :]
            if side == 0:
                mixed = jnp.concatenate([mixed, zero], axis=0)
                query = jnp.concatenate([query, zero], axis=0)
            else:
                mixed = jnp.concatenate([zero, mixed], axis=0)
                query = jnp.concatenate([zero, query], axis=0)
            for tile in range(SLAB // TILE):
                cols = slice(tile * TILE, (tile + 1) * TILE)
                depth = (tile + 1) * TILE if causal else SLAB
                grad = nn(values[:depth], mixed[:, cols])
                power = e_ref[head, :depth, cols]
                score = (power.astype(F32) * (grad - centre[:, cols])).astype(BF)
                dqt_ref[rows, cols] = (nn(kt_ref[rows, :depth], score) * HEAD**-0.5).astype(BF)
                dv_now = nt(power, mixed[:, cols])
                dk_now = nt(score, query[:, cols])
                for part in range(depth // TILE):
                    span = slice(part * TILE, (part + 1) * TILE)
                    dv[part] = dv_now[span] if dv[part] is None else dv[part] + dv_now[span]
                    dk[part] = dk_now[span] if dk[part] is None else dk[part] + dk_now[span]
        for part in range(SLAB // TILE):
            span = slice(part * TILE, (part + 1) * TILE)
            dv_ref[span, pair * PAIR : (pair + 1) * PAIR] = dv[part].astype(BF)
            dk_ref[span, pair * PAIR : (pair + 1) * PAIR] = (dk[part] * (1.0 / LOG2E)).astype(BF)


def self_forward(x_ref, w_ref, vec_ref, u_ref, wt_ref, qt_ref, kt_ref, v_ref, e_ref, r_ref, o_ref, unit_ref, scale_ref, k_s):
    x = x_ref[0]
    qt = (nn(x, w_ref[0]) * QSCALE).astype(BF).T
    qt_ref[0] = qt
    keys = nn(x, w_ref[1]).astype(BF)
    k_s[...] = keys
    kt_ref[0] = keys.T
    values = nn(x, w_ref[2]).astype(BF)
    v_ref[0] = values
    attend_forward(k_s, qt, values.T, u_ref[0], wt_ref[0], e_ref.at[0], o_ref.at[0], r_ref.at[0], True)
    residual = vec_ref[6:7, :] * x.astype(F32) + tn(o_ref[0], w_ref[3])
    unit, scale = norm_forward(residual)
    unit_ref[0] = unit
    scale_ref[0] = scale


def cross_forward(unit1_ref, mem_ref, w_ref, vec_ref, u_ref, wt_ref, qt_ref, kt_ref, v_ref, e_ref, r_ref, o_ref, unit_ref, scale_ref, k_s):
    state = unit1_ref[0] * vec_ref[0:1, :] + vec_ref[3:4, :]
    memory = mem_ref[0]
    qt = (nn(state.astype(BF), w_ref[0]) * QSCALE).astype(BF).T
    qt_ref[0] = qt
    keys = nn(memory, w_ref[1]).astype(BF)
    k_s[...] = keys
    kt_ref[0] = keys.T
    values = nn(memory, w_ref[2]).astype(BF)
    v_ref[0] = values
    attend_forward(k_s, qt, values.T, u_ref[0], wt_ref[0], e_ref.at[0], o_ref.at[0], r_ref.at[0], False)
    residual = vec_ref[7:8, :] * state + tn(o_ref[0], w_ref[3])
    unit, scale = norm_forward(residual)
    unit_ref[0] = unit
    scale_ref[0] = scale


CUBE = 0.044715
ROOT = math.sqrt(2.0 / math.pi)


def feed_both(unit2_ref, cot_ref, ex_ref, co_ref, vec_ref, out_ref, ds_ref, dex_ref, dco_ref, dvec_ref, act_s, slope_s, dex_s, dco_s):
    step = pl.program_id(0)
    steps = pl.num_programs(0)
    hidden_width = ex_ref.shape[1]
    chunk = 512

    @pl.when(step == 0)
    def _():
        dex_s[...] = jnp.zeros_like(dex_s)
        dco_s[...] = jnp.zeros_like(dco_s)
        dvec_ref[...] = jnp.zeros_like(dvec_ref)

    state = unit2_ref[0] * vec_ref[1:2, :] + vec_ref[4:5, :]
    low = state.astype(BF)
    branch = None
    for part in range(hidden_width // chunk):
        cols = slice(part * chunk, (part + 1) * chunk)
        u = nn(low, ex_ref[:, cols])
        square = u * u
        bend = jnp.tanh(u * (ROOT + (ROOT * CUBE) * square))
        half = 0.5 + 0.5 * bend
        active = (u * half).astype(BF)
        act_s[:, cols] = active
        slope_s[:, cols] = half + (u * half) * (1.0 - bend) * (ROOT + (3.0 * ROOT * CUBE) * square)
        now = nn(active, co_ref[cols, :])
        branch = now if branch is None else branch + now
    unit, scale = norm_forward(vec_ref[8:9, :] * state + branch)
    out_ref[0] = (unit * vec_ref[2:3, :] + vec_ref[5:6, :]).astype(BF)
    up = cot_ref[0].astype(F32)
    dvec_ref[0:1, :] += rows_sum(up * unit)
    dvec_ref[1:2, :] += rows_sum(up)
    dres = norm_backward(up, unit, scale, vec_ref[2:3, :])
    dvec_ref[2:3, :] += rows_sum(dres * state)
    dstate = dres * vec_ref[8:9, :]
    dbranch = dres.astype(BF)
    low_t = low.T
    for part in range(hidden_width // chunk):
        cols = slice(part * chunk, (part + 1) * chunk)
        dco_s[cols, :] += tn(act_s[:, cols], dbranch)
        dhid = (nt(dbranch, co_ref[cols, :]) * slope_s[:, cols]).astype(BF)
        dex_s[:, cols] += nn(low_t, dhid)
        dstate = dstate + nt(dhid, ex_ref[:, cols])
    ds_ref[0] = dstate

    @pl.when(step == steps - 1)
    def _():
        dex_ref[...] = dex_s[...].astype(BF)
        dco_ref[...] = dco_s[...].astype(BF)


def cross_backward(ds2_ref, unit2_ref, scale2_ref, unit1_ref, mem_ref, w_ref, vec_ref, qt_ref, kt_ref, v_ref, e_ref, r_ref, o_ref,
                   dmem_ref, ds1_ref, dw_ref, dvec_ref, dqt_s, dk_s, dv_s, dw_s):
    step = pl.program_id(0)
    steps = pl.num_programs(0)

    @pl.when(step == 0)
    def _():
        dw_s[...] = jnp.zeros_like(dw_s)
        dvec_ref[...] = jnp.zeros_like(dvec_ref)

    up = ds2_ref[0]
    unit = unit2_ref[0]
    state = unit1_ref[0] * vec_ref[0:1, :] + vec_ref[3:4, :]
    dvec_ref[0:1, :] += rows_sum(up * unit)
    dvec_ref[1:2, :] += rows_sum(up)
    dres = norm_backward(up, unit, scale2_ref[0], vec_ref[1:2, :])
    dvec_ref[2:3, :] += rows_sum(dres * state)
    dbranch = dres.astype(BF)
    dw_s[3] += nn(o_ref[0], dbranch)
    dmt = nt(w_ref[3], dbranch)
    attend_backward(e_ref.at[0], r_ref.at[0], o_ref.at[0], qt_ref.at[0], kt_ref.at[0], v_ref.at[0], dmt, dqt_s, dk_s, dv_s, False)
    dq = dqt_s[...].T
    ds1_ref[0] = dres * vec_ref[7:8, :] + nt(dq, w_ref[0])
    dw_s[0] += nn(state.astype(BF).T, dq)
    memory_t = mem_ref[0].T
    dk = dk_s[...]
    dv = dv_s[...]
    dw_s[1] += nn(memory_t, dk)
    dw_s[2] += nn(memory_t, dv)
    dmem_ref[0] = nt(dk, w_ref[1]) + nt(dv, w_ref[2])

    @pl.when(step == steps - 1)
    def _():
        dw_ref[...] = dw_s[...].astype(BF)


def self_backward(ds1_ref, unit1_ref, scale1_ref, x_ref, w_ref, vec_ref, qt_ref, kt_ref, v_ref, e_ref, r_ref, o_ref,
                  dx_ref, dw_ref, dvec_ref, dqt_s, dk_s, dv_s, dw_s):
    step = pl.program_id(0)
    steps = pl.num_programs(0)

    @pl.when(step == 0)
    def _():
        dw_s[...] = jnp.zeros_like(dw_s)
        dvec_ref[...] = jnp.zeros_like(dvec_ref)

    up = ds1_ref[0]
    unit = unit1_ref[0]
    x = x_ref[0]
    dvec_ref[0:1, :] += rows_sum(up * unit)
    dvec_ref[1:2, :] += rows_sum(up)
    dres = norm_backward(up, unit, scale1_ref[0], vec_ref[0:1, :])
    dvec_ref[2:3, :] += rows_sum(dres * x.astype(F32))
    dbranch = dres.astype(BF)
    dw_s[3] += nn(o_ref[0], dbranch)
    dmt = nt(w_ref[3], dbranch)
    attend_backward(e_ref.at[0], r_ref.at[0], o_ref.at[0], qt_ref.at[0], kt_ref.at[0], v_ref.at[0], dmt, dqt_s, dk_s, dv_s, True)
    dq = dqt_s[...].T
    dk = dk_s[...]
    dv = dv_s[...]
    dx_ref[0] = dres * vec_ref[6:7, :] + nt(dq, w_ref[0]) + nt(dk, w_ref[1]) + nt(dv, w_ref[2])
    x_t = x.T
    dw_s[0] += nn(x_t, dq)
    dw_s[1] += nn(x_t, dk)
    dw_s[2] += nn(x_t, dv)

    @pl.when(step == steps - 1)
    def _():
        dw_ref[...] = dw_s[...].astype(BF)


def per_slab(*tail):
    return pl.BlockSpec((1,) + tail, lambda m: (m,) + (0,) * len(tail))


def fixed(*shape):
    return pl.BlockSpec(shape, lambda m: (0,) * len(shape))


def shape(dims, kind):
    return jax.ShapeDtypeStruct(tuple(dims), kind)


def params(mib):
    return pltpu.CompilerParams(dimension_semantics=("arbitrary",), vmem_limit_bytes=mib * MIB)


def attention_saved(g):
    return (
        [per_slab(WIDTH, SLAB), per_slab(WIDTH, SLAB), per_slab(SLAB, WIDTH), per_slab(HEADS, SLAB, SLAB), per_slab(HEADS, SLAB), per_slab(WIDTH, SLAB)],
        [shape((g, WIDTH, SLAB), BF), shape((g, WIDTH, SLAB), BF), shape((g, SLAB, WIDTH), BF), shape((g, HEADS, SLAB, SLAB), BF), shape((g, HEADS, SLAB), F32), shape((g, WIDTH, SLAB), BF)],
    )


def run_self_forward(x, w, vec, u, wt):
    g = x.shape[0]
    specs, shapes = attention_saved(g)
    return pl.pallas_call(
        self_forward,
        grid=(g,),
        in_specs=[per_slab(SLAB, WIDTH), fixed(4, WIDTH, WIDTH), fixed(16, WIDTH), per_slab(SLAB, PAIR), per_slab(HEAD, SLAB)],
        out_specs=specs + [per_slab(SLAB, WIDTH), per_slab(SLAB, 1)],
        out_shape=shapes + [shape((g, SLAB, WIDTH), F32), shape((g, SLAB, 1), F32)],
        scratch_shapes=[pltpu.VMEM((SLAB, WIDTH), BF)],
        compiler_params=params(48),
        name="self_forward",
    )(x, w, vec, u, wt)


def run_cross_forward(unit1, memory, w, vec, u, wt):
    g = memory.shape[0]
    specs, shapes = attention_saved(g)
    return pl.pallas_call(
        cross_forward,
        grid=(g,),
        in_specs=[per_slab(SLAB, WIDTH), per_slab(SLAB, WIDTH), fixed(4, WIDTH, WIDTH), fixed(16, WIDTH), per_slab(SLAB, PAIR), per_slab(HEAD, SLAB)],
        out_specs=specs + [per_slab(SLAB, WIDTH), per_slab(SLAB, 1)],
        out_shape=shapes + [shape((g, SLAB, WIDTH), F32), shape((g, SLAB, 1), F32)],
        scratch_shapes=[pltpu.VMEM((SLAB, WIDTH), BF)],
        compiler_params=params(48),
        name="cross_forward",
    )(unit1, memory, w, vec, u, wt)


def run_feed(unit2, cot, ex, co, vec):
    g = unit2.shape[0]
    ff = ex.shape[1]
    return pl.pallas_call(
        feed_both,
        grid=(g,),
        in_specs=[per_slab(SLAB, WIDTH), per_slab(SLAB, WIDTH), fixed(WIDTH, ff), fixed(ff, WIDTH), fixed(16, WIDTH)],
        out_specs=[per_slab(SLAB, WIDTH), per_slab(SLAB, WIDTH), fixed(WIDTH, ff), fixed(ff, WIDTH), fixed(8, WIDTH)],
        out_shape=[shape((g, SLAB, WIDTH), BF), shape((g, SLAB, WIDTH), F32), shape((WIDTH, ff), BF), shape((ff, WIDTH), BF), shape((8, WIDTH), F32)],
        scratch_shapes=[pltpu.VMEM((SLAB, ff), BF), pltpu.VMEM((SLAB, ff), F32), pltpu.VMEM((WIDTH, ff), F32), pltpu.VMEM((ff, WIDTH), F32)],
        compiler_params=params(56),
        name="feed_both",
    )(unit2, cot, ex, co, vec)


def backward_scratch():
    return [pltpu.VMEM((WIDTH, SLAB), BF), pltpu.VMEM((SLAB, WIDTH), BF), pltpu.VMEM((SLAB, WIDTH), BF), pltpu.VMEM((4, WIDTH, WIDTH), F32)]


def run_cross_backward(ds2, unit2, scale2, unit1, memory, w, vec, saved):
    g = memory.shape[0]
    specs, _ = attention_saved(g)
    return pl.pallas_call(
        cross_backward,
        grid=(g,),
        in_specs=[per_slab(SLAB, WIDTH), per_slab(SLAB, WIDTH), per_slab(SLAB, 1), per_slab(SLAB, WIDTH), per_slab(SLAB, WIDTH), fixed(4, WIDTH, WIDTH), fixed(16, WIDTH)] + specs,
        out_specs=[per_slab(SLAB, WIDTH), per_slab(SLAB, WIDTH), fixed(4, WIDTH, WIDTH), fixed(8, WIDTH)],
        out_shape=[shape((g, SLAB, WIDTH), F32), shape((g, SLAB, WIDTH), F32), shape((4, WIDTH, WIDTH), BF), shape((8, WIDTH), F32)],
        scratch_shapes=backward_scratch(),
        compiler_params=params(56),
        name="cross_backward",
    )(ds2, unit2, scale2, unit1, memory, w, vec, *saved)


def run_self_backward(ds1, unit1, scale1, x, w, vec, saved):
    g = x.shape[0]
    specs, _ = attention_saved(g)
    return pl.pallas_call(
        self_backward,
        grid=(g,),
        in_specs=[per_slab(SLAB, WIDTH), per_slab(SLAB, WIDTH), per_slab(SLAB, 1), per_slab(SLAB, WIDTH), fixed(4, WIDTH, WIDTH), fixed(16, WIDTH)] + specs,
        out_specs=[per_slab(SLAB, WIDTH), fixed(4, WIDTH, WIDTH), fixed(8, WIDTH)],
        out_shape=[shape((g, SLAB, WIDTH), F32), shape((4, WIDTH, WIDTH), BF), shape((8, WIDTH), F32)],
        scratch_shapes=backward_scratch(),
        compiler_params=params(56),
        name="self_backward",
    )(ds1, unit1, scale1, x, w, vec, *saved)


def piece_bounds(lengths):
    closing = jnp.cumsum(lengths, axis=-1)
    opening = closing - lengths
    pad = ((0, 0), (0, 0), (0, HEAD - lengths.shape[-1]))
    return jnp.pad(opening, pad), jnp.pad(closing, pad)


def mask_factors(lengths):
    opening, closing = piece_bounds(lengths)
    places = jnp.arange(SLAB, dtype=jnp.int32)
    keys = (opening[:, :, None, :] <= places[:, None]) & (places[:, None] < closing[:, :, None, :])
    keys = jnp.concatenate([keys, keys], axis=-1).astype(BF)
    inside = (opening[:, 0, :, None] <= places) & (places < closing[:, 0, :, None])
    queries = jnp.where(inside, 0.0, FAR).astype(BF)
    return keys[:, 0], keys[:, 1], queries


def adam_update(weight, first_moment, second_moment, gradient, correction):
    first_next = 0.5 * first_moment + 0.5 * gradient
    second_next = 0.5 * second_moment + 0.5 * gradient * gradient
    weight_next = weight - LEARN_RATE * (first_next / correction) / (jnp.sqrt(second_next / correction) + ADAM_EPS)
    return (weight_next, first_next, second_next)


def padded_rows(flat):
    short = -flat.shape[-1] % (16 * WIDTH)
    flat = jnp.pad(flat, ((0, 0), (0, short)))
    return flat.reshape(flat.shape[0], -1, WIDTH)


def stacked_blocks(full, n):
    return full.reshape(full.shape[0], n, -1, WIDTH).transpose(1, 0, 2, 3).reshape(n, -1, WIDTH)


def unstacked(blocks, count):
    n = blocks.shape[0]
    return blocks.reshape(n, count, -1, WIDTH).transpose(1, 0, 2, 3).reshape(count, -1, WIDTH)


def gather(shard):
    return lax.all_gather(shard, "fsdp", axis=0)


def reduce(blocks):
    mine = lax.psum_scatter(blocks, "fsdp", scatter_dimension=0, tiled=False)
    return lax.psum(mine, "dp")


def per_device(
    inputs,
    memory,
    cotangent,
    lengths,
    stacked_weights,
    expand_weights,
    contract_weights,
    scale_vectors,
    stacked_first,
    stacked_second,
    expand_first,
    expand_second,
    contract_first,
    contract_second,
    vector_first,
    vector_second,
):
    n = lax.axis_size("fsdp")
    width = WIDTH // n
    micro = inputs.shape[0]
    slabs = micro * lengths.shape[1]
    x = inputs.reshape(slabs, SLAB, WIDTH)
    mem = memory.reshape(slabs, SLAB, WIDTH)
    cot = cotangent.reshape(slabs, SLAB, WIDTH)
    u_self, u_cross, wt = mask_factors(lengths.reshape(slabs, 2, -1))

    vector_shard = padded_rows(scale_vectors.astype(BF).reshape(1, -1))[0]
    stacked_low = stacked_weights.astype(BF)
    head_shard = jnp.concatenate([stacked_low[:4].reshape(-1, WIDTH), vector_shard], axis=0)
    got_self = gather(head_shard)
    got_cross = gather(stacked_low[4:].reshape(-1, WIDTH))
    got_feed = gather(jnp.concatenate([expand_weights.astype(BF).reshape(-1, WIDTH), contract_weights.astype(BF)], axis=0))
    w_self = unstacked(got_self[:, : 4 * width], 4)
    vec = got_self[:, 4 * width :].reshape(n, -1)[:, : 9 * width].reshape(n, 9, width).transpose(1, 0, 2).reshape(9, WIDTH)
    vec = jnp.pad(vec.astype(F32), ((0, 7), (0, 0)))
    w_cross = unstacked(got_cross, 4)
    hidden = expand_weights.shape[1]
    rows = width * hidden // WIDTH
    ex = got_feed[:, :rows].reshape(WIDTH, hidden)
    co = got_feed[:, rows:].reshape(hidden, WIDTH)

    *saved1, unit1, scale1 = run_self_forward(x, w_self, vec, u_self, wt)
    *saved2, unit2, scale2 = run_cross_forward(unit1, mem, w_cross, vec, u_cross, wt)
    out, ds2, dex, dco, dvec3 = run_feed(unit2, cot, ex, co, vec)
    grad_feed = reduce(jnp.concatenate([dex.reshape(n, rows, WIDTH), dco.reshape(n, -1, WIDTH)], axis=1))
    dmem, ds1, dw_cross, dvec2 = run_cross_backward(ds2, unit2, scale2, unit1, mem, w_cross, vec, saved2)
    grad_cross = reduce(stacked_blocks(dw_cross, n))
    dx, dw_self, dvec1 = run_self_backward(ds1, unit1, scale1, x, w_self, vec, saved1)
    dvec = jnp.stack([d[row] for row in range(3) for d in (dvec1, dvec2, dvec3)])
    dvec = padded_rows(dvec.astype(BF).reshape(9, n, width).transpose(1, 0, 2).reshape(n, -1))
    grad_self = reduce(jnp.concatenate([stacked_blocks(dw_self, n), dvec], axis=1))

    grad_stacked = jnp.concatenate([grad_self[: 4 * width].reshape(4, width, WIDTH), grad_cross.reshape(4, width, WIDTH)], axis=0)
    grad_vector = grad_self[4 * width :].reshape(-1)[: 9 * width].reshape(9, width)
    grad_expand = grad_feed[:rows].reshape(width, hidden)
    grad_contract = grad_feed[rows:]
    correction = 1.0 - 0.5**STEP
    params_now = (stacked_weights, expand_weights, contract_weights, scale_vectors)
    firsts = (stacked_first, expand_first, contract_first, vector_first)
    seconds = (stacked_second, expand_second, contract_second, vector_second)
    grads = (grad_stacked, grad_expand, grad_contract, grad_vector)
    updates = [adam_update(p, f, s, g.astype(F32), correction) for p, f, s, g in zip(params_now, firsts, seconds, grads)]
    return (
        out.reshape(inputs.shape),
        dx.reshape(inputs.shape),
        dmem.reshape(inputs.shape),
        updates[0][0],
        updates[1][0],
        updates[2][0],
        updates[3][0],
        updates[0][1],
        updates[0][2],
        updates[1][1],
        updates[1][2],
        updates[2][1],
        updates[2][2],
        updates[3][1],
        updates[3][2],
    )


def solution(mesh):
    tokens = P(None, ("dp", "fsdp"), None)
    pieces = P(None, ("dp", "fsdp"), None, None)
    stacked = P(None, "fsdp", None)
    rows = P("fsdp", None)
    columns = P(None, "fsdp")
    return jax.shard_map(
        per_device,
        mesh=mesh,
        in_specs=(tokens, tokens, tokens, pieces, stacked, rows, rows, columns) + (stacked, stacked, rows, rows, rows, rows, columns, columns),
        out_specs=(tokens, tokens, tokens, stacked, rows, rows, columns) + (stacked, stacked, rows, rows, rows, rows, columns, columns),
        check_vma=False,
    )
```

```python
import functools
import math

import jax
import jax.numpy as jnp
import numpy as np
from jax import lax
from jax.experimental import pallas as pl
from jax.experimental.pallas import tpu as pltpu
from jax.sharding import PartitionSpec as P

HEADS = 8
HEAD = 64
SLAB = 512
WIDTH = 512
PAIR = 2 * HEAD
STEP = 3
NORM_EPS = 1e-05
ADAM_EPS = 1e-08
LEARN_RATE = 0.2
FAR = -1e30
LOG2E = math.log2(math.e)
QSCALE = HEAD**-0.5 * LOG2E
TILE = 256
BF = jnp.bfloat16
F32 = jnp.float32
MIB = 1 << 20


def nn(a, b):
    return jnp.dot(a, b, preferred_element_type=F32)


def nt(a, b):
    return lax.dot_general(a, b, (((1,), (1,)), ((), ())), preferred_element_type=F32)


def tn(a, b):
    return lax.dot_general(a, b, (((0,), (0,)), ((), ())), preferred_element_type=F32)


def norm_forward(residual, eps=NORM_EPS):
    centred = residual - jnp.mean(residual, axis=-1, keepdims=True)
    spread = jnp.mean(centred * centred, axis=-1, keepdims=True)
    scale = lax.rsqrt(spread + eps)
    return centred * scale, scale


def norm_backward(upstream, unit, scale, gain):
    inner = upstream * gain
    first = jnp.mean(inner, axis=-1, keepdims=True)
    second = jnp.mean(inner * unit, axis=-1, keepdims=True)
    return scale * (inner - first - unit * second)


def rows_sum(values):
    return jnp.sum(values, axis=0, keepdims=True)


def first_lanes(rows):
    return lax.broadcasted_iota(jnp.int32, (rows, PAIR), 1) < HEAD


def attend_forward(q_ref, k_ref, v_ref, queries_in, keys_out, e_ref, o_ref, r_ref, causal):
    low = first_lanes(SLAB)
    ones = jnp.ones((SLAB, PAIR), BF)
    spans = ((0, TILE, TILE), (TILE, SLAB, SLAB)) if causal else ((0, SLAB, SLAB),)
    if causal:
        query_at = lax.broadcasted_iota(jnp.int32, (TILE, TILE), 0)
        key_at = lax.broadcasted_iota(jnp.int32, (TILE, TILE), 1)
        bias = jnp.where(key_at <= query_at, 0.0, FAR).astype(F32)
        blank = jnp.zeros((TILE, TILE), BF)

    def lanes(head):
        return slice(head // 2 * PAIR, (head // 2 + 1) * PAIR)

    def scores(head):
        left, right = q_ref[:, lanes(head)], k_ref[:, lanes(head)]
        if head % 2 == 0:
            left, right = jnp.where(low, left, queries_in), jnp.where(low, right, keys_out)
        else:
            left, right = jnp.where(low, queries_in, left), jnp.where(low, keys_out, right)
        return [nt(left[first:last], right[:depth]) for first, last, depth in spans]

    def powers(head, found):
        results = []
        for (first, last, depth), part in zip(spans, found):
            if causal:
                end = part[:, depth - TILE :] + bias
                part = end if depth == TILE else jnp.concatenate([part[:, : depth - TILE], end], axis=1)
            power = jnp.exp2(part - jnp.max(part, axis=1, keepdims=True)).astype(BF)
            e_ref[head, first:last, :depth] = power
            if depth < SLAB:
                e_ref[head, first:last, depth:] = blank
            results.append(power)
        return results

    def mixes(head, found):
        right = jnp.concatenate([v_ref[:, lanes(head)], ones], axis=1)
        results = []
        for (_, _, depth), power in zip(spans, found):
            mixed = nn(power, right[:depth])
            inverse = 1.0 / mixed[:, PAIR:]
            results.append((mixed[:, :PAIR] * inverse, inverse))
        return results

    def put(pair, even, odd):
        for (first, last, _), (mix_0, inverse_0), (mix_1, inverse_1) in zip(spans, even, odd):
            here = first_lanes(last - first)
            o_ref[first:last, pair * PAIR : (pair + 1) * PAIR] = jnp.where(here, mix_0, mix_1).astype(BF)
            r_ref[first:last, pair * PAIR : (pair + 1) * PAIR] = jnp.where(here, inverse_0, inverse_1)

    following = scores(0)
    before = None
    mixed = {}
    for head in range(HEADS):
        found = following
        if head + 1 < HEADS:
            following = scores(head + 1)
        now = powers(head, found)
        if before is not None:
            mixed[head - 1] = mixes(head - 1, before)
            if head % 2 == 0:
                put(head // 2 - 1, mixed[head - 2], mixed[head - 1])
        before = now
    mixed[HEADS - 1] = mixes(HEADS - 1, before)
    put(HEADS // 2 - 1, mixed[HEADS - 2], mixed[HEADS - 1])


def attend_backward(load_powers, r_ref, o_ref, q_ref, k_ref, v_ref, dm_ref, dq_ref, dkt_ref, dvt_ref):
    low = first_lanes(SLAB)
    lane = lax.broadcasted_iota(jnp.int32, (SLAB, PAIR), 1) % HEAD
    units = jnp.where(lane < 2, 1.0, 0.0).astype(BF)
    none = jnp.zeros((), BF)
    qt = q_ref[...].T
    for pair in range(HEADS // 2):
        lanes = slice(pair * PAIR, (pair + 1) * PAIR)
        mixed = (dm_ref[:, lanes] * r_ref[:, lanes]).astype(BF)
        weighed = mixed.astype(F32) * o_ref[:, lanes].astype(F32)
        keys, values = k_ref[:, lanes], v_ref[:, lanes]
        mixed_t = mixed.T
        dq = []
        for side in range(2):
            head = 2 * pair + side
            rows = slice(head * HEAD, (head + 1) * HEAD)
            mine = low if side == 0 else ~low
            centre = jnp.sum(jnp.where(mine, weighed, 0.0), axis=1, keepdims=True)
            high = centre.astype(BF)
            rest = (centre - high.astype(F32)).astype(BF)
            column = jnp.where(lane == 0, -high, jnp.where(lane == 1, -rest, none))
            grad = nt(jnp.where(mine, mixed, column), jnp.where(mine, values, units))
            power = load_powers(head)
            score = (power.astype(F32) * grad).astype(BF)
            dq.append(nn(score, keys))
            dkt_ref[rows, :] = (nn(qt[rows], score) * (1.0 / LOG2E)).astype(BF)
            dvt_ref[rows, :] = nn(mixed_t[side * HEAD : (side + 1) * HEAD], power).astype(BF)
        dq_ref[:, lanes] = (jnp.where(low, dq[0], dq[1]) * HEAD**-0.5).astype(BF)


def piece_columns(lengths_ref, slab, side):
    column = lax.broadcasted_iota(jnp.int32, (1, PAIR), 1) % HEAD
    opening = jnp.zeros((1, PAIR), jnp.int32)
    closing = jnp.zeros((1, PAIR), jnp.int32)
    total = jnp.int32(0)
    for piece in range(lengths_ref.shape[2]):
        following = total + lengths_ref[slab, side, piece]
        opening = jnp.where(column == piece, total, opening)
        closing = jnp.where(column == piece, following, closing)
        total = following
    place = lax.broadcasted_iota(jnp.int32, (SLAB, PAIR), 0)
    return jnp.where((opening <= place) & (place < closing), 1.0, 0.0).astype(BF)


def outside(columns):
    return jnp.where(columns > 0, 0.0, FAR).astype(BF)


def load_pieces(place_ref, pieces, w_s, sems):
    copies = []
    for blocks in pieces:
        rows = blocks.shape[2]
        for index in range(blocks.shape[0]):
            start = pl.multiple_of(place_ref[len(copies)] * rows, rows)
            copies.append(pltpu.make_async_copy(blocks.at[index], w_s.at[:, pl.ds(start, rows), :], sems.at[len(copies)]))
    for copy in copies:
        copy.start()
    for copy in copies:
        copy.wait()


def load_once(place_ref, pieces, w_s, sems):
    @pl.when(pl.program_id(0) == 0)
    def _():
        load_pieces(place_ref, pieces, w_s, sems)


def self_forward(place_ref, lengths_ref, x_ref, own_ref, other_ref, w_ref, q_ref, k_ref, v_ref, e_ref, r_ref, o_ref, sems):
    load_once(place_ref, (own_ref, other_ref), w_ref, sems)
    x = x_ref[0]
    q_ref[0] = (nn(x, w_ref[0]) * QSCALE).astype(BF)
    k_ref[0] = nn(x, w_ref[1]).astype(BF)
    v_ref[0] = nn(x, w_ref[2]).astype(BF)
    columns = piece_columns(lengths_ref, pl.program_id(0), 0)
    attend_forward(q_ref.at[0], k_ref.at[0], v_ref.at[0], columns, outside(columns), e_ref.at[0], o_ref.at[0], r_ref.at[0], True)


def cross_forward(owners, place_ref, lengths_ref, o1_ref, x_ref, mem_ref, own_ref, other_ref, w_ref, vec_ref, q_ref, k_ref, v_ref, e_ref, r_ref, o_ref,
                  unit1_ref, scale1_ref, unit2_ref, scale2_ref, sems):
    load_once(place_ref, (own_ref, other_ref), w_ref, sems)

    @pl.when(pl.program_id(0) == 0)
    def _():
        rows = WIDTH // owners
        total = w_ref[5, 0:16, :].astype(F32)
        for owner in range(1, owners):
            total = total + w_ref[5, owner * rows : owner * rows + 16, :].astype(F32)
        vec_ref[...] = total

    residual = vec_ref[6:7, :] * x_ref[0].astype(F32) + nn(o1_ref[0], w_ref[0])
    unit, scale = norm_forward(residual)
    unit1_ref[0] = unit
    scale1_ref[0] = scale
    state = unit * vec_ref[0:1, :] + vec_ref[3:4, :]
    memory = mem_ref[0]
    q_ref[0] = (nn(state.astype(BF), w_ref[1]) * QSCALE).astype(BF)
    k_ref[0] = nn(memory, w_ref[2]).astype(BF)
    v_ref[0] = nn(memory, w_ref[3]).astype(BF)
    slab = pl.program_id(0)
    queries_in, keys_out = piece_columns(lengths_ref, slab, 0), outside(piece_columns(lengths_ref, slab, 1))
    attend_forward(q_ref.at[0], k_ref.at[0], v_ref.at[0], queries_in, keys_out, e_ref.at[0], o_ref.at[0], r_ref.at[0], False)
    residual = vec_ref[7:8, :] * state + nn(o_ref[0], w_ref[4])
    unit, scale = norm_forward(residual)
    unit2_ref[0] = unit
    scale2_ref[0] = scale


CUBE = 0.044715
ROOT = math.sqrt(2.0 / math.pi)


def load_feed(place_ref, pieces, ex_s, co_s, sems):
    each = co_s.shape[1]
    copies = []
    number = 0
    for blocks in pieces:
        rows = blocks.shape[2]
        for index in range(blocks.shape[0]):
            start = place_ref[number] * rows
            number += 1
            owner = start // each
            aligned = pl.multiple_of(start, rows)
            copies.append(pltpu.make_async_copy(blocks.at[index, 0:4], ex_s.at[:, pl.ds(aligned, rows), :], sems.at[len(copies)]))
            inside = pl.multiple_of(start - owner * each, rows)
            copies.append(pltpu.make_async_copy(blocks.at[index, 4:8], co_s.at[pl.ds(owner * 4, 4), pl.ds(inside, rows), :], sems.at[len(copies)]))
    for copy in copies:
        copy.start()
    for copy in copies:
        copy.wait()


def feed_both(place_ref, unit2_ref, cot_ref, own_ref, other_ref, vec_ref, out_ref, ds_ref, dw_ref, dvec_ref, act_s, slope_s, dex_s, dco_s, ex_s, co_s, sems):
    step = pl.program_id(0)
    steps = pl.num_programs(0)
    chunk = WIDTH
    chunks = ex_s.shape[0]
    owners = co_s.shape[0] // 4
    each = co_s.shape[1]

    @pl.when(step == 0)
    def _():
        load_feed(place_ref, (own_ref, other_ref), ex_s, co_s, sems)
        dex_s[...] = jnp.zeros_like(dex_s)
        dco_s[...] = jnp.zeros_like(dco_s)
        dvec_ref[...] = jnp.zeros_like(dvec_ref)

    def contract(part):
        return co_s[part * owners : (part + 1) * owners].reshape(chunk, WIDTH)

    state = unit2_ref[0] * vec_ref[1:2, :] + vec_ref[4:5, :]
    low = state.astype(BF)
    branch = None
    for part in range(chunks):
        cols = slice(part * chunk, (part + 1) * chunk)
        u = nn(low, ex_s[part])
        square = u * u
        bend = jnp.tanh(u * (ROOT + (ROOT * CUBE) * square))
        half = 0.5 + 0.5 * bend
        active = (u * half).astype(BF)
        act_s[:, cols] = active
        slope_s[:, cols] = half + (u * half) * (1.0 - bend) * (ROOT + (3.0 * ROOT * CUBE) * square)
        now = nn(active, contract(part))
        branch = now if branch is None else branch + now
    unit, scale = norm_forward(vec_ref[8:9, :] * state + branch)
    out_ref[0] = (unit * vec_ref[2:3, :] + vec_ref[5:6, :]).astype(BF)
    up = cot_ref[0].astype(F32)
    dvec_ref[0:1, :] += rows_sum(up * unit)
    dvec_ref[1:2, :] += rows_sum(up)
    dres = norm_backward(up, unit, scale, vec_ref[2:3, :])
    dvec_ref[2:3, :] += rows_sum(dres * state)
    dstate = dres * vec_ref[8:9, :]
    dbranch = dres.astype(BF)
    low_t = low.T
    for part in range(chunks):
        cols = slice(part * chunk, (part + 1) * chunk)
        dco_s[part] += tn(act_s[:, cols], dbranch)
        dhid = (nt(dbranch, contract(part)) * slope_s[:, cols]).astype(BF)
        dex_s[part] += nn(low_t, dhid)
        dstate = dstate + nt(dhid, ex_s[part])
    ds_ref[0] = dstate

    @pl.when(step == steps - 1)
    def _():
        for owner in range(owners):
            for part in range(4):
                dw_ref[owner, part] = dex_s[part, owner * each : (owner + 1) * each, :].astype(BF)
                row = (owner * 4 + part) * each
                dw_ref[owner, 4 + part] = dco_s[row // chunk, row % chunk : row % chunk + each, :].astype(BF)


def put_gradients(place_ref, dw_s, keep_ref, send_ref, first):
    blocks = keep_ref.shape[0]
    owners = blocks // dw_s.shape[0]
    rows = WIDTH // (2 * owners)
    core = place_ref[0]
    for matrix in range(dw_s.shape[0]):
        for owner in range(owners):
            at = 1 + matrix * owners + owner
            start = pl.multiple_of((2 * owner + core) * rows, rows)
            keep_ref[place_ref[at], first : first + rows, :] = dw_s[matrix, pl.ds(start, rows), :].astype(BF)
            start = pl.multiple_of((2 * owner + 1 - core) * rows, rows)
            send_ref[place_ref[at + blocks], first : first + rows, :] = dw_s[matrix, pl.ds(start, rows), :].astype(BF)


def put_vectors(place_ref, dvec_s, count, keep_ref, send_ref, first):
    blocks = keep_ref.shape[0]
    owners = blocks // count
    columns = WIDTH // (2 * owners)
    core = place_ref[0]
    rows = slice(first, first + 16)
    blank = jnp.zeros((16, WIDTH), BF)
    for block in range(blocks):
        keep_ref[block, rows, :] = blank
        send_ref[block, rows, :] = blank
    for owner in range(owners):
        low = dvec_s[:, 2 * owner * columns : (2 * owner + 1) * columns]
        high = dvec_s[:, (2 * owner + 1) * columns : (2 * owner + 2) * columns]
        rest = jnp.zeros((16, WIDTH - columns), F32)
        own = jnp.where(core == 0, low, high)
        other = jnp.where(core == 0, high, low)
        at = 1 + owner
        keep_ref[place_ref[at], rows, :] = jnp.concatenate([own, rest], axis=1).astype(BF)
        send_ref[place_ref[at + blocks], rows, :] = jnp.concatenate([other, rest], axis=1).astype(BF)


def powers_loader(e_ref, e_s, sems):
    step = pl.program_id(0)
    slabs = e_s.shape[0]

    def copy(slab, head):
        return pltpu.make_async_copy(e_ref.at[slab, head], e_s.at[slab, head], sems.at[slab, head])

    @pl.when(step == 0)
    def _():
        for slab in range(slabs):
            for head in range(HEADS):
                copy(slab, head).start()

    def load(head):
        copy(step, head).wait()
        return e_s[step, head]

    return load


def cross_backward(place_ref, ds2_ref, unit2_ref, scale2_ref, unit1_ref, mem_ref, w_ref, vec_ref, q_ref, k_ref, v_ref, e_ref, r_ref, o_ref,
                   dmem_ref, ds1_ref, keep_ref, send_ref, dvec_ref, dm_s, dq_s, dkt_s, dvt_s, dw_s, e_s, sems):
    step = pl.program_id(0)
    steps = pl.num_programs(0)
    load = powers_loader(e_ref, e_s, sems)

    @pl.when(step == 0)
    def _():
        dw_s[...] = jnp.zeros_like(dw_s)
        dvec_ref[...] = jnp.zeros_like(dvec_ref)

    up = ds2_ref[0]
    unit = unit2_ref[0]
    state = unit1_ref[0] * vec_ref[0:1, :] + vec_ref[3:4, :]
    dvec_ref[0:1, :] += rows_sum(up * unit)
    dvec_ref[1:2, :] += rows_sum(up)
    dres = norm_backward(up, unit, scale2_ref[0], vec_ref[1:2, :])
    dvec_ref[2:3, :] += rows_sum(dres * state)
    dbranch = dres.astype(BF)
    dw_s[3] += nn(o_ref[0].T, dbranch)
    dm_s[...] = nt(dbranch, w_ref[4])
    attend_backward(load, r_ref.at[0], o_ref.at[0], q_ref.at[0], k_ref.at[0], v_ref.at[0], dm_s, dq_s, dkt_s, dvt_s)
    dq = dq_s[...]
    ds1_ref[0] = dres * vec_ref[7:8, :] + nt(dq, w_ref[1])
    dw_s[0] += nn(state.astype(BF).T, dq)
    memory_t = mem_ref[0].T
    dk = dkt_s[...].T
    dv = dvt_s[...].T
    dw_s[1] += nn(memory_t, dk)
    dw_s[2] += nn(memory_t, dv)
    dmem_ref[0] = nt(dk, w_ref[2]) + nt(dv, w_ref[3])

    @pl.when(step == steps - 1)
    def _():
        put_gradients(place_ref, dw_s, keep_ref, send_ref, 0)


def self_backward(place_ref, ds1_ref, unit1_ref, scale1_ref, x_ref, w_ref, w3_ref, vec_ref, dvec2_ref, dvec3_ref, keep2_ref, send2_ref,
                  q_ref, k_ref, v_ref, e_ref, r_ref, o_ref, dx_ref, keep_ref, send_ref, dm_s, dq_s, dkt_s, dvt_s, dw_s, e_s, sems, dvec_s):
    step = pl.program_id(0)
    steps = pl.num_programs(0)
    load = powers_loader(e_ref, e_s, sems)

    @pl.when(step == 0)
    def _():
        dw_s[...] = jnp.zeros_like(dw_s)
        dvec_s[...] = jnp.zeros_like(dvec_s)

    up = ds1_ref[0]
    unit = unit1_ref[0]
    x = x_ref[0]
    dvec_s[0:1, :] += rows_sum(up * unit)
    dvec_s[3:4, :] += rows_sum(up)
    dres = norm_backward(up, unit, scale1_ref[0], vec_ref[0:1, :])
    dvec_s[6:7, :] += rows_sum(dres * x.astype(F32))
    dbranch = dres.astype(BF)
    dw_s[3] += nn(o_ref[0].T, dbranch)
    dm_s[...] = nt(dbranch, w3_ref[0])
    attend_backward(load, r_ref.at[0], o_ref.at[0], q_ref.at[0], k_ref.at[0], v_ref.at[0], dm_s, dq_s, dkt_s, dvt_s)
    dq = dq_s[...]
    dk = dkt_s[...].T
    dv = dvt_s[...].T
    dx_ref[0] = dres * vec_ref[6:7, :] + nt(dq, w_ref[0]) + nt(dk, w_ref[1]) + nt(dv, w_ref[2])
    x_t = x.T
    dw_s[0] += nn(x_t, dq)
    dw_s[1] += nn(x_t, dk)
    dw_s[2] += nn(x_t, dv)

    @pl.when(step == steps - 1)
    def _():
        rows = keep2_ref.shape[1]
        for row in range(3):
            dvec_s[3 * row + 1 : 3 * row + 2, :] = dvec2_ref[row : row + 1, :]
            dvec_s[3 * row + 2 : 3 * row + 3, :] = dvec3_ref[row : row + 1, :]
        put_gradients(place_ref, dw_s, keep_ref, send_ref, 0)
        put_vectors(place_ref, dvec_s, dw_s.shape[0], keep_ref, send_ref, rows)
        keep_ref[:, rows + 16 :, :] = keep2_ref[...]
        send_ref[:, rows + 16 :, :] = send2_ref[...]


def cut_shards(parts_ref, stacked_ref, expand_ref, contract_ref, vec_ref, a_ref, b_ref, c_ref):
    rows = stacked_ref.shape[1]
    half = pl.ds(pl.multiple_of(parts_ref[0] * (rows // 2), rows // 2), rows // 2)
    start = parts_ref[1] * (rows // 4)
    quarter = pl.ds(pl.multiple_of(start, rows // 4), rows // 4)
    for matrix in range(3):
        a_ref[0, matrix] = stacked_ref[matrix, half, :].astype(BF)
    for matrix in range(3, 8):
        b_ref[0, matrix - 3] = stacked_ref[matrix, quarter, :].astype(BF)
    vec = jnp.concatenate([vec_ref[...]] * (WIDTH // vec_ref.shape[1]), axis=1)
    owner = lax.broadcasted_iota(jnp.int32, vec.shape, 1) // vec_ref.shape[1]
    vec = jnp.where(owner == parts_ref[2], vec, 0.0)
    b_ref[0, 5] = jnp.concatenate([vec, jnp.zeros((16 - vec.shape[0], WIDTH), F32)], axis=0).astype(BF)
    for part in range(4):
        c_ref[0, part] = expand_ref[quarter, part * WIDTH : (part + 1) * WIDTH].astype(BF)
        c_ref[0, 4 + part] = contract_ref[pl.ds(pl.multiple_of(part * rows + start, rows // 4), rows // 4), :].astype(BF)


def per_slab(*tail):
    return pl.BlockSpec((1,) + tail, lambda m: (m,) + (0,) * len(tail))


def fixed(*dims):
    return pl.BlockSpec(dims, lambda m: (0,) * len(dims))


def shape(dims, kind):
    return jax.ShapeDtypeStruct(tuple(dims), kind)


def options():
    return pltpu.CompilerParams(dimension_semantics=("arbitrary",), vmem_limit_bytes=60 * MIB)


def estimate(microseconds):
    return pl.CostEstimate(flops=int(microseconds * 1e9), bytes_accessed=1 << 20, transcendentals=0)


SCALARS = pl.BlockSpec(memory_space=pltpu.SMEM)
ANYWHERE = pl.BlockSpec(memory_space=pl.ANY)


def attention_saved(g, powers=None):
    rows = per_slab(SLAB, WIDTH)
    return (
        [rows, rows, rows, powers or per_slab(HEADS, SLAB, SLAB), rows, rows],
        [shape((g, SLAB, WIDTH), BF)] * 3 + [shape((g, HEADS, SLAB, SLAB), BF), shape((g, SLAB, WIDTH), F32), shape((g, SLAB, WIDTH), BF)],
    )


def run_cut_shards(parts, stacked, expand, contract, vec):
    rows = stacked.shape[1]
    whole = pl.BlockSpec(memory_space=pltpu.VMEM)
    return pl.pallas_call(
        cut_shards,
        in_specs=[SCALARS, whole, whole, whole, whole],
        out_specs=[whole, whole, whole],
        out_shape=[shape((1, 3, rows // 2, WIDTH), BF), shape((1, 6, rows // 4, WIDTH), BF), shape((1, 8, rows // 4, WIDTH), BF)],
        compiler_params=pltpu.CompilerParams(vmem_limit_bytes=60 * MIB),
        name="cut_shards",
    )(parts, stacked, expand, contract, vec)


def run_self_forward(place, lengths, x, w):
    g = x.shape[0]
    specs, shapes = attention_saved(g)
    return pl.pallas_call(
        self_forward,
        grid=(g,),
        in_specs=[SCALARS, SCALARS, per_slab(SLAB, WIDTH), ANYWHERE, ANYWHERE],
        out_specs=[fixed(3, WIDTH, WIDTH)] + specs,
        out_shape=[shape((3, WIDTH, WIDTH), BF)] + shapes,
        scratch_shapes=[pltpu.SemaphoreType.DMA((sum(piece.shape[0] for piece in w),))],
        compiler_params=options(),
        cost_estimate=estimate(15),
        name="self_forward",
    )(place, lengths, x, *w)


def run_cross_forward(owners, place, lengths, o1, x, memory, w):
    g = memory.shape[0]
    specs, shapes = attention_saved(g)
    norm_specs, norm_shapes = [per_slab(SLAB, WIDTH), per_slab(SLAB, 1)], [shape((g, SLAB, WIDTH), F32), shape((g, SLAB, 1), F32)]
    return pl.pallas_call(
        functools.partial(cross_forward, owners),
        grid=(g,),
        in_specs=[SCALARS, SCALARS, per_slab(SLAB, WIDTH), per_slab(SLAB, WIDTH), per_slab(SLAB, WIDTH), ANYWHERE, ANYWHERE],
        out_specs=[fixed(6, WIDTH, WIDTH), fixed(16, WIDTH)] + specs + norm_specs * 2,
        out_shape=[shape((6, WIDTH, WIDTH), BF), shape((16, WIDTH), F32)] + shapes + norm_shapes * 2,
        scratch_shapes=[pltpu.SemaphoreType.DMA((sum(piece.shape[0] for piece in w),))],
        compiler_params=options(),
        cost_estimate=estimate(22),
        name="cross_forward",
    )(place, lengths, o1, x, memory, *w)


def run_feed(owners, place, unit2, cot, w, vec):
    g = unit2.shape[0]
    rows = WIDTH // owners
    pieces = sum(piece.shape[0] for piece in w)
    return pl.pallas_call(
        feed_both,
        grid=(g,),
        in_specs=[SCALARS, per_slab(SLAB, WIDTH), per_slab(SLAB, WIDTH), ANYWHERE, ANYWHERE, fixed(16, WIDTH)],
        out_specs=[per_slab(SLAB, WIDTH), per_slab(SLAB, WIDTH), fixed(owners, 8, rows, WIDTH), fixed(8, WIDTH)],
        out_shape=[shape((g, SLAB, WIDTH), BF), shape((g, SLAB, WIDTH), F32), shape((owners, 8, rows, WIDTH), BF), shape((8, WIDTH), F32)],
        scratch_shapes=[
            pltpu.VMEM((SLAB, 4 * WIDTH), BF),
            pltpu.VMEM((SLAB, 4 * WIDTH), F32),
            pltpu.VMEM((4, WIDTH, WIDTH), F32),
            pltpu.VMEM((4, WIDTH, WIDTH), F32),
            pltpu.VMEM((4, WIDTH, WIDTH), BF),
            pltpu.VMEM((4 * owners, rows, WIDTH), BF),
            pltpu.SemaphoreType.DMA((2 * pieces,)),
        ],
        compiler_params=options(),
        cost_estimate=estimate(24),
        name="feed_both",
    )(place, unit2, cot, *w, vec)


def backward_scratch(g):
    return [
        pltpu.VMEM((SLAB, WIDTH), F32),
        pltpu.VMEM((SLAB, WIDTH), BF),
        pltpu.VMEM((WIDTH, SLAB), BF),
        pltpu.VMEM((WIDTH, SLAB), BF),
        pltpu.VMEM((4, WIDTH, WIDTH), F32),
        pltpu.VMEM((g, HEADS, SLAB, SLAB), BF),
        pltpu.SemaphoreType.DMA((g, HEADS)),
    ]


def gradient_blocks(owners, rows):
    return [fixed(4 * owners, rows, WIDTH)] * 2, [shape((4 * owners, rows, WIDTH), BF)] * 2


def run_cross_backward(place, owners, ds2, unit2, scale2, unit1, memory, w, vec, saved):
    g = memory.shape[0]
    specs, _ = attention_saved(g, ANYWHERE)
    block_specs, block_shapes = gradient_blocks(owners, WIDTH // (2 * owners))
    return pl.pallas_call(
        cross_backward,
        grid=(g,),
        in_specs=[SCALARS, per_slab(SLAB, WIDTH), per_slab(SLAB, WIDTH), per_slab(SLAB, 1), per_slab(SLAB, WIDTH), per_slab(SLAB, WIDTH), fixed(6, WIDTH, WIDTH), fixed(16, WIDTH)] + specs,
        out_specs=[per_slab(SLAB, WIDTH), per_slab(SLAB, WIDTH)] + block_specs + [fixed(8, WIDTH)],
        out_shape=[shape((g, SLAB, WIDTH), F32), shape((g, SLAB, WIDTH), F32)] + block_shapes + [shape((8, WIDTH), F32)],
        scratch_shapes=backward_scratch(g),
        compiler_params=options(),
        cost_estimate=estimate(27),
        name="cross_backward",
    )(place, ds2, unit2, scale2, unit1, memory, w, vec, *saved)


def run_self_backward(place, owners, ds1, unit1, scale1, x, w, w_cross, vec, dvec2, dvec3, keep2, send2, saved):
    g = x.shape[0]
    specs, _ = attention_saved(g, ANYWHERE)
    rows = WIDTH // (2 * owners)
    block_specs, block_shapes = gradient_blocks(owners, 2 * rows + 16)
    other_specs, _ = gradient_blocks(owners, rows)
    return pl.pallas_call(
        self_backward,
        grid=(g,),
        in_specs=[SCALARS, per_slab(SLAB, WIDTH), per_slab(SLAB, WIDTH), per_slab(SLAB, 1), per_slab(SLAB, WIDTH), fixed(3, WIDTH, WIDTH), fixed(1, WIDTH, WIDTH), fixed(16, WIDTH), fixed(8, WIDTH), fixed(8, WIDTH)]
        + other_specs
        + specs,
        out_specs=[per_slab(SLAB, WIDTH)] + block_specs,
        out_shape=[shape((g, SLAB, WIDTH), F32)] + block_shapes,
        scratch_shapes=backward_scratch(g) + [pltpu.VMEM((16, WIDTH), F32)],
        compiler_params=options(),
        cost_estimate=estimate(25),
        name="self_backward",
    )(place, ds1, unit1, scale1, x, w, w_cross, vec, dvec2, dvec3, keep2, send2, *saved)


def adam_update(weight, first_moment, second_moment, gradient):
    correction = 1.0 - 0.5**STEP
    first_next = 0.5 * first_moment + 0.5 * gradient
    second_next = 0.5 * second_moment + 0.5 * gradient * gradient
    weight_next = weight - LEARN_RATE * (first_next / correction) / (jnp.sqrt(second_next / correction) + ADAM_EPS)
    return (weight_next, first_next, second_next)


def adam_stacked(order_ref, grad_ref, w_ref, m_ref, s_ref, w_out, m_out, s_out):
    rows = w_ref.shape[1]
    group = pl.program_id(0)

    def update(first):
        for matrix in range(4):
            grad = grad_ref[order_ref[matrix]].astype(F32)[first : first + rows]
            w_out[matrix], m_out[matrix], s_out[matrix] = adam_update(w_ref[matrix], m_ref[matrix], s_ref[matrix], grad)

    @pl.when(group == 0)
    def _():
        update(0)

    @pl.when(group == 1)
    def _():
        update(rows + 16)


def run_adam_stacked(order, grads, weight, first, second):
    rows = weight.shape[1]
    block = pl.BlockSpec((4, rows, WIDTH), lambda group: (group, 0, 0))
    return pl.pallas_call(
        adam_stacked,
        grid=(2,),
        in_specs=[SCALARS, fixed(*grads.shape), block, block, block],
        out_specs=[block, block, block],
        out_shape=[shape(weight.shape, F32)] * 3,
        compiler_params=options(),
        cost_estimate=estimate(4),
        name="adam_stacked",
    )(order, grads, weight, first, second)


def adam_feed(grad_ref, *refs):
    rows = grad_ref.shape[1]
    for part in range(4):
        where = (slice(None), slice(part * WIDTH, (part + 1) * WIDTH))
        refs[6][where], refs[7][where], refs[8][where] = adam_update(*(ref[where] for ref in refs[0:3]), grad_ref[part].astype(F32))
        where = (slice(part * rows, (part + 1) * rows), slice(None))
        refs[9][where], refs[10][where], refs[11][where] = adam_update(*(ref[where] for ref in refs[3:6]), grad_ref[4 + part].astype(F32))


def run_adam_feed(grads, expand, contract):
    arrays = tuple(expand) + tuple(contract)
    return pl.pallas_call(
        adam_feed,
        out_shape=[shape(a.shape, F32) for a in arrays],
        compiler_params=pltpu.CompilerParams(vmem_limit_bytes=60 * MIB),
        cost_estimate=estimate(4),
        name="adam_feed",
    )(grads, *arrays)


class Route:
    def __init__(self, m, n):
        self.m, self.n = m, n
        self.dp_bits = m.bit_length() - 1
        self.line_bits = n.bit_length() - 2
        self.line = n // 2

    def pairs(self, partner):
        return [(d * self.n + f, partner(d, f)) for d in range(self.m) for f in range(self.n)]

    def across_core(self):
        return self.pairs(lambda d, f: d * self.n + (f ^ 1))

    def across_line(self, step):
        def partner(d, f):
            bit = step if f % 2 == 0 else self.line_bits - 1 - step
            return d * self.n + (f ^ (2 << bit))

        return self.pairs(partner)

    def across_dp(self, step):
        def partner(d, f):
            bit = step if f % 2 == 0 else self.dp_bits - 1 - step
            return (d ^ (1 << bit)) * self.n + f

        return self.pairs(partner)

    @staticmethod
    def spot(mask, bits, core):
        return mask if core == 0 else sum(((mask >> b) & 1) << (bits - 1 - b) for b in range(bits))

    def part(self, share, d, f):
        return sum(((d >> (bit if f % 2 == 0 else self.dp_bits - 1 - bit)) & 1) << bit for bit in range(share))

    def gather_table(self, share):
        table = []
        for d in range(self.m):
            for f in range(self.n):
                z, c = divmod(f, 2)
                table.append(
                    [
                        ((2 * (z ^ self.spot(k, self.line_bits, who)) + who) << share) + (self.part(share, d, who) ^ step)
                        for who in (c, 1 - c)
                        for step in range(1 << share)
                        for k in range(self.line)
                    ]
                )
        return np.array(table, np.int32)

    def part_table(self, share):
        return np.array([self.part(share, d, f) for d in range(self.m) for f in range(self.n)], np.int32)

    def reduce_table(self):
        table = []
        for d in range(self.m):
            for f in range(self.n):
                z, c = divmod(f, 2)
                row = [c]
                for who in (c, 1 - c):
                    row += [
                        self.spot(j ^ d, self.dp_bits, who) * self.line + self.spot(owner ^ z, self.line_bits, who)
                        for j in range(self.m)
                        for owner in range(self.line)
                    ]
                row += [self.spot(j ^ d, self.dp_bits, c) for j in range(self.m)]
                table.append(row)
        return np.array(table, np.int32)


BOTH = ("dp", "fsdp")


def after(values, *earlier):
    return lax.optimization_barrier((values,) + earlier)[0]


def doubled(blocks, got):
    return jnp.concatenate([blocks, got], axis=0)


def per_device(
    inputs,
    memory,
    cotangent,
    lengths,
    stacked_weights,
    expand_weights,
    contract_weights,
    scale_vectors,
    stacked_first,
    stacked_second,
    expand_first,
    expand_second,
    contract_first,
    contract_second,
    vector_first,
    vector_second,
):
    m, n = lax.axis_size("dp"), lax.axis_size("fsdp")
    width = WIDTH // n
    slabs = inputs.shape[0] * lengths.shape[1]
    x = inputs.reshape(slabs, SLAB, WIDTH)
    mem = memory.reshape(slabs, SLAB, WIDTH)
    cot = cotangent.reshape(slabs, SLAB, WIDTH)
    by_hand = m == 4 and width == 64 and n == 8
    here = lax.axis_index("fsdp")
    lengths = lengths.reshape(slabs, 2, -1)
    if by_hand:
        route = Route(m, n)
        tables = (route.gather_table(1), route.gather_table(2), route.reduce_table(), route.part_table(1)[:, None], route.part_table(2)[:, None])
        ends = np.cumsum([0] + [table.shape[1] for table in tables])
        row = lax.dynamic_index_in_dim(jnp.asarray(np.concatenate(tables, axis=1)), lax.axis_index("dp") * n + here, keepdims=False)
        halves, quarters, reduced = (row[ends[i] : ends[i + 1]] for i in range(3))

        def swap(blocks, pairs):
            return lax.ppermute(blocks, BOTH, pairs)

        a, b, c = run_cut_shards(jnp.concatenate([row[ends[3] :], here[None]]), stacked_weights, expand_weights, contract_weights, scale_vectors)
        line = [route.across_line(step) for step in range(route.line_bits)]
        across = [route.across_dp(step) for step in range(route.dp_bits)]
        core = route.across_core()
        got = swap(a, line[0])
        a = doubled(a, got)
        b = after(b, got)
        got_a, got_b = swap(a, line[1]), swap(b, line[0])
        a, b = doubled(a, got_a), doubled(b, got_b)
        c = after(c, got_b)
        got_a, got_b, got_c = swap(a, across[0]), swap(b, line[1]), swap(c, line[0])
        a, b, c = doubled(a, got_a), doubled(b, got_b), doubled(c, got_c)
        got_a, got_b, got_c = swap(a, core), swap(b, across[0]), swap(c, line[1])
        b = doubled(b, got_b)
        got_b = swap(b, across[1])
        w_self, *saved1 = run_self_forward(halves, lengths, after(x, b), (a, got_a))
        got_b, got_c = after((got_b, got_c), saved1[-1])
        b, c = doubled(b, got_b), doubled(c, got_c)
        got_b, got_c = swap(b, core), swap(c, across[0])
        c = doubled(c, got_c)
        got_c = swap(c, across[1])
        w_cross, vec, *saved2, unit1, scale1, unit2, scale2 = run_cross_forward(n, quarters, lengths, saved1[-1], after(x, c), mem, (b, got_b))
        got_c = after(got_c, unit2)
        c = doubled(c, got_c)
        out, ds2, dw_feed, dvec3 = run_feed(n, quarters, unit2, cot, (c, swap(c, core)), vec)
        owners = n // 2
    else:
        reduced = jnp.array([0] + [0, 1, 2, 3] * 2, jnp.int32)
        halves = jnp.arange(2, dtype=jnp.int32)
        expand_blocks = jnp.swapaxes(expand_weights.reshape(width, 4, WIDTH), 0, 1)
        vec_shard = lax.dynamic_update_slice(jnp.zeros((16, WIDTH), BF), scale_vectors.astype(BF), (0, here * width))
        all_low = lax.all_gather(stacked_weights.astype(BF), "fsdp", axis=1, tiled=True)
        vec_full = jnp.sum(lax.all_gather(vec_shard, "fsdp", axis=0).astype(F32), axis=0).astype(BF)
        vec_full = jnp.pad(vec_full, ((0, WIDTH - 16), (0, 0)))
        ex = lax.all_gather(expand_blocks.astype(BF), "fsdp", axis=1, tiled=True).reshape(4, 2, -1, WIDTH)
        co = lax.all_gather(contract_weights.astype(BF), "fsdp", axis=0, tiled=True).reshape(2, 4, -1, WIDTH)
        w_self = tuple(all_low[None, :3].reshape(1, 3, 2, -1, WIDTH)[:, :, core] for core in range(2))
        w_cross = jnp.concatenate([all_low[3:], vec_full[None]], axis=0).reshape(1, 6, 2, -1, WIDTH)
        w_feed = tuple(jnp.concatenate([ex[:, core], co[core]], axis=0)[None] for core in range(2))
        w_self, *saved1 = run_self_forward(halves, lengths, x, w_self)
        w_cross, vec, *saved2, unit1, scale1, unit2, scale2 = run_cross_forward(1, halves, lengths, saved1[-1], x, mem, (w_cross[:, :, 0], w_cross[:, :, 1]))
        out, ds2, dw_feed, dvec3 = run_feed(2, halves, unit2, cot, w_feed, vec)
        owners = 1
        dex = jnp.swapaxes(dw_feed[:, :4], 0, 1).reshape(4, n, width, WIDTH)
        dco = dw_feed[:, 4:].reshape(n, 4, width, WIDTH)
        dw_feed = jnp.concatenate([jnp.swapaxes(dex, 0, 1), dco], axis=1)
    grad_feed = lax.psum_scatter(dw_feed, "fsdp", scatter_dimension=0, tiled=False)
    dmem, ds1, keep2, send2, dvec2 = run_cross_backward(reduced, owners, ds2, unit2, scale2, unit1, mem, w_cross, vec, saved2)
    dx, keep, send = run_self_backward(reduced, owners, ds1, unit1, scale1, x, w_self, w_cross, vec, dvec2, dvec3, keep2, send2, saved1)
    if by_hand:
        grad_feed = after(grad_feed, keep)
        got, got_feed = swap(send, core), swap(grad_feed, across[0])
        total = keep + got
        for step in (1, 0):
            half = total.shape[0] // 2
            total = total[:half] + swap(total[half:], across[step])
        grad_feed = after(grad_feed + got_feed, total)
        got_feed = swap(grad_feed, across[1])
        for step in (1, 0):
            half = total.shape[0] // 2
            total = total[:half] + swap(total[half:], line[step])
        for step in (0, 1):
            total = doubled(total, swap(total, across[step]))
        grad_feed = grad_feed + got_feed
        order = reduced[-m:]
        grad_vector = lax.dynamic_index_in_dim(total, order[0], keepdims=False)[width : width + 9, :width]
    else:
        both = jnp.stack([keep, send], axis=1)
        rows = both.shape[2] // 2 - 8
        grad_feed = lax.psum(grad_feed, "dp")
        grad_vector = lax.psum(both[0, :, rows : rows + 9, :rows].astype(F32), BOTH)
        grad_vector = jnp.swapaxes(grad_vector, 0, 1).reshape(9, WIDTH)
        grad_vector = lax.dynamic_slice(grad_vector, (0, here * width), (9, width))
        both = jnp.concatenate([both[:, :, :rows], both[:, :, rows + 16 :]], axis=0).reshape(8, WIDTH, WIDTH)
        both = lax.psum(lax.psum_scatter(both, "fsdp", scatter_dimension=1, tiled=True), "dp")
        total = jnp.concatenate([both[:4], jnp.zeros((4, 16, WIDTH), BF), both[4:]], axis=1)
        order = jnp.arange(4, dtype=jnp.int32)

    stacked_next = run_adam_stacked(order, total, stacked_weights, stacked_first, stacked_second)
    feed_next = run_adam_feed(grad_feed, (expand_weights, expand_first, expand_second), (contract_weights, contract_first, contract_second))
    expand_next, contract_next = feed_next[:3], feed_next[3:]
    vector_next = adam_update(scale_vectors, vector_first, vector_second, grad_vector.astype(F32))
    return (
        out.reshape(inputs.shape),
        dx.reshape(inputs.shape),
        dmem.reshape(inputs.shape),
        stacked_next[0],
        expand_next[0],
        contract_next[0],
        vector_next[0],
        stacked_next[1],
        stacked_next[2],
        expand_next[1],
        expand_next[2],
        contract_next[1],
        contract_next[2],
        vector_next[1],
        vector_next[2],
    )


def solution(mesh):
    tokens = P(None, ("dp", "fsdp"), None)
    pieces = P(None, ("dp", "fsdp"), None, None)
    stacked = P(None, "fsdp", None)
    rows = P("fsdp", None)
    columns = P(None, "fsdp")
    return jax.shard_map(
        per_device,
        mesh=mesh,
        in_specs=(tokens, tokens, tokens, pieces, stacked, rows, rows, columns) + (stacked, stacked, rows, rows, rows, rows, columns, columns),
        out_specs=(tokens, tokens, tokens, stacked, rows, rows, columns) + (stacked, stacked, rows, rows, rows, rows, columns, columns),
        check_vma=False,
    )
```

```python
import functools
import math

import jax
import jax.numpy as jnp
import numpy as np
from jax import lax
from jax.experimental import pallas as pl
from jax.experimental.pallas import tpu as pltpu
from jax.sharding import PartitionSpec as P

HEADS = 8
HEAD = 64
SLAB = 512
WIDTH = 512
PAIR = 2 * HEAD
STEP = 3
NORM_EPS = 1e-05
ADAM_EPS = 1e-08
LEARN_RATE = 0.2
FAR = -1e30
LOG2E = math.log2(math.e)
QSCALE = HEAD**-0.5 * LOG2E
TILE = 256
BF = jnp.bfloat16
F32 = jnp.float32
MIB = 1 << 20


def nn(a, b):
    return jnp.dot(a, b, preferred_element_type=F32)


def nt(a, b):
    return lax.dot_general(a, b, (((1,), (1,)), ((), ())), preferred_element_type=F32)


def tn(a, b):
    return lax.dot_general(a, b, (((0,), (0,)), ((), ())), preferred_element_type=F32)


def norm_forward(residual, eps=NORM_EPS):
    centred = residual - jnp.mean(residual, axis=-1, keepdims=True)
    spread = jnp.mean(centred * centred, axis=-1, keepdims=True)
    scale = lax.rsqrt(spread + eps)
    return centred * scale, scale


def norm_backward(upstream, unit, scale, gain):
    inner = upstream * gain
    first = jnp.mean(inner, axis=-1, keepdims=True)
    second = jnp.mean(inner * unit, axis=-1, keepdims=True)
    return scale * (inner - first - unit * second)


def rows_sum(values):
    return jnp.sum(values, axis=0, keepdims=True)


def first_lanes(rows):
    return lax.broadcasted_iota(jnp.int32, (rows, PAIR), 1) < HEAD


def attend_forward(q_ref, k_ref, v_ref, queries_in, keys_out, e_ref, o_ref, r_ref, causal):
    low = first_lanes(SLAB)
    ones = jnp.ones((SLAB, PAIR), BF)
    spans = ((0, TILE, TILE), (TILE, SLAB, SLAB)) if causal else ((0, SLAB, SLAB),)
    if causal:
        query_at = lax.broadcasted_iota(jnp.int32, (TILE, TILE), 0)
        key_at = lax.broadcasted_iota(jnp.int32, (TILE, TILE), 1)
        bias = jnp.where(key_at <= query_at, 0.0, FAR).astype(F32)
        blank = jnp.zeros((TILE, TILE), BF)

    def lanes(head):
        return slice(head // 2 * PAIR, (head // 2 + 1) * PAIR)

    def scores(head):
        left, right = q_ref[:, lanes(head)], k_ref[:, lanes(head)]
        if head % 2 == 0:
            left, right = jnp.where(low, left, queries_in), jnp.where(low, right, keys_out)
        else:
            left, right = jnp.where(low, queries_in, left), jnp.where(low, keys_out, right)
        return [nt(left[first:last], right[:depth]) for first, last, depth in spans]

    def powers(head, found):
        results = []
        for (first, last, depth), part in zip(spans, found):
            if causal:
                end = part[:, depth - TILE :] + bias
                part = end if depth == TILE else jnp.concatenate([part[:, : depth - TILE], end], axis=1)
            power = jnp.exp2(part - jnp.max(part, axis=1, keepdims=True)).astype(BF)
            e_ref[head, first:last, :depth] = power
            if depth < SLAB:
                e_ref[head, first:last, depth:] = blank
            results.append(power)
        return results

    def mixes(head, found):
        right = jnp.concatenate([v_ref[:, lanes(head)], ones], axis=1)
        results = []
        for (_, _, depth), power in zip(spans, found):
            mixed = nn(power, right[:depth])
            inverse = 1.0 / mixed[:, PAIR:]
            results.append((mixed[:, :PAIR] * inverse, inverse))
        return results

    def put(pair, even, odd):
        for (first, last, _), (mix_0, inverse_0), (mix_1, inverse_1) in zip(spans, even, odd):
            here = first_lanes(last - first)
            o_ref[first:last, pair * PAIR : (pair + 1) * PAIR] = jnp.where(here, mix_0, mix_1).astype(BF)
            r_ref[first:last, pair * PAIR : (pair + 1) * PAIR] = jnp.where(here, inverse_0, inverse_1)

    following = scores(0)
    before = None
    mixed = {}
    for head in range(HEADS):
        found = following
        if head + 1 < HEADS:
            following = scores(head + 1)
        now = powers(head, found)
        if before is not None:
            mixed[head - 1] = mixes(head - 1, before)
            if head % 2 == 0:
                put(head // 2 - 1, mixed[head - 2], mixed[head - 1])
        before = now
    mixed[HEADS - 1] = mixes(HEADS - 1, before)
    put(HEADS // 2 - 1, mixed[HEADS - 2], mixed[HEADS - 1])


def attend_backward(load_powers, r_ref, o_ref, q_ref, k_ref, v_ref, dm_ref, dq_ref, dkt_ref, dvt_ref):
    low = first_lanes(SLAB)
    lane = lax.broadcasted_iota(jnp.int32, (SLAB, PAIR), 1) % HEAD
    units = jnp.where(lane < 2, 1.0, 0.0).astype(BF)
    none = jnp.zeros((), BF)
    qt = q_ref[...].T
    for pair in range(HEADS // 2):
        lanes = slice(pair * PAIR, (pair + 1) * PAIR)
        mixed = (dm_ref[:, lanes] * r_ref[:, lanes]).astype(BF)
        weighed = mixed.astype(F32) * o_ref[:, lanes].astype(F32)
        keys, values = k_ref[:, lanes], v_ref[:, lanes]
        mixed_t = mixed.T
        dq = []
        for side in range(2):
            head = 2 * pair + side
            rows = slice(head * HEAD, (head + 1) * HEAD)
            mine = low if side == 0 else ~low
            centre = jnp.sum(jnp.where(mine, weighed, 0.0), axis=1, keepdims=True)
            high = centre.astype(BF)
            rest = (centre - high.astype(F32)).astype(BF)
            column = jnp.where(lane == 0, -high, jnp.where(lane == 1, -rest, none))
            grad = nt(jnp.where(mine, mixed, column), jnp.where(mine, values, units))
            power = load_powers(head)
            score = (power.astype(F32) * grad).astype(BF)
            dq.append(nn(score, keys))
            dkt_ref[rows, :] = (nn(qt[rows], score) * (1.0 / LOG2E)).astype(BF)
            dvt_ref[rows, :] = nn(mixed_t[side * HEAD : (side + 1) * HEAD], power).astype(BF)
        dq_ref[:, lanes] = (jnp.where(low, dq[0], dq[1]) * HEAD**-0.5).astype(BF)


def piece_columns(lengths_ref, slab, side):
    column = lax.broadcasted_iota(jnp.int32, (1, PAIR), 1) % HEAD
    opening = jnp.zeros((1, PAIR), jnp.int32)
    closing = jnp.zeros((1, PAIR), jnp.int32)
    total = jnp.int32(0)
    for piece in range(lengths_ref.shape[2]):
        following = total + lengths_ref[slab, side, piece]
        opening = jnp.where(column == piece, total, opening)
        closing = jnp.where(column == piece, following, closing)
        total = following
    place = lax.broadcasted_iota(jnp.int32, (SLAB, PAIR), 0)
    return jnp.where((opening <= place) & (place < closing), 1.0, 0.0).astype(BF)


def outside(columns):
    return jnp.where(columns > 0, 0.0, FAR).astype(BF)


def load_pieces(place_ref, pieces, w_s, sems):
    copies = []
    for blocks in pieces:
        rows = blocks.shape[2]
        for index in range(blocks.shape[0]):
            start = pl.multiple_of(place_ref[len(copies)] * rows, rows)
            copies.append(pltpu.make_async_copy(blocks.at[index], w_s.at[:, pl.ds(start, rows), :], sems.at[len(copies)]))
    for copy in copies:
        copy.start()
    for copy in copies:
        copy.wait()


def load_once(place_ref, pieces, w_s, sems):
    @pl.when(pl.program_id(0) == 0)
    def _():
        load_pieces(place_ref, pieces, w_s, sems)


def self_forward(count, place_ref, lengths_ref, x_ref, *refs):
    pieces, (w_ref, q_ref, k_ref, v_ref, e_ref, r_ref, o_ref, sems) = refs[:count], refs[count:]
    load_once(place_ref, pieces, w_ref, sems)
    x = x_ref[0]
    q_ref[0] = (nn(x, w_ref[0]) * QSCALE).astype(BF)
    k_ref[0] = nn(x, w_ref[1]).astype(BF)
    v_ref[0] = nn(x, w_ref[2]).astype(BF)
    columns = piece_columns(lengths_ref, pl.program_id(0), 0)
    attend_forward(q_ref.at[0], k_ref.at[0], v_ref.at[0], columns, outside(columns), e_ref.at[0], o_ref.at[0], r_ref.at[0], True)


def cross_inputs(count, owners, place_ref, o1_ref, x_ref, mem_ref, *refs):
    pieces, (w_ref, vec_ref, q_ref, k_ref, v_ref, unit1_ref, scale1_ref, sems) = refs[:count], refs[count:]
    load_once(place_ref, pieces, w_ref, sems)

    @pl.when(pl.program_id(0) == 0)
    def _():
        rows = WIDTH // owners
        total = w_ref[5, 0:16, :].astype(F32)
        for owner in range(1, owners):
            total = total + w_ref[5, owner * rows : owner * rows + 16, :].astype(F32)
        vec_ref[...] = total

    residual = vec_ref[6:7, :] * x_ref[0].astype(F32) + nn(o1_ref[0], w_ref[0])
    unit, scale = norm_forward(residual)
    unit1_ref[0] = unit
    scale1_ref[0] = scale
    state = unit * vec_ref[0:1, :] + vec_ref[3:4, :]
    memory = mem_ref[0]
    k_ref[0] = nn(memory, w_ref[2]).astype(BF)
    v_ref[0] = nn(memory, w_ref[3]).astype(BF)
    q_ref[0] = (nn(state.astype(BF), w_ref[1]) * QSCALE).astype(BF)


def cross_forward(lengths_ref, q_ref, k_ref, v_ref, unit1_ref, w_ref, vec_ref, e_ref, r_ref, o_ref, unit2_ref, scale2_ref):
    slab = pl.program_id(0)
    queries_in, keys_out = piece_columns(lengths_ref, slab, 0), outside(piece_columns(lengths_ref, slab, 1))
    attend_forward(q_ref.at[0], k_ref.at[0], v_ref.at[0], queries_in, keys_out, e_ref.at[0], o_ref.at[0], r_ref.at[0], False)
    state = unit1_ref[0] * vec_ref[0:1, :] + vec_ref[3:4, :]
    residual = vec_ref[7:8, :] * state + nn(o_ref[0], w_ref[0])
    unit, scale = norm_forward(residual)
    unit2_ref[0] = unit
    scale2_ref[0] = scale


CUBE = 0.044715
ROOT = math.sqrt(2.0 / math.pi)


def load_feed(place_ref, pieces, ex_s, co_s, sems):
    each = co_s.shape[1]
    copies = []
    number = 0
    for blocks in pieces:
        rows = blocks.shape[2]
        for index in range(blocks.shape[0]):
            start = place_ref[number] * rows
            number += 1
            owner = start // each
            aligned = pl.multiple_of(start, rows)
            copies.append(pltpu.make_async_copy(blocks.at[index, 0:4], ex_s.at[:, pl.ds(aligned, rows), :], sems.at[len(copies)]))
            inside = pl.multiple_of(start - owner * each, rows)
            copies.append(pltpu.make_async_copy(blocks.at[index, 4:8], co_s.at[pl.ds(owner * 4, 4), pl.ds(inside, rows), :], sems.at[len(copies)]))
    for copy in copies:
        copy.start()
    for copy in copies:
        copy.wait()


def feed_both(count, place_ref, reduce_ref, unit2_ref, cot_ref, vec_ref, *refs):
    pieces, (out_ref, ds_ref, keep_ref, send_ref, dvec_ref, act_s, slope_s, dex_s, dco_s, ex_s, co_s, sems) = refs[:count], refs[count:]
    step = pl.program_id(0)
    steps = pl.num_programs(0)
    chunk = WIDTH
    chunks = ex_s.shape[0]
    owners = co_s.shape[0] // 4
    each = co_s.shape[1]

    @pl.when(step == 0)
    def _():
        load_feed(place_ref, pieces, ex_s, co_s, sems)
        dex_s[...] = jnp.zeros_like(dex_s)
        dco_s[...] = jnp.zeros_like(dco_s)
        dvec_ref[...] = jnp.zeros_like(dvec_ref)

    def contract(part):
        return co_s[part * owners : (part + 1) * owners].reshape(chunk, WIDTH)

    state = unit2_ref[0] * vec_ref[1:2, :] + vec_ref[4:5, :]
    low = state.astype(BF)
    branch = None
    for part in range(chunks):
        cols = slice(part * chunk, (part + 1) * chunk)
        u = nn(low, ex_s[part])
        square = u * u
        bend = jnp.tanh(u * (ROOT + (ROOT * CUBE) * square))
        half = 0.5 + 0.5 * bend
        active = (u * half).astype(BF)
        act_s[:, cols] = active
        slope_s[:, cols] = half + (u * half) * (1.0 - bend) * (ROOT + (3.0 * ROOT * CUBE) * square)
        now = nn(active, contract(part))
        branch = now if branch is None else branch + now
    unit, scale = norm_forward(vec_ref[8:9, :] * state + branch)
    out_ref[0] = (unit * vec_ref[2:3, :] + vec_ref[5:6, :]).astype(BF)
    up = cot_ref[0].astype(F32)
    dvec_ref[0:1, :] += rows_sum(up * unit)
    dvec_ref[1:2, :] += rows_sum(up)
    dres = norm_backward(up, unit, scale, vec_ref[2:3, :])
    dvec_ref[2:3, :] += rows_sum(dres * state)
    dstate = dres * vec_ref[8:9, :]
    dbranch = dres.astype(BF)
    low_t = low.T
    for part in range(chunks):
        cols = slice(part * chunk, (part + 1) * chunk)
        dco_s[part] += tn(act_s[:, cols], dbranch)
        dhid = (nt(dbranch, contract(part)) * slope_s[:, cols]).astype(BF)
        dex_s[part] += nn(low_t, dhid)
        dstate = dstate + nt(dhid, ex_s[part])
    ds_ref[0] = dstate

    @pl.when(step == steps - 1)
    def _():
        put_feed(reduce_ref, dex_s, dco_s, keep_ref, send_ref)


def put_gradients(place_ref, dw_s, keep_ref, send_ref, first):
    blocks = keep_ref.shape[0]
    owners = blocks // dw_s.shape[0]
    rows = WIDTH // (2 * owners)
    core = place_ref[0]
    for matrix in range(dw_s.shape[0]):
        for owner in range(owners):
            at = 1 + matrix * owners + owner
            start = pl.multiple_of((2 * owner + core) * rows, rows)
            keep_ref[place_ref[at], first : first + rows, :] = dw_s[matrix, pl.ds(start, rows), :].astype(BF)
            start = pl.multiple_of((2 * owner + 1 - core) * rows, rows)
            send_ref[place_ref[at + blocks], first : first + rows, :] = dw_s[matrix, pl.ds(start, rows), :].astype(BF)


def put_vectors(place_ref, dvec_s, count, keep_ref, send_ref, first):
    blocks = keep_ref.shape[0]
    owners = blocks // count
    columns = WIDTH // (2 * owners)
    core = place_ref[0]
    rows = slice(first, first + 16)
    blank = jnp.zeros((16, WIDTH), BF)
    for block in range(blocks):
        keep_ref[block, rows, :] = blank
        send_ref[block, rows, :] = blank
    for owner in range(owners):
        low = dvec_s[:, 2 * owner * columns : (2 * owner + 1) * columns]
        high = dvec_s[:, (2 * owner + 1) * columns : (2 * owner + 2) * columns]
        rest = jnp.zeros((16, WIDTH - columns), F32)
        own = jnp.where(core == 0, low, high)
        other = jnp.where(core == 0, high, low)
        at = 1 + owner
        keep_ref[place_ref[at], rows, :] = jnp.concatenate([own, rest], axis=1).astype(BF)
        send_ref[place_ref[at + blocks], rows, :] = jnp.concatenate([other, rest], axis=1).astype(BF)


def put_feed(place_ref, dex_s, dco_s, keep_ref, send_ref):
    owners, _, each, _ = keep_ref.shape
    core = place_ref[0]
    for owner in range(owners):
        for out_ref, on, at in ((keep_ref, core, place_ref[1 + owner]), (send_ref, 1 - core, place_ref[1 + owners + owner])):
            shard = 2 * owner + on
            start = pl.multiple_of(shard * each, each)
            for part in range(4):
                out_ref[at, part] = dex_s[part, pl.ds(start, each), :].astype(BF)
                row = (shard * 4 + part) * each
                chunk = row // WIDTH
                out_ref[at, 4 + part] = dco_s[chunk, pl.ds(pl.multiple_of(row - chunk * WIDTH, each), each), :].astype(BF)


def powers_loader(e_ref, e_s, sems):
    step = pl.program_id(0)
    slabs = e_s.shape[0]

    def copy(slab, head):
        return pltpu.make_async_copy(e_ref.at[slab, head], e_s.at[slab, head], sems.at[slab, head])

    @pl.when(step == 0)
    def _():
        for slab in range(slabs):
            for head in range(HEADS):
                copy(slab, head).start()

    def load(head):
        copy(step, head).wait()
        return e_s[step, head]

    return load


def cross_backward(ds2_ref, unit2_ref, scale2_ref, unit1_ref, mem_ref, w_ref, vec_ref, q_ref, k_ref, v_ref, e_ref, r_ref, o_ref,
                   dmem_ref, ds1_ref, dw_ref, dvec_ref, dm_s, dq_s, dkt_s, dvt_s, dw_s, e_s, sems):
    step = pl.program_id(0)
    steps = pl.num_programs(0)
    load = powers_loader(e_ref, e_s, sems)

    @pl.when(step == 0)
    def _():
        dw_s[...] = jnp.zeros_like(dw_s)
        dvec_ref[...] = jnp.zeros_like(dvec_ref)

    up = ds2_ref[0]
    unit = unit2_ref[0]
    state = unit1_ref[0] * vec_ref[0:1, :] + vec_ref[3:4, :]
    dvec_ref[0:1, :] += rows_sum(up * unit)
    dvec_ref[1:2, :] += rows_sum(up)
    dres = norm_backward(up, unit, scale2_ref[0], vec_ref[1:2, :])
    dvec_ref[2:3, :] += rows_sum(dres * state)
    dbranch = dres.astype(BF)
    dw_s[3] += nn(o_ref[0].T, dbranch)
    dm_s[...] = nt(dbranch, w_ref[4])
    attend_backward(load, r_ref.at[0], o_ref.at[0], q_ref.at[0], k_ref.at[0], v_ref.at[0], dm_s, dq_s, dkt_s, dvt_s)
    dq = dq_s[...]
    ds1_ref[0] = dres * vec_ref[7:8, :] + nt(dq, w_ref[1])
    dw_s[0] += nn(state.astype(BF).T, dq)
    memory_t = mem_ref[0].T
    dk = dkt_s[...].T
    dv = dvt_s[...].T
    dw_s[1] += nn(memory_t, dk)
    dw_s[2] += nn(memory_t, dv)
    dmem_ref[0] = nt(dk, w_ref[2]) + nt(dv, w_ref[3])

    @pl.when(step == steps - 1)
    def _():
        dw_ref[...] = dw_s[...].astype(BF)


def self_backward(place_ref, ds1_ref, unit1_ref, scale1_ref, x_ref, w_ref, w3_ref, vec_ref, dvec2_ref, dvec3_ref, dw2_ref,
                  q_ref, k_ref, v_ref, e_ref, r_ref, o_ref, dx_ref, keep_ref, send_ref, dm_s, dq_s, dkt_s, dvt_s, dw_s, e_s, sems, dvec_s):
    step = pl.program_id(0)
    steps = pl.num_programs(0)
    load = powers_loader(e_ref, e_s, sems)

    @pl.when(step == 0)
    def _():
        dw_s[...] = jnp.zeros_like(dw_s)
        dvec_s[...] = jnp.zeros_like(dvec_s)

    up = ds1_ref[0]
    unit = unit1_ref[0]
    x = x_ref[0]
    dvec_s[0:1, :] += rows_sum(up * unit)
    dvec_s[3:4, :] += rows_sum(up)
    dres = norm_backward(up, unit, scale1_ref[0], vec_ref[0:1, :])
    dvec_s[6:7, :] += rows_sum(dres * x.astype(F32))
    dbranch = dres.astype(BF)
    dw_s[3] += nn(o_ref[0].T, dbranch)
    dm_s[...] = nt(dbranch, w3_ref[0])
    attend_backward(load, r_ref.at[0], o_ref.at[0], q_ref.at[0], k_ref.at[0], v_ref.at[0], dm_s, dq_s, dkt_s, dvt_s)
    dq = dq_s[...]
    dk = dkt_s[...].T
    dv = dvt_s[...].T
    dx_ref[0] = dres * vec_ref[6:7, :] + nt(dq, w_ref[0]) + nt(dk, w_ref[1]) + nt(dv, w_ref[2])
    x_t = x.T
    dw_s[0] += nn(x_t, dq)
    dw_s[1] += nn(x_t, dk)
    dw_s[2] += nn(x_t, dv)

    @pl.when(step == steps - 1)
    def _():
        for row in range(3):
            dvec_s[3 * row + 1 : 3 * row + 2, :] = dvec2_ref[row : row + 1, :]
            dvec_s[3 * row + 2 : 3 * row + 3, :] = dvec3_ref[row : row + 1, :]
        rows = (keep_ref.shape[1] - 16) // 2
        put_gradients(place_ref, dw_s, keep_ref, send_ref, 0)
        put_vectors(place_ref, dvec_s, dw_s.shape[0], keep_ref, send_ref, rows)
        put_gradients(place_ref, dw2_ref, keep_ref, send_ref, rows + 16)


def cut_shards(parts_ref, stacked_ref, expand_ref, contract_ref, vec_ref, a_ref, b_ref, c_ref):
    rows = stacked_ref.shape[1]
    half = pl.ds(pl.multiple_of(parts_ref[0] * (rows // 2), rows // 2), rows // 2)
    for matrix in range(3):
        a_ref[0, matrix] = stacked_ref[matrix, half, :].astype(BF)
    for matrix in range(3, 8):
        b_ref[0, matrix - 3] = stacked_ref[matrix, half, :].astype(BF)
    vec = jnp.concatenate([vec_ref[...]] * (WIDTH // vec_ref.shape[1]), axis=1)
    owner = lax.broadcasted_iota(jnp.int32, vec.shape, 1) // vec_ref.shape[1]
    vec = jnp.where(owner == parts_ref[2], vec, 0.0)
    b_ref[0, 5] = jnp.concatenate([vec, jnp.zeros((rows // 2 - vec.shape[0], WIDTH), F32)], axis=0).astype(BF)
    for part in range(4):
        start = parts_ref[1] * (rows // 4)
        quarter = pl.ds(pl.multiple_of(start, rows // 4), rows // 4)
        c_ref[0, part] = expand_ref[quarter, part * WIDTH : (part + 1) * WIDTH].astype(BF)
        c_ref[0, 4 + part] = contract_ref[pl.ds(pl.multiple_of(part * rows + start, rows // 4), rows // 4), :].astype(BF)


def per_slab(*tail):
    return pl.BlockSpec((1,) + tail, lambda m: (m,) + (0,) * len(tail))


def fixed(*dims):
    return pl.BlockSpec(dims, lambda m: (0,) * len(dims))


def shape(dims, kind):
    return jax.ShapeDtypeStruct(tuple(dims), kind)


def options():
    return pltpu.CompilerParams(dimension_semantics=("arbitrary",), vmem_limit_bytes=60 * MIB)


def estimate(microseconds):
    return pl.CostEstimate(flops=int(microseconds * 1e9), bytes_accessed=1 << 20, transcendentals=0)


SCALARS = pl.BlockSpec(memory_space=pltpu.SMEM)
ANYWHERE = pl.BlockSpec(memory_space=pl.ANY)


def attention_saved(g, powers=None):
    rows = per_slab(SLAB, WIDTH)
    return (
        [rows, rows, rows, powers or per_slab(HEADS, SLAB, SLAB), rows, rows],
        [shape((g, SLAB, WIDTH), BF)] * 3 + [shape((g, HEADS, SLAB, SLAB), BF), shape((g, SLAB, WIDTH), F32), shape((g, SLAB, WIDTH), BF)],
    )


def run_cut_shards(parts, stacked, expand, contract, vec):
    rows = stacked.shape[1]
    whole = pl.BlockSpec(memory_space=pltpu.VMEM)
    return pl.pallas_call(
        cut_shards,
        in_specs=[SCALARS, whole, whole, whole, whole],
        out_specs=[whole, whole, whole],
        out_shape=[shape((1, 3, rows // 2, WIDTH), BF), shape((1, 6, rows // 2, WIDTH), BF), shape((1, 8, rows // 4, WIDTH), BF)],
        compiler_params=pltpu.CompilerParams(vmem_limit_bytes=60 * MIB),
        name="cut_shards",
    )(parts, stacked, expand, contract, vec)


def run_self_forward(place, lengths, x, w):
    g = x.shape[0]
    specs, shapes = attention_saved(g)
    return pl.pallas_call(
        functools.partial(self_forward, len(w)),
        grid=(g,),
        in_specs=[SCALARS, SCALARS, per_slab(SLAB, WIDTH)] + [ANYWHERE] * len(w),
        out_specs=[fixed(3, WIDTH, WIDTH)] + specs,
        out_shape=[shape((3, WIDTH, WIDTH), BF)] + shapes,
        scratch_shapes=[pltpu.SemaphoreType.DMA((sum(piece.shape[0] for piece in w),))],
        compiler_params=options(),
        cost_estimate=estimate(15),
        name="self_forward",
    )(place, lengths, x, *w)


def run_cross_inputs(owners, place, o1, x, memory, w):
    g = memory.shape[0]
    rows = per_slab(SLAB, WIDTH)
    return pl.pallas_call(
        functools.partial(cross_inputs, len(w), owners),
        grid=(g,),
        in_specs=[SCALARS, rows, rows, rows] + [ANYWHERE] * len(w),
        out_specs=[fixed(6, WIDTH, WIDTH), fixed(16, WIDTH)] + [rows] * 4 + [per_slab(SLAB, 1)],
        out_shape=[shape((6, WIDTH, WIDTH), BF), shape((16, WIDTH), F32)] + [shape((g, SLAB, WIDTH), BF)] * 3 + [shape((g, SLAB, WIDTH), F32), shape((g, SLAB, 1), F32)],
        scratch_shapes=[pltpu.SemaphoreType.DMA((sum(piece.shape[0] for piece in w),))],
        compiler_params=options(),
        cost_estimate=estimate(7),
        name="cross_inputs",
    )(place, o1, x, memory, *w)


def run_cross_forward(lengths, q, k, v, unit1, w, vec):
    g = q.shape[0]
    rows = per_slab(SLAB, WIDTH)
    last = pl.BlockSpec((1, WIDTH, WIDTH), lambda m: (4, 0, 0))
    return pl.pallas_call(
        cross_forward,
        grid=(g,),
        in_specs=[SCALARS, rows, rows, rows, rows, last, fixed(16, WIDTH)],
        out_specs=[per_slab(HEADS, SLAB, SLAB), rows, rows, rows, per_slab(SLAB, 1)],
        out_shape=[shape((g, HEADS, SLAB, SLAB), BF), shape((g, SLAB, WIDTH), F32), shape((g, SLAB, WIDTH), BF), shape((g, SLAB, WIDTH), F32), shape((g, SLAB, 1), F32)],
        compiler_params=options(),
        cost_estimate=estimate(12),
        name="cross_forward",
    )(lengths, q, k, v, unit1, w, vec)


def run_feed(owners, place, reduce, unit2, cot, w, vec):
    g = unit2.shape[0]
    rows = WIDTH // owners
    pieces = sum(piece.shape[0] for piece in w)
    return pl.pallas_call(
        functools.partial(feed_both, len(w)),
        grid=(g,),
        in_specs=[SCALARS, SCALARS, per_slab(SLAB, WIDTH), per_slab(SLAB, WIDTH), fixed(16, WIDTH)] + [ANYWHERE] * len(w),
        out_specs=[per_slab(SLAB, WIDTH), per_slab(SLAB, WIDTH)] + [fixed(owners // 2, 8, rows, WIDTH)] * 2 + [fixed(8, WIDTH)],
        out_shape=[shape((g, SLAB, WIDTH), BF), shape((g, SLAB, WIDTH), F32)] + [shape((owners // 2, 8, rows, WIDTH), BF)] * 2 + [shape((8, WIDTH), F32)],
        scratch_shapes=[
            pltpu.VMEM((SLAB, 4 * WIDTH), BF),
            pltpu.VMEM((SLAB, 4 * WIDTH), F32),
            pltpu.VMEM((4, WIDTH, WIDTH), F32),
            pltpu.VMEM((4, WIDTH, WIDTH), F32),
            pltpu.VMEM((4, WIDTH, WIDTH), BF),
            pltpu.VMEM((4 * owners, rows, WIDTH), BF),
            pltpu.SemaphoreType.DMA((2 * pieces,)),
        ],
        compiler_params=options(),
        cost_estimate=estimate(24),
        name="feed_both",
    )(place, reduce, unit2, cot, vec, *w)


def backward_scratch(g):
    return [
        pltpu.VMEM((SLAB, WIDTH), F32),
        pltpu.VMEM((SLAB, WIDTH), BF),
        pltpu.VMEM((WIDTH, SLAB), BF),
        pltpu.VMEM((WIDTH, SLAB), BF),
        pltpu.VMEM((4, WIDTH, WIDTH), F32),
        pltpu.VMEM((g, HEADS, SLAB, SLAB), BF),
        pltpu.SemaphoreType.DMA((g, HEADS)),
    ]


def run_cross_backward(ds2, unit2, scale2, unit1, memory, w, vec, saved):
    g = memory.shape[0]
    specs, _ = attention_saved(g, ANYWHERE)
    return pl.pallas_call(
        cross_backward,
        grid=(g,),
        in_specs=[per_slab(SLAB, WIDTH), per_slab(SLAB, WIDTH), per_slab(SLAB, 1), per_slab(SLAB, WIDTH), per_slab(SLAB, WIDTH), fixed(6, WIDTH, WIDTH), fixed(16, WIDTH)] + specs,
        out_specs=[per_slab(SLAB, WIDTH), per_slab(SLAB, WIDTH), fixed(4, WIDTH, WIDTH), fixed(8, WIDTH)],
        out_shape=[shape((g, SLAB, WIDTH), F32), shape((g, SLAB, WIDTH), F32), shape((4, WIDTH, WIDTH), BF), shape((8, WIDTH), F32)],
        scratch_shapes=backward_scratch(g),
        compiler_params=options(),
        cost_estimate=estimate(25),
        name="cross_backward",
    )(ds2, unit2, scale2, unit1, memory, w, vec, *saved)


def run_self_backward(place, owners, ds1, unit1, scale1, x, w, w_cross, vec, dvec2, dvec3, dw2, saved):
    g = x.shape[0]
    specs, _ = attention_saved(g, ANYWHERE)
    rows = WIDTH // (2 * owners)
    dims = (4 * owners, 2 * rows + 16, WIDTH)
    return pl.pallas_call(
        self_backward,
        grid=(g,),
        in_specs=[SCALARS, per_slab(SLAB, WIDTH), per_slab(SLAB, WIDTH), per_slab(SLAB, 1), per_slab(SLAB, WIDTH), fixed(3, WIDTH, WIDTH), fixed(1, WIDTH, WIDTH), fixed(16, WIDTH), fixed(8, WIDTH), fixed(8, WIDTH)]
        + [fixed(4, WIDTH, WIDTH)]
        + specs,
        out_specs=[per_slab(SLAB, WIDTH)] + [fixed(*dims)] * 2,
        out_shape=[shape((g, SLAB, WIDTH), F32)] + [shape(dims, BF)] * 2,
        scratch_shapes=backward_scratch(g) + [pltpu.VMEM((16, WIDTH), F32)],
        compiler_params=options(),
        cost_estimate=estimate(25),
        name="self_backward",
    )(place, ds1, unit1, scale1, x, w, w_cross, vec, dvec2, dvec3, dw2, *saved)
def adam_update(weight, first_moment, second_moment, gradient):
    correction = 1.0 - 0.5**STEP
    first_next = 0.5 * first_moment + 0.5 * gradient
    second_next = 0.5 * second_moment + 0.5 * gradient * gradient
    weight_next = weight - LEARN_RATE * (first_next / correction) / (jnp.sqrt(second_next / correction) + ADAM_EPS)
    return (weight_next, first_next, second_next)


def adam_stacked(order_ref, grad_ref, w_ref, m_ref, s_ref, w_out, m_out, s_out):
    rows = w_ref.shape[1]
    group = pl.program_id(0)

    def update(first):
        for matrix in range(4):
            grad = grad_ref[order_ref[matrix]].astype(F32)[first : first + rows]
            w_out[matrix], m_out[matrix], s_out[matrix] = adam_update(w_ref[matrix], m_ref[matrix], s_ref[matrix], grad)

    @pl.when(group == 0)
    def _():
        update(0)

    @pl.when(group == 1)
    def _():
        update(rows + 16)


def run_adam_stacked(order, grads, weight, first, second):
    rows = weight.shape[1]
    block = pl.BlockSpec((4, rows, WIDTH), lambda group: (group, 0, 0))
    return pl.pallas_call(
        adam_stacked,
        grid=(2,),
        in_specs=[SCALARS, fixed(*grads.shape), block, block, block],
        out_specs=[block, block, block],
        out_shape=[shape(weight.shape, F32)] * 3,
        compiler_params=options(),
        cost_estimate=estimate(4),
        name="adam_stacked",
    )(order, grads, weight, first, second)


def adam_feed(grad_ref, *refs):
    rows = grad_ref.shape[1]
    for part in range(4):
        where = (slice(None), slice(part * WIDTH, (part + 1) * WIDTH))
        refs[6][where], refs[7][where], refs[8][where] = adam_update(*(ref[where] for ref in refs[0:3]), grad_ref[part].astype(F32))
        where = (slice(part * rows, (part + 1) * rows), slice(None))
        refs[9][where], refs[10][where], refs[11][where] = adam_update(*(ref[where] for ref in refs[3:6]), grad_ref[4 + part].astype(F32))


def run_adam_feed(grads, expand, contract):
    arrays = tuple(expand) + tuple(contract)
    return pl.pallas_call(
        adam_feed,
        out_shape=[shape(a.shape, F32) for a in arrays],
        compiler_params=pltpu.CompilerParams(vmem_limit_bytes=60 * MIB),
        cost_estimate=estimate(4),
        name="adam_feed",
    )(grads, *arrays)


class Route:
    def __init__(self, m, n):
        self.m, self.n = m, n
        self.dp_bits = m.bit_length() - 1
        self.line_bits = n.bit_length() - 2
        self.line = n // 2

    def pairs(self, partner):
        return [(d * self.n + f, partner(d, f)) for d in range(self.m) for f in range(self.n)]

    def across_core(self):
        return self.pairs(lambda d, f: d * self.n + (f ^ 1))

    def along_line(self, mask):
        return self.pairs(lambda d, f: d * self.n + (f ^ (2 * mask)))

    def across_line(self, step):
        def partner(d, f):
            bit = step if f % 2 == 0 else self.line_bits - 1 - step
            return d * self.n + (f ^ (2 << bit))

        return self.pairs(partner)

    def across_dp(self, step):
        def partner(d, f):
            bit = step if f % 2 == 0 else self.dp_bits - 1 - step
            return (d ^ (1 << bit)) * self.n + f

        return self.pairs(partner)

    @staticmethod
    def spot(mask, bits, core):
        return mask if core == 0 else sum(((mask >> b) & 1) << (bits - 1 - b) for b in range(bits))

    def part(self, share, d, f):
        return sum(((d >> (bit if f % 2 == 0 else self.dp_bits - 1 - bit)) & 1) << bit for bit in range(share))

    def gather_row(self, share, d, f):
        z, c = divmod(f, 2)
        return [
            ((2 * (z ^ k) + who) << share) + (self.part(share, d, who) ^ step)
            for who in (c, 1 - c)
            for step in range(1 << share)
            for k in range(self.line)
        ]

    def reduce_row(self, d, f):
        c = f % 2
        row = [c]
        for who in (c, 1 - c):
            row += [self.spot(j ^ d, self.dp_bits, who) * self.line + owner for j in range(self.m) for owner in range(self.line)]
        return row + [self.spot(j ^ d, self.dp_bits, c) for j in range(self.m)]

    def feed_row(self, d, f):
        z, c = divmod(f, 2)
        return [c] + [self.spot(owner ^ z, self.line_bits, who) for who in (c, 1 - c) for owner in range(self.line)]

    def part_row(self, d, f):
        return [self.part(1, d, f), self.part(2, d, f), f]

    def tables(self):
        kinds = (functools.partial(self.gather_row, 1), functools.partial(self.gather_row, 2), self.reduce_row, self.feed_row, self.part_row)
        rows = [[kind(d, f) for kind in kinds] for d in range(self.m) for f in range(self.n)]
        ends = np.cumsum([0] + [len(row) for row in rows[0]])
        return np.array([sum(row, []) for row in rows], np.int32), ends


BOTH = ("dp", "fsdp")


def after(values, *earlier):
    return lax.optimization_barrier((values,) + earlier)[0]


def doubled(blocks, got):
    return jnp.concatenate([blocks, got], axis=0)


def along_groups(blocks):
    line = blocks.shape[0]
    groups = [[2 * z + core for z in range(line)] for core in range(2)]
    return lax.all_to_all(blocks, "fsdp", 0, 0, tiled=True, axis_index_groups=groups)


def per_device(
    inputs,
    memory,
    cotangent,
    lengths,
    stacked_weights,
    expand_weights,
    contract_weights,
    scale_vectors,
    stacked_first,
    stacked_second,
    expand_first,
    expand_second,
    contract_first,
    contract_second,
    vector_first,
    vector_second,
):
    m, n = lax.axis_size("dp"), lax.axis_size("fsdp")
    width = WIDTH // n
    slabs = inputs.shape[0] * lengths.shape[1]
    x = inputs.reshape(slabs, SLAB, WIDTH)
    mem = memory.reshape(slabs, SLAB, WIDTH)
    cot = cotangent.reshape(slabs, SLAB, WIDTH)
    by_hand = m == 4 and width == 64 and n == 8
    here = lax.axis_index("fsdp")
    lengths = lengths.reshape(slabs, 2, -1)
    if by_hand:
        route = Route(m, n)
        table, ends = route.tables()
        row = lax.dynamic_index_in_dim(jnp.asarray(table), lax.axis_index("dp") * n + here, keepdims=False)
        halves, quarters, reduced, feed_order, parts = (row[ends[i] : ends[i + 1]] for i in range(5))

        def swap(blocks, pairs):
            return lax.ppermute(blocks, BOTH, pairs)

        along = [route.along_line(mask) for mask in range(1, n // 2)]
        line = [route.across_line(step) for step in range(route.line_bits)]
        across = [route.across_dp(step) for step in range(route.dp_bits)]
        core = route.across_core()
        a, b, c = run_cut_shards(parts, stacked_weights, expand_weights, contract_weights, scale_vectors)
        a = jnp.concatenate(lax.optimization_barrier((a, *(swap(a, pairs) for pairs in along))), axis=0)
        b = after(b, a)
        b_line = [swap(b, pairs) for pairs in along]
        a_across, a_core = lax.optimization_barrier((swap(a, across[0]), swap(a, core)))
        w_self, *saved1 = run_self_forward(halves, lengths, x, (a, a_across, a_core, swap(a_across, core)))
        b, c, *b_line = after((b, c, *b_line), saved1[-1])
        b = jnp.concatenate([b, *b_line], axis=0)
        b_across, b_core, *c_line = lax.optimization_barrier((swap(b, across[0]), swap(b, core), *(swap(c, pairs) for pairs in along)))
        c = jnp.concatenate([c, *c_line], axis=0)
        c_across = swap(c, across[0])
        w_cross = (b, b_across, b_core, swap(b_across, core))
        w_cross, vec, *qkv2, unit1, scale1 = run_cross_inputs(n, halves, saved1[-1], x, after(mem, c), w_cross)
        c = doubled(c, after(c_across, unit1))
        c_across, c_core = swap(c, across[1]), swap(c, core)
        *saved2, unit2, scale2 = run_cross_forward(lengths, *qkv2, after(unit1, c), w_cross, vec)
        saved2 = qkv2 + saved2
        c_across = after(c_across, unit2)
        w_feed = (c, c_across, c_core, swap(c_across, core))
        out, ds2, feed_keep, feed_send, dvec3 = run_feed(n, quarters, feed_order, unit2, cot, w_feed, vec)
        feed_got = swap(feed_send, core)
        dmem, ds1, dw2, dvec2 = run_cross_backward(ds2, unit2, scale2, unit1, mem, w_cross, vec, saved2)
        feed_got = after(feed_got, ds1)
        half = n // 4
        feed_out, feed = feed_keep[half:] + feed_got[half:], feed_keep[:half] + feed_got[:half]
        feed_got = swap(feed_out, line[1])
        dx, keep, send = run_self_backward(reduced, n // 2, after(ds1, feed_out), unit1, scale1, x, w_self, w_cross, vec, dvec2, dvec3, dw2, saved1)
        feed_got = after(feed_got, keep)
        got = swap(after(send, feed_got), core)
        out_part, total = keep[8:] + got[8:], keep[:8] + got[:8]
        feed_out, feed = feed[1:] + feed_got[1:], feed[:1] + feed_got[:1]
        got, feed_got = lax.optimization_barrier((swap(out_part, across[1]), swap(after(feed_out, out_part), line[0])))
        out_part, total = total[4:] + got[4:], total[:4] + got[:4]
        got = swap(out_part, across[0])
        feed = feed + feed_got
        total = total + got
        got, feed_got = lax.optimization_barrier((along_groups(total), swap(after(feed, total), across[0])))
        total = jnp.sum(got.astype(F32), axis=0, keepdims=True).astype(BF)
        feed = feed + feed_got
        got, feed_got = lax.optimization_barrier((swap(total, across[0]), swap(feed, across[1])))
        total = doubled(total, got)
        feed_next = run_adam_feed(after((feed + feed_got)[0], total), (expand_weights, expand_first, expand_second), (contract_weights, contract_first, contract_second))
        total = doubled(total, after(swap(total, across[1]), feed_next[0]))
        order = reduced[-m:]
        grad_vector = lax.dynamic_index_in_dim(total, order[0], keepdims=False)[width : width + 9, :width]
        stacked_next = run_adam_stacked(order, total, stacked_weights, stacked_first, stacked_second)
    else:
        reduced, feed_order = jnp.array([0] + [0, 1, 2, 3] * 2, jnp.int32), jnp.zeros((3,), jnp.int32)
        halves = jnp.arange(2, dtype=jnp.int32)
        expand_blocks = jnp.swapaxes(expand_weights.reshape(width, 4, WIDTH), 0, 1)
        vec_shard = lax.dynamic_update_slice(jnp.zeros((16, WIDTH), BF), scale_vectors.astype(BF), (0, here * width))
        all_low = lax.all_gather(stacked_weights.astype(BF), "fsdp", axis=1, tiled=True)
        vec_full = jnp.sum(lax.all_gather(vec_shard, "fsdp", axis=0).astype(F32), axis=0).astype(BF)
        vec_full = jnp.pad(vec_full, ((0, WIDTH - 16), (0, 0)))
        ex = lax.all_gather(expand_blocks.astype(BF), "fsdp", axis=1, tiled=True).reshape(4, 2, -1, WIDTH)
        co = lax.all_gather(contract_weights.astype(BF), "fsdp", axis=0, tiled=True).reshape(2, 4, -1, WIDTH)
        w_self = tuple(all_low[None, :3].reshape(1, 3, 2, -1, WIDTH)[:, :, core] for core in range(2))
        w_cross = jnp.concatenate([all_low[3:], vec_full[None]], axis=0).reshape(1, 6, 2, -1, WIDTH)
        w_feed = tuple(jnp.concatenate([ex[:, core], co[core]], axis=0)[None] for core in range(2))
        w_self, *saved1 = run_self_forward(halves, lengths, x, w_self)
        w_cross, vec, *qkv2, unit1, scale1 = run_cross_inputs(1, halves, saved1[-1], x, mem, (w_cross[:, :, 0], w_cross[:, :, 1]))
        *saved2, unit2, scale2 = run_cross_forward(lengths, *qkv2, unit1, w_cross, vec)
        saved2 = qkv2 + saved2
        out, ds2, feed_keep, feed_send, dvec3 = run_feed(2, halves, feed_order, unit2, cot, w_feed, vec)
        dw_feed = jnp.concatenate([feed_keep, feed_send], axis=0)
        dex = jnp.swapaxes(dw_feed[:, :4], 0, 1).reshape(4, n, width, WIDTH)
        dco = dw_feed[:, 4:].reshape(n, 4, width, WIDTH)
        dw_feed = jnp.concatenate([jnp.swapaxes(dex, 0, 1), dco], axis=1)
        grad_feed = lax.psum(lax.psum_scatter(dw_feed, "fsdp", scatter_dimension=0, tiled=False), "dp")
        dmem, ds1, dw2, dvec2 = run_cross_backward(ds2, unit2, scale2, unit1, mem, w_cross, vec, saved2)
        dx, keep, send = run_self_backward(reduced, 1, ds1, unit1, scale1, x, w_self, w_cross, vec, dvec2, dvec3, dw2, saved1)
        both = jnp.stack([keep, send], axis=1)
        rows = WIDTH // 2
        grad_vector = lax.psum(both[0, :, rows : rows + 9, :rows].astype(F32), BOTH)
        grad_vector = jnp.swapaxes(grad_vector, 0, 1).reshape(9, WIDTH)
        grad_vector = lax.dynamic_slice(grad_vector, (0, here * width), (9, width))
        both = jnp.concatenate([both[:, :, :rows], both[:, :, rows + 16 :]], axis=0).reshape(8, WIDTH, WIDTH)
        both = lax.psum(lax.psum_scatter(both, "fsdp", scatter_dimension=1, tiled=True), "dp")
        stacked_next = adam_update(stacked_weights, stacked_first, stacked_second, both.astype(F32))
        feed_next = run_adam_feed(grad_feed, (expand_weights, expand_first, expand_second), (contract_weights, contract_first, contract_second))
    expand_next, contract_next = feed_next[:3], feed_next[3:]
    vector_next = adam_update(scale_vectors, vector_first, vector_second, grad_vector.astype(F32))
    return (
        out.reshape(inputs.shape),
        dx.reshape(inputs.shape),
        dmem.reshape(inputs.shape),
        stacked_next[0],
        expand_next[0],
        contract_next[0],
        vector_next[0],
        stacked_next[1],
        stacked_next[2],
        expand_next[1],
        expand_next[2],
        contract_next[1],
        contract_next[2],
        vector_next[1],
        vector_next[2],
    )


def solution(mesh):
    tokens = P(None, ("dp", "fsdp"), None)
    pieces = P(None, ("dp", "fsdp"), None, None)
    stacked = P(None, "fsdp", None)
    rows = P("fsdp", None)
    columns = P(None, "fsdp")
    return jax.shard_map(
        per_device,
        mesh=mesh,
        in_specs=(tokens, tokens, tokens, pieces, stacked, rows, rows, columns) + (stacked, stacked, rows, rows, rows, rows, columns, columns),
        out_specs=(tokens, tokens, tokens, stacked, rows, rows, columns) + (stacked, stacked, rows, rows, rows, rows, columns, columns),
        check_vma=False,
    )
```

```python
import functools
import math

import jax
import jax.numpy as jnp
import numpy as np
from jax import lax
from jax.experimental import pallas as pl
from jax.experimental.pallas import tpu as pltpu
from jax.sharding import PartitionSpec as P

HEADS = 8
HEAD = 64
SLAB = 512
WIDTH = 512
PAIR = 2 * HEAD
STEP = 3
NORM_EPS = 1e-05
ADAM_EPS = 1e-08
LEARN_RATE = 0.2
FAR = -1e30
LOG2E = math.log2(math.e)
QSCALE = HEAD**-0.5 * LOG2E
TILE = 256
BF = jnp.bfloat16
F32 = jnp.float32
MIB = 1 << 20
FEED_MIB = 30
CROSS_MIB = 26
SELF_MIB = 40


def nn(a, b):
    return jnp.dot(a, b, preferred_element_type=F32)


def nt(a, b):
    return lax.dot_general(a, b, (((1,), (1,)), ((), ())), preferred_element_type=F32)


def tn(a, b):
    return lax.dot_general(a, b, (((0,), (0,)), ((), ())), preferred_element_type=F32)


def norm_forward(residual, eps=NORM_EPS):
    centred = residual - jnp.mean(residual, axis=-1, keepdims=True)
    spread = jnp.mean(centred * centred, axis=-1, keepdims=True)
    scale = lax.rsqrt(spread + eps)
    return centred * scale, scale


def norm_backward(upstream, unit, scale, gain):
    inner = upstream * gain
    first = jnp.mean(inner, axis=-1, keepdims=True)
    second = jnp.mean(inner * unit, axis=-1, keepdims=True)
    return scale * (inner - first - unit * second)


def rows_sum(values):
    return jnp.sum(values, axis=0, keepdims=True)


def first_lanes(rows):
    return lax.broadcasted_iota(jnp.int32, (rows, PAIR), 1) < HEAD


def attend_forward(q_ref, k_ref, v_ref, queries_in, keys_out, e_ref, o_ref, r_ref, causal, after=None):
    low = first_lanes(SLAB)
    ones = jnp.ones((SLAB, PAIR), BF)
    spans = ((0, TILE, TILE), (TILE, SLAB, SLAB)) if causal else ((0, SLAB, SLAB),)
    if causal:
        query_at = lax.broadcasted_iota(jnp.int32, (TILE, TILE), 0)
        key_at = lax.broadcasted_iota(jnp.int32, (TILE, TILE), 1)
        bias = jnp.where(key_at <= query_at, 0.0, FAR).astype(F32)
        blank = jnp.zeros((TILE, TILE), BF)

    def lanes(head):
        return slice(head // 2 * PAIR, (head // 2 + 1) * PAIR)

    def scores(head):
        left, right = q_ref[:, lanes(head)], k_ref[:, lanes(head)]
        if head % 2 == 0:
            left, right = jnp.where(low, left, queries_in), jnp.where(low, right, keys_out)
        else:
            left, right = jnp.where(low, queries_in, left), jnp.where(low, keys_out, right)
        return [nt(left[first:last], right[:depth]) for first, last, depth in spans]

    def powers(head, found):
        results = []
        for (first, last, depth), part in zip(spans, found):
            if causal:
                end = part[:, depth - TILE :] + bias
                part = end if depth == TILE else jnp.concatenate([part[:, : depth - TILE], end], axis=1)
            power = jnp.exp2(part - jnp.max(part, axis=1, keepdims=True)).astype(BF)
            e_ref[head, first:last, :depth] = power
            if depth < SLAB:
                e_ref[head, first:last, depth:] = blank
            results.append(power)
        if after is not None:
            after(head)
        return results

    def mixes(head, found):
        right = jnp.concatenate([v_ref[:, lanes(head)], ones], axis=1)
        results = []
        for (_, _, depth), power in zip(spans, found):
            mixed = nn(power, right[:depth])
            inverse = 1.0 / mixed[:, PAIR:]
            results.append((mixed[:, :PAIR] * inverse, inverse))
        return results

    def put(pair, even, odd):
        for (first, last, _), (mix_0, inverse_0), (mix_1, inverse_1) in zip(spans, even, odd):
            here = first_lanes(last - first)
            o_ref[first:last, pair * PAIR : (pair + 1) * PAIR] = jnp.where(here, mix_0, mix_1).astype(BF)
            r_ref[first:last, pair * PAIR : (pair + 1) * PAIR] = jnp.where(here, inverse_0, inverse_1).astype(BF)

    following = scores(0)
    earlier = None
    mixed = {}
    for head in range(HEADS):
        found = following
        if head + 1 < HEADS:
            following = scores(head + 1)
        now = powers(head, found)
        if earlier is not None:
            mixed[head - 1] = mixes(head - 1, earlier)
            if head % 2 == 0:
                put(head // 2 - 1, mixed[head - 2], mixed[head - 1])
        earlier = now
    mixed[HEADS - 1] = mixes(HEADS - 1, earlier)
    put(HEADS // 2 - 1, mixed[HEADS - 2], mixed[HEADS - 1])


def attend_backward(e_ref, r_ref, o_ref, q_ref, k_ref, v_ref, dm_ref, dq_ref, dkt_ref, dvt_ref):
    low = first_lanes(SLAB)
    lane = lax.broadcasted_iota(jnp.int32, (SLAB, PAIR), 1) % HEAD
    units = jnp.where(lane < 2, 1.0, 0.0).astype(BF)
    none = jnp.zeros((), BF)
    qt = q_ref[...].T
    for pair in range(HEADS // 2):
        lanes = slice(pair * PAIR, (pair + 1) * PAIR)
        mixed = (dm_ref[:, lanes] * r_ref[:, lanes].astype(F32)).astype(BF)
        weighed = mixed.astype(F32) * o_ref[:, lanes].astype(F32)
        keys, values = k_ref[:, lanes], v_ref[:, lanes]
        mixed_t = mixed.T
        dq = []
        for side in range(2):
            head = 2 * pair + side
            rows = slice(head * HEAD, (head + 1) * HEAD)
            mine = low if side == 0 else ~low
            centre = jnp.sum(jnp.where(mine, weighed, 0.0), axis=1, keepdims=True)
            high = centre.astype(BF)
            rest = (centre - high.astype(F32)).astype(BF)
            column = jnp.where(lane == 0, -high, jnp.where(lane == 1, -rest, none))
            grad = nt(jnp.where(mine, mixed, column), jnp.where(mine, values, units))
            power = e_ref[head]
            score = (power.astype(F32) * grad).astype(BF)
            dq.append(nn(score, keys))
            dkt_ref[rows, :] = (nn(qt[rows], score) * (1.0 / LOG2E)).astype(BF)
            dvt_ref[rows, :] = nn(mixed_t[side * HEAD : (side + 1) * HEAD], power).astype(BF)
        dq_ref[:, lanes] = (jnp.where(low, dq[0], dq[1]) * HEAD**-0.5).astype(BF)


def piece_columns(lengths_ref, slab, side):
    column = lax.broadcasted_iota(jnp.int32, (1, PAIR), 1) % HEAD
    opening = jnp.zeros((1, PAIR), jnp.int32)
    closing = jnp.zeros((1, PAIR), jnp.int32)
    total = jnp.int32(0)
    for piece in range(lengths_ref.shape[2]):
        following = total + lengths_ref[slab, side, piece]
        opening = jnp.where(column == piece, total, opening)
        closing = jnp.where(column == piece, following, closing)
        total = following
    place = lax.broadcasted_iota(jnp.int32, (SLAB, PAIR), 0)
    return jnp.where((opening <= place) & (place < closing), 1.0, 0.0).astype(BF)


def outside(columns):
    return jnp.where(columns > 0, 0.0, FAR).astype(BF)


def load_pieces(place_ref, pieces, w_s, sems):
    copies = []
    for blocks in pieces:
        rows = blocks.shape[2]
        for index in range(blocks.shape[0]):
            start = pl.multiple_of(place_ref[len(copies)] * rows, rows)
            copies.append(pltpu.make_async_copy(blocks.at[index], w_s.at[:, pl.ds(start, rows), :], sems.at[len(copies)]))
    for copy in copies:
        copy.start()
    for copy in copies:
        copy.wait()


def load_once(place_ref, pieces, w_s, sems):
    @pl.when(pl.program_id(0) == 0)
    def _():
        load_pieces(place_ref, pieces, w_s, sems)


def here(*refs):
    step = pl.program_id(0)
    return [ref.at[step if ref.shape[0] > 1 else 0] for ref in refs]


def self_forward(count, place_ref, lengths_ref, x_ref, *refs):
    pieces, (w_ref, q_ref, k_ref, v_ref, e_ref, r_ref, o_ref, e_s, sems, e_sems) = refs[:count], refs[count:]
    load_once(place_ref, pieces, w_ref, sems)
    x_ref, q_ref, k_ref, v_ref, r_ref, o_ref = here(x_ref, q_ref, k_ref, v_ref, r_ref, o_ref)
    step = pl.program_id(0)

    def store(slab, head):
        return pltpu.make_async_copy(e_s.at[slab, head], e_ref.at[slab, head], e_sems.at[slab, head])

    x = x_ref[...]
    q_ref[...] = (nn(x, w_ref[0]) * QSCALE).astype(BF)
    k_ref[...] = nn(x, w_ref[1]).astype(BF)
    v_ref[...] = nn(x, w_ref[2]).astype(BF)
    columns = piece_columns(lengths_ref, pl.program_id(0), 0)
    attend_forward(q_ref, k_ref, v_ref, columns, outside(columns), e_s.at[step], o_ref, r_ref, True, lambda head: store(step, head).start())

    @pl.when(step == pl.num_programs(0) - 1)
    def _():
        for slab in range(e_s.shape[0]):
            for head in range(HEADS):
                store(slab, head).wait()


def cross_inputs(count, owners, place_ref, o1_ref, x_ref, mem_ref, *refs):
    pieces, (w_ref, vec_ref, q_ref, k_ref, v_ref, unit1_ref, kept1_ref, scale1_ref, low1_ref, sems) = refs[:count], refs[count:]
    load_once(place_ref, pieces, w_ref, sems)

    @pl.when(pl.program_id(0) == 0)
    def _():
        rows = WIDTH // owners
        total = w_ref[5, 0:16, :].astype(F32)
        for owner in range(1, owners):
            total = total + w_ref[5, owner * rows : owner * rows + 16, :].astype(F32)
        vec_ref[...] = total

    o1_ref, x_ref, mem_ref, q_ref, k_ref, v_ref = here(o1_ref, x_ref, mem_ref, q_ref, k_ref, v_ref)
    unit1_ref, kept1_ref, scale1_ref, low1_ref = here(unit1_ref, kept1_ref, scale1_ref, low1_ref)
    residual = vec_ref[6:7, :] * x_ref[...].astype(F32) + nn(o1_ref[...], w_ref[4])
    unit, scale = norm_forward(residual)
    unit1_ref[...] = unit
    kept1_ref[...] = unit
    scale1_ref[...] = scale
    low = (unit * vec_ref[0:1, :] + vec_ref[3:4, :]).astype(BF)
    low1_ref[...] = low
    memory = mem_ref[...]
    k_ref[...] = nn(memory, w_ref[1]).astype(BF)
    v_ref[...] = nn(memory, w_ref[2]).astype(BF)
    q_ref[...] = (nn(low, w_ref[0]) * QSCALE).astype(BF)


def cross_forward(lengths_ref, q_ref, k_ref, v_ref, unit1_ref, w_ref, vec_ref, e_ref, r_ref, o_ref, unit2_ref, kept2_ref, scale2_ref):
    slab = pl.program_id(0)
    q_ref, k_ref, v_ref, unit1_ref, e_ref, r_ref, o_ref = here(q_ref, k_ref, v_ref, unit1_ref, e_ref, r_ref, o_ref)
    unit2_ref, kept2_ref, scale2_ref = here(unit2_ref, kept2_ref, scale2_ref)
    queries_in, keys_out = piece_columns(lengths_ref, slab, 0), outside(piece_columns(lengths_ref, slab, 1))
    attend_forward(q_ref, k_ref, v_ref, queries_in, keys_out, e_ref, o_ref, r_ref, False)
    state = unit1_ref[...] * vec_ref[0:1, :] + vec_ref[3:4, :]
    residual = vec_ref[7:8, :] * state + nn(o_ref[...], w_ref[0])
    unit, scale = norm_forward(residual)
    unit2_ref[...] = unit
    kept2_ref[...] = unit
    scale2_ref[...] = scale


CUBE = 0.044715
ROOT = math.sqrt(2.0 / math.pi)


def feed_copies(place_ref, pieces, ex_s, co_s, sems):
    each = co_s.shape[1]
    first, second = [], []
    for blocks in pieces:
        rows = blocks.shape[2]
        for index in range(blocks.shape[0]):
            number = len(first)
            start = place_ref[number] * rows
            owner = start // each
            aligned = pl.multiple_of(start, rows)
            first.append(pltpu.make_async_copy(blocks.at[index, 0:4], ex_s.at[:, pl.ds(aligned, rows), :], sems.at[0, number]))
            inside = pl.multiple_of(start - owner * each, rows)
            second.append(pltpu.make_async_copy(blocks.at[index, 4:8], co_s.at[pl.ds(owner * 4, 4), pl.ds(inside, rows), :], sems.at[1, number]))
    return first, second


def feed_both(count, place_ref, reduce_ref, unit2_ref, cot_ref, vec_ref, *refs):
    pieces, refs = refs[:count], refs[count:]
    out_ref, ds_ref, keep_ref, send_ref, dvec_ref, act_s, slope_s, branch_s, low_s, dbranch_s, cot_s, out_s, dex_s, dco_s, ex_s, co_s, sems, own_sems = refs
    slabs = unit2_ref.shape[0]
    chunks = ex_s.shape[0]
    owners = co_s.shape[0] // 4
    first, second = feed_copies(place_ref, pieces, ex_s, co_s, sems)
    cot_copy = pltpu.make_async_copy(cot_ref, cot_s, own_sems.at[0])
    out_copy = pltpu.make_async_copy(out_s, out_ref, own_sems.at[1])
    for copy in first + second + [cot_copy]:
        copy.start()

    def rows(slab):
        return slice(slab * SLAB, (slab + 1) * SLAB)

    def contract(part):
        return co_s[part * owners : (part + 1) * owners].reshape(WIDTH, WIDTH)

    def state(slab):
        return unit2_ref[slab] * vec_ref[1:2, :] + vec_ref[4:5, :]

    for slab in range(slabs):
        low_s[rows(slab), :] = state(slab).astype(BF)
    for copy in first:
        copy.wait()
    for part in range(chunks):
        u = nn(low_s[...], ex_s[part])
        square = u * u
        bend = jnp.tanh(u * (ROOT + (ROOT * CUBE) * square))
        half = 0.5 + 0.5 * bend
        act_s[part] = (u * half).astype(BF)
        slope_s[part] = half + (u * half) * (1.0 - bend) * (ROOT + (3.0 * ROOT * CUBE) * square)
        if part == 0:
            for copy in second:
                copy.wait()
            branch_s[...] = nn(act_s[part], contract(part))
        else:
            branch_s[...] += nn(act_s[part], contract(part))
    cot_copy.wait()
    for slab in range(slabs):
        now = state(slab)
        unit, scale = norm_forward(vec_ref[8:9, :] * now + branch_s[rows(slab), :])
        out_s[slab] = (unit * vec_ref[2:3, :] + vec_ref[5:6, :]).astype(BF)
        up = cot_s[slab].astype(F32)
        dres = norm_backward(up, unit, scale, vec_ref[2:3, :])
        sums = (rows_sum(up * unit), rows_sum(up), rows_sum(dres * now))
        for row, value in enumerate(sums):
            if slab == 0:
                dvec_ref[row : row + 1, :] = value
            else:
                dvec_ref[row : row + 1, :] += value
        branch_s[rows(slab), :] = dres * vec_ref[8:9, :]
        dbranch_s[rows(slab), :] = dres.astype(BF)
    out_copy.start()
    low_t = low_s[...].T
    for part in range(chunks):
        dco_s[part] = tn(act_s[part], dbranch_s[...]).astype(BF)
        dhid = (nt(dbranch_s[...], contract(part)) * slope_s[part]).astype(BF)
        dex_s[part] = nn(low_t, dhid).astype(BF)
        branch_s[...] += nt(dhid, ex_s[part])
    for slab in range(slabs):
        ds_ref[slab] = branch_s[rows(slab), :]
    put_feed(reduce_ref, dex_s, dco_s, keep_ref, send_ref)
    out_copy.wait()


def put_gradients(place_ref, dw_s, keep_ref, send_ref, first):
    blocks = keep_ref.shape[0]
    owners = blocks // dw_s.shape[0]
    rows = WIDTH // (2 * owners)
    core = place_ref[0]
    for matrix in range(dw_s.shape[0]):
        for owner in range(owners):
            at = 1 + matrix * owners + owner
            start = pl.multiple_of((2 * owner + core) * rows, rows)
            keep_ref[place_ref[at], first : first + rows, :] = dw_s[matrix, pl.ds(start, rows), :]
            start = pl.multiple_of((2 * owner + 1 - core) * rows, rows)
            send_ref[place_ref[at + blocks], first : first + rows, :] = dw_s[matrix, pl.ds(start, rows), :]


def put_vectors(place_ref, dvec_s, count, keep_ref, send_ref, first):
    blocks = keep_ref.shape[0]
    owners = blocks // count
    columns = WIDTH // (2 * owners)
    core = place_ref[0]
    rows = slice(first, first + 16)
    blank = jnp.zeros((16, WIDTH), BF)
    for block in range(blocks):
        keep_ref[block, rows, :] = blank
        send_ref[block, rows, :] = blank
    for owner in range(owners):
        low = dvec_s[:, 2 * owner * columns : (2 * owner + 1) * columns]
        high = dvec_s[:, (2 * owner + 1) * columns : (2 * owner + 2) * columns]
        rest = jnp.zeros((16, WIDTH - columns), F32)
        own = jnp.where(core == 0, low, high)
        other = jnp.where(core == 0, high, low)
        at = 1 + owner
        keep_ref[place_ref[at], rows, :] = jnp.concatenate([own, rest], axis=1).astype(BF)
        send_ref[place_ref[at + blocks], rows, :] = jnp.concatenate([other, rest], axis=1).astype(BF)


def put_feed(place_ref, dex_s, dco_s, keep_ref, send_ref):
    owners, _, each, _ = keep_ref.shape
    core = place_ref[0]
    for owner in range(owners):
        for out_ref, on, at in ((keep_ref, core, place_ref[1 + owner]), (send_ref, 1 - core, place_ref[1 + owners + owner])):
            shard = 2 * owner + on
            start = pl.multiple_of(shard * each, each)
            for part in range(4):
                out_ref[at, part] = dex_s[part, pl.ds(start, each), :]
                row = (shard * 4 + part) * each
                chunk = row // WIDTH
                out_ref[at, 4 + part] = dco_s[chunk, pl.ds(pl.multiple_of(row - chunk * WIDTH, each), each), :]


def fetcher(pairs, sems):
    step = pl.program_id(0)

    def copy(number, slab):
        return pltpu.make_async_copy(pairs[number][0].at[slab], pairs[number][1].at[slab], sems.at[number, slab])

    @pl.when(step == 0)
    def _():
        for slab in range(pairs[0][1].shape[0]):
            for number in range(len(pairs)):
                copy(number, slab).start()

    def wait(first, last):
        for number in range(first, last):
            copy(number, step).wait()

    return wait


def all_rows(ref):
    return ref[...].reshape(-1, WIDTH)


def cross_backward(ds2_ref, unit2_ref, scale2_ref, w_ref, vec_ref, q_ref, k_ref, v_ref, r_ref, o_ref, low1_ref, mem_ref, e_ref,
                   dmem_ref, ds1_ref, dw_ref, dvec_ref, q_s, k_s, v_s, r_s, o_s, low1_s, mem_s, dm_s, dq_s, dk_s, dv_s, dbranch_s, dkt_s, dvt_s, sems):
    step = pl.program_id(0)
    wait = fetcher([(q_ref, q_s), (k_ref, k_s), (v_ref, v_s), (r_ref, r_s), (o_ref, o_s), (low1_ref, low1_s), (mem_ref, mem_s)], sems)

    @pl.when(step == 0)
    def _():
        dvec_ref[...] = jnp.zeros_like(dvec_ref)

    ds2_ref, unit2_ref, scale2_ref, dmem_ref, ds1_ref = here(ds2_ref, unit2_ref, scale2_ref, dmem_ref, ds1_ref)
    up = ds2_ref[...]
    unit = unit2_ref[...]
    dvec_ref[0:1, :] += rows_sum(up * unit)
    dvec_ref[1:2, :] += rows_sum(up)
    dres = norm_backward(up, unit, scale2_ref[...], vec_ref[1:2, :])
    dbranch = dres.astype(BF)
    dbranch_s[step] = dbranch
    dm_s[...] = nt(dbranch, w_ref[3])
    ds1_ref[...] = dres * vec_ref[7:8, :]
    wait(0, 5)
    attend_backward(e_ref.at[step], r_s.at[step], o_s.at[step], q_s.at[step], k_s.at[step], v_s.at[step], dm_s, dq_s.at[step], dkt_s, dvt_s)
    wait(5, 7)
    dvec_ref[2:3, :] += rows_sum(dbranch_s[step].astype(F32) * low1_s[step].astype(F32))
    ds1_ref[...] += nt(dq_s[step], w_ref[0])
    dk = dkt_s[...].T
    dv = dvt_s[...].T
    dk_s[step] = dk
    dv_s[step] = dv
    dmem_ref[...] = nt(dk, w_ref[1]) + nt(dv, w_ref[2])

    @pl.when(step == pl.num_programs(0) - 1)
    def _():
        dw_ref[0] = tn(all_rows(low1_s), all_rows(dq_s)).astype(BF)
        memory_t = all_rows(mem_s).T
        dw_ref[1] = nn(memory_t, all_rows(dk_s)).astype(BF)
        dw_ref[2] = nn(memory_t, all_rows(dv_s)).astype(BF)
        dw_ref[3] = tn(all_rows(o_s), all_rows(dbranch_s)).astype(BF)


def self_backward(place_ref, ds1_ref, unit1_ref, scale1_ref, w3_ref, vec_ref, dvec2_ref, dvec3_ref, q_ref, k_ref, v_ref, r_ref, o_ref, x_ref, e_ref, w_ref, dw2_ref,
                  dx_ref, keep_ref, send_ref, q_s, k_s, v_s, r_s, o_s, x_s, e_s, w_s, dw2_s, dm_s, dq_s, dk_s, dv_s, dbranch_s, dkt_s, dvt_s, dw_s, dvec_s, sems, late_sems):
    step = pl.program_id(0)
    late = [pltpu.make_async_copy(w_ref, w_s, late_sems.at[0]), pltpu.make_async_copy(dw2_ref, dw2_s, late_sems.at[1])]
    wait = fetcher([(e_ref, e_s), (q_ref, q_s), (k_ref, k_s), (v_ref, v_s), (r_ref, r_s), (o_ref, o_s), (x_ref, x_s)], sems)

    @pl.when(step == 0)
    def _():
        for copy in late:
            copy.start()
        dvec_s[...] = jnp.zeros_like(dvec_s)

    ds1_ref, unit1_ref, scale1_ref, dx_ref = here(ds1_ref, unit1_ref, scale1_ref, dx_ref)
    up = ds1_ref[...]
    unit = unit1_ref[...]
    dvec_s[0:1, :] += rows_sum(up * unit)
    dvec_s[3:4, :] += rows_sum(up)
    dres = norm_backward(up, unit, scale1_ref[...], vec_ref[0:1, :])
    dbranch = dres.astype(BF)
    dbranch_s[step] = dbranch
    dm_s[...] = nt(dbranch, w3_ref[0])
    dx_ref[...] = dres * vec_ref[6:7, :]
    wait(0, 6)
    attend_backward(e_s.at[step], r_s.at[step], o_s.at[step], q_s.at[step], k_s.at[step], v_s.at[step], dm_s, dq_s.at[step], dkt_s, dvt_s)
    dk = dkt_s[...].T
    dv = dvt_s[...].T
    dk_s[step] = dk
    dv_s[step] = dv
    wait(6, 7)
    dvec_s[6:7, :] += rows_sum(dbranch_s[step].astype(F32) * x_s[step].astype(F32))

    @pl.when(step == 0)
    def _():
        for copy in late:
            copy.wait()

    dx_ref[...] += nt(dq_s[step], w_s[0]) + nt(dk, w_s[1]) + nt(dv, w_s[2])

    @pl.when(step == pl.num_programs(0) - 1)
    def _():
        x_t = all_rows(x_s).T
        dw_s[0] = nn(x_t, all_rows(dq_s)).astype(BF)
        dw_s[1] = nn(x_t, all_rows(dk_s)).astype(BF)
        dw_s[2] = nn(x_t, all_rows(dv_s)).astype(BF)
        dw_s[3] = tn(all_rows(o_s), all_rows(dbranch_s)).astype(BF)
        for row in range(3):
            dvec_s[3 * row + 1 : 3 * row + 2, :] = dvec2_ref[row : row + 1, :]
            dvec_s[3 * row + 2 : 3 * row + 3, :] = dvec3_ref[row : row + 1, :]
        rows = (keep_ref.shape[1] - 16) // 2
        put_gradients(place_ref, dw_s, keep_ref, send_ref, 0)
        put_vectors(place_ref, dvec_s, dw_s.shape[0], keep_ref, send_ref, rows)
        put_gradients(place_ref, dw2_s, keep_ref, send_ref, rows + 16)


def cut_shards(parts_ref, stacked_ref, expand_ref, contract_ref, vec_ref, a_ref, b_ref, c_ref):
    rows = stacked_ref.shape[1]
    half = pl.ds(pl.multiple_of(parts_ref[0] * (rows // 2), rows // 2), rows // 2)
    for matrix in range(3):
        a_ref[0, matrix] = stacked_ref[matrix, half, :].astype(BF)
    start = parts_ref[1] * (rows // 4)
    quarter = pl.ds(pl.multiple_of(start, rows // 4), rows // 4)
    for index, matrix in enumerate((4, 5, 6, 7, 3)):
        b_ref[0, index] = stacked_ref[matrix, quarter, :].astype(BF)
    vec = jnp.concatenate([vec_ref[...]] * (WIDTH // vec_ref.shape[1]), axis=1)
    owner = lax.broadcasted_iota(jnp.int32, vec.shape, 1) // vec_ref.shape[1]
    vec = jnp.where(owner == parts_ref[2], vec, 0.0)
    b_ref[0, 5] = jnp.concatenate([vec, jnp.zeros((rows // 4 - vec.shape[0], WIDTH), F32)], axis=0).astype(BF)
    for part in range(4):
        c_ref[0, part] = expand_ref[quarter, part * WIDTH : (part + 1) * WIDTH].astype(BF)
        c_ref[0, 4 + part] = contract_ref[pl.ds(pl.multiple_of(part * rows + start, rows // 4), rows // 4), :].astype(BF)


def per_slab(*tail):
    return pl.BlockSpec((1,) + tail, lambda m: (m,) + (0,) * len(tail))


def fixed(*dims):
    return pl.BlockSpec(dims, lambda m: (0,) * len(dims), pipeline_mode=pl.Buffered(1))


def shape(dims, kind):
    return jax.ShapeDtypeStruct(tuple(dims), kind)


def options(mib):
    return pltpu.CompilerParams(dimension_semantics=("arbitrary",), vmem_limit_bytes=mib * MIB)


def estimate(microseconds):
    return pl.CostEstimate(flops=int(microseconds * 1e9), bytes_accessed=1 << 20, transcendentals=0)


SCALARS = pl.BlockSpec(memory_space=pltpu.SMEM)
ANYWHERE = pl.BlockSpec(memory_space=pl.ANY)
RESIDENT = pl.BlockSpec(memory_space=pltpu.VMEM)
ROWS = per_slab(SLAB, WIDTH)
SCALE = per_slab(SLAB, 1)


def near(*arrays):
    return tuple(pltpu.with_memory_space_constraint(array, pltpu.VMEM) for array in arrays)


def far(*arrays):
    return tuple(pltpu.with_memory_space_constraint(array, pltpu.HBM) for array in arrays)


def near_shape(dims, kind):
    return pltpu.VMEM(tuple(dims), kind)


def far_shape(dims, kind):
    return pltpu.HBM(tuple(dims), kind)


def slabs(g, kind, place=far_shape):
    return place((g, SLAB, WIDTH), kind)


def powers_shape(g, place):
    return place((g, HEADS, SLAB, SLAB), BF)


def run_cut_shards(parts, stacked, expand, contract, vec):
    rows = stacked.shape[1]
    whole = pl.BlockSpec(memory_space=pltpu.VMEM)
    return pl.pallas_call(
        cut_shards,
        in_specs=[SCALARS, whole, whole, whole, whole],
        out_specs=[whole, whole, whole],
        out_shape=[shape((1, 3, rows // 2, WIDTH), BF), shape((1, 6, rows // 4, WIDTH), BF), shape((1, 8, rows // 4, WIDTH), BF)],
        compiler_params=pltpu.CompilerParams(vmem_limit_bytes=60 * MIB),
        name="cut_shards",
    )(parts, stacked, expand, contract, vec)


def run_self_forward(place, lengths, x, w):
    g = x.shape[0]
    return pl.pallas_call(
        functools.partial(self_forward, len(w)),
        grid=(g,),
        in_specs=[SCALARS, SCALARS, ROWS] + [ANYWHERE] * len(w),
        out_specs=[fixed(3, WIDTH, WIDTH), ROWS, ROWS, ROWS, ANYWHERE, ROWS, RESIDENT],
        out_shape=[far_shape((3, WIDTH, WIDTH), BF)] + [slabs(g, BF)] * 3 + [powers_shape(g, far_shape), slabs(g, BF), slabs(g, BF, near_shape)],
        scratch_shapes=[pltpu.VMEM((g, HEADS, SLAB, SLAB), BF), pltpu.SemaphoreType.DMA((sum(piece.shape[0] for piece in w),)), pltpu.SemaphoreType.DMA((g, HEADS))],
        compiler_params=options(32),
        cost_estimate=estimate(12),
        name="self_forward",
    )(place, lengths, x, *w)


def run_cross_inputs(owners, place, o1, x, memory, w):
    g = memory.shape[0]
    return pl.pallas_call(
        functools.partial(cross_inputs, len(w), owners),
        grid=(g,),
        in_specs=[SCALARS, RESIDENT, ROWS, ROWS] + [ANYWHERE] * len(w),
        out_specs=[fixed(6, WIDTH, WIDTH), fixed(16, WIDTH), ROWS, ROWS, ROWS, RESIDENT, ROWS, SCALE, ROWS],
        out_shape=[far_shape((6, WIDTH, WIDTH), BF), far_shape((16, WIDTH), F32)]
        + [slabs(g, BF)] * 3
        + [slabs(g, F32, near_shape), slabs(g, F32), far_shape((g, SLAB, 1), F32), slabs(g, BF)],
        scratch_shapes=[pltpu.SemaphoreType.DMA((sum(piece.shape[0] for piece in w),))],
        compiler_params=options(24),
        cost_estimate=estimate(7),
        name="cross_inputs",
    )(place, *near(o1), x, memory, *w)


def run_cross_forward(lengths, q, k, v, unit1, w, vec):
    g = q.shape[0]
    last = pl.BlockSpec((1, WIDTH, WIDTH), lambda m: (3, 0, 0))
    return pl.pallas_call(
        cross_forward,
        grid=(g,),
        in_specs=[SCALARS, ROWS, ROWS, ROWS, RESIDENT, last, fixed(16, WIDTH)],
        out_specs=[RESIDENT, ROWS, ROWS, RESIDENT, ROWS, SCALE],
        out_shape=[powers_shape(g, near_shape), slabs(g, BF), slabs(g, BF), slabs(g, F32, near_shape), slabs(g, F32), far_shape((g, SLAB, 1), F32)],
        compiler_params=options(24),
        cost_estimate=estimate(11),
        name="cross_forward",
    )(lengths, *far(q, k, v), *near(unit1), *far(w, vec))


def run_feed(owners, place, reduce, unit2, cot, w, vec):
    g = unit2.shape[0]
    rows = WIDTH // owners
    pieces = sum(piece.shape[0] for piece in w)
    dims = (owners // 2, 8, rows, WIDTH)
    tokens = g * SLAB
    return pl.pallas_call(
        functools.partial(feed_both, len(w)),
        grid=(1,),
        in_specs=[SCALARS, SCALARS, RESIDENT, ANYWHERE, fixed(16, WIDTH)] + [ANYWHERE] * len(w),
        out_specs=[ANYWHERE, RESIDENT, RESIDENT, RESIDENT, fixed(8, WIDTH)],
        out_shape=[slabs(g, BF), slabs(g, F32, near_shape)] + [near_shape(dims, BF)] * 2 + [far_shape((8, WIDTH), F32)],
        scratch_shapes=[
            pltpu.VMEM((4, tokens, WIDTH), BF),
            pltpu.VMEM((4, tokens, WIDTH), F32),
            pltpu.VMEM((tokens, WIDTH), F32),
            pltpu.VMEM((tokens, WIDTH), BF),
            pltpu.VMEM((tokens, WIDTH), BF),
            pltpu.VMEM((g, SLAB, WIDTH), BF),
            pltpu.VMEM((g, SLAB, WIDTH), BF),
            pltpu.VMEM((4, WIDTH, WIDTH), BF),
            pltpu.VMEM((4, WIDTH, WIDTH), BF),
            pltpu.VMEM((4, WIDTH, WIDTH), BF),
            pltpu.VMEM((4 * owners, rows, WIDTH), BF),
            pltpu.SemaphoreType.DMA((2, pieces)),
            pltpu.SemaphoreType.DMA((2,)),
        ],
        compiler_params=options(FEED_MIB),
        cost_estimate=estimate(24),
        name="feed_both",
    )(place, reduce, *near(unit2), cot, *far(vec), *w)


def slab_scratch(g, kinds):
    return [pltpu.VMEM((g, SLAB, WIDTH), kind) for kind in kinds]


def run_cross_backward(ds2, unit2, scale2, low1, memory, w, vec, saved):
    g = memory.shape[0]
    q, k, v, e, r, o = saved
    return pl.pallas_call(
        cross_backward,
        grid=(g,),
        in_specs=[RESIDENT, ROWS, SCALE, fixed(4, WIDTH, WIDTH), fixed(16, WIDTH)] + [ANYWHERE] * 7 + [RESIDENT],
        out_specs=[ROWS, RESIDENT, fixed(4, WIDTH, WIDTH), fixed(8, WIDTH)],
        out_shape=[slabs(g, F32), slabs(g, F32, near_shape), far_shape((4, WIDTH, WIDTH), BF), far_shape((8, WIDTH), F32)],
        scratch_shapes=slab_scratch(g, [BF] * 7)
        + [pltpu.VMEM((SLAB, WIDTH), F32)]
        + slab_scratch(g, [BF] * 4)
        + [pltpu.VMEM((WIDTH, SLAB), BF)] * 2
        + [pltpu.SemaphoreType.DMA((7, g))],
        compiler_params=options(CROSS_MIB),
        cost_estimate=estimate(22),
        name="cross_backward",
    )(*near(ds2), *far(unit2, scale2, w, vec, q, k, v, r, o, low1), memory, *near(e))


def run_self_backward(place, owners, ds1, unit1, scale1, x, w, w_cross, vec, dvec2, dvec3, dw2, saved):
    g = x.shape[0]
    rows = WIDTH // (2 * owners)
    dims = (4 * owners, 2 * rows + 16, WIDTH)
    q, k, v, e, r, o = saved
    third = pl.BlockSpec((1, WIDTH, WIDTH), lambda m: (4, 0, 0))
    return pl.pallas_call(
        self_backward,
        grid=(g,),
        in_specs=[SCALARS, RESIDENT, ROWS, SCALE, third, fixed(16, WIDTH), fixed(8, WIDTH), fixed(8, WIDTH)] + [ANYWHERE] * 9,
        out_specs=[ROWS] + [fixed(*dims)] * 2,
        out_shape=[slabs(g, F32)] + [far_shape(dims, BF)] * 2,
        scratch_shapes=slab_scratch(g, [BF] * 6)
        + [pltpu.VMEM((g, HEADS, SLAB, SLAB), BF), pltpu.VMEM((3, WIDTH, WIDTH), BF), pltpu.VMEM((4, WIDTH, WIDTH), BF), pltpu.VMEM((SLAB, WIDTH), F32)]
        + slab_scratch(g, [BF] * 4)
        + [pltpu.VMEM((WIDTH, SLAB), BF)] * 2
        + [pltpu.VMEM((4, WIDTH, WIDTH), BF), pltpu.VMEM((16, WIDTH), F32), pltpu.SemaphoreType.DMA((7, g)), pltpu.SemaphoreType.DMA((2,))],
        compiler_params=options(SELF_MIB),
        cost_estimate=estimate(22),
        name="self_backward",
    )(place, *near(ds1), *far(unit1, scale1, w_cross, vec, dvec2, dvec3, q, k, v, r, o), x, *far(e, w, dw2))
def adam_update(weight, first_moment, second_moment, gradient):
    correction = 1.0 - 0.5**STEP
    first_next = 0.5 * first_moment + 0.5 * gradient
    second_next = 0.5 * second_moment + 0.5 * gradient * gradient
    weight_next = weight - LEARN_RATE * (first_next / correction) / (jnp.sqrt(second_next / correction) + ADAM_EPS)
    return (weight_next, first_next, second_next)


def adam_stacked(order_ref, grad_ref, w_ref, m_ref, s_ref, w_out, m_out, s_out):
    rows = w_ref.shape[1]
    group = pl.program_id(0)

    def update(first):
        for matrix in range(4):
            grad = grad_ref[order_ref[matrix]].astype(F32)[first : first + rows]
            w_out[matrix], m_out[matrix], s_out[matrix] = adam_update(w_ref[matrix], m_ref[matrix], s_ref[matrix], grad)

    @pl.when(group == 0)
    def _():
        update(0)

    @pl.when(group == 1)
    def _():
        update(rows + 16)


def run_adam_stacked(order, grads, weight, first, second):
    rows = weight.shape[1]
    block = pl.BlockSpec((4, rows, WIDTH), lambda group: (group, 0, 0))
    return pl.pallas_call(
        adam_stacked,
        grid=(2,),
        in_specs=[SCALARS, fixed(*grads.shape), block, block, block],
        out_specs=[block, block, block],
        out_shape=[shape(weight.shape, F32)] * 3,
        compiler_params=options(24),
        cost_estimate=estimate(4),
        name="adam_stacked",
    )(order, grads, weight, first, second)


def adam_feed(grad_ref, *refs):
    rows = grad_ref.shape[1]
    for part in range(4):
        where = (slice(None), slice(part * WIDTH, (part + 1) * WIDTH))
        refs[6][where], refs[7][where], refs[8][where] = adam_update(*(ref[where] for ref in refs[0:3]), grad_ref[part].astype(F32))
        where = (slice(part * rows, (part + 1) * rows), slice(None))
        refs[9][where], refs[10][where], refs[11][where] = adam_update(*(ref[where] for ref in refs[3:6]), grad_ref[4 + part].astype(F32))


def run_adam_feed(grads, expand, contract):
    arrays = tuple(expand) + tuple(contract)
    return pl.pallas_call(
        adam_feed,
        out_shape=[shape(a.shape, F32) for a in arrays],
        compiler_params=pltpu.CompilerParams(vmem_limit_bytes=24 * MIB),
        cost_estimate=estimate(4),
        name="adam_feed",
    )(grads, *arrays)


class Route:
    def __init__(self, m, n):
        self.m, self.n = m, n
        self.dp_bits = m.bit_length() - 1
        self.line_bits = n.bit_length() - 2
        self.line = n // 2

    def pairs(self, partner):
        return [(d * self.n + f, partner(d, f)) for d in range(self.m) for f in range(self.n)]

    def across_core(self):
        return self.pairs(lambda d, f: d * self.n + (f ^ 1))

    def along_line(self, mask):
        return self.pairs(lambda d, f: d * self.n + (f ^ (2 * mask)))

    def across_line(self, step):
        def partner(d, f):
            bit = step if f % 2 == 0 else self.line_bits - 1 - step
            return d * self.n + (f ^ (2 << bit))

        return self.pairs(partner)

    def across_dp(self, step):
        def partner(d, f):
            bit = step if f % 2 == 0 else self.dp_bits - 1 - step
            return (d ^ (1 << bit)) * self.n + f

        return self.pairs(partner)

    @staticmethod
    def spot(mask, bits, core):
        return mask if core == 0 else sum(((mask >> b) & 1) << (bits - 1 - b) for b in range(bits))

    def part(self, share, d, f):
        return sum(((d >> (bit if f % 2 == 0 else self.dp_bits - 1 - bit)) & 1) << bit for bit in range(share))

    def gather_row(self, share, d, f):
        z, c = divmod(f, 2)
        return [
            ((2 * (z ^ k) + who) << share) + (self.part(share, d, who) ^ step)
            for who in (c, 1 - c)
            for step in range(1 << share)
            for k in range(self.line)
        ]

    def reduce_row(self, d, f):
        z, c = divmod(f, 2)
        row = [c]
        for who in (c, 1 - c):
            line = [self.spot(owner ^ z, self.line_bits, who) for owner in range(self.line)]
            row += [self.spot(j ^ d, self.dp_bits, who) * self.line + at for j in range(self.m) for at in line]
        return row + [self.spot(j ^ d, self.dp_bits, c) for j in range(self.m)]

    def feed_row(self, d, f):
        z, c = divmod(f, 2)
        return [c] + [self.spot(owner ^ z, self.line_bits, who) for who in (c, 1 - c) for owner in range(self.line)]

    def part_row(self, d, f):
        return [self.part(1, d, f), self.part(2, d, f), f]

    def tables(self):
        kinds = (functools.partial(self.gather_row, 1), functools.partial(self.gather_row, 2), self.reduce_row, self.feed_row, self.part_row)
        rows = [[kind(d, f) for kind in kinds] for d in range(self.m) for f in range(self.n)]
        ends = np.cumsum([0] + [len(row) for row in rows[0]])
        return np.array([sum(row, []) for row in rows], np.int32), ends


BOTH = ("dp", "fsdp")


def after(values, *earlier):
    return lax.optimization_barrier((values,) + earlier)[0]


def doubled(blocks, got):
    return jnp.concatenate([blocks, got], axis=0)


def per_device(
    inputs,
    memory,
    cotangent,
    lengths,
    stacked_weights,
    expand_weights,
    contract_weights,
    scale_vectors,
    stacked_first,
    stacked_second,
    expand_first,
    expand_second,
    contract_first,
    contract_second,
    vector_first,
    vector_second,
):
    m, n = lax.axis_size("dp"), lax.axis_size("fsdp")
    width = WIDTH // n
    slabs = inputs.shape[0] * lengths.shape[1]
    x = inputs.reshape(slabs, SLAB, WIDTH)
    mem = memory.reshape(slabs, SLAB, WIDTH)
    cot = cotangent.reshape(slabs, SLAB, WIDTH)
    by_hand = m == 4 and width == 64 and n == 8
    here = lax.axis_index("fsdp")
    lengths = lengths.reshape(slabs, 2, -1)
    if by_hand:
        route = Route(m, n)
        table, ends = route.tables()
        row = lax.dynamic_index_in_dim(jnp.asarray(table), lax.axis_index("dp") * n + here, keepdims=False)
        halves, quarters, reduced, feed_order, parts = (row[ends[i] : ends[i + 1]] for i in range(5))

        def swap(blocks, pairs):
            return lax.ppermute(blocks, BOTH, pairs)

        along = [route.along_line(mask) for mask in range(1, n // 2)]
        line = [route.across_line(step) for step in range(route.line_bits)]
        across = [route.across_dp(step) for step in range(route.dp_bits)]
        core = route.across_core()
        a, b, c = run_cut_shards(parts, stacked_weights, expand_weights, contract_weights, scale_vectors)
        a = jnp.concatenate(lax.optimization_barrier((a, *(swap(a, pairs) for pairs in along))), axis=0)
        b = after(b, a)
        a_across, a_core, *b_line = lax.optimization_barrier((swap(a, across[0]), swap(a, core), *(swap(b, pairs) for pairs in along)))
        b = jnp.concatenate([b, *b_line], axis=0)
        c = after(c, b)
        b_across, c_line = swap(b, across[0]), [swap(c, pairs) for pairs in along]
        w_self, *saved1 = run_self_forward(halves, lengths, after(x, b), (a, a_across, a_core, swap(a_across, core)))
        b_across, *c_line = after((b_across, *c_line), saved1[-1])
        c = jnp.concatenate([c, *c_line], axis=0)
        b = doubled(b, after(b_across, c))
        b_across, b_core = swap(b, across[1]), swap(b, core)
        c_across = swap(c, across[0])
        w_cross = (b, b_across, b_core, swap(b_across, core))
        w_cross, vec, *qkv2, unit1, kept1, scale1, low1 = run_cross_inputs(n, quarters, saved1[-1], x, mem, w_cross)
        c = doubled(c, after(c_across, unit1))
        c_across, c_core = swap(c, across[1]), swap(c, core)
        *saved2, unit2, kept2, scale2 = run_cross_forward(lengths, *qkv2, after(unit1, c), w_cross, vec)
        saved2 = qkv2 + saved2
        c_across = after(c_across, unit2)
        w_feed = (c, c_across, c_core, swap(c_across, core))
        out, ds2, feed_keep, feed_send, dvec3 = run_feed(n, quarters, feed_order, unit2, cot, w_feed, vec)
        feed_got = swap(feed_send, core)
        dmem, ds1, dw2, dvec2 = run_cross_backward(ds2, kept2, scale2, low1, mem, w_cross, vec, saved2)
        feed_got = after(feed_got, ds1)
        half = n // 4
        feed_out, feed = feed_keep[half:] + feed_got[half:], feed_keep[:half] + feed_got[:half]
        feed_got = swap(feed_out, line[1])
        dx, keep, send = run_self_backward(reduced, n // 2, after(ds1, feed_out), kept1, scale1, x, w_self, w_cross, vec, dvec2, dvec3, dw2, saved1)
        feed_got = after(feed_got, keep)
        got = swap(after(send, feed_got), core)
        out_part, total = keep[8:] + got[8:], keep[:8] + got[:8]
        feed_out, feed = feed[1:] + feed_got[1:], feed[:1] + feed_got[:1]
        got, feed_got = lax.optimization_barrier((swap(out_part, across[1]), swap(after(feed_out, out_part), line[0])))
        out_part, total = total[4:] + got[4:], total[:4] + got[:4]
        got = swap(out_part, across[0])
        feed = feed + feed_got
        total = total + got
        out_part, total = total[2:], total[:2]
        got, feed_got = lax.optimization_barrier((swap(out_part, line[1]), swap(after(feed, out_part), across[0])))
        out_part, total = total[1:] + got[1:], total[:1] + got[:1]
        feed = feed + feed_got
        got, feed_got = lax.optimization_barrier((swap(out_part, line[0]), swap(after(feed, out_part), across[1])))
        total = total + got
        feed = feed + feed_got
        total = doubled(total, swap(total, across[0]))
        feed_next = run_adam_feed(after(feed[0], total), (expand_weights, expand_first, expand_second), (contract_weights, contract_first, contract_second))
        total = doubled(total, after(swap(total, across[1]), feed_next[0]))
        order = reduced[-m:]
        grad_vector = lax.dynamic_index_in_dim(total, order[0], keepdims=False)[width : width + 9, :width]
        stacked_next = run_adam_stacked(order, total, stacked_weights, stacked_first, stacked_second)
    else:
        reduced, feed_order = jnp.array([0] + [0, 1, 2, 3] * 2, jnp.int32), jnp.zeros((3,), jnp.int32)
        halves = jnp.arange(2, dtype=jnp.int32)
        expand_blocks = jnp.swapaxes(expand_weights.reshape(width, 4, WIDTH), 0, 1)
        vec_shard = lax.dynamic_update_slice(jnp.zeros((16, WIDTH), BF), scale_vectors.astype(BF), (0, here * width))
        all_low = lax.all_gather(stacked_weights.astype(BF), "fsdp", axis=1, tiled=True)
        vec_full = jnp.sum(lax.all_gather(vec_shard, "fsdp", axis=0).astype(F32), axis=0).astype(BF)
        vec_full = jnp.pad(vec_full, ((0, WIDTH - 16), (0, 0)))
        ex = lax.all_gather(expand_blocks.astype(BF), "fsdp", axis=1, tiled=True).reshape(4, 2, -1, WIDTH)
        co = lax.all_gather(contract_weights.astype(BF), "fsdp", axis=0, tiled=True).reshape(2, 4, -1, WIDTH)
        w_self = tuple(all_low[None, :3].reshape(1, 3, 2, -1, WIDTH)[:, :, core] for core in range(2))
        w_cross = jnp.concatenate([all_low[4:], all_low[3:4], vec_full[None]], axis=0).reshape(1, 6, 2, -1, WIDTH)
        w_feed = tuple(jnp.concatenate([ex[:, core], co[core]], axis=0)[None] for core in range(2))
        w_self, *saved1 = run_self_forward(halves, lengths, x, w_self)
        w_cross, vec, *qkv2, unit1, kept1, scale1, low1 = run_cross_inputs(1, halves, saved1[-1], x, mem, (w_cross[:, :, 0], w_cross[:, :, 1]))
        *saved2, unit2, kept2, scale2 = run_cross_forward(lengths, *qkv2, unit1, w_cross, vec)
        saved2 = qkv2 + saved2
        out, ds2, feed_keep, feed_send, dvec3 = run_feed(2, halves, feed_order, unit2, cot, w_feed, vec)
        dw_feed = jnp.concatenate([feed_keep, feed_send], axis=0)
        dex = jnp.swapaxes(dw_feed[:, :4], 0, 1).reshape(4, n, width, WIDTH)
        dco = dw_feed[:, 4:].reshape(n, 4, width, WIDTH)
        dw_feed = jnp.concatenate([jnp.swapaxes(dex, 0, 1), dco], axis=1)
        grad_feed = lax.psum(lax.psum_scatter(dw_feed, "fsdp", scatter_dimension=0, tiled=False), "dp")
        dmem, ds1, dw2, dvec2 = run_cross_backward(ds2, kept2, scale2, low1, mem, w_cross, vec, saved2)
        dx, keep, send = run_self_backward(reduced, 1, ds1, kept1, scale1, x, w_self, w_cross, vec, dvec2, dvec3, dw2, saved1)
        both = jnp.stack([keep, send], axis=1)
        rows = WIDTH // 2
        grad_vector = lax.psum(both[0, :, rows : rows + 9, :rows].astype(F32), BOTH)
        grad_vector = jnp.swapaxes(grad_vector, 0, 1).reshape(9, WIDTH)
        grad_vector = lax.dynamic_slice(grad_vector, (0, here * width), (9, width))
        both = jnp.concatenate([both[:, :, :rows], both[:, :, rows + 16 :]], axis=0).reshape(8, WIDTH, WIDTH)
        both = lax.psum(lax.psum_scatter(both, "fsdp", scatter_dimension=1, tiled=True), "dp")
        stacked_next = adam_update(stacked_weights, stacked_first, stacked_second, both.astype(F32))
        feed_next = run_adam_feed(grad_feed, (expand_weights, expand_first, expand_second), (contract_weights, contract_first, contract_second))
    expand_next, contract_next = feed_next[:3], feed_next[3:]
    vector_next = adam_update(scale_vectors, vector_first, vector_second, grad_vector.astype(F32))
    return (
        out.reshape(inputs.shape),
        dx.reshape(inputs.shape),
        dmem.reshape(inputs.shape),
        stacked_next[0],
        expand_next[0],
        contract_next[0],
        vector_next[0],
        stacked_next[1],
        stacked_next[2],
        expand_next[1],
        expand_next[2],
        contract_next[1],
        contract_next[2],
        vector_next[1],
        vector_next[2],
    )


def solution(mesh):
    tokens = P(None, ("dp", "fsdp"), None)
    pieces = P(None, ("dp", "fsdp"), None, None)
    stacked = P(None, "fsdp", None)
    rows = P("fsdp", None)
    columns = P(None, "fsdp")
    return jax.shard_map(
        per_device,
        mesh=mesh,
        in_specs=(tokens, tokens, tokens, pieces, stacked, rows, rows, columns) + (stacked, stacked, rows, rows, rows, rows, columns, columns),
        out_specs=(tokens, tokens, tokens, stacked, rows, rows, columns) + (stacked, stacked, rows, rows, rows, rows, columns, columns),
        check_vma=False,
    )
```

```python
import functools
import math

import jax
import jax.numpy as jnp
import numpy as np
from jax import lax
from jax.experimental import pallas as pl
from jax.experimental.pallas import tpu as pltpu
from jax.sharding import PartitionSpec as P

HEADS = 8
HEAD = 64
SLAB = 512
WIDTH = 512
PAIR = 2 * HEAD
STEP = 3
NORM_EPS = 1e-05
ADAM_EPS = 1e-08
LEARN_RATE = 0.2
FAR = -1e30
LOG2E = math.log2(math.e)
QSCALE = HEAD**-0.5 * LOG2E
TILE = 256
BF = jnp.bfloat16
F32 = jnp.float32
MIB = 1 << 20
FEED_MIB = 30
CROSS_MIB = 26
SELF_MIB = 40


def nn(a, b):
    return jnp.dot(a, b, preferred_element_type=F32)


def nt(a, b):
    return lax.dot_general(a, b, (((1,), (1,)), ((), ())), preferred_element_type=F32)


def tn(a, b):
    return lax.dot_general(a, b, (((0,), (0,)), ((), ())), preferred_element_type=F32)


def norm_forward(residual, eps=NORM_EPS):
    centred = residual - jnp.mean(residual, axis=-1, keepdims=True)
    spread = jnp.mean(centred * centred, axis=-1, keepdims=True)
    scale = lax.rsqrt(spread + eps)
    return centred * scale, scale


def norm_backward(upstream, unit, scale, gain):
    inner = upstream * gain
    first = jnp.mean(inner, axis=-1, keepdims=True)
    second = jnp.mean(inner * unit, axis=-1, keepdims=True)
    return scale * (inner - first - unit * second)


def rows_sum(values):
    return jnp.sum(values, axis=0, keepdims=True)


def first_lanes(rows):
    return lax.broadcasted_iota(jnp.int32, (rows, PAIR), 1) < HEAD


def attend_forward(q_ref, k_ref, v_ref, queries_in, keys_out, e_ref, o_ref, r_ref, causal, after=None):
    low = first_lanes(SLAB)
    ones = jnp.ones((SLAB, PAIR), BF)
    spans = ((0, TILE, TILE), (TILE, SLAB, SLAB)) if causal else ((0, SLAB, SLAB),)
    if causal:
        query_at = lax.broadcasted_iota(jnp.int32, (TILE, TILE), 0)
        key_at = lax.broadcasted_iota(jnp.int32, (TILE, TILE), 1)
        bias = jnp.where(key_at <= query_at, 0.0, FAR).astype(F32)
        blank = jnp.zeros((TILE, TILE), BF)

    def lanes(head):
        return slice(head // 2 * PAIR, (head // 2 + 1) * PAIR)

    def scores(head):
        left, right = q_ref[:, lanes(head)], k_ref[:, lanes(head)]
        if head % 2 == 0:
            left, right = jnp.where(low, left, queries_in), jnp.where(low, right, keys_out)
        else:
            left, right = jnp.where(low, queries_in, left), jnp.where(low, keys_out, right)
        return [nt(left[first:last], right[:depth]) for first, last, depth in spans]

    def powers(head, found):
        results = []
        for (first, last, depth), part in zip(spans, found):
            if causal:
                end = part[:, depth - TILE :] + bias
                part = end if depth == TILE else jnp.concatenate([part[:, : depth - TILE], end], axis=1)
            power = jnp.exp2(part - jnp.max(part, axis=1, keepdims=True)).astype(BF)
            e_ref[head, first:last, :depth] = power
            if depth < SLAB:
                e_ref[head, first:last, depth:] = blank
            results.append(power)
        if after is not None:
            after(head)
        return results

    def mixes(head, found):
        right = jnp.concatenate([v_ref[:, lanes(head)], ones], axis=1)
        results = []
        for (_, _, depth), power in zip(spans, found):
            mixed = nn(power, right[:depth])
            inverse = 1.0 / mixed[:, PAIR:]
            results.append((mixed[:, :PAIR] * inverse, inverse))
        return results

    def put(pair, even, odd):
        for (first, last, _), (mix_0, inverse_0), (mix_1, inverse_1) in zip(spans, even, odd):
            here = first_lanes(last - first)
            o_ref[first:last, pair * PAIR : (pair + 1) * PAIR] = jnp.where(here, mix_0, mix_1).astype(BF)
            r_ref[first:last, pair * PAIR : (pair + 1) * PAIR] = jnp.where(here, inverse_0, inverse_1).astype(BF)

    following = scores(0)
    earlier = None
    mixed = {}
    for head in range(HEADS):
        found = following
        if head + 1 < HEADS:
            following = scores(head + 1)
        now = powers(head, found)
        if earlier is not None:
            mixed[head - 1] = mixes(head - 1, earlier)
            if head % 2 == 0:
                put(head // 2 - 1, mixed[head - 2], mixed[head - 1])
        earlier = now
    mixed[HEADS - 1] = mixes(HEADS - 1, earlier)
    put(HEADS // 2 - 1, mixed[HEADS - 2], mixed[HEADS - 1])


def attend_backward(e_ref, r_ref, o_ref, q_ref, k_ref, v_ref, dm_ref, dq_ref, dkt_ref, dvt_ref):
    low = first_lanes(SLAB)
    lane = lax.broadcasted_iota(jnp.int32, (SLAB, PAIR), 1) % HEAD
    units = jnp.where(lane < 2, 1.0, 0.0).astype(BF)
    none = jnp.zeros((), BF)
    qt = q_ref[...].T
    for pair in range(HEADS // 2):
        lanes = slice(pair * PAIR, (pair + 1) * PAIR)
        mixed = (dm_ref[:, lanes] * r_ref[:, lanes].astype(F32)).astype(BF)
        weighed = mixed.astype(F32) * o_ref[:, lanes].astype(F32)
        keys, values = k_ref[:, lanes], v_ref[:, lanes]
        mixed_t = mixed.T
        dq = []
        for side in range(2):
            head = 2 * pair + side
            rows = slice(head * HEAD, (head + 1) * HEAD)
            mine = low if side == 0 else ~low
            centre = jnp.sum(jnp.where(mine, weighed, 0.0), axis=1, keepdims=True)
            high = centre.astype(BF)
            rest = (centre - high.astype(F32)).astype(BF)
            column = jnp.where(lane == 0, -high, jnp.where(lane == 1, -rest, none))
            grad = nt(jnp.where(mine, mixed, column), jnp.where(mine, values, units))
            power = e_ref[head]
            score = (power.astype(F32) * grad).astype(BF)
            dq.append(nn(score, keys))
            dkt_ref[rows, :] = (nn(qt[rows], score) * (1.0 / LOG2E)).astype(BF)
            dvt_ref[rows, :] = nn(mixed_t[side * HEAD : (side + 1) * HEAD], power).astype(BF)
        dq_ref[:, lanes] = (jnp.where(low, dq[0], dq[1]) * HEAD**-0.5).astype(BF)


def piece_columns(lengths_ref, slab, side):
    column = lax.broadcasted_iota(jnp.int32, (1, PAIR), 1) % HEAD
    opening = jnp.zeros((1, PAIR), jnp.int32)
    closing = jnp.zeros((1, PAIR), jnp.int32)
    total = jnp.int32(0)
    for piece in range(lengths_ref.shape[2]):
        following = total + lengths_ref[slab, side, piece]
        opening = jnp.where(column == piece, total, opening)
        closing = jnp.where(column == piece, following, closing)
        total = following
    place = lax.broadcasted_iota(jnp.int32, (SLAB, PAIR), 0)
    return jnp.where((opening <= place) & (place < closing), 1.0, 0.0).astype(BF)


def outside(columns):
    return jnp.where(columns > 0, 0.0, FAR).astype(BF)


def load_pieces(place_ref, first, pieces, w_s, sems):
    copies = []
    for blocks in pieces:
        rows = blocks.shape[2]
        for index in range(blocks.shape[0]):
            start = pl.multiple_of(place_ref[first + len(copies)] * rows, rows)
            copies.append(pltpu.make_async_copy(blocks.at[index], w_s.at[:, pl.ds(start, rows), :], sems.at[len(copies)]))
    for copy in copies:
        copy.start()
    for copy in copies:
        copy.wait()


def load_once(place_ref, first, pieces, w_s, sems):
    @pl.when(pl.program_id(0) == 0)
    def _():
        load_pieces(place_ref, first, pieces, w_s, sems)


def here(*refs):
    step = pl.program_id(0)
    return [ref.at[step if ref.shape[0] > 1 else 0] for ref in refs]


def self_forward(count, first, place_ref, lengths_ref, x_ref, *refs):
    pieces, (w_ref, q_ref, k_ref, v_ref, e_ref, r_ref, o_ref, e_s, sems, e_sems) = refs[:count], refs[count:]
    load_once(place_ref, first, pieces, w_ref, sems)
    x_ref, q_ref, k_ref, v_ref, r_ref, o_ref = here(x_ref, q_ref, k_ref, v_ref, r_ref, o_ref)
    step = pl.program_id(0)

    def store(slab, head):
        return pltpu.make_async_copy(e_s.at[slab, head], e_ref.at[slab, head], e_sems.at[slab, head])

    x = x_ref[...]
    q_ref[...] = (nn(x, w_ref[0]) * QSCALE).astype(BF)
    k_ref[...] = nn(x, w_ref[1]).astype(BF)
    v_ref[...] = nn(x, w_ref[2]).astype(BF)
    columns = piece_columns(lengths_ref, pl.program_id(0), 0)
    attend_forward(q_ref, k_ref, v_ref, columns, outside(columns), e_s.at[step], o_ref, r_ref, True, lambda head: store(step, head).start())

    @pl.when(step == pl.num_programs(0) - 1)
    def _():
        for slab in range(e_s.shape[0]):
            for head in range(HEADS):
                store(slab, head).wait()


def cross_inputs(count, first, owners, place_ref, o1_ref, x_ref, mem_ref, *refs):
    pieces, (w_ref, vec_ref, q_ref, k_ref, v_ref, unit1_ref, kept1_ref, scale1_ref, low1_ref, sems) = refs[:count], refs[count:]
    load_once(place_ref, first, pieces, w_ref, sems)

    @pl.when(pl.program_id(0) == 0)
    def _():
        rows = WIDTH // owners
        total = w_ref[5, 0:16, :].astype(F32)
        for owner in range(1, owners):
            total = total + w_ref[5, owner * rows : owner * rows + 16, :].astype(F32)
        vec_ref[...] = total

    o1_ref, x_ref, mem_ref, q_ref, k_ref, v_ref = here(o1_ref, x_ref, mem_ref, q_ref, k_ref, v_ref)
    unit1_ref, kept1_ref, scale1_ref, low1_ref = here(unit1_ref, kept1_ref, scale1_ref, low1_ref)
    residual = vec_ref[6:7, :] * x_ref[...].astype(F32) + nn(o1_ref[...], w_ref[4])
    unit, scale = norm_forward(residual)
    unit1_ref[...] = unit
    kept1_ref[...] = unit
    scale1_ref[...] = scale
    low = (unit * vec_ref[0:1, :] + vec_ref[3:4, :]).astype(BF)
    low1_ref[...] = low
    memory = mem_ref[...]
    k_ref[...] = nn(memory, w_ref[1]).astype(BF)
    v_ref[...] = nn(memory, w_ref[2]).astype(BF)
    q_ref[...] = (nn(low, w_ref[0]) * QSCALE).astype(BF)


def cross_forward(lengths_ref, q_ref, k_ref, v_ref, unit1_ref, w_ref, vec_ref, e_ref, r_ref, o_ref, unit2_ref, kept2_ref, scale2_ref):
    slab = pl.program_id(0)
    q_ref, k_ref, v_ref, unit1_ref, e_ref, r_ref, o_ref = here(q_ref, k_ref, v_ref, unit1_ref, e_ref, r_ref, o_ref)
    unit2_ref, kept2_ref, scale2_ref = here(unit2_ref, kept2_ref, scale2_ref)
    queries_in, keys_out = piece_columns(lengths_ref, slab, 0), outside(piece_columns(lengths_ref, slab, 1))
    attend_forward(q_ref, k_ref, v_ref, queries_in, keys_out, e_ref, o_ref, r_ref, False)
    state = unit1_ref[...] * vec_ref[0:1, :] + vec_ref[3:4, :]
    residual = vec_ref[7:8, :] * state + nn(o_ref[...], w_ref[0])
    unit, scale = norm_forward(residual)
    unit2_ref[...] = unit
    kept2_ref[...] = unit
    scale2_ref[...] = scale


CUBE = 0.044715
ROOT = math.sqrt(2.0 / math.pi)


def feed_copies(place_ref, begin, pieces, ex_s, co_s, sems):
    each = co_s.shape[1]
    first, second = [], []
    for blocks in pieces:
        rows = blocks.shape[2]
        for index in range(blocks.shape[0]):
            number = len(first)
            start = place_ref[begin + number] * rows
            owner = start // each
            aligned = pl.multiple_of(start, rows)
            first.append(pltpu.make_async_copy(blocks.at[index, 0:4], ex_s.at[:, pl.ds(aligned, rows), :], sems.at[0, number]))
            inside = pl.multiple_of(start - owner * each, rows)
            second.append(pltpu.make_async_copy(blocks.at[index, 4:8], co_s.at[pl.ds(owner * 4, 4), pl.ds(inside, rows), :], sems.at[1, number]))
    return first, second


def feed_both(count, begin, reduce_at, place_ref, unit2_ref, cot_ref, vec_ref, *refs):
    pieces, refs = refs[:count], refs[count:]
    out_ref, ds_ref, keep_ref, send_ref, dvec_ref, act_s, slope_s, branch_s, low_s, dbranch_s, cot_s, out_s, dex_s, dco_s, ex_s, co_s, sems, own_sems = refs
    slabs = unit2_ref.shape[0]
    chunks = ex_s.shape[0]
    owners = co_s.shape[0] // 4
    first, second = feed_copies(place_ref, begin, pieces, ex_s, co_s, sems)
    cot_copy = pltpu.make_async_copy(cot_ref, cot_s, own_sems.at[0])
    out_copy = pltpu.make_async_copy(out_s, out_ref, own_sems.at[1])
    for copy in first + second + [cot_copy]:
        copy.start()

    def rows(slab):
        return slice(slab * SLAB, (slab + 1) * SLAB)

    def contract(part):
        return co_s[part * owners : (part + 1) * owners].reshape(WIDTH, WIDTH)

    def state(slab):
        return unit2_ref[slab] * vec_ref[1:2, :] + vec_ref[4:5, :]

    for slab in range(slabs):
        low_s[rows(slab), :] = state(slab).astype(BF)
    for copy in first:
        copy.wait()
    for part in range(chunks):
        u = nn(low_s[...], ex_s[part])
        square = u * u
        bend = jnp.tanh(u * (ROOT + (ROOT * CUBE) * square))
        half = 0.5 + 0.5 * bend
        act_s[part] = (u * half).astype(BF)
        slope_s[part] = half + (u * half) * (1.0 - bend) * (ROOT + (3.0 * ROOT * CUBE) * square)
        if part == 0:
            for copy in second:
                copy.wait()
            branch_s[...] = nn(act_s[part], contract(part))
        else:
            branch_s[...] += nn(act_s[part], contract(part))
    cot_copy.wait()
    for slab in range(slabs):
        now = state(slab)
        unit, scale = norm_forward(vec_ref[8:9, :] * now + branch_s[rows(slab), :])
        out_s[slab] = (unit * vec_ref[2:3, :] + vec_ref[5:6, :]).astype(BF)
        up = cot_s[slab].astype(F32)
        dres = norm_backward(up, unit, scale, vec_ref[2:3, :])
        sums = (rows_sum(up * unit), rows_sum(up), rows_sum(dres * now))
        for row, value in enumerate(sums):
            if slab == 0:
                dvec_ref[row : row + 1, :] = value
            else:
                dvec_ref[row : row + 1, :] += value
        branch_s[rows(slab), :] = dres * vec_ref[8:9, :]
        dbranch_s[rows(slab), :] = dres.astype(BF)
    out_copy.start()
    low_t = low_s[...].T
    for part in range(chunks):
        dco_s[part] = tn(act_s[part], dbranch_s[...]).astype(BF)
        dhid = (nt(dbranch_s[...], contract(part)) * slope_s[part]).astype(BF)
        dex_s[part] = nn(low_t, dhid).astype(BF)
        branch_s[...] += nt(dhid, ex_s[part])
    for slab in range(slabs):
        ds_ref[slab] = branch_s[rows(slab), :]
    put_feed(place_ref, reduce_at, dex_s, dco_s, keep_ref, send_ref)
    out_copy.wait()


def put_gradients(place_ref, begin, dw_s, keep_ref, send_ref, first):
    blocks = keep_ref.shape[0]
    owners = blocks // dw_s.shape[0]
    rows = WIDTH // (2 * owners)
    core = place_ref[begin]
    for matrix in range(dw_s.shape[0]):
        for owner in range(owners):
            at = begin + 1 + matrix * owners + owner
            start = pl.multiple_of((2 * owner + core) * rows, rows)
            keep_ref[place_ref[at], first : first + rows, :] = dw_s[matrix, pl.ds(start, rows), :]
            start = pl.multiple_of((2 * owner + 1 - core) * rows, rows)
            send_ref[place_ref[at + blocks], first : first + rows, :] = dw_s[matrix, pl.ds(start, rows), :]


def put_vectors(place_ref, begin, dvec_s, count, keep_ref, send_ref, first):
    blocks = keep_ref.shape[0]
    owners = blocks // count
    columns = WIDTH // (2 * owners)
    core = place_ref[begin]
    rows = slice(first, first + 16)
    blank = jnp.zeros((16, WIDTH), BF)
    for block in range(blocks):
        keep_ref[block, rows, :] = blank
        send_ref[block, rows, :] = blank
    for owner in range(owners):
        low = dvec_s[:, 2 * owner * columns : (2 * owner + 1) * columns]
        high = dvec_s[:, (2 * owner + 1) * columns : (2 * owner + 2) * columns]
        rest = jnp.zeros((16, WIDTH - columns), F32)
        own = jnp.where(core == 0, low, high)
        other = jnp.where(core == 0, high, low)
        at = begin + 1 + owner
        keep_ref[place_ref[at], rows, :] = jnp.concatenate([own, rest], axis=1).astype(BF)
        send_ref[place_ref[at + blocks], rows, :] = jnp.concatenate([other, rest], axis=1).astype(BF)


def put_feed(place_ref, begin, dex_s, dco_s, keep_ref, send_ref):
    blocks = keep_ref.shape[0]
    owners = blocks // 4
    each = keep_ref.shape[1] // 2
    core = place_ref[begin]
    for pair in range(4):
        for owner in range(owners):
            at = begin + 1 + pair * owners + owner
            for out_ref, on, block in ((keep_ref, core, place_ref[at]), (send_ref, 1 - core, place_ref[at + blocks])):
                shard = 2 * owner + on
                for side in range(2):
                    number = 2 * pair + side
                    rows = slice(side * each, (side + 1) * each)
                    if number < 4:
                        out_ref[block, rows, :] = dex_s[number, pl.ds(pl.multiple_of(shard * each, each), each), :]
                    else:
                        row = (shard * 4 + number - 4) * each
                        chunk = row // WIDTH
                        out_ref[block, rows, :] = dco_s[chunk, pl.ds(pl.multiple_of(row - chunk * WIDTH, each), each), :]


def fetcher(pairs, sems):
    step = pl.program_id(0)

    def copy(number, slab):
        return pltpu.make_async_copy(pairs[number][0].at[slab], pairs[number][1].at[slab], sems.at[number, slab])

    @pl.when(step == 0)
    def _():
        for slab in range(pairs[0][1].shape[0]):
            for number in range(len(pairs)):
                copy(number, slab).start()

    def wait(first, last):
        for number in range(first, last):
            copy(number, step).wait()

    return wait


def all_rows(ref):
    return ref[...].reshape(-1, WIDTH)


def cross_backward(begin, place_ref, ds2_ref, unit2_ref, scale2_ref, w_ref, vec_ref, q_ref, k_ref, v_ref, r_ref, o_ref, low1_ref, mem_ref, e_ref,
                   ds1_ref, dk_ref, dv_ref, keep_ref, send_ref, dvec_ref,
                   q_s, k_s, v_s, r_s, o_s, low1_s, mem_s, dm_s, dq_s, dk_s, dv_s, dbranch_s, dkt_s, dvt_s, dw_s, sems, out_sems):
    step = pl.program_id(0)
    steps = pl.num_programs(0)
    wait = fetcher([(q_ref, q_s), (k_ref, k_s), (v_ref, v_s), (r_ref, r_s), (o_ref, o_s), (low1_ref, low1_s), (mem_ref, mem_s)], sems)
    outward = [pltpu.make_async_copy(dk_s, dk_ref, out_sems.at[0]), pltpu.make_async_copy(dv_s, dv_ref, out_sems.at[1])]

    @pl.when(step == 0)
    def _():
        dvec_ref[...] = jnp.zeros_like(dvec_ref)

    ds2_ref, unit2_ref, scale2_ref, ds1_ref = here(ds2_ref, unit2_ref, scale2_ref, ds1_ref)
    up = ds2_ref[...]
    unit = unit2_ref[...]
    dvec_ref[0:1, :] += rows_sum(up * unit)
    dvec_ref[1:2, :] += rows_sum(up)
    dres = norm_backward(up, unit, scale2_ref[...], vec_ref[1:2, :])
    dbranch = dres.astype(BF)
    dbranch_s[step] = dbranch
    dm_s[...] = nt(dbranch, w_ref[3])
    ds1_ref[...] = dres * vec_ref[7:8, :]
    wait(0, 5)
    attend_backward(e_ref.at[step], r_s.at[step], o_s.at[step], q_s.at[step], k_s.at[step], v_s.at[step], dm_s, dq_s.at[step], dkt_s, dvt_s)
    wait(5, 7)
    dvec_ref[2:3, :] += rows_sum(dbranch_s[step].astype(F32) * low1_s[step].astype(F32))
    ds1_ref[...] += nt(dq_s[step], w_ref[0])
    dk_s[step] = dkt_s[...].T
    dv_s[step] = dvt_s[...].T

    @pl.when(step == steps - 1)
    def _():
        for copy in outward:
            copy.start()
        dw_s[0] = tn(all_rows(low1_s), all_rows(dq_s)).astype(BF)
        memory_t = all_rows(mem_s).T
        dw_s[1] = nn(memory_t, all_rows(dk_s)).astype(BF)
        dw_s[2] = nn(memory_t, all_rows(dv_s)).astype(BF)
        dw_s[3] = tn(all_rows(o_s), all_rows(dbranch_s)).astype(BF)
        put_gradients(place_ref, begin, dw_s, keep_ref, send_ref, 0)
        for copy in outward:
            copy.wait()


def self_backward(ds1_ref, unit1_ref, scale1_ref, w3_ref, vec_ref, q_ref, k_ref, v_ref, r_ref, o_ref, x_ref, e_ref,
                  part_ref, dq_ref, dk_ref, dv_ref, dbranch_ref, dvec_ref, q_s, k_s, v_s, r_s, o_s, x_s, e_s, dm_s, dkt_s, dvt_s, sems):
    step = pl.program_id(0)
    wait = fetcher([(e_ref, e_s), (q_ref, q_s), (k_ref, k_s), (v_ref, v_s), (r_ref, r_s), (o_ref, o_s), (x_ref, x_s)], sems)

    @pl.when(step == 0)
    def _():
        dvec_ref[...] = jnp.zeros_like(dvec_ref)

    ds1_ref, unit1_ref, scale1_ref, part_ref, dq_ref, dk_ref, dv_ref, dbranch_ref = here(ds1_ref, unit1_ref, scale1_ref, part_ref, dq_ref, dk_ref, dv_ref, dbranch_ref)
    up = ds1_ref[...]
    unit = unit1_ref[...]
    dvec_ref[0:1, :] += rows_sum(up * unit)
    dvec_ref[1:2, :] += rows_sum(up)
    dres = norm_backward(up, unit, scale1_ref[...], vec_ref[0:1, :])
    dbranch = dres.astype(BF)
    dbranch_ref[...] = dbranch
    dm_s[...] = nt(dbranch, w3_ref[0])
    part_ref[...] = dres * vec_ref[6:7, :]
    wait(0, 6)
    attend_backward(e_s.at[step], r_s.at[step], o_s.at[step], q_s.at[step], k_s.at[step], v_s.at[step], dm_s, dq_ref, dkt_s, dvt_s)
    dk_ref[...] = dkt_s[...].T
    dv_ref[...] = dvt_s[...].T
    wait(6, 7)
    dvec_ref[2:3, :] += rows_sum(dbranch_ref[...].astype(F32) * x_s[step].astype(F32))


def self_weights(begin, place_ref, dq_ref, dk_ref, dv_ref, dbranch_ref, o_ref, x_ref, dvec1_ref, dvec2_ref, dvec3_ref, keep_ref, send_ref, o_s, x_s, dw_s, dvec_s, sems):
    copies = [pltpu.make_async_copy(x_ref, x_s, sems.at[0]), pltpu.make_async_copy(o_ref, o_s, sems.at[1])]
    for copy in copies:
        copy.start()
    dvec_s[...] = jnp.zeros_like(dvec_s)
    for row in range(3):
        for number, ref in enumerate((dvec1_ref, dvec2_ref, dvec3_ref)):
            dvec_s[3 * row + number : 3 * row + number + 1, :] = ref[row : row + 1, :]
    copies[0].wait()
    x_t = all_rows(x_s).T
    dw_s[0] = nn(x_t, all_rows(dq_ref)).astype(BF)
    dw_s[1] = nn(x_t, all_rows(dk_ref)).astype(BF)
    dw_s[2] = nn(x_t, all_rows(dv_ref)).astype(BF)
    copies[1].wait()
    dw_s[3] = tn(all_rows(o_s), all_rows(dbranch_ref)).astype(BF)
    put_gradients(place_ref, begin, dw_s, keep_ref, send_ref, 0)
    put_vectors(place_ref, begin, dvec_s, dw_s.shape[0], keep_ref, send_ref, keep_ref.shape[1] - 16)


def input_gradients(part_ref, dq_ref, dk_ref, dv_ref, w_ref, dk2_ref, dv2_ref, w2_ref, dx_ref, dmem_ref):
    part_ref, dq_ref, dk_ref, dv_ref, dk2_ref, dv2_ref, dx_ref, dmem_ref = here(part_ref, dq_ref, dk_ref, dv_ref, dk2_ref, dv2_ref, dx_ref, dmem_ref)
    dx_ref[...] = part_ref[...] + nt(dq_ref[...], w_ref[0]) + nt(dk_ref[...], w_ref[1]) + nt(dv_ref[...], w_ref[2])
    dmem_ref[...] = nt(dk2_ref[...], w2_ref[1]) + nt(dv2_ref[...], w2_ref[2])


def cut_shards(at, place_ref, stacked_ref, expand_ref, contract_ref, vec_ref, a_ref, b_ref, c_ref, a_s, b_s, ex_s, co_s, vec_s, sems):
    rows = stacked_ref.shape[1]
    half = pl.ds(pl.multiple_of(place_ref[at] * (rows // 2), rows // 2), rows // 2)
    start = pl.multiple_of(place_ref[at + 1] * (rows // 4), rows // 4)
    quarter = pl.ds(start, rows // 4)
    copies = [
        pltpu.make_async_copy(stacked_ref.at[0:3, half, :], a_s, sems.at[0]),
        pltpu.make_async_copy(stacked_ref.at[3:8, quarter, :], b_s, sems.at[1]),
        pltpu.make_async_copy(vec_ref, vec_s, sems.at[2]),
        pltpu.make_async_copy(expand_ref.at[quarter, :], ex_s, sems.at[3]),
    ]
    copies += [
        pltpu.make_async_copy(contract_ref.at[pl.ds(pl.multiple_of(part * rows + start, rows // 4), rows // 4), :], co_s.at[part], sems.at[4 + part])
        for part in range(4)
    ]
    for copy in copies:
        copy.start()
    for copy in copies:
        copy.wait()
    a_ref[0] = a_s[...].astype(BF)
    for index, matrix in enumerate((4, 5, 6, 7, 3)):
        b_ref[0, index] = b_s[matrix - 3].astype(BF)
    vec = jnp.concatenate([vec_s[...]] * (WIDTH // vec_ref.shape[1]), axis=1)
    owner = lax.broadcasted_iota(jnp.int32, vec.shape, 1) // vec_ref.shape[1]
    vec = jnp.where(owner == place_ref[at + 2], vec, 0.0)
    b_ref[0, 5] = jnp.concatenate([vec, jnp.zeros((rows // 4 - vec.shape[0], WIDTH), F32)], axis=0).astype(BF)
    for part in range(4):
        c_ref[0, part] = ex_s[:, part * WIDTH : (part + 1) * WIDTH].astype(BF)
        c_ref[0, 4 + part] = co_s[part].astype(BF)


def per_slab(*tail):
    return pl.BlockSpec((1,) + tail, lambda m: (m,) + (0,) * len(tail))


def fixed(*dims):
    return pl.BlockSpec(dims, lambda m: (0,) * len(dims), pipeline_mode=pl.Buffered(1))


def shape(dims, kind):
    return jax.ShapeDtypeStruct(tuple(dims), kind)


def options(mib):
    return pltpu.CompilerParams(dimension_semantics=("arbitrary",), vmem_limit_bytes=mib * MIB)


def estimate(microseconds):
    return pl.CostEstimate(flops=int(microseconds * 1e9), bytes_accessed=1 << 20, transcendentals=0)


SCALARS = pl.BlockSpec(memory_space=pltpu.SMEM)
ANYWHERE = pl.BlockSpec(memory_space=pl.ANY)
RESIDENT = pl.BlockSpec(memory_space=pltpu.VMEM)
ROWS = per_slab(SLAB, WIDTH)
SCALE = per_slab(SLAB, 1)


def near(*arrays):
    return tuple(pltpu.with_memory_space_constraint(array, pltpu.VMEM) for array in arrays)


def far(*arrays):
    return tuple(pltpu.with_memory_space_constraint(array, pltpu.HBM) for array in arrays)


def near_shape(dims, kind):
    return pltpu.VMEM(tuple(dims), kind)


def far_shape(dims, kind):
    return pltpu.HBM(tuple(dims), kind)


def slabs(g, kind, place=far_shape):
    return place((g, SLAB, WIDTH), kind)


def powers_shape(g, place):
    return place((g, HEADS, SLAB, SLAB), BF)


def run_cut_shards(at, place, stacked, expand, contract, vec):
    rows = stacked.shape[1]
    return pl.pallas_call(
        functools.partial(cut_shards, at),
        in_specs=[SCALARS] + [ANYWHERE] * 4,
        out_specs=[RESIDENT] * 3,
        out_shape=[shape((1, 3, rows // 2, WIDTH), BF), shape((1, 6, rows // 4, WIDTH), BF), shape((1, 8, rows // 4, WIDTH), BF)],
        scratch_shapes=[
            pltpu.VMEM((3, rows // 2, WIDTH), F32),
            pltpu.VMEM((5, rows // 4, WIDTH), F32),
            pltpu.VMEM((rows // 4, expand.shape[1]), F32),
            pltpu.VMEM((4, rows // 4, WIDTH), F32),
            pltpu.VMEM(vec.shape, F32),
            pltpu.SemaphoreType.DMA((8,)),
        ],
        compiler_params=pltpu.CompilerParams(vmem_limit_bytes=16 * MIB),
        name="cut_shards",
    )(place, *far(stacked, expand, contract, vec))


def run_self_forward(first, place, lengths, x, w):
    g = x.shape[0]
    return pl.pallas_call(
        functools.partial(self_forward, len(w), first),
        grid=(g,),
        in_specs=[SCALARS, SCALARS, ROWS] + [ANYWHERE] * len(w),
        out_specs=[fixed(3, WIDTH, WIDTH), ROWS, ROWS, ROWS, ANYWHERE, ROWS, RESIDENT],
        out_shape=[far_shape((3, WIDTH, WIDTH), BF)] + [slabs(g, BF)] * 3 + [powers_shape(g, far_shape), slabs(g, BF), slabs(g, BF, near_shape)],
        scratch_shapes=[pltpu.VMEM((g, HEADS, SLAB, SLAB), BF), pltpu.SemaphoreType.DMA((sum(piece.shape[0] for piece in w),)), pltpu.SemaphoreType.DMA((g, HEADS))],
        compiler_params=options(32),
        cost_estimate=estimate(12),
        name="self_forward",
    )(place, lengths, x, *w)


def run_cross_inputs(first, owners, place, o1, x, memory, w):
    g = memory.shape[0]
    return pl.pallas_call(
        functools.partial(cross_inputs, len(w), first, owners),
        grid=(g,),
        in_specs=[SCALARS, RESIDENT, ROWS, ROWS] + [ANYWHERE] * len(w),
        out_specs=[fixed(6, WIDTH, WIDTH), fixed(16, WIDTH), ROWS, ROWS, ROWS, RESIDENT, ROWS, SCALE, ROWS],
        out_shape=[far_shape((6, WIDTH, WIDTH), BF), far_shape((16, WIDTH), F32)]
        + [slabs(g, BF)] * 3
        + [slabs(g, F32, near_shape), slabs(g, F32), far_shape((g, SLAB, 1), F32), slabs(g, BF)],
        scratch_shapes=[pltpu.SemaphoreType.DMA((sum(piece.shape[0] for piece in w),))],
        compiler_params=options(24),
        cost_estimate=estimate(7),
        name="cross_inputs",
    )(place, *near(o1), x, memory, *w)


def run_cross_forward(lengths, q, k, v, unit1, w, vec):
    g = q.shape[0]
    last = pl.BlockSpec((1, WIDTH, WIDTH), lambda m: (3, 0, 0))
    return pl.pallas_call(
        cross_forward,
        grid=(g,),
        in_specs=[SCALARS, ROWS, ROWS, ROWS, RESIDENT, last, fixed(16, WIDTH)],
        out_specs=[RESIDENT, ROWS, ROWS, RESIDENT, ROWS, SCALE],
        out_shape=[powers_shape(g, near_shape), slabs(g, BF), slabs(g, BF), slabs(g, F32, near_shape), slabs(g, F32), far_shape((g, SLAB, 1), F32)],
        compiler_params=options(24),
        cost_estimate=estimate(11),
        name="cross_forward",
    )(lengths, *far(q, k, v), *near(unit1), *far(w, vec))


def run_feed(begin, reduce_at, owners, place, unit2, cot, w, vec):
    g = unit2.shape[0]
    rows = WIDTH // owners
    pieces = sum(piece.shape[0] for piece in w)
    dims = (2 * owners, 2 * rows, WIDTH)
    tokens = g * SLAB
    return pl.pallas_call(
        functools.partial(feed_both, len(w), begin, reduce_at),
        grid=(1,),
        in_specs=[SCALARS, RESIDENT, ANYWHERE, fixed(16, WIDTH)] + [ANYWHERE] * len(w),
        out_specs=[ANYWHERE, RESIDENT, RESIDENT, RESIDENT, fixed(8, WIDTH)],
        out_shape=[slabs(g, BF), slabs(g, F32, near_shape)] + [near_shape(dims, BF)] * 2 + [far_shape((8, WIDTH), F32)],
        scratch_shapes=[
            pltpu.VMEM((4, tokens, WIDTH), BF),
            pltpu.VMEM((4, tokens, WIDTH), F32),
            pltpu.VMEM((tokens, WIDTH), F32),
            pltpu.VMEM((tokens, WIDTH), BF),
            pltpu.VMEM((tokens, WIDTH), BF),
            pltpu.VMEM((g, SLAB, WIDTH), BF),
            pltpu.VMEM((g, SLAB, WIDTH), BF),
            pltpu.VMEM((4, WIDTH, WIDTH), BF),
            pltpu.VMEM((4, WIDTH, WIDTH), BF),
            pltpu.VMEM((4, WIDTH, WIDTH), BF),
            pltpu.VMEM((4 * owners, rows, WIDTH), BF),
            pltpu.SemaphoreType.DMA((2, pieces)),
            pltpu.SemaphoreType.DMA((2,)),
        ],
        compiler_params=options(FEED_MIB),
        cost_estimate=estimate(24),
        name="feed_both",
    )(place, *near(unit2), cot, *far(vec), *w)


def slab_scratch(g, kinds):
    return [pltpu.VMEM((g, SLAB, WIDTH), kind) for kind in kinds]


def run_cross_backward(begin, place, owners, ds2, unit2, scale2, low1, memory, w, vec, saved):
    g = memory.shape[0]
    dims = (4 * owners, WIDTH // (2 * owners), WIDTH)
    q, k, v, e, r, o = saved
    return pl.pallas_call(
        functools.partial(cross_backward, begin),
        grid=(g,),
        in_specs=[SCALARS, RESIDENT, ROWS, SCALE, fixed(4, WIDTH, WIDTH), fixed(16, WIDTH)] + [ANYWHERE] * 7 + [RESIDENT],
        out_specs=[RESIDENT, ANYWHERE, ANYWHERE, RESIDENT, RESIDENT, fixed(8, WIDTH)],
        out_shape=[slabs(g, F32, near_shape), slabs(g, BF), slabs(g, BF), near_shape(dims, BF), near_shape(dims, BF), far_shape((8, WIDTH), F32)],
        scratch_shapes=slab_scratch(g, [BF] * 7)
        + [pltpu.VMEM((SLAB, WIDTH), F32)]
        + slab_scratch(g, [BF] * 4)
        + [pltpu.VMEM((WIDTH, SLAB), BF)] * 2
        + [pltpu.VMEM((4, WIDTH, WIDTH), BF), pltpu.SemaphoreType.DMA((7, g)), pltpu.SemaphoreType.DMA((2,))],
        compiler_params=options(CROSS_MIB),
        cost_estimate=estimate(19),
        name="cross_backward",
    )(place, *near(ds2), *far(unit2, scale2, w, vec, q, k, v, r, o, low1), memory, *near(e))


def run_self_backward(ds1, unit1, scale1, x, w_cross, vec, saved):
    g = x.shape[0]
    q, k, v, e, r, o = saved
    third = pl.BlockSpec((1, WIDTH, WIDTH), lambda m: (4, 0, 0))
    return pl.pallas_call(
        self_backward,
        grid=(g,),
        in_specs=[RESIDENT, ROWS, SCALE, third, fixed(16, WIDTH)] + [ANYWHERE] * 7,
        out_specs=[ROWS] + [RESIDENT] * 4 + [fixed(8, WIDTH)],
        out_shape=[slabs(g, F32)] + [slabs(g, BF, near_shape)] * 4 + [far_shape((8, WIDTH), F32)],
        scratch_shapes=slab_scratch(g, [BF] * 6)
        + [pltpu.VMEM((g, HEADS, SLAB, SLAB), BF), pltpu.VMEM((SLAB, WIDTH), F32)]
        + [pltpu.VMEM((WIDTH, SLAB), BF)] * 2
        + [pltpu.SemaphoreType.DMA((7, g))],
        compiler_params=options(SELF_MIB),
        cost_estimate=estimate(17),
        name="self_backward",
    )(*near(ds1), *far(unit1, scale1, w_cross, vec, q, k, v, r, o), x, *far(e))


def run_self_weights(begin, place, owners, x, o, grads, dvecs):
    g = x.shape[0]
    dims = (4 * owners, WIDTH // (2 * owners) + 16, WIDTH)
    return pl.pallas_call(
        functools.partial(self_weights, begin),
        grid=(1,),
        in_specs=[SCALARS] + [RESIDENT] * 4 + [ANYWHERE] * 2 + [fixed(8, WIDTH)] * 3,
        out_specs=[RESIDENT] * 2,
        out_shape=[near_shape(dims, BF)] * 2,
        scratch_shapes=slab_scratch(g, [BF] * 2) + [pltpu.VMEM((4, WIDTH, WIDTH), BF), pltpu.VMEM((16, WIDTH), F32), pltpu.SemaphoreType.DMA((2,))],
        compiler_params=options(24),
        cost_estimate=estimate(4),
        name="self_weights",
    )(place, *near(*grads), *far(o), x, *far(*dvecs))


def run_input_gradients(part, dq, dk, dv, w, dk2, dv2, w2):
    g = part.shape[0]
    return pl.pallas_call(
        input_gradients,
        grid=(g,),
        in_specs=[ROWS] + [RESIDENT] * 3 + [fixed(3, WIDTH, WIDTH), ROWS, ROWS, fixed(3, WIDTH, WIDTH)],
        out_specs=[ROWS, ROWS],
        out_shape=[slabs(g, F32), slabs(g, F32)],
        compiler_params=options(28),
        cost_estimate=estimate(6),
        name="input_gradients",
    )(*far(part), *near(dq, dk, dv), *far(w, dk2, dv2, w2))
def adam_update(weight, first_moment, second_moment, gradient):
    correction = 1.0 - 0.5**STEP
    first_next = 0.5 * first_moment + 0.5 * gradient
    second_next = 0.5 * second_moment + 0.5 * gradient * gradient
    weight_next = weight - LEARN_RATE * (first_next / correction) / (jnp.sqrt(second_next / correction) + ADAM_EPS)
    return (weight_next, first_next, second_next)


def picked(order, parts):
    inside = order % 2
    return jnp.where(order < 2, parts[0][inside].astype(F32), parts[1][inside].astype(F32))


def adam_stacked(at, place_ref, low_ref, high_ref, w_ref, m_ref, s_ref, vw_ref, vm_ref, vs_ref, w_out, m_out, s_out, vw_out, vm_out, vs_out):
    rows = w_ref.shape[1]
    group = pl.program_id(0)

    def update(first):
        for matrix in range(4):
            grad = picked(place_ref[at + matrix], (low_ref, high_ref))[first : first + rows]
            w_out[matrix], m_out[matrix], s_out[matrix] = adam_update(w_ref[matrix], m_ref[matrix], s_ref[matrix], grad)

    @pl.when(group == 0)
    def _():
        update(0)
        grad = picked(place_ref[at], (low_ref, high_ref))[rows : rows + vw_ref.shape[0], : vw_ref.shape[1]]
        vw_out[...], vm_out[...], vs_out[...] = adam_update(vw_ref[...], vm_ref[...], vs_ref[...], grad)

    @pl.when(group == 1)
    def _():
        update(rows + 16)


def run_adam_stacked(at, place, low, high, stacked, vectors):
    rows = stacked[0].shape[1]
    block = pl.BlockSpec((4, rows, WIDTH), lambda group: (group, 0, 0))
    vector = fixed(*vectors[0].shape)
    return pl.pallas_call(
        functools.partial(adam_stacked, at),
        grid=(2,),
        in_specs=[SCALARS, fixed(*low.shape), fixed(*high.shape)] + [block] * 3 + [vector] * 3,
        out_specs=[block] * 3 + [vector] * 3,
        out_shape=[shape(a.shape, F32) for a in tuple(stacked) + tuple(vectors)],
        compiler_params=options(24),
        cost_estimate=estimate(4),
        name="adam_stacked",
    )(place, low, high, *stacked, *vectors)


def adam_feed(at, place_ref, low_ref, high_ref, *refs):
    rows = low_ref.shape[1] // 2

    def grad(number):
        return picked(place_ref[at + number // 2], (low_ref, high_ref))[number % 2 * rows : (number % 2 + 1) * rows]

    for part in range(4):
        where = (slice(None), slice(part * WIDTH, (part + 1) * WIDTH))
        refs[6][where], refs[7][where], refs[8][where] = adam_update(*(ref[where] for ref in refs[0:3]), grad(part))
        where = (slice(part * rows, (part + 1) * rows), slice(None))
        refs[9][where], refs[10][where], refs[11][where] = adam_update(*(ref[where] for ref in refs[3:6]), grad(4 + part))


def run_adam_feed(at, place, low, high, expand, contract):
    arrays = tuple(expand) + tuple(contract)
    whole = pl.BlockSpec(memory_space=pltpu.VMEM)
    return pl.pallas_call(
        functools.partial(adam_feed, at),
        in_specs=[SCALARS] + [whole] * 8,
        out_specs=[whole] * 6,
        out_shape=[shape(a.shape, F32) for a in arrays],
        compiler_params=pltpu.CompilerParams(vmem_limit_bytes=24 * MIB),
        cost_estimate=estimate(4),
        name="adam_feed",
    )(place, low, high, *arrays)


class Route:
    def __init__(self, m, n):
        self.m, self.n = m, n
        self.dp_bits = m.bit_length() - 1
        self.line_bits = n.bit_length() - 2
        self.line = n // 2

    def pairs(self, partner):
        return [(d * self.n + f, partner(d, f)) for d in range(self.m) for f in range(self.n)]

    def across_core(self):
        return self.pairs(lambda d, f: d * self.n + (f ^ 1))

    def along_line(self, mask):
        return self.pairs(lambda d, f: d * self.n + (f ^ (2 * mask)))

    def across_line(self, step):
        return self.pairs(lambda d, f: d * self.n + (f ^ (2 << (self.line_bits - 1 - step))))

    def across_dp(self, step):
        def partner(d, f):
            bit = step if f % 2 == 0 else self.dp_bits - 1 - step
            return (d ^ (1 << bit)) * self.n + f

        return self.pairs(partner)

    @staticmethod
    def spot(mask, bits, core):
        return mask if core == 0 else sum(((mask >> b) & 1) << (bits - 1 - b) for b in range(bits))

    def part(self, share, d, f):
        return sum(((d >> (bit if f % 2 == 0 else self.dp_bits - 1 - bit)) & 1) << bit for bit in range(share))

    def gather_row(self, share, d, f):
        z, c = divmod(f, 2)
        return [
            ((2 * (z ^ k) + who) << share) + (self.part(share, d, who) ^ step)
            for who in (c, 1 - c)
            for step in range(1 << share)
            for k in range(self.line)
        ]

    def reduce_row(self, d, f):
        z, c = divmod(f, 2)
        row = [c]
        for who in (c, 1 - c):
            line = [self.spot(owner ^ z, self.line_bits, 1) for owner in range(self.line)]
            row += [self.spot(j ^ d, self.dp_bits, who) * self.line + at for j in range(self.m) for at in line]
        return row + [self.spot(j ^ d, self.dp_bits, c) for j in range(self.m)]

    def part_row(self, d, f):
        return [self.part(1, d, f), self.part(2, d, f), f]

    def tables(self):
        kinds = (functools.partial(self.gather_row, 1), functools.partial(self.gather_row, 2), self.reduce_row, self.part_row)
        rows = [[kind(d, f) for kind in kinds] for d in range(self.m) for f in range(self.n)]
        ends = np.cumsum([0] + [len(row) for row in rows[0]])
        return np.array([sum(row, []) for row in rows], np.int32), ends


BOTH = ("dp", "fsdp")


def after(values, *earlier):
    return lax.optimization_barrier((values,) + earlier)[0]


def doubled(blocks, got):
    return jnp.concatenate([blocks, got], axis=0)


def per_device(
    inputs,
    memory,
    cotangent,
    lengths,
    stacked_weights,
    expand_weights,
    contract_weights,
    scale_vectors,
    stacked_first,
    stacked_second,
    expand_first,
    expand_second,
    contract_first,
    contract_second,
    vector_first,
    vector_second,
):
    m, n = lax.axis_size("dp"), lax.axis_size("fsdp")
    width = WIDTH // n
    slabs = inputs.shape[0] * lengths.shape[1]
    x = inputs.reshape(slabs, SLAB, WIDTH)
    mem = memory.reshape(slabs, SLAB, WIDTH)
    cot = cotangent.reshape(slabs, SLAB, WIDTH)
    by_hand = m == 4 and width == 64 and n == 8
    here = lax.axis_index("fsdp")
    lengths = lengths.reshape(slabs, 2, -1)
    if by_hand:
        route = Route(m, n)
        table, ends = route.tables()
        row = lax.dynamic_index_in_dim(jnp.asarray(table), lax.axis_index("dp") * n + here, keepdims=False)
        halves, quarters, reduced, parts = (int(end) for end in ends[:4])
        order = parts - m

        def swap(blocks, pairs):
            return lax.ppermute(blocks, BOTH, pairs)

        along = [route.along_line(mask) for mask in range(1, n // 2)]
        line = [route.across_line(step) for step in range(route.line_bits)]
        across = [route.across_dp(step) for step in range(route.dp_bits)]
        core = route.across_core()
        a, b, c = run_cut_shards(parts, row, stacked_weights, expand_weights, contract_weights, scale_vectors)
        got = lax.optimization_barrier(tuple(swap(a, pairs) for pairs in along) + tuple(swap(b, pairs) for pairs in along))
        a, b = jnp.concatenate([a, *got[:3]], axis=0), jnp.concatenate([b, *got[3:]], axis=0)
        a_across, a_core, b_across = lax.optimization_barrier((swap(a, across[0]), swap(a, core), swap(b, across[0])))
        b = doubled(b, b_across)
        c = after(c, b)
        b_across, b_core, c_line = swap(b, across[1]), swap(b, core), [swap(c, pairs) for pairs in along]
        w_self, *saved1 = run_self_forward(halves, row, lengths, after(x, b), (a, a_across, a_core, swap(a_across, core)))
        b_across, *c_line = after((b_across, *c_line), saved1[-1])
        c = jnp.concatenate([c, *c_line], axis=0)
        b_across = after(b_across, c)
        c_across = swap(c, across[0])
        w_cross = (b, b_across, b_core, swap(b_across, core))
        w_cross, vec, *qkv2, unit1, kept1, scale1, low1 = run_cross_inputs(quarters, n, row, saved1[-1], x, mem, w_cross)
        c = doubled(c, after(c_across, unit1))
        c_across, c_core = swap(c, across[1]), swap(c, core)
        *saved2, unit2, kept2, scale2 = run_cross_forward(lengths, *qkv2, after(unit1, c), w_cross, vec)
        saved2 = qkv2 + saved2
        c_across = after(c_across, unit2)
        w_feed = (c, c_across, c_core, swap(c_across, core))
        out, ds2, feed_keep, feed_send, dvec3 = run_feed(quarters, reduced, n, row, unit2, cot, w_feed, vec)
        feed_got = swap(feed_send, core)
        ds1, dk2, dv2, cross_keep, cross_send, dvec2 = run_cross_backward(reduced, row, n // 2, ds2, kept2, scale2, low1, mem, w_cross, vec, saved2)
        feed_got = after(feed_got, ds1)
        feed_out, feed = feed_keep[8:] + feed_got[8:], feed_keep[:8] + feed_got[:8]
        feed_got, cross_got = swap(feed_out, across[1]), swap(cross_send, core)
        part, dq, dk, dv, dbranch, dvec1 = run_self_backward(after(ds1, feed_out), kept1, scale1, x, w_cross, vec, saved1)
        feed_got, cross_got = after((feed_got, cross_got), dq)
        feed_out, feed = feed[4:] + feed_got[4:], feed[:4] + feed_got[:4]
        cross_out, cross = cross_keep[8:] + cross_got[8:], cross_keep[:8] + cross_got[:8]
        feed_got, cross_got = swap(feed_out, across[0]), swap(cross_out, across[1])
        keep, send = run_self_weights(reduced, row, n // 2, x, saved1[-1], after((dq, dk, dv, dbranch), cross_out, feed_out), (dvec1, dvec2, dvec3))
        got = swap(send, core)
        dx, dmem = run_input_gradients(after(part, send), dq, dk, dv, w_self, dk2, dv2, w_cross)
        got = after(got, dx)
        out_part, total = keep[8:] + got[8:], keep[:8] + got[:8]
        feed_got, cross_got = after((feed_got, cross_got), got)
        feed = feed + feed_got
        feed_out, feed = feed[2:], feed[:2]
        got, feed_got = lax.optimization_barrier((swap(out_part, across[1]), swap(after(feed_out, out_part), line[1])))
        out_part = jnp.concatenate([total[4:] + got[4:], cross[4:] + cross_got[4:]], axis=1)
        total = jnp.concatenate([total[:4] + got[:4], cross[:4] + cross_got[:4]], axis=1)
        feed_out, feed = feed[1:] + feed_got[1:], feed[:1] + feed_got[:1]
        got, feed_got = lax.optimization_barrier((swap(out_part, across[0]), swap(after(feed_out, out_part), line[0])))
        out_part, total = total[2:] + got[2:], total[:2] + got[:2]
        feed = feed + feed_got
        got, feed_got = lax.optimization_barrier((swap(out_part, line[1]), swap(after(feed, out_part), across[0])))
        out_part, total = total[1:] + got[1:], total[:1] + got[:1]
        feed = doubled(feed, feed_got)
        got, feed_got = lax.optimization_barrier((swap(out_part, line[0]), swap(after(feed, out_part), across[1])))
        total = total + got
        total = doubled(total, swap(total, across[0]))
        feed_next = run_adam_feed(order, row, after(feed, total), feed_got, (expand_weights, expand_first, expand_second), (contract_weights, contract_first, contract_second))
        got = after(swap(total, across[1]), feed_next[0])
        *stacked_next, vw, vm, vs = run_adam_stacked(order, row, total, got, (stacked_weights, stacked_first, stacked_second), (scale_vectors, vector_first, vector_second))
        vector_next = (vw, vm, vs)
    else:
        row = jnp.array([0, 1, 0] + [0, 1, 2, 3] * 2, jnp.int32)
        expand_blocks = jnp.swapaxes(expand_weights.reshape(width, 4, WIDTH), 0, 1)
        vec_shard = lax.dynamic_update_slice(jnp.zeros((16, WIDTH), BF), scale_vectors.astype(BF), (0, here * width))
        all_low = lax.all_gather(stacked_weights.astype(BF), "fsdp", axis=1, tiled=True)
        vec_full = jnp.sum(lax.all_gather(vec_shard, "fsdp", axis=0).astype(F32), axis=0).astype(BF)
        vec_full = jnp.pad(vec_full, ((0, WIDTH - 16), (0, 0)))
        ex = lax.all_gather(expand_blocks.astype(BF), "fsdp", axis=1, tiled=True).reshape(4, 2, -1, WIDTH)
        co = lax.all_gather(contract_weights.astype(BF), "fsdp", axis=0, tiled=True).reshape(2, 4, -1, WIDTH)
        w_self = tuple(all_low[None, :3].reshape(1, 3, 2, -1, WIDTH)[:, :, core] for core in range(2))
        w_cross = jnp.concatenate([all_low[4:], all_low[3:4], vec_full[None]], axis=0).reshape(1, 6, 2, -1, WIDTH)
        w_feed = tuple(jnp.concatenate([ex[:, core], co[core]], axis=0)[None] for core in range(2))
        w_self, *saved1 = run_self_forward(0, row, lengths, x, w_self)
        w_cross, vec, *qkv2, unit1, kept1, scale1, low1 = run_cross_inputs(0, 1, row, saved1[-1], x, mem, (w_cross[:, :, 0], w_cross[:, :, 1]))
        *saved2, unit2, kept2, scale2 = run_cross_forward(lengths, *qkv2, unit1, w_cross, vec)
        saved2 = qkv2 + saved2
        out, ds2, feed_keep, feed_send, dvec3 = run_feed(0, 2, 2, row, unit2, cot, w_feed, vec)
        dw_feed = jnp.stack([feed_keep, feed_send]).reshape(2, 8, WIDTH // 2, WIDTH)
        dex = jnp.swapaxes(dw_feed[:, :4], 0, 1).reshape(4, n, width, WIDTH)
        dco = dw_feed[:, 4:].reshape(n, 4, width, WIDTH)
        dw_feed = jnp.concatenate([jnp.swapaxes(dex, 0, 1), dco], axis=1)
        grad_feed = lax.psum(lax.psum_scatter(dw_feed, "fsdp", scatter_dimension=0, tiled=False), "dp")
        ds1, dk2, dv2, cross_keep, cross_send, dvec2 = run_cross_backward(2, row, 1, ds2, kept2, scale2, low1, mem, w_cross, vec, saved2)
        part, dq, dk, dv, dbranch, dvec1 = run_self_backward(ds1, kept1, scale1, x, w_cross, vec, saved1)
        keep, send = run_self_weights(2, row, 1, x, saved1[-1], (dq, dk, dv, dbranch), (dvec1, dvec2, dvec3))
        dx, dmem = run_input_gradients(part, dq, dk, dv, w_self, dk2, dv2, w_cross)
        both, cross_both = jnp.stack([keep, send], axis=1), jnp.stack([cross_keep, cross_send], axis=1)
        rows = WIDTH // 2
        grad_vector = lax.psum(both[0, :, rows : rows + 9, :rows].astype(F32), BOTH)
        grad_vector = jnp.swapaxes(grad_vector, 0, 1).reshape(9, WIDTH)
        grad_vector = lax.dynamic_slice(grad_vector, (0, here * width), (9, width))
        both = jnp.concatenate([both[:, :, :rows], cross_both], axis=0).reshape(8, WIDTH, WIDTH)
        both = lax.psum(lax.psum_scatter(both, "fsdp", scatter_dimension=1, tiled=True), "dp")
        stacked_next = adam_update(stacked_weights, stacked_first, stacked_second, both.astype(F32))
        vector_next = adam_update(scale_vectors, vector_first, vector_second, grad_vector)
        feed_next = run_adam_feed(0, jnp.arange(4, dtype=jnp.int32), *grad_feed.reshape(2, 2, 2 * width, WIDTH), (expand_weights, expand_first, expand_second), (contract_weights, contract_first, contract_second))
    expand_next, contract_next = feed_next[:3], feed_next[3:]
    return (
        out.reshape(inputs.shape),
        dx.reshape(inputs.shape),
        dmem.reshape(inputs.shape),
        stacked_next[0],
        expand_next[0],
        contract_next[0],
        vector_next[0],
        stacked_next[1],
        stacked_next[2],
        expand_next[1],
        expand_next[2],
        contract_next[1],
        contract_next[2],
        vector_next[1],
        vector_next[2],
    )


def solution(mesh):
    tokens = P(None, ("dp", "fsdp"), None)
    pieces = P(None, ("dp", "fsdp"), None, None)
    stacked = P(None, "fsdp", None)
    rows = P("fsdp", None)
    columns = P(None, "fsdp")
    return jax.shard_map(
        per_device,
        mesh=mesh,
        in_specs=(tokens, tokens, tokens, pieces, stacked, rows, rows, columns) + (stacked, stacked, rows, rows, rows, rows, columns, columns),
        out_specs=(tokens, tokens, tokens, stacked, rows, rows, columns) + (stacked, stacked, rows, rows, rows, rows, columns, columns),
        check_vma=False,
    )
```

```python
import functools
import math

import jax
import jax.numpy as jnp
import numpy as np
from jax import lax
from jax.experimental import pallas as pl
from jax.experimental.pallas import tpu as pltpu
from jax.sharding import PartitionSpec as P

HEADS = 8
HEAD = 64
SLAB = 512
WIDTH = 512
PAIR = 2 * HEAD
STEP = 3
NORM_EPS = 1e-05
ADAM_EPS = 1e-08
LEARN_RATE = 0.2
FAR = -1e30
LOG2E = math.log2(math.e)
QSCALE = HEAD**-0.5 * LOG2E
TILE = 256
BF = jnp.bfloat16
F32 = jnp.float32
MIB = 1 << 20
FEED_MIB = 30
CROSS_MIB = 24
SELF_MIB = 40


def nn(a, b):
    return jnp.dot(a, b, preferred_element_type=F32)


def nt(a, b):
    return lax.dot_general(a, b, (((1,), (1,)), ((), ())), preferred_element_type=F32)


def tn(a, b):
    return lax.dot_general(a, b, (((0,), (0,)), ((), ())), preferred_element_type=F32)


def norm_forward(residual, eps=NORM_EPS):
    centred = residual - jnp.mean(residual, axis=-1, keepdims=True)
    spread = jnp.mean(centred * centred, axis=-1, keepdims=True)
    scale = lax.rsqrt(spread + eps)
    return centred * scale, scale


def norm_backward(upstream, unit, scale, gain):
    inner = upstream * gain
    first = jnp.mean(inner, axis=-1, keepdims=True)
    second = jnp.mean(inner * unit, axis=-1, keepdims=True)
    return scale * (inner - first - unit * second)


def rows_sum(values):
    return jnp.sum(values, axis=0, keepdims=True)


def first_lanes(rows):
    return lax.broadcasted_iota(jnp.int32, (rows, PAIR), 1) < HEAD


def attend_forward(q_ref, k_ref, v_ref, queries_in, keys_out, e_ref, o_ref, r_ref, causal, after=None):
    low = first_lanes(SLAB)
    ones = jnp.ones((SLAB, PAIR), BF)
    spans = ((0, TILE, TILE), (TILE, SLAB, SLAB)) if causal else ((0, SLAB, SLAB),)
    if causal:
        query_at = lax.broadcasted_iota(jnp.int32, (TILE, TILE), 0)
        key_at = lax.broadcasted_iota(jnp.int32, (TILE, TILE), 1)
        bias = jnp.where(key_at <= query_at, 0.0, FAR).astype(F32)
        blank = jnp.zeros((TILE, TILE), BF)

    def lanes(head):
        return slice(head // 2 * PAIR, (head // 2 + 1) * PAIR)

    def scores(head):
        left, right = q_ref[:, lanes(head)], k_ref[:, lanes(head)]
        if head % 2 == 0:
            left, right = jnp.where(low, left, queries_in), jnp.where(low, right, keys_out)
        else:
            left, right = jnp.where(low, queries_in, left), jnp.where(low, keys_out, right)
        return [nt(left[first:last], right[:depth]) for first, last, depth in spans]

    def powers(head, found):
        results = []
        for (first, last, depth), part in zip(spans, found):
            if causal:
                end = part[:, depth - TILE :] + bias
                part = end if depth == TILE else jnp.concatenate([part[:, : depth - TILE], end], axis=1)
            power = jnp.exp2(part - jnp.max(part, axis=1, keepdims=True)).astype(BF)
            e_ref[head, first:last, :depth] = power
            if depth < SLAB:
                e_ref[head, first:last, depth:] = blank
            results.append(power)
        if after is not None:
            after(head)
        return results

    def mixes(head, found):
        right = jnp.concatenate([v_ref[:, lanes(head)], ones], axis=1)
        results = []
        for (_, _, depth), power in zip(spans, found):
            mixed = nn(power, right[:depth])
            inverse = 1.0 / mixed[:, PAIR:]
            results.append((mixed[:, :PAIR] * inverse, inverse))
        return results

    def put(pair, even, odd):
        for (first, last, _), (mix_0, inverse_0), (mix_1, inverse_1) in zip(spans, even, odd):
            here = first_lanes(last - first)
            o_ref[first:last, pair * PAIR : (pair + 1) * PAIR] = jnp.where(here, mix_0, mix_1).astype(BF)
            r_ref[first:last, pair * PAIR : (pair + 1) * PAIR] = jnp.where(here, inverse_0, inverse_1).astype(BF)

    following = scores(0)
    earlier = None
    mixed = {}
    for head in range(HEADS):
        found = following
        if head + 1 < HEADS:
            following = scores(head + 1)
        now = powers(head, found)
        if earlier is not None:
            mixed[head - 1] = mixes(head - 1, earlier)
            if head % 2 == 0:
                put(head // 2 - 1, mixed[head - 2], mixed[head - 1])
        earlier = now
    mixed[HEADS - 1] = mixes(HEADS - 1, earlier)
    put(HEADS // 2 - 1, mixed[HEADS - 2], mixed[HEADS - 1])


def attend_backward(e_ref, r_ref, o_ref, q_ref, k_ref, v_ref, dm_ref, dq_ref, dkt_ref, dvt_ref):
    low = first_lanes(SLAB)
    lane = lax.broadcasted_iota(jnp.int32, (SLAB, PAIR), 1) % HEAD
    units = jnp.where(lane < 2, 1.0, 0.0).astype(BF)
    none = jnp.zeros((), BF)
    qt = q_ref[...].T
    for pair in range(HEADS // 2):
        lanes = slice(pair * PAIR, (pair + 1) * PAIR)
        mixed = (dm_ref[:, lanes] * r_ref[:, lanes].astype(F32)).astype(BF)
        weighed = mixed.astype(F32) * o_ref[:, lanes].astype(F32)
        keys, values = k_ref[:, lanes], v_ref[:, lanes]
        mixed_t = mixed.T
        dq = []
        for side in range(2):
            head = 2 * pair + side
            rows = slice(head * HEAD, (head + 1) * HEAD)
            mine = low if side == 0 else ~low
            centre = jnp.sum(jnp.where(mine, weighed, 0.0), axis=1, keepdims=True)
            high = centre.astype(BF)
            rest = (centre - high.astype(F32)).astype(BF)
            column = jnp.where(lane == 0, -high, jnp.where(lane == 1, -rest, none))
            grad = nt(jnp.where(mine, mixed, column), jnp.where(mine, values, units))
            power = e_ref[head]
            score = (power.astype(F32) * grad).astype(BF)
            dq.append(nn(score, keys))
            dkt_ref[rows, :] = (nn(qt[rows], score) * (1.0 / LOG2E)).astype(BF)
            dvt_ref[rows, :] = nn(mixed_t[side * HEAD : (side + 1) * HEAD], power).astype(BF)
        dq_ref[:, lanes] = (jnp.where(low, dq[0], dq[1]) * HEAD**-0.5).astype(BF)


def piece_columns(lengths_ref, slab, side):
    column = lax.broadcasted_iota(jnp.int32, (1, PAIR), 1) % HEAD
    opening = jnp.zeros((1, PAIR), jnp.int32)
    closing = jnp.zeros((1, PAIR), jnp.int32)
    total = jnp.int32(0)
    for piece in range(lengths_ref.shape[2]):
        following = total + lengths_ref[slab, side, piece]
        opening = jnp.where(column == piece, total, opening)
        closing = jnp.where(column == piece, following, closing)
        total = following
    place = lax.broadcasted_iota(jnp.int32, (SLAB, PAIR), 0)
    return jnp.where((opening <= place) & (place < closing), 1.0, 0.0).astype(BF)


def outside(columns):
    return jnp.where(columns > 0, 0.0, FAR).astype(BF)


def load_pieces(place_ref, first, pieces, w_s, sems):
    copies = []
    for blocks in pieces:
        rows = blocks.shape[2]
        for index in range(blocks.shape[0]):
            start = pl.multiple_of(place_ref[first + len(copies)] * rows, rows)
            copies.append(pltpu.make_async_copy(blocks.at[index], w_s.at[:, pl.ds(start, rows), :], sems.at[len(copies)]))
    for copy in copies:
        copy.start()
    for copy in copies:
        copy.wait()


def load_once(place_ref, first, pieces, w_s, sems):
    @pl.when(pl.program_id(0) == 0)
    def _():
        load_pieces(place_ref, first, pieces, w_s, sems)


def here(*refs):
    step = pl.program_id(0)
    return [ref.at[step if ref.shape[0] > 1 else 0] for ref in refs]


def self_forward(count, first, place_ref, lengths_ref, x_ref, *refs):
    pieces, (out_ref, q_ref, k_ref, v_ref, e_ref, r_ref, o_ref, w_ref, e_s, sems, e_sems, out_sem) = refs[:count], refs[count:]
    load_once(place_ref, first, pieces, w_ref, sems)
    pass_on = pltpu.make_async_copy(w_ref, out_ref, out_sem)
    x_ref, q_ref, k_ref, v_ref, r_ref, o_ref = here(x_ref, q_ref, k_ref, v_ref, r_ref, o_ref)
    step = pl.program_id(0)

    @pl.when(step == 0)
    def _():
        pass_on.start()

    def store(slab, head):
        return pltpu.make_async_copy(e_s.at[slab, head], e_ref.at[slab, head], e_sems.at[slab, head])

    x = x_ref[...]
    q_ref[...] = (nn(x, w_ref[0]) * QSCALE).astype(BF)
    k_ref[...] = nn(x, w_ref[1]).astype(BF)
    v_ref[...] = nn(x, w_ref[2]).astype(BF)
    columns = piece_columns(lengths_ref, pl.program_id(0), 0)
    attend_forward(q_ref, k_ref, v_ref, columns, outside(columns), e_s.at[step], o_ref, r_ref, True, lambda head: store(step, head).start())

    @pl.when(step == pl.num_programs(0) - 1)
    def _():
        pass_on.wait()
        for slab in range(e_s.shape[0]):
            for head in range(HEADS):
                store(slab, head).wait()


def cross_inputs(count, first, owners, place_ref, o1_ref, x_ref, mem_ref, *refs):
    pieces, (out_ref, vec_ref, q_ref, k_ref, v_ref, unit1_ref, kept1_ref, scale1_ref, low1_ref, w_ref, sems, out_sem) = refs[:count], refs[count:]
    load_once(place_ref, first, pieces, w_ref, sems)
    pass_on = pltpu.make_async_copy(w_ref, out_ref, out_sem)

    @pl.when(pl.program_id(0) == 0)
    def _():
        pass_on.start()
        rows = WIDTH // owners
        total = w_ref[5, 0:16, :].astype(F32)
        for owner in range(1, owners):
            total = total + w_ref[5, owner * rows : owner * rows + 16, :].astype(F32)
        vec_ref[...] = total

    o1_ref, x_ref, mem_ref, q_ref, k_ref, v_ref = here(o1_ref, x_ref, mem_ref, q_ref, k_ref, v_ref)
    unit1_ref, kept1_ref, scale1_ref, low1_ref = here(unit1_ref, kept1_ref, scale1_ref, low1_ref)
    residual = vec_ref[6:7, :] * x_ref[...].astype(F32) + nn(o1_ref[...], w_ref[4])
    unit, scale = norm_forward(residual)
    unit1_ref[...] = unit
    kept1_ref[...] = unit
    scale1_ref[...] = scale
    low = (unit * vec_ref[0:1, :] + vec_ref[3:4, :]).astype(BF)
    low1_ref[...] = low
    memory = mem_ref[...]
    k_ref[...] = nn(memory, w_ref[1]).astype(BF)
    v_ref[...] = nn(memory, w_ref[2]).astype(BF)
    q_ref[...] = (nn(low, w_ref[0]) * QSCALE).astype(BF)

    @pl.when(pl.program_id(0) == pl.num_programs(0) - 1)
    def _():
        pass_on.wait()


def cross_forward(lengths_ref, q_ref, k_ref, v_ref, e_ref, r_ref, o_ref, kept_ref):
    slab = pl.program_id(0)
    q_ref, k_ref, v_ref, e_ref, r_ref, o_ref, kept_ref = here(q_ref, k_ref, v_ref, e_ref, r_ref, o_ref, kept_ref)
    queries_in, keys_out = piece_columns(lengths_ref, slab, 0), outside(piece_columns(lengths_ref, slab, 1))
    attend_forward(q_ref, k_ref, v_ref, queries_in, keys_out, e_ref, o_ref, r_ref, False)
    kept_ref[...] = o_ref[...]


CUBE = 0.044715
ROOT = math.sqrt(2.0 / math.pi)


def feed_copies(place_ref, begin, first, second, ex_s, co_s, sems):
    each = co_s.shape[1]
    results = [], []
    for side, pieces in enumerate((first, second)):
        for blocks in pieces:
            rows = blocks.shape[2]
            for index in range(blocks.shape[0]):
                number = len(results[side])
                start = place_ref[begin + number] * rows
                owner = start // each
                if side == 0:
                    goal = ex_s.at[:, pl.ds(pl.multiple_of(start, rows), rows), :]
                else:
                    goal = co_s.at[pl.ds(owner * 4, 4), pl.ds(pl.multiple_of(start - owner * each, rows), rows), :]
                results[side].append(pltpu.make_async_copy(blocks.at[index], goal, sems.at[side, number]))
    return results


def feed_both(count, begin, reduce_at, place_ref, o2_ref, unit1_ref, w_ref, cot_ref, vec_ref, *refs):
    pieces, refs = refs[: 2 * count], refs[2 * count :]
    (out_ref, ds_ref, unit_s, scale_ref, keep_ref, send_ref, dvec_ref,
     act_s, slope_s, branch_s, low_s, dbranch_s, cot_s, out_s, dex_s, dco_s, ex_s, co_s, sems, own_sems) = refs
    slabs = unit_s.shape[0]
    chunks = ex_s.shape[0]
    owners = co_s.shape[0] // 4
    first, second = feed_copies(place_ref, begin, pieces[:count], pieces[count:], ex_s, co_s, sems)
    cot_copy = pltpu.make_async_copy(cot_ref, cot_s, own_sems.at[0])
    out_copy = pltpu.make_async_copy(out_s, out_ref, own_sems.at[1])
    for copy in first + second + [cot_copy]:
        copy.start()

    def rows(slab):
        return slice(slab * SLAB, (slab + 1) * SLAB)

    def contract(part):
        return co_s[part * owners : (part + 1) * owners].reshape(WIDTH, WIDTH)

    def state(slab):
        return unit_s[slab] * vec_ref[1:2, :] + vec_ref[4:5, :]

    for slab in range(slabs):
        before = unit1_ref[slab] * vec_ref[0:1, :] + vec_ref[3:4, :]
        unit_s[slab], scale_ref[slab] = norm_forward(vec_ref[7:8, :] * before + nn(o2_ref[slab], w_ref[0]))
        low_s[rows(slab), :] = state(slab).astype(BF)
    for copy in first:
        copy.wait()
    following = nn(low_s[...], ex_s[0])
    for part in range(chunks):
        u = following
        if part + 1 < chunks:
            following = nn(low_s[...], ex_s[part + 1])
        square = u * u
        bend = jnp.tanh(u * (ROOT + (ROOT * CUBE) * square))
        half = 0.5 + 0.5 * bend
        act_s[part] = (u * half).astype(BF)
        slope_s[part] = half + (u * half) * (1.0 - bend) * (ROOT + (3.0 * ROOT * CUBE) * square)
        if part == 0:
            for copy in second:
                copy.wait()
            branch_s[...] = nn(act_s[part], contract(part))
        else:
            branch_s[...] += nn(act_s[part], contract(part))
    cot_copy.wait()
    for slab in range(slabs):
        now = state(slab)
        unit, scale = norm_forward(vec_ref[8:9, :] * now + branch_s[rows(slab), :])
        out_s[slab] = (unit * vec_ref[2:3, :] + vec_ref[5:6, :]).astype(BF)
        up = cot_s[slab].astype(F32)
        dres = norm_backward(up, unit, scale, vec_ref[2:3, :])
        sums = (rows_sum(up * unit), rows_sum(up), rows_sum(dres * now))
        for row, value in enumerate(sums):
            if slab == 0:
                dvec_ref[row : row + 1, :] = value
            else:
                dvec_ref[row : row + 1, :] += value
        branch_s[rows(slab), :] = dres * vec_ref[8:9, :]
        dbranch_s[rows(slab), :] = dres.astype(BF)
    out_copy.start()
    low_t = low_s[...].T
    for part in range(chunks):
        dco_s[part] = tn(act_s[part], dbranch_s[...]).astype(BF)
        dhid = (nt(dbranch_s[...], contract(part)) * slope_s[part]).astype(BF)
        dex_s[part] = nn(low_t, dhid).astype(BF)
        branch_s[...] += nt(dhid, ex_s[part])
    for slab in range(slabs):
        ds_ref[slab] = branch_s[rows(slab), :]
    put_feed(place_ref, reduce_at, dex_s, dco_s, keep_ref, send_ref)
    out_copy.wait()


def put_gradients(place_ref, begin, dw_s, keep_ref, send_ref, first):
    blocks = keep_ref.shape[0]
    owners = blocks // dw_s.shape[0]
    rows = WIDTH // (2 * owners)
    core = place_ref[begin]
    for matrix in range(dw_s.shape[0]):
        for owner in range(owners):
            at = begin + 1 + matrix * owners + owner
            start = pl.multiple_of((2 * owner + core) * rows, rows)
            keep_ref[place_ref[at], first : first + rows, :] = dw_s[matrix, pl.ds(start, rows), :]
            start = pl.multiple_of((2 * owner + 1 - core) * rows, rows)
            send_ref[place_ref[at + blocks], first : first + rows, :] = dw_s[matrix, pl.ds(start, rows), :]


def put_vectors(place_ref, begin, dvec_s, count, keep_ref, send_ref, first):
    blocks = keep_ref.shape[0]
    owners = blocks // count
    columns = WIDTH // (2 * owners)
    core = place_ref[begin]
    rows = slice(first, first + 16)
    blank = jnp.zeros((16, WIDTH), BF)
    for block in range(blocks):
        keep_ref[block, rows, :] = blank
        send_ref[block, rows, :] = blank
    for owner in range(owners):
        low = dvec_s[:, 2 * owner * columns : (2 * owner + 1) * columns]
        high = dvec_s[:, (2 * owner + 1) * columns : (2 * owner + 2) * columns]
        rest = jnp.zeros((16, WIDTH - columns), F32)
        own = jnp.where(core == 0, low, high)
        other = jnp.where(core == 0, high, low)
        at = begin + 1 + owner
        keep_ref[place_ref[at], rows, :] = jnp.concatenate([own, rest], axis=1).astype(BF)
        send_ref[place_ref[at + blocks], rows, :] = jnp.concatenate([other, rest], axis=1).astype(BF)


def put_feed(place_ref, begin, dex_s, dco_s, keep_ref, send_ref):
    blocks = keep_ref.shape[0]
    owners = blocks // 4
    each = keep_ref.shape[1] // 2
    core = place_ref[begin]
    for pair in range(4):
        for owner in range(owners):
            at = begin + 1 + pair * owners + owner
            for out_ref, on, block in ((keep_ref, core, place_ref[at]), (send_ref, 1 - core, place_ref[at + blocks])):
                shard = 2 * owner + on
                for side in range(2):
                    number = 2 * pair + side
                    rows = slice(side * each, (side + 1) * each)
                    if number < 4:
                        out_ref[block, rows, :] = dex_s[number, pl.ds(pl.multiple_of(shard * each, each), each), :]
                    else:
                        row = (shard * 4 + number - 4) * each
                        chunk = row // WIDTH
                        out_ref[block, rows, :] = dco_s[chunk, pl.ds(pl.multiple_of(row - chunk * WIDTH, each), each), :]


def fetcher(pairs, sems):
    step = pl.program_id(0)

    def copy(number, slab):
        return pltpu.make_async_copy(pairs[number][0].at[slab], pairs[number][1].at[slab], sems.at[number, slab])

    @pl.when(step == 0)
    def _():
        for slab in range(pairs[0][1].shape[0]):
            for number in range(len(pairs)):
                copy(number, slab).start()

    def wait(first, last):
        for number in range(first, last):
            copy(number, step).wait()

    return wait


def all_rows(ref):
    return ref[...].reshape(-1, WIDTH)


def cross_backward(begin, place_ref, ds2_ref, unit2_ref, scale2_ref, w_ref, vec_ref, q_ref, k_ref, v_ref, r_ref, o_ref, low1_ref, mem_ref, e_ref,
                   ds1_ref, dk_ref, dv_ref, keep_ref, send_ref, dvec_ref,
                   q_s, k_s, v_s, r_s, o_s, low1_s, mem_s, w_s, dm_s, dq_s, dk_s, dv_s, dbranch_s, dkt_s, dvt_s, dw_s, sems, out_sems, w_sems):
    step = pl.program_id(0)
    steps = pl.num_programs(0)
    w_copies = [pltpu.make_async_copy(w_ref.at[3], w_s.at[3], w_sems.at[0]), pltpu.make_async_copy(w_ref.at[0:3], w_s.at[0:3], w_sems.at[1])]

    @pl.when(step == 0)
    def _():
        w_copies[0].start()

    wait = fetcher([(q_ref, q_s), (k_ref, k_s), (v_ref, v_s), (r_ref, r_s), (o_ref, o_s), (low1_ref, low1_s), (mem_ref, mem_s)], sems)
    outward = [pltpu.make_async_copy(dk_s, dk_ref, out_sems.at[0]), pltpu.make_async_copy(dv_s, dv_ref, out_sems.at[1])]

    @pl.when(step == 0)
    def _():
        w_copies[1].start()
        dvec_ref[...] = jnp.zeros_like(dvec_ref)

    ds2_ref, unit2_ref, scale2_ref, ds1_ref = here(ds2_ref, unit2_ref, scale2_ref, ds1_ref)
    up = ds2_ref[...]
    unit = unit2_ref[...]
    dvec_ref[0:1, :] += rows_sum(up * unit)
    dvec_ref[1:2, :] += rows_sum(up)
    dres = norm_backward(up, unit, scale2_ref[...], vec_ref[1:2, :])
    dbranch = dres.astype(BF)
    dbranch_s[step] = dbranch

    @pl.when(step == 0)
    def _():
        w_copies[0].wait()

    dm_s[...] = nt(dbranch, w_s[3])
    ds1_ref[...] = dres * vec_ref[7:8, :]
    wait(0, 5)
    attend_backward(e_ref.at[step], r_s.at[step], o_s.at[step], q_s.at[step], k_s.at[step], v_s.at[step], dm_s, dq_s.at[step], dkt_s, dvt_s)
    wait(5, 7)
    dvec_ref[2:3, :] += rows_sum(dbranch_s[step].astype(F32) * low1_s[step].astype(F32))

    @pl.when(step == 0)
    def _():
        w_copies[1].wait()

    ds1_ref[...] += nt(dq_s[step], w_s[0])
    dk_s[step] = dkt_s[...].T
    dv_s[step] = dvt_s[...].T

    @pl.when(step == steps - 1)
    def _():
        for copy in outward:
            copy.start()
        dw_s[0] = tn(all_rows(low1_s), all_rows(dq_s)).astype(BF)
        memory_t = all_rows(mem_s).T
        dw_s[1] = nn(memory_t, all_rows(dk_s)).astype(BF)
        dw_s[2] = nn(memory_t, all_rows(dv_s)).astype(BF)
        dw_s[3] = tn(all_rows(o_s), all_rows(dbranch_s)).astype(BF)
        put_gradients(place_ref, begin, dw_s, keep_ref, send_ref, 0)
        for copy in outward:
            copy.wait()


def self_backward(ds1_ref, unit1_ref, scale1_ref, w3_ref, vec_ref, q_ref, k_ref, v_ref, r_ref, o_ref, x_ref, e_ref,
                  part_ref, dq_ref, dk_ref, dv_ref, dbranch_ref, dvec_ref, q_s, k_s, v_s, r_s, o_s, x_s, e_s, dm_s, dkt_s, dvt_s, sems):
    step = pl.program_id(0)
    wait = fetcher([(e_ref, e_s), (q_ref, q_s), (k_ref, k_s), (v_ref, v_s), (r_ref, r_s), (o_ref, o_s), (x_ref, x_s)], sems)

    @pl.when(step == 0)
    def _():
        dvec_ref[...] = jnp.zeros_like(dvec_ref)

    ds1_ref, unit1_ref, scale1_ref, part_ref, dq_ref, dk_ref, dv_ref, dbranch_ref = here(ds1_ref, unit1_ref, scale1_ref, part_ref, dq_ref, dk_ref, dv_ref, dbranch_ref)
    up = ds1_ref[...]
    unit = unit1_ref[...]
    dvec_ref[0:1, :] += rows_sum(up * unit)
    dvec_ref[1:2, :] += rows_sum(up)
    dres = norm_backward(up, unit, scale1_ref[...], vec_ref[0:1, :])
    dbranch = dres.astype(BF)
    dbranch_ref[...] = dbranch
    dm_s[...] = nt(dbranch, w3_ref[0])
    part_ref[...] = dres * vec_ref[6:7, :]
    wait(0, 6)
    attend_backward(e_s.at[step], r_s.at[step], o_s.at[step], q_s.at[step], k_s.at[step], v_s.at[step], dm_s, dq_ref, dkt_s, dvt_s)
    dk_ref[...] = dkt_s[...].T
    dv_ref[...] = dvt_s[...].T
    wait(6, 7)
    dvec_ref[2:3, :] += rows_sum(dbranch_ref[...].astype(F32) * x_s[step].astype(F32))


def self_weights(begin, place_ref, dq_ref, dk_ref, dv_ref, dbranch_ref, o_ref, x_ref, dvec1_ref, dvec2_ref, dvec3_ref, keep_ref, send_ref, o_s, x_s, dw_s, dvec_s, sems):
    copies = [pltpu.make_async_copy(x_ref, x_s, sems.at[0]), pltpu.make_async_copy(o_ref, o_s, sems.at[1])]
    for copy in copies:
        copy.start()
    dvec_s[...] = jnp.zeros_like(dvec_s)
    for row in range(3):
        for number, ref in enumerate((dvec1_ref, dvec2_ref, dvec3_ref)):
            dvec_s[3 * row + number : 3 * row + number + 1, :] = ref[row : row + 1, :]
    copies[0].wait()
    x_t = all_rows(x_s).T
    dw_s[0] = nn(x_t, all_rows(dq_ref)).astype(BF)
    dw_s[1] = nn(x_t, all_rows(dk_ref)).astype(BF)
    dw_s[2] = nn(x_t, all_rows(dv_ref)).astype(BF)
    copies[1].wait()
    dw_s[3] = tn(all_rows(o_s), all_rows(dbranch_ref)).astype(BF)
    put_gradients(place_ref, begin, dw_s, keep_ref, send_ref, 0)
    put_vectors(place_ref, begin, dvec_s, dw_s.shape[0], keep_ref, send_ref, keep_ref.shape[1] - 16)


def input_gradients(part_ref, dq_ref, dk_ref, dv_ref, w_ref, dk2_ref, dv2_ref, w2_ref, dx_ref, dmem_ref):
    part_ref, dq_ref, dk_ref, dv_ref, dk2_ref, dv2_ref, dx_ref, dmem_ref = here(part_ref, dq_ref, dk_ref, dv_ref, dk2_ref, dv2_ref, dx_ref, dmem_ref)
    dx_ref[...] = part_ref[...] + nt(dq_ref[...], w_ref[0]) + nt(dk_ref[...], w_ref[1]) + nt(dv_ref[...], w_ref[2])
    dmem_ref[...] = nt(dk2_ref[...], w2_ref[1]) + nt(dv2_ref[...], w2_ref[2])


def cut_shards(at, place_ref, stacked_ref, expand_ref, contract_ref, vec_ref, a_ref, b_ref, c_ref, a_s, b_s, ex_s, co_s, vec_s, sems):
    rows = stacked_ref.shape[1]
    middle = pl.multiple_of(place_ref[at] * (rows // 2), rows // 2)
    half = pl.ds(middle, rows // 2)
    start = pl.multiple_of(place_ref[at + 1] * (rows // 4), rows // 4)
    quarter = pl.ds(start, rows // 4)
    copies = [
        pltpu.make_async_copy(stacked_ref.at[0:3, half, :], a_s, sems.at[0]),
        pltpu.make_async_copy(stacked_ref.at[3:8, quarter, :], b_s, sems.at[1]),
        pltpu.make_async_copy(vec_ref, vec_s, sems.at[2]),
        pltpu.make_async_copy(expand_ref.at[half, :], ex_s, sems.at[3]),
    ]
    copies += [
        pltpu.make_async_copy(contract_ref.at[pl.ds(pl.multiple_of(part * rows + middle, rows // 2), rows // 2), :], co_s.at[part], sems.at[4 + part])
        for part in range(4)
    ]
    for copy in copies:
        copy.start()
    for copy in copies:
        copy.wait()
    a_ref[0] = a_s[...].astype(BF)
    for index, matrix in enumerate((4, 5, 6, 7, 3)):
        b_ref[0, index] = b_s[matrix - 3].astype(BF)
    vec = jnp.concatenate([vec_s[...]] * (WIDTH // vec_ref.shape[1]), axis=1)
    owner = lax.broadcasted_iota(jnp.int32, vec.shape, 1) // vec_ref.shape[1]
    vec = jnp.where(owner == place_ref[at + 2], vec, 0.0)
    b_ref[0, 5] = jnp.concatenate([vec, jnp.zeros((rows // 4 - vec.shape[0], WIDTH), F32)], axis=0).astype(BF)
    for part in range(4):
        c_ref[0, part] = ex_s[:, part * WIDTH : (part + 1) * WIDTH].astype(BF)
        c_ref[0, 4 + part] = co_s[part].astype(BF)


def per_slab(*tail):
    return pl.BlockSpec((1,) + tail, lambda m: (m,) + (0,) * len(tail))


def fixed(*dims):
    return pl.BlockSpec(dims, lambda m: (0,) * len(dims), pipeline_mode=pl.Buffered(1))


def shape(dims, kind):
    return jax.ShapeDtypeStruct(tuple(dims), kind)


def options(mib):
    return pltpu.CompilerParams(dimension_semantics=("arbitrary",), vmem_limit_bytes=mib * MIB)


def estimate(microseconds):
    return pl.CostEstimate(flops=int(microseconds * 1e9), bytes_accessed=1 << 20, transcendentals=0)


SCALARS = pl.BlockSpec(memory_space=pltpu.SMEM)
ANYWHERE = pl.BlockSpec(memory_space=pl.ANY)
RESIDENT = pl.BlockSpec(memory_space=pltpu.VMEM)
ROWS = per_slab(SLAB, WIDTH)
SCALE = per_slab(SLAB, 1)


def near(*arrays):
    return tuple(pltpu.with_memory_space_constraint(array, pltpu.VMEM) for array in arrays)


def far(*arrays):
    return tuple(pltpu.with_memory_space_constraint(array, pltpu.HBM) for array in arrays)


def near_shape(dims, kind):
    return pltpu.VMEM(tuple(dims), kind)


def far_shape(dims, kind):
    return pltpu.HBM(tuple(dims), kind)


def slabs(g, kind, place=far_shape):
    return place((g, SLAB, WIDTH), kind)


def powers_shape(g, place):
    return place((g, HEADS, SLAB, SLAB), BF)


def run_cut_shards(at, place, stacked, expand, contract, vec):
    rows = stacked.shape[1]
    return pl.pallas_call(
        functools.partial(cut_shards, at),
        in_specs=[SCALARS] + [ANYWHERE] * 4,
        out_specs=[RESIDENT] * 3,
        out_shape=[shape((1, 3, rows // 2, WIDTH), BF), shape((1, 6, rows // 4, WIDTH), BF), shape((1, 8, rows // 2, WIDTH), BF)],
        scratch_shapes=[
            pltpu.VMEM((3, rows // 2, WIDTH), F32),
            pltpu.VMEM((5, rows // 4, WIDTH), F32),
            pltpu.VMEM((rows // 2, expand.shape[1]), F32),
            pltpu.VMEM((4, rows // 2, WIDTH), F32),
            pltpu.VMEM(vec.shape, F32),
            pltpu.SemaphoreType.DMA((8,)),
        ],
        compiler_params=pltpu.CompilerParams(vmem_limit_bytes=16 * MIB),
        name="cut_shards",
    )(place, *far(stacked, expand, contract, vec))


def run_self_forward(first, place, lengths, x, w):
    g = x.shape[0]
    return pl.pallas_call(
        functools.partial(self_forward, len(w), first),
        grid=(g,),
        in_specs=[SCALARS, SCALARS, ROWS] + [ANYWHERE] * len(w),
        out_specs=[ANYWHERE, ROWS, ROWS, ROWS, ANYWHERE, ROWS, RESIDENT],
        out_shape=[far_shape((3, WIDTH, WIDTH), BF)] + [slabs(g, BF)] * 3 + [powers_shape(g, far_shape), slabs(g, BF), slabs(g, BF, near_shape)],
        scratch_shapes=[pltpu.VMEM((3, WIDTH, WIDTH), BF), pltpu.VMEM((g, HEADS, SLAB, SLAB), BF), pltpu.SemaphoreType.DMA((sum(piece.shape[0] for piece in w),)), pltpu.SemaphoreType.DMA((g, HEADS)), pltpu.SemaphoreType.DMA],
        compiler_params=options(32),
        cost_estimate=estimate(12),
        name="self_forward",
    )(place, lengths, x, *w)


def run_cross_inputs(first, owners, place, o1, x, memory, w):
    g = memory.shape[0]
    return pl.pallas_call(
        functools.partial(cross_inputs, len(w), first, owners),
        grid=(g,),
        in_specs=[SCALARS, RESIDENT, ROWS, ROWS] + [ANYWHERE] * len(w),
        out_specs=[ANYWHERE, fixed(16, WIDTH), ROWS, ROWS, ROWS, RESIDENT, ROWS, SCALE, ROWS],
        out_shape=[far_shape((6, WIDTH, WIDTH), BF), far_shape((16, WIDTH), F32)]
        + [slabs(g, BF)] * 3
        + [slabs(g, F32, near_shape), slabs(g, F32), far_shape((g, SLAB, 1), F32), slabs(g, BF)],
        scratch_shapes=[pltpu.VMEM((6, WIDTH, WIDTH), BF), pltpu.SemaphoreType.DMA((sum(piece.shape[0] for piece in w),)), pltpu.SemaphoreType.DMA],
        compiler_params=options(24),
        cost_estimate=estimate(7),
        name="cross_inputs",
    )(place, *near(o1), x, memory, *w)


def run_cross_forward(lengths, q, k, v):
    g = q.shape[0]
    return pl.pallas_call(
        cross_forward,
        grid=(g,),
        in_specs=[SCALARS, ROWS, ROWS, ROWS],
        out_specs=[RESIDENT, ROWS, RESIDENT, ROWS],
        out_shape=[powers_shape(g, near_shape), slabs(g, BF), slabs(g, BF, near_shape), slabs(g, BF)],
        compiler_params=options(24),
        cost_estimate=estimate(10),
        name="cross_forward",
    )(lengths, *far(q, k, v))


def run_feed(begin, reduce_at, owners, place, o2, unit1, w_cross, cot, first, second, vec):
    g = unit1.shape[0]
    rows = WIDTH // owners
    pieces = sum(piece.shape[0] for piece in first)
    dims = (2 * owners, 2 * rows, WIDTH)
    tokens = g * SLAB
    last = pl.BlockSpec((1, WIDTH, WIDTH), lambda m: (3, 0, 0))
    return pl.pallas_call(
        functools.partial(feed_both, len(first), begin, reduce_at),
        grid=(1,),
        in_specs=[SCALARS, RESIDENT, RESIDENT, last, ANYWHERE, fixed(16, WIDTH)] + [ANYWHERE] * (2 * len(first)),
        out_specs=[ANYWHERE, RESIDENT, RESIDENT, fixed(g, SLAB, 1), RESIDENT, RESIDENT, fixed(8, WIDTH)],
        out_shape=[slabs(g, BF), slabs(g, F32, near_shape), slabs(g, F32, near_shape), far_shape((g, SLAB, 1), F32)] + [near_shape(dims, BF)] * 2 + [far_shape((8, WIDTH), F32)],
        scratch_shapes=[
            pltpu.VMEM((4, tokens, WIDTH), BF),
            pltpu.VMEM((4, tokens, WIDTH), F32),
            pltpu.VMEM((tokens, WIDTH), F32),
            pltpu.VMEM((tokens, WIDTH), BF),
            pltpu.VMEM((tokens, WIDTH), BF),
            pltpu.VMEM((g, SLAB, WIDTH), BF),
            pltpu.VMEM((g, SLAB, WIDTH), BF),
            pltpu.VMEM((4, WIDTH, WIDTH), BF),
            pltpu.VMEM((4, WIDTH, WIDTH), BF),
            pltpu.VMEM((4, WIDTH, WIDTH), BF),
            pltpu.VMEM((4 * owners, rows, WIDTH), BF),
            pltpu.SemaphoreType.DMA((2, pieces)),
            pltpu.SemaphoreType.DMA((2,)),
        ],
        compiler_params=options(FEED_MIB),
        cost_estimate=estimate(24),
        name="feed_both",
    )(place, *near(o2, unit1), *far(w_cross), cot, *far(vec), *first, *second)


def slab_scratch(g, kinds):
    return [pltpu.VMEM((g, SLAB, WIDTH), kind) for kind in kinds]


def run_cross_backward(begin, place, owners, ds2, unit2, scale2, low1, memory, w, vec, saved):
    g = memory.shape[0]
    dims = (4 * owners, WIDTH // (2 * owners), WIDTH)
    q, k, v, e, r, o = saved
    return pl.pallas_call(
        functools.partial(cross_backward, begin),
        grid=(g,),
        in_specs=[SCALARS, RESIDENT, RESIDENT, SCALE, ANYWHERE, fixed(16, WIDTH)] + [ANYWHERE] * 7 + [RESIDENT],
        out_specs=[RESIDENT, ANYWHERE, ANYWHERE, RESIDENT, RESIDENT, fixed(8, WIDTH)],
        out_shape=[slabs(g, F32, near_shape), slabs(g, BF), slabs(g, BF), near_shape(dims, BF), near_shape(dims, BF), far_shape((8, WIDTH), F32)],
        scratch_shapes=slab_scratch(g, [BF] * 7)
        + [pltpu.VMEM((4, WIDTH, WIDTH), BF), pltpu.VMEM((SLAB, WIDTH), F32)]
        + slab_scratch(g, [BF] * 4)
        + [pltpu.VMEM((WIDTH, SLAB), BF)] * 2
        + [pltpu.VMEM((4, WIDTH, WIDTH), BF), pltpu.SemaphoreType.DMA((7, g)), pltpu.SemaphoreType.DMA((2,)), pltpu.SemaphoreType.DMA((2,))],
        compiler_params=options(CROSS_MIB),
        cost_estimate=estimate(19),
        name="cross_backward",
    )(place, *near(ds2, unit2), *far(scale2, w, vec, q, k, v, r, o, low1), memory, *near(e))


def run_self_backward(ds1, unit1, scale1, x, w_cross, vec, saved):
    g = x.shape[0]
    q, k, v, e, r, o = saved
    third = pl.BlockSpec((1, WIDTH, WIDTH), lambda m: (4, 0, 0))
    return pl.pallas_call(
        self_backward,
        grid=(g,),
        in_specs=[RESIDENT, ROWS, SCALE, third, fixed(16, WIDTH)] + [ANYWHERE] * 7,
        out_specs=[ROWS] + [RESIDENT] * 4 + [fixed(8, WIDTH)],
        out_shape=[slabs(g, F32)] + [slabs(g, BF, near_shape)] * 4 + [far_shape((8, WIDTH), F32)],
        scratch_shapes=slab_scratch(g, [BF] * 6)
        + [pltpu.VMEM((g, HEADS, SLAB, SLAB), BF), pltpu.VMEM((SLAB, WIDTH), F32)]
        + [pltpu.VMEM((WIDTH, SLAB), BF)] * 2
        + [pltpu.SemaphoreType.DMA((7, g))],
        compiler_params=options(SELF_MIB),
        cost_estimate=estimate(17),
        name="self_backward",
    )(*near(ds1), *far(unit1, scale1, w_cross, vec, q, k, v, r, o), x, *far(e))


def run_self_weights(begin, place, owners, x, o, grads, dvecs):
    g = x.shape[0]
    dims = (4 * owners, WIDTH // (2 * owners) + 16, WIDTH)
    return pl.pallas_call(
        functools.partial(self_weights, begin),
        grid=(1,),
        in_specs=[SCALARS] + [RESIDENT] * 4 + [ANYWHERE] * 2 + [fixed(8, WIDTH)] * 3,
        out_specs=[RESIDENT] * 2,
        out_shape=[near_shape(dims, BF)] * 2,
        scratch_shapes=slab_scratch(g, [BF] * 2) + [pltpu.VMEM((4, WIDTH, WIDTH), BF), pltpu.VMEM((16, WIDTH), F32), pltpu.SemaphoreType.DMA((2,))],
        compiler_params=options(24),
        cost_estimate=estimate(4),
        name="self_weights",
    )(place, *near(*grads), *far(o), x, *far(*dvecs))


def run_input_gradients(part, dq, dk, dv, w, dk2, dv2, w2):
    g = part.shape[0]
    return pl.pallas_call(
        input_gradients,
        grid=(g,),
        in_specs=[ROWS] + [RESIDENT] * 3 + [fixed(3, WIDTH, WIDTH), ROWS, ROWS, fixed(3, WIDTH, WIDTH)],
        out_specs=[ROWS, ROWS],
        out_shape=[slabs(g, F32), slabs(g, F32)],
        compiler_params=options(28),
        cost_estimate=estimate(6),
        name="input_gradients",
    )(*far(part), *near(dq, dk, dv), *far(w, dk2, dv2, w2))
def adam_update(weight, first_moment, second_moment, gradient):
    correction = 1.0 - 0.5**STEP
    first_next = 0.5 * first_moment + 0.5 * gradient
    second_next = 0.5 * second_moment + 0.5 * gradient * gradient
    weight_next = weight - LEARN_RATE * (first_next / correction) / (jnp.sqrt(second_next / correction) + ADAM_EPS)
    return (weight_next, first_next, second_next)


def picked(order, parts):
    value = parts[0]
    for number in range(1, len(parts)):
        value = jnp.where(order == number, parts[number], value)
    return value.astype(F32)


def adam_stacked(at, place_ref, part_0, part_1, part_2, part_3, w_ref, m_ref, s_ref, vw_ref, vm_ref, vs_ref, w_out, m_out, s_out, vw_out, vm_out, vs_out):
    rows = w_ref.shape[1]
    group = pl.program_id(0)
    parts = (part_0, part_1, part_2, part_3)

    def update(first):
        for matrix in range(4):
            grad = picked(place_ref[at + matrix], [part[0, first : first + rows, :] for part in parts])
            w_out[matrix], m_out[matrix], s_out[matrix] = adam_update(w_ref[matrix], m_ref[matrix], s_ref[matrix], grad)

    @pl.when(group == 0)
    def _():
        update(0)
        grad = picked(place_ref[at], [part[0, rows : rows + 16, :] for part in parts])
        vw_out[...], vm_out[...], vs_out[...] = adam_update(vw_ref[...], vm_ref[...], vs_ref[...], grad[: vw_ref.shape[0], : vw_ref.shape[1]])

    @pl.when(group == 1)
    def _():
        update(rows + 16)


def run_adam_stacked(at, place, parts, stacked, vectors):
    rows = stacked[0].shape[1]
    block = pl.BlockSpec((4, rows, WIDTH), lambda group: (group, 0, 0))
    vector = fixed(*vectors[0].shape)
    return pl.pallas_call(
        functools.partial(adam_stacked, at),
        grid=(2,),
        in_specs=[SCALARS] + [fixed(*part.shape) for part in parts] + [block] * 3 + [vector] * 3,
        out_specs=[block] * 3 + [vector] * 3,
        out_shape=[shape(a.shape, F32) for a in tuple(stacked) + tuple(vectors)],
        compiler_params=options(24),
        cost_estimate=estimate(4),
        name="adam_stacked",
    )(place, *parts, *stacked, *vectors)


def adam_feed(at, place_ref, low_ref, high_ref, *refs):
    rows = low_ref.shape[1] // 2

    def grad(number):
        span = slice(number % 2 * rows, (number % 2 + 1) * rows)
        return picked(place_ref[at + number // 2], [ref[block, span, :] for ref in (low_ref, high_ref) for block in range(2)])

    for part in range(4):
        where = (slice(None), slice(part * WIDTH, (part + 1) * WIDTH))
        refs[6][where], refs[7][where], refs[8][where] = adam_update(*(ref[where] for ref in refs[0:3]), grad(part))
        where = (slice(part * rows, (part + 1) * rows), slice(None))
        refs[9][where], refs[10][where], refs[11][where] = adam_update(*(ref[where] for ref in refs[3:6]), grad(4 + part))


def run_adam_feed(at, place, low, high, expand, contract):
    arrays = tuple(expand) + tuple(contract)
    whole = pl.BlockSpec(memory_space=pltpu.VMEM)
    return pl.pallas_call(
        functools.partial(adam_feed, at),
        in_specs=[SCALARS] + [whole] * 8,
        out_specs=[whole] * 6,
        out_shape=[shape(a.shape, F32) for a in arrays],
        compiler_params=pltpu.CompilerParams(vmem_limit_bytes=24 * MIB),
        cost_estimate=estimate(4),
        name="adam_feed",
    )(place, low, high, *arrays)


class Route:
    def __init__(self, m, n):
        self.m, self.n = m, n
        self.dp_bits = m.bit_length() - 1
        self.line_bits = n.bit_length() - 2
        self.line = n // 2

    def pairs(self, partner):
        return [(d * self.n + f, partner(d, f)) for d in range(self.m) for f in range(self.n)]

    def across_core(self):
        return self.pairs(lambda d, f: d * self.n + (f ^ 1))

    def along_line(self, mask):
        return self.pairs(lambda d, f: d * self.n + (f ^ (2 * mask)))

    def among_dp(self, mask):
        return self.pairs(lambda d, f: (d ^ mask) * self.n + f)

    def across_line(self, step):
        return self.pairs(lambda d, f: d * self.n + (f ^ (2 << (self.line_bits - 1 - step))))

    def across_dp(self, step):
        def partner(d, f):
            bit = step if f % 2 == 0 else self.dp_bits - 1 - step
            return (d ^ (1 << bit)) * self.n + f

        return self.pairs(partner)

    @staticmethod
    def spot(mask, bits, core):
        return mask if core == 0 else sum(((mask >> b) & 1) << (bits - 1 - b) for b in range(bits))

    def part(self, share, d, f):
        return sum(((d >> (bit if f % 2 == 0 else self.dp_bits - 1 - bit)) & 1) << bit for bit in range(share))

    def gather_row(self, share, d, f):
        z, c = divmod(f, 2)
        return [
            ((2 * (z ^ k) + who) << share) + (self.part(share, d, who) ^ step)
            for who in (c, 1 - c)
            for step in range(1 << share)
            for k in range(self.line)
        ]

    def reduce_row(self, d, f):
        z, c = divmod(f, 2)
        row = [c]
        for who in (c, 1 - c):
            line = [self.spot(owner ^ z, self.line_bits, 1) for owner in range(self.line)]
            row += [self.spot(j ^ d, self.dp_bits, who) * self.line + at for j in range(self.m) for at in line]
        return row + [self.spot(j ^ d, self.dp_bits, c) for j in range(self.m)] + [j ^ d for j in range(self.m)]

    def part_row(self, d, f):
        return [self.part(1, d, f), self.part(2, d, f), f]

    def tables(self):
        kinds = (functools.partial(self.gather_row, 1), functools.partial(self.gather_row, 2), self.reduce_row, self.part_row)
        rows = [[kind(d, f) for kind in kinds] for d in range(self.m) for f in range(self.n)]
        ends = np.cumsum([0] + [len(row) for row in rows[0]])
        return np.array([sum(row, []) for row in rows], np.int32), ends


BOTH = ("dp", "fsdp")


def after(values, *earlier):
    return lax.optimization_barrier((values,) + earlier)[0]


def doubled(blocks, got):
    return jnp.concatenate([blocks, got], axis=0)


def per_device(
    inputs,
    memory,
    cotangent,
    lengths,
    stacked_weights,
    expand_weights,
    contract_weights,
    scale_vectors,
    stacked_first,
    stacked_second,
    expand_first,
    expand_second,
    contract_first,
    contract_second,
    vector_first,
    vector_second,
):
    m, n = lax.axis_size("dp"), lax.axis_size("fsdp")
    width = WIDTH // n
    slabs = inputs.shape[0] * lengths.shape[1]
    x = inputs.reshape(slabs, SLAB, WIDTH)
    mem = memory.reshape(slabs, SLAB, WIDTH)
    cot = cotangent.reshape(slabs, SLAB, WIDTH)
    by_hand = m == 4 and width == 64 and n == 8
    here = lax.axis_index("fsdp")
    lengths = lengths.reshape(slabs, 2, -1)
    if by_hand:
        route = Route(m, n)
        table, ends = route.tables()
        row = lax.dynamic_index_in_dim(jnp.asarray(table), lax.axis_index("dp") * n + here, keepdims=False)
        halves, quarters, reduced, parts = (int(end) for end in ends[:4])
        order, holder = parts - 2 * m, parts - m

        def swap(blocks, pairs):
            return lax.ppermute(blocks, BOTH, pairs)

        along = [route.along_line(mask) for mask in range(1, n // 2)]
        line = [route.across_line(step) for step in range(route.line_bits)]
        across = [route.across_dp(step) for step in range(route.dp_bits)]
        core = route.across_core()
        a, b, c = run_cut_shards(parts, row, stacked_weights, expand_weights, contract_weights, scale_vectors)
        got = lax.optimization_barrier(tuple(swap(a, pairs) for pairs in along) + tuple(swap(b, pairs) for pairs in along))
        a, b = jnp.concatenate([a, *got[:3]], axis=0), jnp.concatenate([b, *got[3:]], axis=0)
        c = after(c, b)
        a_across, a_core, b_across, c_1, c_2 = lax.optimization_barrier((swap(a, across[0]), swap(a, core), swap(b, across[0]), swap(c, along[0]), swap(c, along[1])))
        b = doubled(b, b_across)
        b_across, b_core, c_3 = swap(b, across[1]), swap(b, core), swap(after(c, b), along[2])
        w_self, *saved1 = run_self_forward(halves, row, lengths, after(x, b), (a, a_across, a_core, swap(a_across, core)))
        b_across, c_3 = after((b_across, c_3), saved1[-1])
        ex, co = (jnp.concatenate([part[:, span] for part in (c, c_1, c_2, c_3)], axis=0) for span in (slice(0, 4), slice(4, 8)))
        b_across = after(b_across, ex)
        ex_across = swap(ex, across[0])
        w_cross = (b, b_across, b_core, swap(b_across, core))
        w_cross, vec, *qkv2, unit1, kept1, scale1, low1 = run_cross_inputs(quarters, n, row, saved1[-1], x, mem, w_cross)
        ex_across = after(ex_across, unit1)
        co_across = swap(after(co, ex_across), across[0])
        ex_core, co_core, ex_last = swap(ex, core), swap(co, core), swap(ex_across, core)
        e2, r2, o2, kept_o2 = run_cross_forward(lengths, *qkv2)
        saved2 = (*qkv2, e2, r2, kept_o2)
        co_across = after(co_across, o2)
        w_feed = ((ex, ex_across, ex_core, ex_last), (co, co_across, co_core, swap(co_across, core)))
        out, ds2, kept2, scale2, feed_keep, feed_send, dvec3 = run_feed(halves, reduced, n, row, o2, unit1, w_cross, cot, *w_feed, vec)
        feed_got = swap(feed_send, core)
        ds1, dk2, dv2, cross_keep, cross_send, dvec2 = run_cross_backward(reduced, row, n // 2, ds2, kept2, scale2, low1, mem, w_cross, vec, saved2)
        feed_got = after(feed_got, ds1)
        feed_out, feed = feed_keep[8:] + feed_got[8:], feed_keep[:8] + feed_got[:8]
        feed_got, cross_got = swap(feed_out, across[1]), swap(cross_send, core)
        part, dq, dk, dv, dbranch, dvec1 = run_self_backward(after(ds1, feed_out), kept1, scale1, x, w_cross, vec, saved1)
        feed_got, cross_got = after((feed_got, cross_got), dq)
        feed_out, feed = feed[4:] + feed_got[4:], feed[:4] + feed_got[:4]
        cross_out, cross = cross_keep[8:] + cross_got[8:], cross_keep[:8] + cross_got[:8]
        feed_got, cross_got = swap(feed_out, across[0]), swap(cross_out, across[1])
        keep, send = run_self_weights(reduced, row, n // 2, x, saved1[-1], after((dq, dk, dv, dbranch), cross_out, feed_out), (dvec1, dvec2, dvec3))
        got = swap(send, core)
        dx, dmem = run_input_gradients(after(part, send), dq, dk, dv, w_self, dk2, dv2, w_cross)
        got = after(got, dx)
        out_part, total = keep[8:] + got[8:], keep[:8] + got[:8]
        feed_got, cross_got = after((feed_got, cross_got), got)
        feed = feed + feed_got
        feed_out, feed = feed[2:], feed[:2]
        got, feed_got = lax.optimization_barrier((swap(out_part, across[1]), swap(after(feed_out, out_part), line[1])))
        out_part = jnp.concatenate([total[4:] + got[4:], cross[4:] + cross_got[4:]], axis=1)
        total = jnp.concatenate([total[:4] + got[:4], cross[:4] + cross_got[:4]], axis=1)
        feed_out, feed = feed[1:] + feed_got[1:], feed[:1] + feed_got[:1]
        got, feed_got = lax.optimization_barrier((swap(out_part, across[0]), swap(after(feed_out, out_part), line[0])))
        out_part, total = total[2:] + got[2:], total[:2] + got[:2]
        feed = feed + feed_got
        got, feed_got = lax.optimization_barrier((swap(out_part, line[1]), swap(after(feed, out_part), across[0])))
        out_part, total = total[1:] + got[1:], total[:1] + got[:1]
        feed = doubled(feed, feed_got)
        got, feed_got = lax.optimization_barrier((swap(out_part, line[0]), swap(after(feed, out_part), across[1])))
        total = total + got
        feed_next = run_adam_feed(order, row, after(feed, total), feed_got, (expand_weights, expand_first, expand_second), (contract_weights, contract_first, contract_second))
        got = lax.optimization_barrier(tuple(swap(total, route.among_dp(mask)) for mask in range(1, m)))
        got = after(got, feed_next[0])
        *stacked_next, vw, vm, vs = run_adam_stacked(holder, row, (total, *got), (stacked_weights, stacked_first, stacked_second), (scale_vectors, vector_first, vector_second))
        vector_next = (vw, vm, vs)
    else:
        row = jnp.array([0, 1, 0] + [0, 1, 2, 3] * 2, jnp.int32)
        expand_blocks = jnp.swapaxes(expand_weights.reshape(width, 4, WIDTH), 0, 1)
        vec_shard = lax.dynamic_update_slice(jnp.zeros((16, WIDTH), BF), scale_vectors.astype(BF), (0, here * width))
        all_low = lax.all_gather(stacked_weights.astype(BF), "fsdp", axis=1, tiled=True)
        vec_full = jnp.sum(lax.all_gather(vec_shard, "fsdp", axis=0).astype(F32), axis=0).astype(BF)
        vec_full = jnp.pad(vec_full, ((0, WIDTH - 16), (0, 0)))
        ex = lax.all_gather(expand_blocks.astype(BF), "fsdp", axis=1, tiled=True).reshape(4, 2, -1, WIDTH)
        co = lax.all_gather(contract_weights.astype(BF), "fsdp", axis=0, tiled=True).reshape(2, 4, -1, WIDTH)
        w_self = tuple(all_low[None, :3].reshape(1, 3, 2, -1, WIDTH)[:, :, core] for core in range(2))
        w_cross = jnp.concatenate([all_low[4:], all_low[3:4], vec_full[None]], axis=0).reshape(1, 6, 2, -1, WIDTH)
        w_feed = tuple(ex[None, :, core] for core in range(2)), tuple(co[None, core] for core in range(2))
        w_self, *saved1 = run_self_forward(0, row, lengths, x, w_self)
        w_cross, vec, *qkv2, unit1, kept1, scale1, low1 = run_cross_inputs(0, 1, row, saved1[-1], x, mem, (w_cross[:, :, 0], w_cross[:, :, 1]))
        e2, r2, o2, kept_o2 = run_cross_forward(lengths, *qkv2)
        saved2 = (*qkv2, e2, r2, kept_o2)
        out, ds2, kept2, scale2, feed_keep, feed_send, dvec3 = run_feed(0, 2, 2, row, o2, unit1, w_cross, cot, *w_feed, vec)
        dw_feed = jnp.stack([feed_keep, feed_send]).reshape(2, 8, WIDTH // 2, WIDTH)
        dex = jnp.swapaxes(dw_feed[:, :4], 0, 1).reshape(4, n, width, WIDTH)
        dco = dw_feed[:, 4:].reshape(n, 4, width, WIDTH)
        dw_feed = jnp.concatenate([jnp.swapaxes(dex, 0, 1), dco], axis=1)
        grad_feed = lax.psum(lax.psum_scatter(dw_feed, "fsdp", scatter_dimension=0, tiled=False), "dp")
        ds1, dk2, dv2, cross_keep, cross_send, dvec2 = run_cross_backward(2, row, 1, ds2, kept2, scale2, low1, mem, w_cross, vec, saved2)
        part, dq, dk, dv, dbranch, dvec1 = run_self_backward(ds1, kept1, scale1, x, w_cross, vec, saved1)
        keep, send = run_self_weights(2, row, 1, x, saved1[-1], (dq, dk, dv, dbranch), (dvec1, dvec2, dvec3))
        dx, dmem = run_input_gradients(part, dq, dk, dv, w_self, dk2, dv2, w_cross)
        both, cross_both = jnp.stack([keep, send], axis=1), jnp.stack([cross_keep, cross_send], axis=1)
        rows = WIDTH // 2
        grad_vector = lax.psum(both[0, :, rows : rows + 9, :rows].astype(F32), BOTH)
        grad_vector = jnp.swapaxes(grad_vector, 0, 1).reshape(9, WIDTH)
        grad_vector = lax.dynamic_slice(grad_vector, (0, here * width), (9, width))
        both = jnp.concatenate([both[:, :, :rows], cross_both], axis=0).reshape(8, WIDTH, WIDTH)
        both = lax.psum(lax.psum_scatter(both, "fsdp", scatter_dimension=1, tiled=True), "dp")
        stacked_next = adam_update(stacked_weights, stacked_first, stacked_second, both.astype(F32))
        vector_next = adam_update(scale_vectors, vector_first, vector_second, grad_vector)
        feed_next = run_adam_feed(0, jnp.arange(4, dtype=jnp.int32), *grad_feed.reshape(2, 2, 2 * width, WIDTH), (expand_weights, expand_first, expand_second), (contract_weights, contract_first, contract_second))
    expand_next, contract_next = feed_next[:3], feed_next[3:]
    return (
        out.reshape(inputs.shape),
        dx.reshape(inputs.shape),
        dmem.reshape(inputs.shape),
        stacked_next[0],
        expand_next[0],
        contract_next[0],
        vector_next[0],
        stacked_next[1],
        stacked_next[2],
        expand_next[1],
        expand_next[2],
        contract_next[1],
        contract_next[2],
        vector_next[1],
        vector_next[2],
    )


def solution(mesh):
    tokens = P(None, ("dp", "fsdp"), None)
    pieces = P(None, ("dp", "fsdp"), None, None)
    stacked = P(None, "fsdp", None)
    rows = P("fsdp", None)
    columns = P(None, "fsdp")
    return jax.shard_map(
        per_device,
        mesh=mesh,
        in_specs=(tokens, tokens, tokens, pieces, stacked, rows, rows, columns) + (stacked, stacked, rows, rows, rows, rows, columns, columns),
        out_specs=(tokens, tokens, tokens, stacked, rows, rows, columns) + (stacked, stacked, rows, rows, rows, rows, columns, columns),
        check_vma=False,
    )
```

```python
import functools
import math

import jax
import jax.numpy as jnp
import numpy as np
from jax import lax
from jax.experimental import pallas as pl
from jax.experimental.pallas import tpu as pltpu
from jax.sharding import PartitionSpec as P

HEADS = 8
HEAD = 64
SLAB = 512
WIDTH = 512
PAIR = 2 * HEAD
STEP = 3
NORM_EPS = 1e-05
ADAM_EPS = 1e-08
LEARN_RATE = 0.2
FAR = -1e30
LOG2E = math.log2(math.e)
QSCALE = HEAD**-0.5 * LOG2E
TILE = 256
BF = jnp.bfloat16
F32 = jnp.float32
MIB = 1 << 20
FEED_MIB = 30
CROSS_MIB = 24
SELF_MIB = 40


def nn(a, b):
    return jnp.dot(a, b, preferred_element_type=F32)


def nt(a, b):
    return lax.dot_general(a, b, (((1,), (1,)), ((), ())), preferred_element_type=F32)


def tn(a, b):
    return lax.dot_general(a, b, (((0,), (0,)), ((), ())), preferred_element_type=F32)


def norm_forward(residual, eps=NORM_EPS):
    centred = residual - jnp.mean(residual, axis=-1, keepdims=True)
    spread = jnp.mean(centred * centred, axis=-1, keepdims=True)
    scale = lax.rsqrt(spread + eps)
    return centred * scale, scale


def norm_backward(upstream, unit, scale, gain):
    inner = upstream * gain
    first = jnp.mean(inner, axis=-1, keepdims=True)
    second = jnp.mean(inner * unit, axis=-1, keepdims=True)
    return scale * (inner - first - unit * second)


def rows_sum(values):
    return jnp.sum(values, axis=0, keepdims=True)


def first_lanes(rows):
    return lax.broadcasted_iota(jnp.int32, (rows, PAIR), 1) < HEAD


def attend_forward(q_ref, k_ref, v_ref, queries_in, keys_out, e_ref, o_ref, r_ref, causal, after=None):
    low = first_lanes(SLAB)
    ones = jnp.ones((SLAB, PAIR), BF)
    spans = ((0, TILE, TILE), (TILE, SLAB, SLAB)) if causal else ((0, SLAB, SLAB),)
    if causal:
        query_at = lax.broadcasted_iota(jnp.int32, (TILE, TILE), 0)
        key_at = lax.broadcasted_iota(jnp.int32, (TILE, TILE), 1)
        bias = jnp.where(key_at <= query_at, 0.0, FAR).astype(F32)
        blank = jnp.zeros((TILE, TILE), BF)

    def lanes(head):
        return slice(head // 2 * PAIR, (head // 2 + 1) * PAIR)

    def scores(head):
        left, right = q_ref[:, lanes(head)], k_ref[:, lanes(head)]
        if head % 2 == 0:
            left, right = jnp.where(low, left, queries_in), jnp.where(low, right, keys_out)
        else:
            left, right = jnp.where(low, queries_in, left), jnp.where(low, keys_out, right)
        return [nt(left[first:last], right[:depth]) for first, last, depth in spans]

    def powers(head, found):
        results = []
        for (first, last, depth), part in zip(spans, found):
            if causal:
                end = part[:, depth - TILE :] + bias
                part = end if depth == TILE else jnp.concatenate([part[:, : depth - TILE], end], axis=1)
            power = jnp.exp2(part - jnp.max(part, axis=1, keepdims=True)).astype(BF)
            e_ref[head, first:last, :depth] = power
            if depth < SLAB:
                e_ref[head, first:last, depth:] = blank
            results.append(power)
        if after is not None:
            after(head)
        return results

    def mixes(head, found):
        right = jnp.concatenate([v_ref[:, lanes(head)], ones], axis=1)
        results = []
        for (_, _, depth), power in zip(spans, found):
            mixed = nn(power, right[:depth])
            inverse = 1.0 / mixed[:, PAIR:]
            results.append((mixed[:, :PAIR] * inverse, inverse))
        return results

    def put(pair, even, odd):
        for (first, last, _), (mix_0, inverse_0), (mix_1, inverse_1) in zip(spans, even, odd):
            here = first_lanes(last - first)
            o_ref[first:last, pair * PAIR : (pair + 1) * PAIR] = jnp.where(here, mix_0, mix_1).astype(BF)
            r_ref[first:last, pair * PAIR : (pair + 1) * PAIR] = jnp.where(here, inverse_0, inverse_1).astype(BF)

    following = scores(0)
    earlier = None
    mixed = {}
    for head in range(HEADS):
        found = following
        if head + 1 < HEADS:
            following = scores(head + 1)
        now = powers(head, found)
        if earlier is not None:
            mixed[head - 1] = mixes(head - 1, earlier)
            if head % 2 == 0:
                put(head // 2 - 1, mixed[head - 2], mixed[head - 1])
        earlier = now
    mixed[HEADS - 1] = mixes(HEADS - 1, earlier)
    put(HEADS // 2 - 1, mixed[HEADS - 2], mixed[HEADS - 1])


def attend_backward(e_ref, r_ref, o_ref, q_ref, k_ref, v_ref, dm_ref, dq_ref, dkt_ref, dvt_ref):
    low = first_lanes(SLAB)
    lane = lax.broadcasted_iota(jnp.int32, (SLAB, PAIR), 1) % HEAD
    units = jnp.where(lane < 2, 1.0, 0.0).astype(BF)
    none = jnp.zeros((), BF)
    qt = q_ref[...].T
    for pair in range(HEADS // 2):
        lanes = slice(pair * PAIR, (pair + 1) * PAIR)
        mixed = (dm_ref[:, lanes] * r_ref[:, lanes].astype(F32)).astype(BF)
        weighed = mixed.astype(F32) * o_ref[:, lanes].astype(F32)
        keys, values = k_ref[:, lanes], v_ref[:, lanes]
        mixed_t = mixed.T
        dq = []
        for side in range(2):
            head = 2 * pair + side
            rows = slice(head * HEAD, (head + 1) * HEAD)
            mine = low if side == 0 else ~low
            centre = jnp.sum(jnp.where(mine, weighed, 0.0), axis=1, keepdims=True)
            high = centre.astype(BF)
            rest = (centre - high.astype(F32)).astype(BF)
            column = jnp.where(lane == 0, -high, jnp.where(lane == 1, -rest, none))
            grad = nt(jnp.where(mine, mixed, column), jnp.where(mine, values, units))
            power = e_ref[head]
            score = (power.astype(F32) * grad).astype(BF)
            dq.append(nn(score, keys))
            dkt_ref[rows, :] = (nn(qt[rows], score) * (1.0 / LOG2E)).astype(BF)
            dvt_ref[rows, :] = nn(mixed_t[side * HEAD : (side + 1) * HEAD], power).astype(BF)
        dq_ref[:, lanes] = (jnp.where(low, dq[0], dq[1]) * HEAD**-0.5).astype(BF)


def piece_columns(lengths_ref, slab, side):
    column = lax.broadcasted_iota(jnp.int32, (1, PAIR), 1) % HEAD
    opening = jnp.zeros((1, PAIR), jnp.int32)
    closing = jnp.zeros((1, PAIR), jnp.int32)
    total = jnp.int32(0)
    for piece in range(lengths_ref.shape[2]):
        following = total + lengths_ref[slab, side, piece]
        opening = jnp.where(column == piece, total, opening)
        closing = jnp.where(column == piece, following, closing)
        total = following
    place = lax.broadcasted_iota(jnp.int32, (SLAB, PAIR), 0)
    return jnp.where((opening <= place) & (place < closing), 1.0, 0.0).astype(BF)


def outside(columns):
    return jnp.where(columns > 0, 0.0, FAR).astype(BF)


def load_pieces(place_ref, first, pieces, w_s, sems):
    copies = []
    for blocks in pieces:
        rows = blocks.shape[2]
        for index in range(blocks.shape[0]):
            start = pl.multiple_of(place_ref[first + len(copies)] * rows, rows)
            copies.append(pltpu.make_async_copy(blocks.at[index], w_s.at[:, pl.ds(start, rows), :], sems.at[len(copies)]))
    for copy in copies:
        copy.start()
    for copy in copies:
        copy.wait()


def load_once(place_ref, first, pieces, w_s, sems):
    @pl.when(pl.program_id(0) == 0)
    def _():
        load_pieces(place_ref, first, pieces, w_s, sems)


def here(*refs):
    step = pl.program_id(0)
    return [ref.at[step if ref.shape[0] > 1 else 0] for ref in refs]


def self_forward(count, first, place_ref, lengths_ref, x_ref, *refs):
    pieces, (out_ref, q_ref, k_ref, v_ref, e_ref, r_ref, o_ref, w_ref, e_s, sems, e_sems, out_sem) = refs[:count], refs[count:]
    load_once(place_ref, first, pieces, w_ref, sems)
    pass_on = pltpu.make_async_copy(w_ref, out_ref, out_sem)
    x_ref, q_ref, k_ref, v_ref, r_ref, o_ref = here(x_ref, q_ref, k_ref, v_ref, r_ref, o_ref)
    step = pl.program_id(0)

    @pl.when(step == 0)
    def _():
        pass_on.start()

    def store(slab, head):
        return pltpu.make_async_copy(e_s.at[slab, head], e_ref.at[slab, head], e_sems.at[slab, head])

    x = x_ref[...]
    q_ref[...] = (nn(x, w_ref[0]) * QSCALE).astype(BF)
    k_ref[...] = nn(x, w_ref[1]).astype(BF)
    v_ref[...] = nn(x, w_ref[2]).astype(BF)
    columns = piece_columns(lengths_ref, pl.program_id(0), 0)
    attend_forward(q_ref, k_ref, v_ref, columns, outside(columns), e_s.at[step], o_ref, r_ref, True, lambda head: store(step, head).start())

    @pl.when(step == pl.num_programs(0) - 1)
    def _():
        pass_on.wait()
        for slab in range(e_s.shape[0]):
            for head in range(HEADS):
                store(slab, head).wait()


def cross_inputs(count, first, owners, place_ref, o1_ref, x_ref, mem_ref, *refs):
    pieces, refs = refs[:count], refs[count:]
    out_ref, vec_ref, q_ref, k_ref, v_ref, q_kept, k_kept, v_kept, unit1_ref, kept1_ref, scale1_ref, low1_ref, w_ref, sems, out_sem = refs
    load_once(place_ref, first, pieces, w_ref, sems)
    pass_on = pltpu.make_async_copy(w_ref, out_ref, out_sem)

    @pl.when(pl.program_id(0) == 0)
    def _():
        pass_on.start()
        rows = WIDTH // owners
        total = w_ref[5, 0:16, :].astype(F32)
        for owner in range(1, owners):
            total = total + w_ref[5, owner * rows : owner * rows + 16, :].astype(F32)
        vec_ref[...] = total

    o1_ref, x_ref, mem_ref, q_ref, k_ref, v_ref = here(o1_ref, x_ref, mem_ref, q_ref, k_ref, v_ref)
    q_kept, k_kept, v_kept = here(q_kept, k_kept, v_kept)
    unit1_ref, kept1_ref, scale1_ref, low1_ref = here(unit1_ref, kept1_ref, scale1_ref, low1_ref)
    residual = vec_ref[6:7, :] * x_ref[...].astype(F32) + nn(o1_ref[...], w_ref[4])
    unit, scale = norm_forward(residual)
    unit1_ref[...] = unit
    kept1_ref[...] = unit
    scale1_ref[...] = scale
    low = (unit * vec_ref[0:1, :] + vec_ref[3:4, :]).astype(BF)
    low1_ref[...] = low
    memory = mem_ref[...]
    for once, kept, value in ((k_ref, k_kept, nn(memory, w_ref[1])), (v_ref, v_kept, nn(memory, w_ref[2])), (q_ref, q_kept, nn(low, w_ref[0]) * QSCALE)):
        value = value.astype(BF)
        once[...] = value
        kept[...] = value

    @pl.when(pl.program_id(0) == pl.num_programs(0) - 1)
    def _():
        pass_on.wait()


def cross_forward(lengths_ref, q_ref, k_ref, v_ref, e_ref, r_ref, o_ref, kept_ref):
    slab = pl.program_id(0)
    q_ref, k_ref, v_ref, e_ref, r_ref, o_ref, kept_ref = here(q_ref, k_ref, v_ref, e_ref, r_ref, o_ref, kept_ref)
    queries_in, keys_out = piece_columns(lengths_ref, slab, 0), outside(piece_columns(lengths_ref, slab, 1))
    attend_forward(q_ref, k_ref, v_ref, queries_in, keys_out, e_ref, o_ref, r_ref, False)
    kept_ref[...] = o_ref[...]


CUBE = 0.044715
ROOT = math.sqrt(2.0 / math.pi)


def feed_copies(place_ref, begin, first, second, ex_s, co_s, sems):
    each = co_s.shape[1]
    results = [], []
    for side, pieces in enumerate((first, second)):
        for blocks in pieces:
            rows = blocks.shape[2]
            for index in range(blocks.shape[0]):
                number = len(results[side])
                start = place_ref[begin + number] * rows
                owner = start // each
                if side == 0:
                    goal = ex_s.at[:, pl.ds(pl.multiple_of(start, rows), rows), :]
                else:
                    goal = co_s.at[pl.ds(owner * 4, 4), pl.ds(pl.multiple_of(start - owner * each, rows), rows), :]
                results[side].append(pltpu.make_async_copy(blocks.at[index], goal, sems.at[side, number]))
    return results


def feed_both(count, begin, reduce_at, place_ref, o2_ref, unit1_ref, w_ref, cot_ref, vec_ref, *refs):
    pieces, refs = refs[: 2 * count], refs[2 * count :]
    (out_ref, ds_ref, unit_s, scale_ref, keep_ref, send_ref, dvec_ref,
     act_s, slope_s, branch_s, low_s, dbranch_s, cot_s, out_s, dex_s, dco_s, ex_s, co_s, sems, own_sems) = refs
    slabs = unit_s.shape[0]
    chunks = ex_s.shape[0]
    owners = co_s.shape[0] // 4
    first, second = feed_copies(place_ref, begin, pieces[:count], pieces[count:], ex_s, co_s, sems)
    cot_copy = pltpu.make_async_copy(cot_ref, cot_s, own_sems.at[0])
    out_copy = pltpu.make_async_copy(out_s, out_ref, own_sems.at[1])
    for copy in first + second + [cot_copy]:
        copy.start()

    def rows(slab):
        return slice(slab * SLAB, (slab + 1) * SLAB)

    def contract(part):
        return co_s[part * owners : (part + 1) * owners].reshape(WIDTH, WIDTH)

    def state(slab):
        return unit_s[slab] * vec_ref[1:2, :] + vec_ref[4:5, :]

    for slab in range(slabs):
        before = unit1_ref[slab] * vec_ref[0:1, :] + vec_ref[3:4, :]
        unit_s[slab], scale_ref[slab] = norm_forward(vec_ref[7:8, :] * before + nn(o2_ref[slab], w_ref[0]))
        low_s[rows(slab), :] = state(slab).astype(BF)
    for copy in first:
        copy.wait()
    following = nn(low_s[...], ex_s[0])
    for part in range(chunks):
        u = following
        if part + 1 < chunks:
            following = nn(low_s[...], ex_s[part + 1])
        square = u * u
        bend = jnp.tanh(u * (ROOT + (ROOT * CUBE) * square))
        half = 0.5 + 0.5 * bend
        act_s[part] = (u * half).astype(BF)
        slope_s[part] = half + (u * half) * (1.0 - bend) * (ROOT + (3.0 * ROOT * CUBE) * square)
        if part == 0:
            for copy in second:
                copy.wait()
            branch_s[...] = nn(act_s[part], contract(part))
        else:
            branch_s[...] += nn(act_s[part], contract(part))
    cot_copy.wait()
    for slab in range(slabs):
        now = state(slab)
        unit, scale = norm_forward(vec_ref[8:9, :] * now + branch_s[rows(slab), :])
        out_s[slab] = (unit * vec_ref[2:3, :] + vec_ref[5:6, :]).astype(BF)
        up = cot_s[slab].astype(F32)
        dres = norm_backward(up, unit, scale, vec_ref[2:3, :])
        sums = (rows_sum(up * unit), rows_sum(up), rows_sum(dres * now))
        for row, value in enumerate(sums):
            if slab == 0:
                dvec_ref[row : row + 1, :] = value
            else:
                dvec_ref[row : row + 1, :] += value
        branch_s[rows(slab), :] = dres * vec_ref[8:9, :]
        dbranch_s[rows(slab), :] = dres.astype(BF)
    out_copy.start()
    low_t = low_s[...].T
    for part in range(chunks):
        dco_s[part] = tn(act_s[part], dbranch_s[...]).astype(BF)
        dhid = (nt(dbranch_s[...], contract(part)) * slope_s[part]).astype(BF)
        dex_s[part] = nn(low_t, dhid).astype(BF)
        branch_s[...] += nt(dhid, ex_s[part])
    for slab in range(slabs):
        ds_ref[slab] = branch_s[rows(slab), :]
    put_feed(place_ref, reduce_at, dex_s, dco_s, keep_ref, send_ref)
    out_copy.wait()


def put_gradients(place_ref, begin, dw_s, keep_ref, send_ref, first):
    blocks = keep_ref.shape[0]
    owners = blocks // dw_s.shape[0]
    rows = WIDTH // (2 * owners)
    core = place_ref[begin]
    for matrix in range(dw_s.shape[0]):
        for owner in range(owners):
            at = begin + 1 + matrix * owners + owner
            start = pl.multiple_of((2 * owner + core) * rows, rows)
            keep_ref[place_ref[at], first : first + rows, :] = dw_s[matrix, pl.ds(start, rows), :]
            start = pl.multiple_of((2 * owner + 1 - core) * rows, rows)
            send_ref[place_ref[at + blocks], first : first + rows, :] = dw_s[matrix, pl.ds(start, rows), :]


def put_vectors(place_ref, begin, dvec_s, count, keep_ref, send_ref, first):
    blocks = keep_ref.shape[0]
    owners = blocks // count
    columns = WIDTH // (2 * owners)
    core = place_ref[begin]
    rows = slice(first, first + 16)
    blank = jnp.zeros((16, WIDTH), BF)
    for block in range(blocks):
        keep_ref[block, rows, :] = blank
        send_ref[block, rows, :] = blank
    for owner in range(owners):
        low = dvec_s[:, 2 * owner * columns : (2 * owner + 1) * columns]
        high = dvec_s[:, (2 * owner + 1) * columns : (2 * owner + 2) * columns]
        rest = jnp.zeros((16, WIDTH - columns), F32)
        own = jnp.where(core == 0, low, high)
        other = jnp.where(core == 0, high, low)
        at = begin + 1 + owner
        keep_ref[place_ref[at], rows, :] = jnp.concatenate([own, rest], axis=1).astype(BF)
        send_ref[place_ref[at + blocks], rows, :] = jnp.concatenate([other, rest], axis=1).astype(BF)


def put_feed(place_ref, begin, dex_s, dco_s, keep_ref, send_ref):
    blocks = keep_ref.shape[0]
    owners = blocks // 4
    each = keep_ref.shape[1] // 2
    core = place_ref[begin]
    for pair in range(4):
        for owner in range(owners):
            at = begin + 1 + pair * owners + owner
            for out_ref, on, block in ((keep_ref, core, place_ref[at]), (send_ref, 1 - core, place_ref[at + blocks])):
                shard = 2 * owner + on
                for side in range(2):
                    number = 2 * pair + side
                    rows = slice(side * each, (side + 1) * each)
                    if number < 4:
                        out_ref[block, rows, :] = dex_s[number, pl.ds(pl.multiple_of(shard * each, each), each), :]
                    else:
                        row = (shard * 4 + number - 4) * each
                        chunk = row // WIDTH
                        out_ref[block, rows, :] = dco_s[chunk, pl.ds(pl.multiple_of(row - chunk * WIDTH, each), each), :]


def fetcher(pairs, sems):
    step = pl.program_id(0)

    def copy(number, slab):
        return pltpu.make_async_copy(pairs[number][0].at[slab], pairs[number][1].at[slab], sems.at[number, slab])

    @pl.when(step == 0)
    def _():
        for slab in range(pairs[0][1].shape[0]):
            for number in range(len(pairs)):
                copy(number, slab).start()

    def wait(first, last):
        for number in range(first, last):
            copy(number, step).wait()

    return wait


def all_rows(ref):
    return ref[...].reshape(-1, WIDTH)


def cross_backward(begin, place_ref, ds2_ref, unit2_ref, scale2_ref, w_ref, vec_ref, q_ref, k_ref, v_ref, r_ref, o_ref, low1_ref, mem_ref, e_ref,
                   ds1_ref, dk_ref, dv_ref, keep_ref, send_ref, dvec_ref,
                   q_s, k_s, v_s, r_s, o_s, low1_s, mem_s, w_s, dm_s, dq_s, dk_s, dv_s, dbranch_s, dkt_s, dvt_s, dw_s, sems, out_sems, w_sems):
    step = pl.program_id(0)
    steps = pl.num_programs(0)
    w_copies = [pltpu.make_async_copy(w_ref.at[3], w_s.at[3], w_sems.at[0]), pltpu.make_async_copy(w_ref.at[0:3], w_s.at[0:3], w_sems.at[1])]

    @pl.when(step == 0)
    def _():
        w_copies[0].start()

    wait = fetcher([(q_ref, q_s), (k_ref, k_s), (v_ref, v_s), (r_ref, r_s), (o_ref, o_s), (low1_ref, low1_s), (mem_ref, mem_s)], sems)
    outward = [pltpu.make_async_copy(dk_s, dk_ref, out_sems.at[0]), pltpu.make_async_copy(dv_s, dv_ref, out_sems.at[1])]

    @pl.when(step == 0)
    def _():
        w_copies[1].start()
        dvec_ref[...] = jnp.zeros_like(dvec_ref)

    ds2_ref, unit2_ref, scale2_ref, ds1_ref = here(ds2_ref, unit2_ref, scale2_ref, ds1_ref)
    up = ds2_ref[...]
    unit = unit2_ref[...]
    dvec_ref[0:1, :] += rows_sum(up * unit)
    dvec_ref[1:2, :] += rows_sum(up)
    dres = norm_backward(up, unit, scale2_ref[...], vec_ref[1:2, :])
    dbranch = dres.astype(BF)
    dbranch_s[step] = dbranch

    @pl.when(step == 0)
    def _():
        w_copies[0].wait()

    dm_s[...] = nt(dbranch, w_s[3])
    ds1_ref[...] = dres * vec_ref[7:8, :]
    wait(0, 5)
    attend_backward(e_ref.at[step], r_s.at[step], o_s.at[step], q_s.at[step], k_s.at[step], v_s.at[step], dm_s, dq_s.at[step], dkt_s, dvt_s)
    wait(5, 7)
    dvec_ref[2:3, :] += rows_sum(dbranch_s[step].astype(F32) * low1_s[step].astype(F32))

    @pl.when(step == 0)
    def _():
        w_copies[1].wait()

    ds1_ref[...] += nt(dq_s[step], w_s[0])
    dk_s[step] = dkt_s[...].T
    dv_s[step] = dvt_s[...].T

    @pl.when(step == steps - 1)
    def _():
        for copy in outward:
            copy.start()
        dw_s[0] = tn(all_rows(low1_s), all_rows(dq_s)).astype(BF)
        memory_t = all_rows(mem_s).T
        dw_s[1] = nn(memory_t, all_rows(dk_s)).astype(BF)
        dw_s[2] = nn(memory_t, all_rows(dv_s)).astype(BF)
        dw_s[3] = tn(all_rows(o_s), all_rows(dbranch_s)).astype(BF)
        put_gradients(place_ref, begin, dw_s, keep_ref, send_ref, 0)
        for copy in outward:
            copy.wait()


def self_backward(ds1_ref, unit1_ref, scale1_ref, w3_ref, vec_ref, q_ref, k_ref, v_ref, r_ref, o_ref, x_ref, e_ref,
                  part_ref, dq_ref, dk_ref, dv_ref, dbranch_ref, o_s, x_s, dvec_ref, q_s, k_s, v_s, r_s, e_s, dm_s, dkt_s, dvt_s, sems):
    step = pl.program_id(0)
    wait = fetcher([(e_ref, e_s), (q_ref, q_s), (k_ref, k_s), (v_ref, v_s), (r_ref, r_s), (o_ref, o_s), (x_ref, x_s)], sems)

    @pl.when(step == 0)
    def _():
        dvec_ref[...] = jnp.zeros_like(dvec_ref)

    ds1_ref, unit1_ref, scale1_ref, part_ref, dq_ref, dk_ref, dv_ref, dbranch_ref = here(ds1_ref, unit1_ref, scale1_ref, part_ref, dq_ref, dk_ref, dv_ref, dbranch_ref)
    up = ds1_ref[...]
    unit = unit1_ref[...]
    dvec_ref[0:1, :] += rows_sum(up * unit)
    dvec_ref[1:2, :] += rows_sum(up)
    dres = norm_backward(up, unit, scale1_ref[...], vec_ref[0:1, :])
    dbranch = dres.astype(BF)
    dbranch_ref[...] = dbranch
    dm_s[...] = nt(dbranch, w3_ref[0])
    part_ref[...] = dres * vec_ref[6:7, :]
    wait(0, 6)
    attend_backward(e_s.at[step], r_s.at[step], o_s.at[step], q_s.at[step], k_s.at[step], v_s.at[step], dm_s, dq_ref, dkt_s, dvt_s)
    dk_ref[...] = dkt_s[...].T
    dv_ref[...] = dvt_s[...].T
    wait(6, 7)
    dvec_ref[2:3, :] += rows_sum(dbranch_ref[...].astype(F32) * x_s[step].astype(F32))


def self_weights(begin, place_ref, dq_ref, dk_ref, dv_ref, dbranch_ref, o_ref, x_ref, dvec1_ref, dvec2_ref, dvec3_ref, keep_ref, send_ref, dw_s, dvec_s):
    dvec_s[...] = jnp.zeros_like(dvec_s)
    for row in range(3):
        for number, ref in enumerate((dvec1_ref, dvec2_ref, dvec3_ref)):
            dvec_s[3 * row + number : 3 * row + number + 1, :] = ref[row : row + 1, :]
    x_t = all_rows(x_ref).T
    dw_s[0] = nn(x_t, all_rows(dq_ref)).astype(BF)
    dw_s[1] = nn(x_t, all_rows(dk_ref)).astype(BF)
    dw_s[2] = nn(x_t, all_rows(dv_ref)).astype(BF)
    dw_s[3] = tn(all_rows(o_ref), all_rows(dbranch_ref)).astype(BF)
    put_gradients(place_ref, begin, dw_s, keep_ref, send_ref, 0)
    put_vectors(place_ref, begin, dvec_s, dw_s.shape[0], keep_ref, send_ref, keep_ref.shape[1] - 16)


def input_gradients(part_ref, dq_ref, dk_ref, dv_ref, w_ref, dk2_ref, dv2_ref, w2_ref, dx_ref, dmem_ref):
    part_ref, dq_ref, dk_ref, dv_ref, dk2_ref, dv2_ref, dx_ref, dmem_ref = here(part_ref, dq_ref, dk_ref, dv_ref, dk2_ref, dv2_ref, dx_ref, dmem_ref)
    dx_ref[...] = part_ref[...] + nt(dq_ref[...], w_ref[0]) + nt(dk_ref[...], w_ref[1]) + nt(dv_ref[...], w_ref[2])
    dmem_ref[...] = nt(dk2_ref[...], w2_ref[1]) + nt(dv2_ref[...], w2_ref[2])


def cut_shards(at, place_ref, stacked_ref, expand_ref, contract_ref, vec_ref, a_ref, b_ref, c_ref, a_s, b_s, ex_s, co_s, vec_s, sems):
    rows = stacked_ref.shape[1]
    middle = pl.multiple_of(place_ref[at] * (rows // 2), rows // 2)
    half = pl.ds(middle, rows // 2)
    start = pl.multiple_of(place_ref[at + 1] * (rows // 4), rows // 4)
    quarter = pl.ds(start, rows // 4)
    copies = [
        pltpu.make_async_copy(stacked_ref.at[0:3, half, :], a_s, sems.at[0]),
        pltpu.make_async_copy(stacked_ref.at[3:8, quarter, :], b_s, sems.at[1]),
        pltpu.make_async_copy(vec_ref, vec_s, sems.at[2]),
        pltpu.make_async_copy(expand_ref.at[half, :], ex_s, sems.at[3]),
    ]
    copies += [
        pltpu.make_async_copy(contract_ref.at[pl.ds(pl.multiple_of(part * rows + middle, rows // 2), rows // 2), :], co_s.at[part], sems.at[4 + part])
        for part in range(4)
    ]
    for copy in copies:
        copy.start()
    for copy in copies:
        copy.wait()
    a_ref[0] = a_s[...].astype(BF)
    for index, matrix in enumerate((4, 5, 6, 7, 3)):
        b_ref[0, index] = b_s[matrix - 3].astype(BF)
    vec = jnp.concatenate([vec_s[...]] * (WIDTH // vec_ref.shape[1]), axis=1)
    owner = lax.broadcasted_iota(jnp.int32, vec.shape, 1) // vec_ref.shape[1]
    vec = jnp.where(owner == place_ref[at + 2], vec, 0.0)
    b_ref[0, 5] = jnp.concatenate([vec, jnp.zeros((rows // 4 - vec.shape[0], WIDTH), F32)], axis=0).astype(BF)
    for part in range(4):
        c_ref[0, part] = ex_s[:, part * WIDTH : (part + 1) * WIDTH].astype(BF)
        c_ref[0, 4 + part] = co_s[part].astype(BF)


def per_slab(*tail):
    return pl.BlockSpec((1,) + tail, lambda m: (m,) + (0,) * len(tail))


def fixed(*dims):
    return pl.BlockSpec(dims, lambda m: (0,) * len(dims), pipeline_mode=pl.Buffered(1))


def shape(dims, kind):
    return jax.ShapeDtypeStruct(tuple(dims), kind)


def options(mib):
    return pltpu.CompilerParams(dimension_semantics=("arbitrary",), vmem_limit_bytes=mib * MIB)


def estimate(microseconds):
    return pl.CostEstimate(flops=int(microseconds * 1e9), bytes_accessed=1 << 20, transcendentals=0)


SCALARS = pl.BlockSpec(memory_space=pltpu.SMEM)
ANYWHERE = pl.BlockSpec(memory_space=pl.ANY)
RESIDENT = pl.BlockSpec(memory_space=pltpu.VMEM)
ROWS = per_slab(SLAB, WIDTH)
SCALE = per_slab(SLAB, 1)


def near(*arrays):
    return tuple(pltpu.with_memory_space_constraint(array, pltpu.VMEM) for array in arrays)


def far(*arrays):
    return tuple(pltpu.with_memory_space_constraint(array, pltpu.HBM) for array in arrays)


def near_shape(dims, kind):
    return pltpu.VMEM(tuple(dims), kind)


def far_shape(dims, kind):
    return pltpu.HBM(tuple(dims), kind)


def slabs(g, kind, place=far_shape):
    return place((g, SLAB, WIDTH), kind)


def powers_shape(g, place):
    return place((g, HEADS, SLAB, SLAB), BF)


def run_cut_shards(at, place, stacked, expand, contract, vec):
    rows = stacked.shape[1]
    return pl.pallas_call(
        functools.partial(cut_shards, at),
        in_specs=[SCALARS] + [ANYWHERE] * 4,
        out_specs=[RESIDENT] * 3,
        out_shape=[shape((1, 3, rows // 2, WIDTH), BF), shape((1, 6, rows // 4, WIDTH), BF), shape((1, 8, rows // 2, WIDTH), BF)],
        scratch_shapes=[
            pltpu.VMEM((3, rows // 2, WIDTH), F32),
            pltpu.VMEM((5, rows // 4, WIDTH), F32),
            pltpu.VMEM((rows // 2, expand.shape[1]), F32),
            pltpu.VMEM((4, rows // 2, WIDTH), F32),
            pltpu.VMEM(vec.shape, F32),
            pltpu.SemaphoreType.DMA((8,)),
        ],
        compiler_params=pltpu.CompilerParams(vmem_limit_bytes=16 * MIB),
        name="cut_shards",
    )(place, *far(stacked, expand, contract, vec))


def run_self_forward(first, place, lengths, x, w):
    g = x.shape[0]
    return pl.pallas_call(
        functools.partial(self_forward, len(w), first),
        grid=(g,),
        in_specs=[SCALARS, SCALARS, ROWS] + [ANYWHERE] * len(w),
        out_specs=[ANYWHERE, ROWS, ROWS, ROWS, ANYWHERE, ROWS, RESIDENT],
        out_shape=[far_shape((3, WIDTH, WIDTH), BF)] + [slabs(g, BF)] * 3 + [powers_shape(g, far_shape), slabs(g, BF), slabs(g, BF, near_shape)],
        scratch_shapes=[pltpu.VMEM((3, WIDTH, WIDTH), BF), pltpu.VMEM((g, HEADS, SLAB, SLAB), BF), pltpu.SemaphoreType.DMA((sum(piece.shape[0] for piece in w),)), pltpu.SemaphoreType.DMA((g, HEADS)), pltpu.SemaphoreType.DMA],
        compiler_params=options(32),
        cost_estimate=estimate(12),
        name="self_forward",
    )(place, lengths, x, *w)


def run_cross_inputs(first, owners, place, o1, x, memory, w):
    g = memory.shape[0]
    return pl.pallas_call(
        functools.partial(cross_inputs, len(w), first, owners),
        grid=(g,),
        in_specs=[SCALARS, RESIDENT, ROWS, ROWS] + [ANYWHERE] * len(w),
        out_specs=[ANYWHERE, fixed(16, WIDTH), RESIDENT, RESIDENT, RESIDENT, ROWS, ROWS, ROWS, RESIDENT, ROWS, SCALE, ROWS],
        out_shape=[far_shape((6, WIDTH, WIDTH), BF), far_shape((16, WIDTH), F32)]
        + [slabs(g, BF, near_shape)] * 3
        + [slabs(g, BF)] * 3
        + [slabs(g, F32, near_shape), slabs(g, F32), far_shape((g, SLAB, 1), F32), slabs(g, BF)],
        scratch_shapes=[pltpu.VMEM((6, WIDTH, WIDTH), BF), pltpu.SemaphoreType.DMA((sum(piece.shape[0] for piece in w),)), pltpu.SemaphoreType.DMA],
        compiler_params=options(24),
        cost_estimate=estimate(7),
        name="cross_inputs",
    )(place, *near(o1), x, memory, *w)


def run_cross_forward(lengths, q, k, v):
    g = q.shape[0]
    return pl.pallas_call(
        cross_forward,
        grid=(g,),
        in_specs=[SCALARS] + [RESIDENT] * 3,
        out_specs=[RESIDENT, ROWS, RESIDENT, ROWS],
        out_shape=[powers_shape(g, near_shape), slabs(g, BF), slabs(g, BF, near_shape), slabs(g, BF)],
        compiler_params=options(24),
        cost_estimate=estimate(10),
        name="cross_forward",
    )(lengths, *near(q, k, v))


def run_feed(begin, reduce_at, owners, place, o2, unit1, w_cross, cot, first, second, vec):
    g = unit1.shape[0]
    rows = WIDTH // owners
    pieces = sum(piece.shape[0] for piece in first)
    dims = (2 * owners, 2 * rows, WIDTH)
    tokens = g * SLAB
    last = pl.BlockSpec((1, WIDTH, WIDTH), lambda m: (3, 0, 0))
    return pl.pallas_call(
        functools.partial(feed_both, len(first), begin, reduce_at),
        grid=(1,),
        in_specs=[SCALARS, RESIDENT, RESIDENT, last, ANYWHERE, fixed(16, WIDTH)] + [ANYWHERE] * (2 * len(first)),
        out_specs=[ANYWHERE, RESIDENT, RESIDENT, fixed(g, SLAB, 1), RESIDENT, RESIDENT, fixed(8, WIDTH)],
        out_shape=[slabs(g, BF), slabs(g, F32, near_shape), slabs(g, F32, near_shape), far_shape((g, SLAB, 1), F32)] + [near_shape(dims, BF)] * 2 + [far_shape((8, WIDTH), F32)],
        scratch_shapes=[
            pltpu.VMEM((4, tokens, WIDTH), BF),
            pltpu.VMEM((4, tokens, WIDTH), F32),
            pltpu.VMEM((tokens, WIDTH), F32),
            pltpu.VMEM((tokens, WIDTH), BF),
            pltpu.VMEM((tokens, WIDTH), BF),
            pltpu.VMEM((g, SLAB, WIDTH), BF),
            pltpu.VMEM((g, SLAB, WIDTH), BF),
            pltpu.VMEM((4, WIDTH, WIDTH), BF),
            pltpu.VMEM((4, WIDTH, WIDTH), BF),
            pltpu.VMEM((4, WIDTH, WIDTH), BF),
            pltpu.VMEM((4 * owners, rows, WIDTH), BF),
            pltpu.SemaphoreType.DMA((2, pieces)),
            pltpu.SemaphoreType.DMA((2,)),
        ],
        compiler_params=options(FEED_MIB),
        cost_estimate=estimate(24),
        name="feed_both",
    )(place, *near(o2, unit1), *far(w_cross), cot, *far(vec), *first, *second)


def slab_scratch(g, kinds):
    return [pltpu.VMEM((g, SLAB, WIDTH), kind) for kind in kinds]


def run_cross_backward(begin, place, owners, ds2, unit2, scale2, low1, memory, w, vec, saved):
    g = memory.shape[0]
    dims = (4 * owners, WIDTH // (2 * owners), WIDTH)
    q, k, v, e, r, o = saved
    return pl.pallas_call(
        functools.partial(cross_backward, begin),
        grid=(g,),
        in_specs=[SCALARS, RESIDENT, RESIDENT, SCALE, ANYWHERE, fixed(16, WIDTH)] + [ANYWHERE] * 7 + [RESIDENT],
        out_specs=[RESIDENT, ANYWHERE, ANYWHERE, RESIDENT, RESIDENT, fixed(8, WIDTH)],
        out_shape=[slabs(g, F32, near_shape), slabs(g, BF), slabs(g, BF), near_shape(dims, BF), near_shape(dims, BF), far_shape((8, WIDTH), F32)],
        scratch_shapes=slab_scratch(g, [BF] * 7)
        + [pltpu.VMEM((4, WIDTH, WIDTH), BF), pltpu.VMEM((SLAB, WIDTH), F32)]
        + slab_scratch(g, [BF] * 4)
        + [pltpu.VMEM((WIDTH, SLAB), BF)] * 2
        + [pltpu.VMEM((4, WIDTH, WIDTH), BF), pltpu.SemaphoreType.DMA((7, g)), pltpu.SemaphoreType.DMA((2,)), pltpu.SemaphoreType.DMA((2,))],
        compiler_params=options(CROSS_MIB),
        cost_estimate=estimate(19),
        name="cross_backward",
    )(place, *near(ds2, unit2), *far(scale2, w, vec, q, k, v, r, o, low1), memory, *near(e))


def run_self_backward(ds1, unit1, scale1, x, w_cross, vec, saved):
    g = x.shape[0]
    q, k, v, e, r, o = saved
    third = pl.BlockSpec((1, WIDTH, WIDTH), lambda m: (4, 0, 0))
    return pl.pallas_call(
        self_backward,
        grid=(g,),
        in_specs=[RESIDENT, ROWS, SCALE, third, fixed(16, WIDTH)] + [ANYWHERE] * 7,
        out_specs=[ROWS] + [RESIDENT] * 6 + [fixed(8, WIDTH)],
        out_shape=[slabs(g, F32)] + [slabs(g, BF, near_shape)] * 6 + [far_shape((8, WIDTH), F32)],
        scratch_shapes=slab_scratch(g, [BF] * 4)
        + [pltpu.VMEM((g, HEADS, SLAB, SLAB), BF), pltpu.VMEM((SLAB, WIDTH), F32)]
        + [pltpu.VMEM((WIDTH, SLAB), BF)] * 2
        + [pltpu.SemaphoreType.DMA((7, g))],
        compiler_params=options(SELF_MIB),
        cost_estimate=estimate(17),
        name="self_backward",
    )(*near(ds1), *far(unit1, scale1, w_cross, vec, q, k, v, r, o), x, *far(e))


def run_self_weights(begin, place, owners, grads, dvecs):
    dims = (4 * owners, WIDTH // (2 * owners) + 16, WIDTH)
    return pl.pallas_call(
        functools.partial(self_weights, begin),
        grid=(1,),
        in_specs=[SCALARS] + [RESIDENT] * 6 + [fixed(8, WIDTH)] * 3,
        out_specs=[RESIDENT] * 2,
        out_shape=[near_shape(dims, BF)] * 2,
        scratch_shapes=[pltpu.VMEM((4, WIDTH, WIDTH), BF), pltpu.VMEM((16, WIDTH), F32)],
        compiler_params=options(20),
        cost_estimate=estimate(4),
        name="self_weights",
    )(place, *near(*grads), *far(*dvecs))


def run_input_gradients(part, dq, dk, dv, w, dk2, dv2, w2):
    g = part.shape[0]
    return pl.pallas_call(
        input_gradients,
        grid=(g,),
        in_specs=[ROWS] + [RESIDENT] * 3 + [fixed(3, WIDTH, WIDTH), ROWS, ROWS, fixed(3, WIDTH, WIDTH)],
        out_specs=[ROWS, ROWS],
        out_shape=[slabs(g, F32), slabs(g, F32)],
        compiler_params=options(28),
        cost_estimate=estimate(6),
        name="input_gradients",
    )(*far(part), *near(dq, dk, dv), *far(w, dk2, dv2, w2))
def adam_update(weight, first_moment, second_moment, gradient):
    correction = 1.0 - 0.5**STEP
    first_next = 0.5 * first_moment + 0.5 * gradient
    second_next = 0.5 * second_moment + 0.5 * gradient * gradient
    weight_next = weight - LEARN_RATE * (first_next / correction) / (jnp.sqrt(second_next / correction) + ADAM_EPS)
    return (weight_next, first_next, second_next)


def picked(order, parts):
    value = parts[0]
    for number in range(1, len(parts)):
        value = jnp.where(order == number, parts[number], value)
    return value.astype(F32)


def adam_stacked(at, place_ref, part_0, part_1, part_2, part_3, w_ref, m_ref, s_ref, vw_ref, vm_ref, vs_ref, w_out, m_out, s_out, vw_out, vm_out, vs_out):
    rows = w_ref.shape[1]
    group = pl.program_id(0)
    parts = (part_0, part_1, part_2, part_3)

    def update(first):
        for matrix in range(4):
            grad = picked(place_ref[at + matrix], [part[0, first : first + rows, :] for part in parts])
            w_out[matrix], m_out[matrix], s_out[matrix] = adam_update(w_ref[matrix], m_ref[matrix], s_ref[matrix], grad)

    @pl.when(group == 0)
    def _():
        update(0)
        grad = picked(place_ref[at], [part[0, rows : rows + 16, :] for part in parts])
        vw_out[...], vm_out[...], vs_out[...] = adam_update(vw_ref[...], vm_ref[...], vs_ref[...], grad[: vw_ref.shape[0], : vw_ref.shape[1]])

    @pl.when(group == 1)
    def _():
        update(rows + 16)


def run_adam_stacked(at, place, parts, stacked, vectors):
    rows = stacked[0].shape[1]
    block = pl.BlockSpec((4, rows, WIDTH), lambda group: (group, 0, 0))
    vector = fixed(*vectors[0].shape)
    return pl.pallas_call(
        functools.partial(adam_stacked, at),
        grid=(2,),
        in_specs=[SCALARS] + [fixed(*part.shape) for part in parts] + [block] * 3 + [vector] * 3,
        out_specs=[block] * 3 + [vector] * 3,
        out_shape=[shape(a.shape, F32) for a in tuple(stacked) + tuple(vectors)],
        compiler_params=options(24),
        cost_estimate=estimate(4),
        name="adam_stacked",
    )(place, *parts, *stacked, *vectors)


def adam_feed(at, place_ref, low_ref, high_ref, *refs):
    rows = low_ref.shape[1] // 2

    def grad(number):
        span = slice(number % 2 * rows, (number % 2 + 1) * rows)
        return picked(place_ref[at + number // 2], [ref[block, span, :] for ref in (low_ref, high_ref) for block in range(2)])

    for part in range(4):
        where = (slice(None), slice(part * WIDTH, (part + 1) * WIDTH))
        refs[6][where], refs[7][where], refs[8][where] = adam_update(*(ref[where] for ref in refs[0:3]), grad(part))
        where = (slice(part * rows, (part + 1) * rows), slice(None))
        refs[9][where], refs[10][where], refs[11][where] = adam_update(*(ref[where] for ref in refs[3:6]), grad(4 + part))


def run_adam_feed(at, place, low, high, expand, contract):
    arrays = tuple(expand) + tuple(contract)
    whole = pl.BlockSpec(memory_space=pltpu.VMEM)
    return pl.pallas_call(
        functools.partial(adam_feed, at),
        in_specs=[SCALARS] + [whole] * 8,
        out_specs=[whole] * 6,
        out_shape=[shape(a.shape, F32) for a in arrays],
        compiler_params=pltpu.CompilerParams(vmem_limit_bytes=24 * MIB),
        cost_estimate=estimate(4),
        name="adam_feed",
    )(place, low, high, *arrays)


class Route:
    def __init__(self, m, n):
        self.m, self.n = m, n
        self.dp_bits = m.bit_length() - 1
        self.line_bits = n.bit_length() - 2
        self.line = n // 2

    def pairs(self, partner):
        return [(d * self.n + f, partner(d, f)) for d in range(self.m) for f in range(self.n)]

    def across_core(self):
        return self.pairs(lambda d, f: d * self.n + (f ^ 1))

    def along_line(self, mask):
        return self.pairs(lambda d, f: d * self.n + (f ^ (2 * mask)))

    def among_dp(self, mask):
        return self.pairs(lambda d, f: (d ^ mask) * self.n + f)

    def across_line(self, step):
        return self.pairs(lambda d, f: d * self.n + (f ^ (2 << (self.line_bits - 1 - step))))

    def across_dp(self, step):
        def partner(d, f):
            bit = step if f % 2 == 0 else self.dp_bits - 1 - step
            return (d ^ (1 << bit)) * self.n + f

        return self.pairs(partner)

    @staticmethod
    def spot(mask, bits, core):
        return mask if core == 0 else sum(((mask >> b) & 1) << (bits - 1 - b) for b in range(bits))

    def part(self, share, d, f):
        return sum(((d >> (bit if f % 2 == 0 else self.dp_bits - 1 - bit)) & 1) << bit for bit in range(share))

    def gather_row(self, share, d, f):
        z, c = divmod(f, 2)
        return [
            ((2 * (z ^ k) + who) << share) + (self.part(share, d, who) ^ step)
            for who in (c, 1 - c)
            for step in range(1 << share)
            for k in range(self.line)
        ]

    def reduce_row(self, d, f):
        z, c = divmod(f, 2)
        row = [c]
        for who in (c, 1 - c):
            line = [self.spot(owner ^ z, self.line_bits, 1) for owner in range(self.line)]
            row += [self.spot(j ^ d, self.dp_bits, who) * self.line + at for j in range(self.m) for at in line]
        return row + [self.spot(j ^ d, self.dp_bits, c) for j in range(self.m)] + [j ^ d for j in range(self.m)]

    def part_row(self, d, f):
        return [self.part(1, d, f), self.part(2, d, f), f]

    def tables(self):
        kinds = (functools.partial(self.gather_row, 1), functools.partial(self.gather_row, 2), self.reduce_row, self.part_row)
        rows = [[kind(d, f) for kind in kinds] for d in range(self.m) for f in range(self.n)]
        ends = np.cumsum([0] + [len(row) for row in rows[0]])
        return np.array([sum(row, []) for row in rows], np.int32), ends


BOTH = ("dp", "fsdp")


def after(values, *earlier):
    return lax.optimization_barrier((values,) + earlier)[0]


def doubled(blocks, got):
    return jnp.concatenate([blocks, got], axis=0)


def per_device(
    inputs,
    memory,
    cotangent,
    lengths,
    stacked_weights,
    expand_weights,
    contract_weights,
    scale_vectors,
    stacked_first,
    stacked_second,
    expand_first,
    expand_second,
    contract_first,
    contract_second,
    vector_first,
    vector_second,
):
    m, n = lax.axis_size("dp"), lax.axis_size("fsdp")
    width = WIDTH // n
    slabs = inputs.shape[0] * lengths.shape[1]
    x = inputs.reshape(slabs, SLAB, WIDTH)
    mem = memory.reshape(slabs, SLAB, WIDTH)
    cot = cotangent.reshape(slabs, SLAB, WIDTH)
    by_hand = m == 4 and width == 64 and n == 8
    here = lax.axis_index("fsdp")
    lengths = lengths.reshape(slabs, 2, -1)
    if by_hand:
        route = Route(m, n)
        table, ends = route.tables()
        row = lax.dynamic_index_in_dim(jnp.asarray(table), lax.axis_index("dp") * n + here, keepdims=False)
        halves, quarters, reduced, parts = (int(end) for end in ends[:4])
        order, holder = parts - 2 * m, parts - m

        def swap(blocks, pairs):
            return lax.ppermute(blocks, BOTH, pairs)

        along = [route.along_line(mask) for mask in range(1, n // 2)]
        line = [route.across_line(step) for step in range(route.line_bits)]
        across = [route.across_dp(step) for step in range(route.dp_bits)]
        core = route.across_core()
        a, b, c = run_cut_shards(parts, row, stacked_weights, expand_weights, contract_weights, scale_vectors)
        got = lax.optimization_barrier(tuple(swap(a, pairs) for pairs in along) + tuple(swap(b, pairs) for pairs in along))
        a, b = jnp.concatenate([a, *got[:3]], axis=0), jnp.concatenate([b, *got[3:]], axis=0)
        c = after(c, got)
        c_1, c_2, a_across, b_across, a_core = lax.optimization_barrier((swap(c, along[0]), swap(c, along[1]), swap(a, across[0]), swap(b, across[0]), swap(a, core)))
        b = doubled(b, b_across)
        b_across, b_core, c_3 = swap(b, across[1]), swap(b, core), swap(after(c, b), along[2])
        w_self, *saved1 = run_self_forward(halves, row, lengths, after(x, b), (a, a_across, a_core, swap(a_across, core)))
        b_across, c_3 = after((b_across, c_3), saved1[-1])
        ex, co = (jnp.concatenate([part[:, span] for part in (c, c_1, c_2, c_3)], axis=0) for span in (slice(0, 4), slice(4, 8)))
        b_across = after(b_across, ex)
        ex_across = swap(ex, across[0])
        w_cross = (b, b_across, b_core, swap(b_across, core))
        w_cross, vec, q2, k2, v2, *qkv2, unit1, kept1, scale1, low1 = run_cross_inputs(quarters, n, row, saved1[-1], x, mem, w_cross)
        ex_across = after(ex_across, unit1)
        co_across = swap(after(co, ex_across), across[0])
        ex_core, co_core, ex_last = swap(ex, core), swap(co, core), swap(ex_across, core)
        e2, r2, o2, kept_o2 = run_cross_forward(lengths, q2, k2, v2)
        saved2 = (*qkv2, e2, r2, kept_o2)
        co_across = after(co_across, o2)
        w_feed = ((ex, ex_across, ex_core, ex_last), (co, co_across, co_core, swap(co_across, core)))
        out, ds2, kept2, scale2, feed_keep, feed_send, dvec3 = run_feed(halves, reduced, n, row, o2, unit1, w_cross, cot, *w_feed, vec)
        feed_got = swap(feed_send, core)
        ds1, dk2, dv2, cross_keep, cross_send, dvec2 = run_cross_backward(reduced, row, n // 2, ds2, kept2, scale2, low1, mem, w_cross, vec, saved2)
        feed_got = after(feed_got, ds1)
        feed_out, feed = feed_keep[8:] + feed_got[8:], feed_keep[:8] + feed_got[:8]
        feed_got, cross_got = swap(feed_out, across[1]), swap(cross_send, core)
        part, dq, dk, dv, *others, dvec1 = run_self_backward(after(ds1, feed_out), kept1, scale1, x, w_cross, vec, saved1)
        feed_got, cross_got = after((feed_got, cross_got), dq)
        feed_out, feed = feed[4:] + feed_got[4:], feed[:4] + feed_got[:4]
        cross_out, cross = cross_keep[8:] + cross_got[8:], cross_keep[:8] + cross_got[:8]
        feed_got, cross_got = swap(feed_out, across[0]), swap(cross_out, across[1])
        keep, send = run_self_weights(reduced, row, n // 2, after((dq, dk, dv, *others), cross_out, feed_out), (dvec1, dvec2, dvec3))
        got = swap(send, core)
        dx, dmem = run_input_gradients(after(part, send), dq, dk, dv, w_self, dk2, dv2, w_cross)
        got = after(got, dx)
        out_part, total = keep[8:] + got[8:], keep[:8] + got[:8]
        feed_got, cross_got = after((feed_got, cross_got), got)
        feed = feed + feed_got
        feed_out, feed = feed[2:], feed[:2]
        got, feed_got = lax.optimization_barrier((swap(out_part, across[1]), swap(after(feed_out, out_part), line[1])))
        out_part = jnp.concatenate([total[4:] + got[4:], cross[4:] + cross_got[4:]], axis=1)
        total = jnp.concatenate([total[:4] + got[:4], cross[:4] + cross_got[:4]], axis=1)
        feed_out, feed = feed[1:] + feed_got[1:], feed[:1] + feed_got[:1]
        got, feed_got = lax.optimization_barrier((swap(out_part, across[0]), swap(after(feed_out, out_part), line[0])))
        out_part, total = total[2:] + got[2:], total[:2] + got[:2]
        feed = feed + feed_got
        got, feed_got = lax.optimization_barrier((swap(out_part, line[1]), swap(after(feed, out_part), across[0])))
        out_part, total = total[1:] + got[1:], total[:1] + got[:1]
        feed = doubled(feed, feed_got)
        got, feed_got = lax.optimization_barrier((swap(out_part, line[0]), swap(after(feed, out_part), across[1])))
        total = total + got
        feed_next = run_adam_feed(order, row, after(feed, total), feed_got, (expand_weights, expand_first, expand_second), (contract_weights, contract_first, contract_second))
        got = lax.optimization_barrier(tuple(swap(total, route.among_dp(mask)) for mask in range(1, m)))
        got = after(got, feed_next[0])
        *stacked_next, vw, vm, vs = run_adam_stacked(holder, row, (total, *got), (stacked_weights, stacked_first, stacked_second), (scale_vectors, vector_first, vector_second))
        vector_next = (vw, vm, vs)
    else:
        row = jnp.array([0, 1, 0] + [0, 1, 2, 3] * 2, jnp.int32)
        expand_blocks = jnp.swapaxes(expand_weights.reshape(width, 4, WIDTH), 0, 1)
        vec_shard = lax.dynamic_update_slice(jnp.zeros((16, WIDTH), BF), scale_vectors.astype(BF), (0, here * width))
        all_low = lax.all_gather(stacked_weights.astype(BF), "fsdp", axis=1, tiled=True)
        vec_full = jnp.sum(lax.all_gather(vec_shard, "fsdp", axis=0).astype(F32), axis=0).astype(BF)
        vec_full = jnp.pad(vec_full, ((0, WIDTH - 16), (0, 0)))
        ex = lax.all_gather(expand_blocks.astype(BF), "fsdp", axis=1, tiled=True).reshape(4, 2, -1, WIDTH)
        co = lax.all_gather(contract_weights.astype(BF), "fsdp", axis=0, tiled=True).reshape(2, 4, -1, WIDTH)
        w_self = tuple(all_low[None, :3].reshape(1, 3, 2, -1, WIDTH)[:, :, core] for core in range(2))
        w_cross = jnp.concatenate([all_low[4:], all_low[3:4], vec_full[None]], axis=0).reshape(1, 6, 2, -1, WIDTH)
        w_feed = tuple(ex[None, :, core] for core in range(2)), tuple(co[None, core] for core in range(2))
        w_self, *saved1 = run_self_forward(0, row, lengths, x, w_self)
        w_cross, vec, q2, k2, v2, *qkv2, unit1, kept1, scale1, low1 = run_cross_inputs(0, 1, row, saved1[-1], x, mem, (w_cross[:, :, 0], w_cross[:, :, 1]))
        e2, r2, o2, kept_o2 = run_cross_forward(lengths, q2, k2, v2)
        saved2 = (*qkv2, e2, r2, kept_o2)
        out, ds2, kept2, scale2, feed_keep, feed_send, dvec3 = run_feed(0, 2, 2, row, o2, unit1, w_cross, cot, *w_feed, vec)
        dw_feed = jnp.stack([feed_keep, feed_send]).reshape(2, 8, WIDTH // 2, WIDTH)
        dex = jnp.swapaxes(dw_feed[:, :4], 0, 1).reshape(4, n, width, WIDTH)
        dco = dw_feed[:, 4:].reshape(n, 4, width, WIDTH)
        dw_feed = jnp.concatenate([jnp.swapaxes(dex, 0, 1), dco], axis=1)
        grad_feed = lax.psum(lax.psum_scatter(dw_feed, "fsdp", scatter_dimension=0, tiled=False), "dp")
        ds1, dk2, dv2, cross_keep, cross_send, dvec2 = run_cross_backward(2, row, 1, ds2, kept2, scale2, low1, mem, w_cross, vec, saved2)
        part, dq, dk, dv, *others, dvec1 = run_self_backward(ds1, kept1, scale1, x, w_cross, vec, saved1)
        keep, send = run_self_weights(2, row, 1, (dq, dk, dv, *others), (dvec1, dvec2, dvec3))
        dx, dmem = run_input_gradients(part, dq, dk, dv, w_self, dk2, dv2, w_cross)
        both, cross_both = jnp.stack([keep, send], axis=1), jnp.stack([cross_keep, cross_send], axis=1)
        rows = WIDTH // 2
        grad_vector = lax.psum(both[0, :, rows : rows + 9, :rows].astype(F32), BOTH)
        grad_vector = jnp.swapaxes(grad_vector, 0, 1).reshape(9, WIDTH)
        grad_vector = lax.dynamic_slice(grad_vector, (0, here * width), (9, width))
        both = jnp.concatenate([both[:, :, :rows], cross_both], axis=0).reshape(8, WIDTH, WIDTH)
        both = lax.psum(lax.psum_scatter(both, "fsdp", scatter_dimension=1, tiled=True), "dp")
        stacked_next = adam_update(stacked_weights, stacked_first, stacked_second, both.astype(F32))
        vector_next = adam_update(scale_vectors, vector_first, vector_second, grad_vector)
        feed_next = run_adam_feed(0, jnp.arange(4, dtype=jnp.int32), *grad_feed.reshape(2, 2, 2 * width, WIDTH), (expand_weights, expand_first, expand_second), (contract_weights, contract_first, contract_second))
    expand_next, contract_next = feed_next[:3], feed_next[3:]
    return (
        out.reshape(inputs.shape),
        dx.reshape(inputs.shape),
        dmem.reshape(inputs.shape),
        stacked_next[0],
        expand_next[0],
        contract_next[0],
        vector_next[0],
        stacked_next[1],
        stacked_next[2],
        expand_next[1],
        expand_next[2],
        contract_next[1],
        contract_next[2],
        vector_next[1],
        vector_next[2],
    )


def solution(mesh):
    tokens = P(None, ("dp", "fsdp"), None)
    pieces = P(None, ("dp", "fsdp"), None, None)
    stacked = P(None, "fsdp", None)
    rows = P("fsdp", None)
    columns = P(None, "fsdp")
    return jax.shard_map(
        per_device,
        mesh=mesh,
        in_specs=(tokens, tokens, tokens, pieces, stacked, rows, rows, columns) + (stacked, stacked, rows, rows, rows, rows, columns, columns),
        out_specs=(tokens, tokens, tokens, stacked, rows, rows, columns) + (stacked, stacked, rows, rows, rows, rows, columns, columns),
        check_vma=False,
    )
```

```python
import functools
import math

import jax
import jax.numpy as jnp
import numpy as np
from jax import lax
from jax.experimental import pallas as pl
from jax.experimental.pallas import tpu as pltpu
from jax.sharding import PartitionSpec as P

HEADS = 8
HEAD = 64
SLAB = 512
WIDTH = 512
PAIR = 2 * HEAD
STEP = 3
NORM_EPS = 1e-05
ADAM_EPS = 1e-08
LEARN_RATE = 0.2
FAR = -1e30
LOG2E = math.log2(math.e)
QSCALE = HEAD**-0.5 * LOG2E
TILE = 256
BF = jnp.bfloat16
F32 = jnp.float32
MIB = 1 << 20
FEED_MIB = 30
CROSS_MIB = 24
SELF_MIB = 40


def nn(a, b):
    return jnp.dot(a, b, preferred_element_type=F32)


def nt(a, b):
    return lax.dot_general(a, b, (((1,), (1,)), ((), ())), preferred_element_type=F32)


def tn(a, b):
    return lax.dot_general(a, b, (((0,), (0,)), ((), ())), preferred_element_type=F32)


def norm_forward(residual, eps=NORM_EPS):
    centred = residual - jnp.mean(residual, axis=-1, keepdims=True)
    spread = jnp.mean(centred * centred, axis=-1, keepdims=True)
    scale = lax.rsqrt(spread + eps)
    return centred * scale, scale


def norm_backward(upstream, unit, scale, gain):
    inner = upstream * gain
    first = jnp.mean(inner, axis=-1, keepdims=True)
    second = jnp.mean(inner * unit, axis=-1, keepdims=True)
    return scale * (inner - first - unit * second)


def rows_sum(values):
    return jnp.sum(values, axis=0, keepdims=True)


def first_lanes(rows):
    return lax.broadcasted_iota(jnp.int32, (rows, PAIR), 1) < HEAD


def attend_forward(q_ref, k_ref, v_ref, queries_in, keys_out, e_ref, o_ref, r_ref, causal, after=None):
    low = first_lanes(SLAB)
    ones = jnp.ones((SLAB, PAIR), BF)
    spans = ((0, TILE, TILE), (TILE, SLAB, SLAB)) if causal else ((0, SLAB, SLAB),)
    if causal:
        query_at = lax.broadcasted_iota(jnp.int32, (TILE, TILE), 0)
        key_at = lax.broadcasted_iota(jnp.int32, (TILE, TILE), 1)
        bias = jnp.where(key_at <= query_at, 0.0, FAR).astype(F32)
        blank = jnp.zeros((TILE, TILE), BF)

    def lanes(head):
        return slice(head // 2 * PAIR, (head // 2 + 1) * PAIR)

    def scores(head):
        left, right = q_ref[:, lanes(head)], k_ref[:, lanes(head)]
        if head % 2 == 0:
            left, right = jnp.where(low, left, queries_in), jnp.where(low, right, keys_out)
        else:
            left, right = jnp.where(low, queries_in, left), jnp.where(low, keys_out, right)
        return [nt(left[first:last], right[:depth]) for first, last, depth in spans]

    def powers(head, found):
        results = []
        for (first, last, depth), part in zip(spans, found):
            if causal:
                end = part[:, depth - TILE :] + bias
                part = end if depth == TILE else jnp.concatenate([part[:, : depth - TILE], end], axis=1)
            power = jnp.exp2(part - jnp.max(part, axis=1, keepdims=True)).astype(BF)
            e_ref[head, first:last, :depth] = power
            if depth < SLAB:
                e_ref[head, first:last, depth:] = blank
            results.append(power)
        if after is not None:
            after(head)
        return results

    def mixes(head, found):
        right = jnp.concatenate([v_ref[:, lanes(head)], ones], axis=1)
        results = []
        for (_, _, depth), power in zip(spans, found):
            mixed = nn(power, right[:depth])
            inverse = 1.0 / mixed[:, PAIR:]
            results.append((mixed[:, :PAIR] * inverse, inverse))
        return results

    def put(pair, even, odd):
        for (first, last, _), (mix_0, inverse_0), (mix_1, inverse_1) in zip(spans, even, odd):
            here = first_lanes(last - first)
            o_ref[first:last, pair * PAIR : (pair + 1) * PAIR] = jnp.where(here, mix_0, mix_1).astype(BF)
            r_ref[first:last, pair * PAIR : (pair + 1) * PAIR] = jnp.where(here, inverse_0, inverse_1).astype(BF)

    following = scores(0)
    earlier = None
    mixed = {}
    for head in range(HEADS):
        found = following
        if head + 1 < HEADS:
            following = scores(head + 1)
        now = powers(head, found)
        if earlier is not None:
            mixed[head - 1] = mixes(head - 1, earlier)
            if head % 2 == 0:
                put(head // 2 - 1, mixed[head - 2], mixed[head - 1])
        earlier = now
    mixed[HEADS - 1] = mixes(HEADS - 1, earlier)
    put(HEADS // 2 - 1, mixed[HEADS - 2], mixed[HEADS - 1])


def attend_backward(e_ref, r_ref, o_ref, q_ref, k_ref, v_ref, dm_ref, dq_ref, dkt_ref, dvt_ref):
    low = first_lanes(SLAB)
    lane = lax.broadcasted_iota(jnp.int32, (SLAB, PAIR), 1) % HEAD
    units = jnp.where(lane < 2, 1.0, 0.0).astype(BF)
    none = jnp.zeros((), BF)
    qt = q_ref[...].T
    for pair in range(HEADS // 2):
        lanes = slice(pair * PAIR, (pair + 1) * PAIR)
        mixed = (dm_ref[:, lanes] * r_ref[:, lanes].astype(F32)).astype(BF)
        weighed = mixed.astype(F32) * o_ref[:, lanes].astype(F32)
        keys, values = k_ref[:, lanes], v_ref[:, lanes]
        mixed_t = mixed.T
        dq = []
        for side in range(2):
            head = 2 * pair + side
            rows = slice(head * HEAD, (head + 1) * HEAD)
            mine = low if side == 0 else ~low
            centre = jnp.sum(jnp.where(mine, weighed, 0.0), axis=1, keepdims=True)
            high = centre.astype(BF)
            rest = (centre - high.astype(F32)).astype(BF)
            column = jnp.where(lane == 0, -high, jnp.where(lane == 1, -rest, none))
            grad = nt(jnp.where(mine, mixed, column), jnp.where(mine, values, units))
            power = e_ref[head]
            score = (power.astype(F32) * grad).astype(BF)
            dq.append(nn(score, keys))
            dkt_ref[rows, :] = (nn(qt[rows], score) * (1.0 / LOG2E)).astype(BF)
            dvt_ref[rows, :] = nn(mixed_t[side * HEAD : (side + 1) * HEAD], power).astype(BF)
        dq_ref[:, lanes] = (jnp.where(low, dq[0], dq[1]) * HEAD**-0.5).astype(BF)


def piece_columns(lengths_ref, slab, side):
    column = lax.broadcasted_iota(jnp.int32, (1, PAIR), 1) % HEAD
    opening = jnp.zeros((1, PAIR), jnp.int32)
    closing = jnp.zeros((1, PAIR), jnp.int32)
    total = jnp.int32(0)
    for piece in range(lengths_ref.shape[2]):
        following = total + lengths_ref[slab, side, piece]
        opening = jnp.where(column == piece, total, opening)
        closing = jnp.where(column == piece, following, closing)
        total = following
    place = lax.broadcasted_iota(jnp.int32, (SLAB, PAIR), 0)
    return jnp.where((opening <= place) & (place < closing), 1.0, 0.0).astype(BF)


def outside(columns):
    return jnp.where(columns > 0, 0.0, FAR).astype(BF)


def load_pieces(place_ref, first, pieces, w_s, sems):
    copies = []
    for blocks in pieces:
        rows = blocks.shape[2]
        for index in range(blocks.shape[0]):
            start = pl.multiple_of(place_ref[first + len(copies)] * rows, rows)
            copies.append(pltpu.make_async_copy(blocks.at[index], w_s.at[:, pl.ds(start, rows), :], sems.at[len(copies)]))
    for copy in copies:
        copy.start()
    for copy in copies:
        copy.wait()


def load_once(place_ref, first, pieces, w_s, sems):
    @pl.when(pl.program_id(0) == 0)
    def _():
        load_pieces(place_ref, first, pieces, w_s, sems)


def here(*refs):
    step = pl.program_id(0)
    return [ref.at[step if ref.shape[0] > 1 else 0] for ref in refs]


def self_forward(count, first, place_ref, lengths_ref, x_ref, *refs):
    pieces, (out_ref, q_ref, k_ref, v_ref, e_ref, r_ref, o_ref, w_ref, e_s, sems, e_sems, out_sem) = refs[:count], refs[count:]
    load_once(place_ref, first, pieces, w_ref, sems)
    pass_on = pltpu.make_async_copy(w_ref, out_ref, out_sem)
    x_ref, q_ref, k_ref, v_ref, r_ref, o_ref = here(x_ref, q_ref, k_ref, v_ref, r_ref, o_ref)
    step = pl.program_id(0)

    @pl.when(step == 0)
    def _():
        pass_on.start()

    def store(slab, head):
        return pltpu.make_async_copy(e_s.at[slab, head], e_ref.at[slab, head], e_sems.at[slab, head])

    x = x_ref[...]
    q_ref[...] = (nn(x, w_ref[0]) * QSCALE).astype(BF)
    k_ref[...] = nn(x, w_ref[1]).astype(BF)
    v_ref[...] = nn(x, w_ref[2]).astype(BF)
    columns = piece_columns(lengths_ref, pl.program_id(0), 0)
    attend_forward(q_ref, k_ref, v_ref, columns, outside(columns), e_s.at[step], o_ref, r_ref, True, lambda head: store(step, head).start())

    @pl.when(step == pl.num_programs(0) - 1)
    def _():
        pass_on.wait()
        for slab in range(e_s.shape[0]):
            for head in range(HEADS):
                store(slab, head).wait()


def cross_inputs(count, first, owners, place_ref, o1_ref, x_ref, mem_ref, *refs):
    pieces, refs = refs[:count], refs[count:]
    out_ref, vec_ref, q_ref, k_ref, v_ref, q_kept, k_kept, v_kept, unit1_ref, kept1_ref, scale1_ref, low1_ref, w_ref, sems, out_sem = refs
    load_once(place_ref, first, pieces, w_ref, sems)
    pass_on = pltpu.make_async_copy(w_ref, out_ref, out_sem)

    @pl.when(pl.program_id(0) == 0)
    def _():
        pass_on.start()
        rows = WIDTH // owners
        total = w_ref[5, 0:16, :].astype(F32)
        for owner in range(1, owners):
            total = total + w_ref[5, owner * rows : owner * rows + 16, :].astype(F32)
        vec_ref[...] = total

    o1_ref, x_ref, mem_ref, q_ref, k_ref, v_ref = here(o1_ref, x_ref, mem_ref, q_ref, k_ref, v_ref)
    q_kept, k_kept, v_kept = here(q_kept, k_kept, v_kept)
    unit1_ref, kept1_ref, scale1_ref, low1_ref = here(unit1_ref, kept1_ref, scale1_ref, low1_ref)
    residual = vec_ref[6:7, :] * x_ref[...].astype(F32) + nn(o1_ref[...], w_ref[4])
    unit, scale = norm_forward(residual)
    unit1_ref[...] = unit
    kept1_ref[...] = unit
    scale1_ref[...] = scale
    low = (unit * vec_ref[0:1, :] + vec_ref[3:4, :]).astype(BF)
    low1_ref[...] = low
    memory = mem_ref[...]
    for once, kept, value in ((k_ref, k_kept, nn(memory, w_ref[1])), (v_ref, v_kept, nn(memory, w_ref[2])), (q_ref, q_kept, nn(low, w_ref[0]) * QSCALE)):
        value = value.astype(BF)
        once[...] = value
        kept[...] = value

    @pl.when(pl.program_id(0) == pl.num_programs(0) - 1)
    def _():
        pass_on.wait()


def cross_forward(lengths_ref, q_ref, k_ref, v_ref, e_ref, r_ref, o_ref, kept_ref):
    slab = pl.program_id(0)
    q_ref, k_ref, v_ref, e_ref, r_ref, o_ref, kept_ref = here(q_ref, k_ref, v_ref, e_ref, r_ref, o_ref, kept_ref)
    queries_in, keys_out = piece_columns(lengths_ref, slab, 0), outside(piece_columns(lengths_ref, slab, 1))
    attend_forward(q_ref, k_ref, v_ref, queries_in, keys_out, e_ref, o_ref, r_ref, False)
    kept_ref[...] = o_ref[...]


CUBE = 0.044715
ROOT = math.sqrt(2.0 / math.pi)


def feed_copies(place_ref, begin, first, second, ex_s, co_s, sems):
    each = co_s.shape[1]
    results = [], []
    for side, pieces in enumerate((first, second)):
        for blocks in pieces:
            rows = blocks.shape[2]
            for index in range(blocks.shape[0]):
                number = len(results[side])
                start = place_ref[begin + number] * rows
                owner = start // each
                if side == 0:
                    goal = ex_s.at[:, pl.ds(pl.multiple_of(start, rows), rows), :]
                else:
                    goal = co_s.at[pl.ds(owner * 4, 4), pl.ds(pl.multiple_of(start - owner * each, rows), rows), :]
                results[side].append(pltpu.make_async_copy(blocks.at[index], goal, sems.at[side, number]))
    return results


def feed_both(count, begin, reduce_at, place_ref, o2_ref, unit1_ref, w_ref, cot_ref, vec_ref, *refs):
    pieces, refs = refs[: 2 * count], refs[2 * count :]
    (out_ref, ds_ref, unit_s, scale_ref, keep_ref, send_ref, dvec_ref,
     act_s, slope_s, branch_s, low_s, dbranch_s, cot_s, out_s, dex_s, dco_s, ex_s, co_s, sems, own_sems) = refs
    slabs = unit_s.shape[0]
    chunks = ex_s.shape[0]
    owners = co_s.shape[0] // 4
    first, second = feed_copies(place_ref, begin, pieces[:count], pieces[count:], ex_s, co_s, sems)
    cot_copy = pltpu.make_async_copy(cot_ref, cot_s, own_sems.at[0])
    out_copy = pltpu.make_async_copy(out_s, out_ref, own_sems.at[1])
    for copy in first + second + [cot_copy]:
        copy.start()

    def rows(slab):
        return slice(slab * SLAB, (slab + 1) * SLAB)

    def contract(part):
        return co_s[part * owners : (part + 1) * owners].reshape(WIDTH, WIDTH)

    def state(slab):
        return unit_s[slab] * vec_ref[1:2, :] + vec_ref[4:5, :]

    for slab in range(slabs):
        before = unit1_ref[slab] * vec_ref[0:1, :] + vec_ref[3:4, :]
        unit_s[slab], scale_ref[slab] = norm_forward(vec_ref[7:8, :] * before + nn(o2_ref[slab], w_ref[0]))
        low_s[rows(slab), :] = state(slab).astype(BF)
    for copy in first:
        copy.wait()
    following = nn(low_s[...], ex_s[0])
    for part in range(chunks):
        u = following
        if part + 1 < chunks:
            following = nn(low_s[...], ex_s[part + 1])
        square = u * u
        bend = jnp.tanh(u * (ROOT + (ROOT * CUBE) * square))
        half = 0.5 + 0.5 * bend
        act_s[part] = (u * half).astype(BF)
        slope_s[part] = half + (u * half) * (1.0 - bend) * (ROOT + (3.0 * ROOT * CUBE) * square)
        if part == 0:
            for copy in second:
                copy.wait()
            branch_s[...] = nn(act_s[part], contract(part))
        else:
            branch_s[...] += nn(act_s[part], contract(part))
    cot_copy.wait()
    for slab in range(slabs):
        now = state(slab)
        unit, scale = norm_forward(vec_ref[8:9, :] * now + branch_s[rows(slab), :])
        out_s[slab] = (unit * vec_ref[2:3, :] + vec_ref[5:6, :]).astype(BF)
        up = cot_s[slab].astype(F32)
        dres = norm_backward(up, unit, scale, vec_ref[2:3, :])
        sums = (rows_sum(up * unit), rows_sum(up), rows_sum(dres * now))
        for row, value in enumerate(sums):
            if slab == 0:
                dvec_ref[row : row + 1, :] = value
            else:
                dvec_ref[row : row + 1, :] += value
        branch_s[rows(slab), :] = dres * vec_ref[8:9, :]
        dbranch_s[rows(slab), :] = dres.astype(BF)
    out_copy.start()
    low_t = low_s[...].T
    for part in range(chunks):
        dco_s[part] = tn(act_s[part], dbranch_s[...]).astype(BF)
        dhid = (nt(dbranch_s[...], contract(part)) * slope_s[part]).astype(BF)
        dex_s[part] = nn(low_t, dhid).astype(BF)
        branch_s[...] += nt(dhid, ex_s[part])
    for slab in range(slabs):
        ds_ref[slab] = branch_s[rows(slab), :]
    put_feed(place_ref, reduce_at, dex_s, dco_s, keep_ref, send_ref)
    out_copy.wait()


def put_gradients(place_ref, begin, dw_s, keep_ref, send_ref, first):
    blocks = keep_ref.shape[0]
    owners = blocks // dw_s.shape[0]
    rows = WIDTH // (2 * owners)
    core = place_ref[begin]
    for matrix in range(dw_s.shape[0]):
        for owner in range(owners):
            at = begin + 1 + matrix * owners + owner
            start = pl.multiple_of((2 * owner + core) * rows, rows)
            keep_ref[place_ref[at], first : first + rows, :] = dw_s[matrix, pl.ds(start, rows), :]
            start = pl.multiple_of((2 * owner + 1 - core) * rows, rows)
            send_ref[place_ref[at + blocks], first : first + rows, :] = dw_s[matrix, pl.ds(start, rows), :]


def put_vectors(place_ref, begin, dvec_s, count, keep_ref, send_ref, first):
    blocks = keep_ref.shape[0]
    owners = blocks // count
    columns = WIDTH // (2 * owners)
    core = place_ref[begin]
    rows = slice(first, first + 16)
    blank = jnp.zeros((16, WIDTH), BF)
    for block in range(blocks):
        keep_ref[block, rows, :] = blank
        send_ref[block, rows, :] = blank
    for owner in range(owners):
        low = dvec_s[:, 2 * owner * columns : (2 * owner + 1) * columns]
        high = dvec_s[:, (2 * owner + 1) * columns : (2 * owner + 2) * columns]
        rest = jnp.zeros((16, WIDTH - columns), F32)
        own = jnp.where(core == 0, low, high)
        other = jnp.where(core == 0, high, low)
        at = begin + 1 + owner
        keep_ref[place_ref[at], rows, :] = jnp.concatenate([own, rest], axis=1).astype(BF)
        send_ref[place_ref[at + blocks], rows, :] = jnp.concatenate([other, rest], axis=1).astype(BF)


def put_feed(place_ref, begin, dex_s, dco_s, keep_ref, send_ref):
    blocks = keep_ref.shape[0]
    owners = blocks // 4
    each = keep_ref.shape[1] // 2
    core = place_ref[begin]
    for pair in range(4):
        for owner in range(owners):
            at = begin + 1 + pair * owners + owner
            for out_ref, on, block in ((keep_ref, core, place_ref[at]), (send_ref, 1 - core, place_ref[at + blocks])):
                shard = 2 * owner + on
                for side in range(2):
                    number = 2 * pair + side
                    rows = slice(side * each, (side + 1) * each)
                    if number < 4:
                        out_ref[block, rows, :] = dex_s[number, pl.ds(pl.multiple_of(shard * each, each), each), :]
                    else:
                        row = (shard * 4 + number - 4) * each
                        chunk = row // WIDTH
                        out_ref[block, rows, :] = dco_s[chunk, pl.ds(pl.multiple_of(row - chunk * WIDTH, each), each), :]


def fetcher(pairs, sems):
    step = pl.program_id(0)

    def copy(number, slab):
        return pltpu.make_async_copy(pairs[number][0].at[slab], pairs[number][1].at[slab], sems.at[number, slab])

    @pl.when(step == 0)
    def _():
        for slab in range(pairs[0][1].shape[0]):
            for number in range(len(pairs)):
                copy(number, slab).start()

    def wait(first, last):
        for number in range(first, last):
            copy(number, step).wait()

    return wait


def all_rows(ref):
    return ref[...].reshape(-1, WIDTH)


def cross_backward(begin, place_ref, ds2_ref, unit2_ref, scale2_ref, w_ref, vec_ref, q_ref, k_ref, v_ref, r_ref, o_ref, low1_ref, mem_ref, e_ref,
                   ds1_ref, dk_ref, dv_ref, keep_ref, send_ref, dvec_ref,
                   q_s, k_s, v_s, r_s, o_s, low1_s, mem_s, w_s, dm_s, dq_s, dk_s, dv_s, dbranch_s, dkt_s, dvt_s, dw_s, sems, out_sems, w_sems):
    step = pl.program_id(0)
    steps = pl.num_programs(0)
    w_copies = [pltpu.make_async_copy(w_ref.at[3], w_s.at[3], w_sems.at[0]), pltpu.make_async_copy(w_ref.at[0:3], w_s.at[0:3], w_sems.at[1])]

    @pl.when(step == 0)
    def _():
        w_copies[0].start()

    wait = fetcher([(q_ref, q_s), (k_ref, k_s), (v_ref, v_s), (r_ref, r_s), (o_ref, o_s), (low1_ref, low1_s), (mem_ref, mem_s)], sems)
    outward = [pltpu.make_async_copy(dk_s, dk_ref, out_sems.at[0]), pltpu.make_async_copy(dv_s, dv_ref, out_sems.at[1])]

    @pl.when(step == 0)
    def _():
        w_copies[1].start()
        dvec_ref[...] = jnp.zeros_like(dvec_ref)

    ds2_ref, unit2_ref, scale2_ref, ds1_ref = here(ds2_ref, unit2_ref, scale2_ref, ds1_ref)
    up = ds2_ref[...]
    unit = unit2_ref[...]
    dvec_ref[0:1, :] += rows_sum(up * unit)
    dvec_ref[1:2, :] += rows_sum(up)
    dres = norm_backward(up, unit, scale2_ref[...], vec_ref[1:2, :])
    dbranch = dres.astype(BF)
    dbranch_s[step] = dbranch

    @pl.when(step == 0)
    def _():
        w_copies[0].wait()

    dm_s[...] = nt(dbranch, w_s[3])
    ds1_ref[...] = dres * vec_ref[7:8, :]
    wait(0, 5)
    attend_backward(e_ref.at[step], r_s.at[step], o_s.at[step], q_s.at[step], k_s.at[step], v_s.at[step], dm_s, dq_s.at[step], dkt_s, dvt_s)
    wait(5, 7)
    dvec_ref[2:3, :] += rows_sum(dbranch_s[step].astype(F32) * low1_s[step].astype(F32))

    @pl.when(step == 0)
    def _():
        w_copies[1].wait()

    ds1_ref[...] += nt(dq_s[step], w_s[0])
    dk_s[step] = dkt_s[...].T
    dv_s[step] = dvt_s[...].T

    @pl.when(step == steps - 1)
    def _():
        for copy in outward:
            copy.start()
        dw_s[0] = tn(all_rows(low1_s), all_rows(dq_s)).astype(BF)
        memory_t = all_rows(mem_s).T
        dw_s[1] = nn(memory_t, all_rows(dk_s)).astype(BF)
        dw_s[2] = nn(memory_t, all_rows(dv_s)).astype(BF)
        dw_s[3] = tn(all_rows(o_s), all_rows(dbranch_s)).astype(BF)
        put_gradients(place_ref, begin, dw_s, keep_ref, send_ref, 0)
        for copy in outward:
            copy.wait()


def self_backward(ds1_ref, unit1_ref, scale1_ref, w3_ref, vec_ref, q_ref, k_ref, v_ref, r_ref, o_ref, x_ref, e_ref,
                  part_ref, dq_ref, dk_ref, dv_ref, dbranch_ref, o_s, x_s, dvec_ref, q_s, k_s, v_s, r_s, e_s, dm_s, dkt_s, dvt_s, sems):
    step = pl.program_id(0)
    wait = fetcher([(e_ref, e_s), (q_ref, q_s), (k_ref, k_s), (v_ref, v_s), (r_ref, r_s), (o_ref, o_s), (x_ref, x_s)], sems)

    @pl.when(step == 0)
    def _():
        dvec_ref[...] = jnp.zeros_like(dvec_ref)

    ds1_ref, unit1_ref, scale1_ref, part_ref, dq_ref, dk_ref, dv_ref, dbranch_ref = here(ds1_ref, unit1_ref, scale1_ref, part_ref, dq_ref, dk_ref, dv_ref, dbranch_ref)
    up = ds1_ref[...]
    unit = unit1_ref[...]
    dvec_ref[0:1, :] += rows_sum(up * unit)
    dvec_ref[1:2, :] += rows_sum(up)
    dres = norm_backward(up, unit, scale1_ref[...], vec_ref[0:1, :])
    dbranch = dres.astype(BF)
    dbranch_ref[...] = dbranch
    dm_s[...] = nt(dbranch, w3_ref[0])
    part_ref[...] = dres * vec_ref[6:7, :]
    wait(0, 6)
    attend_backward(e_s.at[step], r_s.at[step], o_s.at[step], q_s.at[step], k_s.at[step], v_s.at[step], dm_s, dq_ref, dkt_s, dvt_s)
    dk_ref[...] = dkt_s[...].T
    dv_ref[...] = dvt_s[...].T
    wait(6, 7)
    dvec_ref[2:3, :] += rows_sum(dbranch_ref[...].astype(F32) * x_s[step].astype(F32))


def self_weights(begin, place_ref, dq_ref, dk_ref, dv_ref, dbranch_ref, o_ref, x_ref, dvec1_ref, dvec2_ref, dvec3_ref, keep_ref, send_ref, dw_s, dvec_s):
    dvec_s[...] = jnp.zeros_like(dvec_s)
    for row in range(3):
        for number, ref in enumerate((dvec1_ref, dvec2_ref, dvec3_ref)):
            dvec_s[3 * row + number : 3 * row + number + 1, :] = ref[row : row + 1, :]
    x_t = all_rows(x_ref).T
    dw_s[0] = nn(x_t, all_rows(dq_ref)).astype(BF)
    dw_s[1] = nn(x_t, all_rows(dk_ref)).astype(BF)
    dw_s[2] = nn(x_t, all_rows(dv_ref)).astype(BF)
    dw_s[3] = tn(all_rows(o_ref), all_rows(dbranch_ref)).astype(BF)
    put_gradients(place_ref, begin, dw_s, keep_ref, send_ref, 0)
    put_vectors(place_ref, begin, dvec_s, dw_s.shape[0], keep_ref, send_ref, keep_ref.shape[1] - 16)


def input_gradients(part_ref, dq_ref, dk_ref, dv_ref, w_ref, dk2_ref, dv2_ref, w2_ref, dx_ref, dmem_ref):
    part_ref, dq_ref, dk_ref, dv_ref, dk2_ref, dv2_ref, dx_ref, dmem_ref = here(part_ref, dq_ref, dk_ref, dv_ref, dk2_ref, dv2_ref, dx_ref, dmem_ref)
    dx_ref[...] = part_ref[...] + nt(dq_ref[...], w_ref[0]) + nt(dk_ref[...], w_ref[1]) + nt(dv_ref[...], w_ref[2])
    dmem_ref[...] = nt(dk2_ref[...], w2_ref[1]) + nt(dv2_ref[...], w2_ref[2])


def cut_shards(at, place_ref, stacked_ref, expand_ref, contract_ref, vec_ref, a_ref, b_ref, c_ref, a_s, b_s, ex_s, co_s, vec_s, sems):
    rows = stacked_ref.shape[1]
    middle = pl.multiple_of(place_ref[at] * (rows // 2), rows // 2)
    half = pl.ds(middle, rows // 2)
    start = pl.multiple_of(place_ref[at + 1] * (rows // 4), rows // 4)
    quarter = pl.ds(start, rows // 4)
    copies = [
        pltpu.make_async_copy(stacked_ref.at[0:3, half, :], a_s, sems.at[0]),
        pltpu.make_async_copy(stacked_ref.at[3:8, quarter, :], b_s, sems.at[1]),
        pltpu.make_async_copy(vec_ref, vec_s, sems.at[2]),
        pltpu.make_async_copy(expand_ref.at[half, :], ex_s, sems.at[3]),
    ]
    copies += [
        pltpu.make_async_copy(contract_ref.at[pl.ds(pl.multiple_of(part * rows + middle, rows // 2), rows // 2), :], co_s.at[part], sems.at[4 + part])
        for part in range(4)
    ]
    for copy in copies:
        copy.start()
    for copy in copies:
        copy.wait()
    a_ref[0] = a_s[...].astype(BF)
    for index, matrix in enumerate((4, 5, 6, 7, 3)):
        b_ref[0, index] = b_s[matrix - 3].astype(BF)
    vec = jnp.concatenate([vec_s[...]] * (WIDTH // vec_ref.shape[1]), axis=1)
    owner = lax.broadcasted_iota(jnp.int32, vec.shape, 1) // vec_ref.shape[1]
    vec = jnp.where(owner == place_ref[at + 2], vec, 0.0)
    b_ref[0, 5] = jnp.concatenate([vec, jnp.zeros((rows // 4 - vec.shape[0], WIDTH), F32)], axis=0).astype(BF)
    for part in range(4):
        c_ref[0, part] = ex_s[:, part * WIDTH : (part + 1) * WIDTH].astype(BF)
        c_ref[0, 4 + part] = co_s[part].astype(BF)


def per_slab(*tail):
    return pl.BlockSpec((1,) + tail, lambda m: (m,) + (0,) * len(tail))


def fixed(*dims):
    return pl.BlockSpec(dims, lambda m: (0,) * len(dims), pipeline_mode=pl.Buffered(1))


def shape(dims, kind):
    return jax.ShapeDtypeStruct(tuple(dims), kind)


def options(mib):
    return pltpu.CompilerParams(dimension_semantics=("arbitrary",), vmem_limit_bytes=mib * MIB)


def estimate(microseconds):
    return pl.CostEstimate(flops=int(microseconds * 1e9), bytes_accessed=1 << 20, transcendentals=0)


SCALARS = pl.BlockSpec(memory_space=pltpu.SMEM)
ANYWHERE = pl.BlockSpec(memory_space=pl.ANY)
RESIDENT = pl.BlockSpec(memory_space=pltpu.VMEM)
ROWS = per_slab(SLAB, WIDTH)
SCALE = per_slab(SLAB, 1)


def near(*arrays):
    return tuple(pltpu.with_memory_space_constraint(array, pltpu.VMEM) for array in arrays)


def far(*arrays):
    return tuple(pltpu.with_memory_space_constraint(array, pltpu.HBM) for array in arrays)


def near_shape(dims, kind):
    return pltpu.VMEM(tuple(dims), kind)


def far_shape(dims, kind):
    return pltpu.HBM(tuple(dims), kind)


def slabs(g, kind, place=far_shape):
    return place((g, SLAB, WIDTH), kind)


def powers_shape(g, place):
    return place((g, HEADS, SLAB, SLAB), BF)


def run_cut_shards(at, place, stacked, expand, contract, vec):
    rows = stacked.shape[1]
    return pl.pallas_call(
        functools.partial(cut_shards, at),
        in_specs=[SCALARS] + [ANYWHERE] * 4,
        out_specs=[RESIDENT] * 3,
        out_shape=[shape((1, 3, rows // 2, WIDTH), BF), shape((1, 6, rows // 4, WIDTH), BF), shape((1, 8, rows // 2, WIDTH), BF)],
        scratch_shapes=[
            pltpu.VMEM((3, rows // 2, WIDTH), F32),
            pltpu.VMEM((5, rows // 4, WIDTH), F32),
            pltpu.VMEM((rows // 2, expand.shape[1]), F32),
            pltpu.VMEM((4, rows // 2, WIDTH), F32),
            pltpu.VMEM(vec.shape, F32),
            pltpu.SemaphoreType.DMA((8,)),
        ],
        compiler_params=pltpu.CompilerParams(vmem_limit_bytes=16 * MIB),
        name="cut_shards",
    )(place, *far(stacked, expand, contract, vec))


def run_self_forward(first, place, lengths, x, w):
    g = x.shape[0]
    return pl.pallas_call(
        functools.partial(self_forward, len(w), first),
        grid=(g,),
        in_specs=[SCALARS, SCALARS, ROWS] + [ANYWHERE] * len(w),
        out_specs=[ANYWHERE, ROWS, ROWS, ROWS, ANYWHERE, ROWS, RESIDENT],
        out_shape=[far_shape((3, WIDTH, WIDTH), BF)] + [slabs(g, BF)] * 3 + [powers_shape(g, far_shape), slabs(g, BF), slabs(g, BF, near_shape)],
        scratch_shapes=[pltpu.VMEM((3, WIDTH, WIDTH), BF), pltpu.VMEM((g, HEADS, SLAB, SLAB), BF), pltpu.SemaphoreType.DMA((sum(piece.shape[0] for piece in w),)), pltpu.SemaphoreType.DMA((g, HEADS)), pltpu.SemaphoreType.DMA],
        compiler_params=options(32),
        cost_estimate=estimate(12),
        name="self_forward",
    )(place, lengths, x, *w)


def run_cross_inputs(first, owners, place, o1, x, memory, w):
    g = memory.shape[0]
    return pl.pallas_call(
        functools.partial(cross_inputs, len(w), first, owners),
        grid=(g,),
        in_specs=[SCALARS, RESIDENT, ROWS, ROWS] + [ANYWHERE] * len(w),
        out_specs=[ANYWHERE, fixed(16, WIDTH), RESIDENT, RESIDENT, RESIDENT, ROWS, ROWS, ROWS, RESIDENT, ROWS, SCALE, ROWS],
        out_shape=[far_shape((6, WIDTH, WIDTH), BF), far_shape((16, WIDTH), F32)]
        + [slabs(g, BF, near_shape)] * 3
        + [slabs(g, BF)] * 3
        + [slabs(g, F32, near_shape), slabs(g, F32), far_shape((g, SLAB, 1), F32), slabs(g, BF)],
        scratch_shapes=[pltpu.VMEM((6, WIDTH, WIDTH), BF), pltpu.SemaphoreType.DMA((sum(piece.shape[0] for piece in w),)), pltpu.SemaphoreType.DMA],
        compiler_params=options(24),
        cost_estimate=estimate(7),
        name="cross_inputs",
    )(place, *near(o1), x, memory, *w)


def run_cross_forward(lengths, q, k, v):
    g = q.shape[0]
    return pl.pallas_call(
        cross_forward,
        grid=(g,),
        in_specs=[SCALARS] + [RESIDENT] * 3,
        out_specs=[RESIDENT, ROWS, RESIDENT, ROWS],
        out_shape=[powers_shape(g, near_shape), slabs(g, BF), slabs(g, BF, near_shape), slabs(g, BF)],
        compiler_params=options(24),
        cost_estimate=estimate(10),
        name="cross_forward",
    )(lengths, *near(q, k, v))


def run_feed(begin, reduce_at, owners, place, o2, unit1, w_cross, cot, first, second, vec):
    g = unit1.shape[0]
    rows = WIDTH // owners
    pieces = sum(piece.shape[0] for piece in first)
    dims = (2 * owners, 2 * rows, WIDTH)
    tokens = g * SLAB
    last = pl.BlockSpec((1, WIDTH, WIDTH), lambda m: (3, 0, 0))
    return pl.pallas_call(
        functools.partial(feed_both, len(first), begin, reduce_at),
        grid=(1,),
        in_specs=[SCALARS, RESIDENT, RESIDENT, last, ANYWHERE, fixed(16, WIDTH)] + [ANYWHERE] * (2 * len(first)),
        out_specs=[ANYWHERE, RESIDENT, RESIDENT, fixed(g, SLAB, 1), RESIDENT, RESIDENT, fixed(8, WIDTH)],
        out_shape=[slabs(g, BF), slabs(g, F32, near_shape), slabs(g, F32, near_shape), far_shape((g, SLAB, 1), F32)] + [near_shape(dims, BF)] * 2 + [far_shape((8, WIDTH), F32)],
        scratch_shapes=[
            pltpu.VMEM((4, tokens, WIDTH), BF),
            pltpu.VMEM((4, tokens, WIDTH), F32),
            pltpu.VMEM((tokens, WIDTH), F32),
            pltpu.VMEM((tokens, WIDTH), BF),
            pltpu.VMEM((tokens, WIDTH), BF),
            pltpu.VMEM((g, SLAB, WIDTH), BF),
            pltpu.VMEM((g, SLAB, WIDTH), BF),
            pltpu.VMEM((4, WIDTH, WIDTH), BF),
            pltpu.VMEM((4, WIDTH, WIDTH), BF),
            pltpu.VMEM((4, WIDTH, WIDTH), BF),
            pltpu.VMEM((4 * owners, rows, WIDTH), BF),
            pltpu.SemaphoreType.DMA((2, pieces)),
            pltpu.SemaphoreType.DMA((2,)),
        ],
        compiler_params=options(FEED_MIB),
        cost_estimate=estimate(24),
        name="feed_both",
    )(place, *near(o2, unit1), *far(w_cross), cot, *far(vec), *first, *second)


def slab_scratch(g, kinds):
    return [pltpu.VMEM((g, SLAB, WIDTH), kind) for kind in kinds]


def run_cross_backward(begin, place, owners, ds2, unit2, scale2, low1, memory, w, vec, saved):
    g = memory.shape[0]
    dims = (4 * owners, WIDTH // (2 * owners), WIDTH)
    q, k, v, e, r, o = saved
    return pl.pallas_call(
        functools.partial(cross_backward, begin),
        grid=(g,),
        in_specs=[SCALARS, RESIDENT, RESIDENT, SCALE, ANYWHERE, fixed(16, WIDTH)] + [ANYWHERE] * 7 + [RESIDENT],
        out_specs=[RESIDENT, ANYWHERE, ANYWHERE, RESIDENT, RESIDENT, fixed(8, WIDTH)],
        out_shape=[slabs(g, F32, near_shape), slabs(g, BF), slabs(g, BF), near_shape(dims, BF), near_shape(dims, BF), far_shape((8, WIDTH), F32)],
        scratch_shapes=slab_scratch(g, [BF] * 7)
        + [pltpu.VMEM((4, WIDTH, WIDTH), BF), pltpu.VMEM((SLAB, WIDTH), F32)]
        + slab_scratch(g, [BF] * 4)
        + [pltpu.VMEM((WIDTH, SLAB), BF)] * 2
        + [pltpu.VMEM((4, WIDTH, WIDTH), BF), pltpu.SemaphoreType.DMA((7, g)), pltpu.SemaphoreType.DMA((2,)), pltpu.SemaphoreType.DMA((2,))],
        compiler_params=options(CROSS_MIB),
        cost_estimate=estimate(19),
        name="cross_backward",
    )(place, *near(ds2, unit2), *far(scale2, w, vec, q, k, v, r, o, low1), memory, *near(e))


def run_self_backward(ds1, unit1, scale1, x, w_cross, vec, saved):
    g = x.shape[0]
    q, k, v, e, r, o = saved
    third = pl.BlockSpec((1, WIDTH, WIDTH), lambda m: (4, 0, 0))
    return pl.pallas_call(
        self_backward,
        grid=(g,),
        in_specs=[RESIDENT, ROWS, SCALE, third, fixed(16, WIDTH)] + [ANYWHERE] * 7,
        out_specs=[ROWS] + [RESIDENT] * 6 + [fixed(8, WIDTH)],
        out_shape=[slabs(g, F32)] + [slabs(g, BF, near_shape)] * 6 + [far_shape((8, WIDTH), F32)],
        scratch_shapes=slab_scratch(g, [BF] * 4)
        + [pltpu.VMEM((g, HEADS, SLAB, SLAB), BF), pltpu.VMEM((SLAB, WIDTH), F32)]
        + [pltpu.VMEM((WIDTH, SLAB), BF)] * 2
        + [pltpu.SemaphoreType.DMA((7, g))],
        compiler_params=options(SELF_MIB),
        cost_estimate=estimate(17),
        name="self_backward",
    )(*near(ds1), *far(unit1, scale1, w_cross, vec, q, k, v, r, o), x, *far(e))


def run_self_weights(begin, place, owners, grads, dvecs):
    dims = (4 * owners, WIDTH // (2 * owners) + 16, WIDTH)
    return pl.pallas_call(
        functools.partial(self_weights, begin),
        grid=(1,),
        in_specs=[SCALARS] + [RESIDENT] * 6 + [fixed(8, WIDTH)] * 3,
        out_specs=[RESIDENT] * 2,
        out_shape=[near_shape(dims, BF)] * 2,
        scratch_shapes=[pltpu.VMEM((4, WIDTH, WIDTH), BF), pltpu.VMEM((16, WIDTH), F32)],
        compiler_params=options(20),
        cost_estimate=estimate(4),
        name="self_weights",
    )(place, *near(*grads), *far(*dvecs))


def run_input_gradients(part, dq, dk, dv, w, dk2, dv2, w2):
    g = part.shape[0]
    return pl.pallas_call(
        input_gradients,
        grid=(g,),
        in_specs=[ROWS] + [RESIDENT] * 3 + [fixed(3, WIDTH, WIDTH), ROWS, ROWS, fixed(3, WIDTH, WIDTH)],
        out_specs=[ROWS, ROWS],
        out_shape=[slabs(g, F32), slabs(g, F32)],
        compiler_params=options(28),
        cost_estimate=estimate(6),
        name="input_gradients",
    )(*far(part), *near(dq, dk, dv), *far(w, dk2, dv2, w2))
def adam_update(weight, first_moment, second_moment, gradient):
    correction = 1.0 - 0.5**STEP
    first_next = 0.5 * first_moment + 0.5 * gradient
    second_next = 0.5 * second_moment + 0.5 * gradient * gradient
    weight_next = weight - LEARN_RATE * (first_next / correction) / (jnp.sqrt(second_next / correction) + ADAM_EPS)
    return (weight_next, first_next, second_next)


def picked(order, parts):
    value = parts[0]
    for number in range(1, len(parts)):
        value = jnp.where(order == number, parts[number], value)
    return value.astype(F32)


def adam_stacked(at, place_ref, part_0, part_1, part_2, part_3, w_ref, m_ref, s_ref, vw_ref, vm_ref, vs_ref, w_out, m_out, s_out, vw_out, vm_out, vs_out):
    rows = w_ref.shape[1]
    group = pl.program_id(0)
    parts = (part_0, part_1, part_2, part_3)

    def update(first):
        for matrix in range(4):
            grad = picked(place_ref[at + matrix], [part[0, first : first + rows, :] for part in parts])
            w_out[matrix], m_out[matrix], s_out[matrix] = adam_update(w_ref[matrix], m_ref[matrix], s_ref[matrix], grad)

    @pl.when(group == 0)
    def _():
        update(0)
        grad = picked(place_ref[at], [part[0, rows : rows + 16, :] for part in parts])
        vw_out[...], vm_out[...], vs_out[...] = adam_update(vw_ref[...], vm_ref[...], vs_ref[...], grad[: vw_ref.shape[0], : vw_ref.shape[1]])

    @pl.when(group == 1)
    def _():
        update(rows + 16)


def run_adam_stacked(at, place, parts, stacked, vectors):
    rows = stacked[0].shape[1]
    block = pl.BlockSpec((4, rows, WIDTH), lambda group: (group, 0, 0))
    vector = fixed(*vectors[0].shape)
    return pl.pallas_call(
        functools.partial(adam_stacked, at),
        grid=(2,),
        in_specs=[SCALARS] + [fixed(*part.shape) for part in parts] + [block] * 3 + [vector] * 3,
        out_specs=[block] * 3 + [vector] * 3,
        out_shape=[shape(a.shape, F32) for a in tuple(stacked) + tuple(vectors)],
        compiler_params=options(24),
        cost_estimate=estimate(4),
        name="adam_stacked",
    )(place, *parts, *stacked, *vectors)


def adam_feed(at, place_ref, part_0, part_1, part_2, part_3, *refs):
    rows = part_0.shape[1] // 2
    parts = (part_0, part_1, part_2, part_3)

    def grad(number):
        span = slice(number % 2 * rows, (number % 2 + 1) * rows)
        return picked(place_ref[at + number // 2], [part[0, span, :] for part in parts])

    for part in range(4):
        where = (slice(None), slice(part * WIDTH, (part + 1) * WIDTH))
        refs[6][where], refs[7][where], refs[8][where] = adam_update(*(ref[where] for ref in refs[0:3]), grad(part))
        where = (slice(part * rows, (part + 1) * rows), slice(None))
        refs[9][where], refs[10][where], refs[11][where] = adam_update(*(ref[where] for ref in refs[3:6]), grad(4 + part))


def run_adam_feed(at, place, parts, expand, contract):
    arrays = tuple(expand) + tuple(contract)
    whole = pl.BlockSpec(memory_space=pltpu.VMEM)
    return pl.pallas_call(
        functools.partial(adam_feed, at),
        in_specs=[SCALARS] + [whole] * 10,
        out_specs=[whole] * 6,
        out_shape=[shape(a.shape, F32) for a in arrays],
        compiler_params=pltpu.CompilerParams(vmem_limit_bytes=24 * MIB),
        cost_estimate=estimate(4),
        name="adam_feed",
    )(place, *parts, *arrays)


class Route:
    def __init__(self, m, n):
        self.m, self.n = m, n
        self.dp_bits = m.bit_length() - 1
        self.line_bits = n.bit_length() - 2
        self.line = n // 2

    def pairs(self, partner):
        return [(d * self.n + f, partner(d, f)) for d in range(self.m) for f in range(self.n)]

    def across_core(self):
        return self.pairs(lambda d, f: d * self.n + (f ^ 1))

    def along_line(self, mask):
        return self.pairs(lambda d, f: d * self.n + (f ^ (2 * mask)))

    def among_dp(self, mask):
        return self.pairs(lambda d, f: (d ^ mask) * self.n + f)

    def across_line(self, step):
        return self.pairs(lambda d, f: d * self.n + (f ^ (2 << (self.line_bits - 1 - step))))

    def across_dp(self, step):
        def partner(d, f):
            bit = step if f % 2 == 0 else self.dp_bits - 1 - step
            return (d ^ (1 << bit)) * self.n + f

        return self.pairs(partner)

    @staticmethod
    def spot(mask, bits, core):
        return mask if core == 0 else sum(((mask >> b) & 1) << (bits - 1 - b) for b in range(bits))

    def part(self, share, d, f):
        return sum(((d >> (bit if f % 2 == 0 else self.dp_bits - 1 - bit)) & 1) << bit for bit in range(share))

    def gather_row(self, share, d, f):
        z, c = divmod(f, 2)
        return [
            ((2 * (z ^ k) + who) << share) + (self.part(share, d, who) ^ step)
            for who in (c, 1 - c)
            for step in range(1 << share)
            for k in range(self.line)
        ]

    def reduce_row(self, d, f):
        z, c = divmod(f, 2)
        row = [c]
        for who in (c, 1 - c):
            line = [self.spot(owner ^ z, self.line_bits, 1) for owner in range(self.line)]
            row += [self.spot(j ^ d, self.dp_bits, who) * self.line + at for j in range(self.m) for at in line]
        return row + [self.spot(j ^ d, self.dp_bits, c) for j in range(self.m)] + [j ^ d for j in range(self.m)]

    def part_row(self, d, f):
        return [self.part(1, d, f), self.part(2, d, f), f]

    def tables(self):
        kinds = (functools.partial(self.gather_row, 1), functools.partial(self.gather_row, 2), self.reduce_row, self.part_row)
        rows = [[kind(d, f) for kind in kinds] for d in range(self.m) for f in range(self.n)]
        ends = np.cumsum([0] + [len(row) for row in rows[0]])
        return np.array([sum(row, []) for row in rows], np.int32), ends


BOTH = ("dp", "fsdp")


def after(values, *earlier):
    return lax.optimization_barrier((values,) + earlier)[0]


def doubled(blocks, got):
    return jnp.concatenate([blocks, got], axis=0)


def per_device(
    inputs,
    memory,
    cotangent,
    lengths,
    stacked_weights,
    expand_weights,
    contract_weights,
    scale_vectors,
    stacked_first,
    stacked_second,
    expand_first,
    expand_second,
    contract_first,
    contract_second,
    vector_first,
    vector_second,
):
    m, n = lax.axis_size("dp"), lax.axis_size("fsdp")
    width = WIDTH // n
    slabs = inputs.shape[0] * lengths.shape[1]
    x = inputs.reshape(slabs, SLAB, WIDTH)
    mem = memory.reshape(slabs, SLAB, WIDTH)
    cot = cotangent.reshape(slabs, SLAB, WIDTH)
    by_hand = m == 4 and width == 64 and n == 8
    here = lax.axis_index("fsdp")
    lengths = lengths.reshape(slabs, 2, -1)
    if by_hand:
        route = Route(m, n)
        table, ends = route.tables()
        row = lax.dynamic_index_in_dim(jnp.asarray(table), lax.axis_index("dp") * n + here, keepdims=False)
        halves, quarters, reduced, parts = (int(end) for end in ends[:4])
        order, holder = parts - 2 * m, parts - m

        def swap(blocks, pairs):
            return lax.ppermute(blocks, BOTH, pairs)

        along = [route.along_line(mask) for mask in range(1, n // 2)]
        line = [route.across_line(step) for step in range(route.line_bits)]
        across = [route.across_dp(step) for step in range(route.dp_bits)]
        core = route.across_core()
        a, b, c = run_cut_shards(parts, row, stacked_weights, expand_weights, contract_weights, scale_vectors)
        got = lax.optimization_barrier(tuple(swap(a, pairs) for pairs in along) + tuple(swap(b, pairs) for pairs in along))
        a, b = jnp.concatenate([a, *got[:3]], axis=0), jnp.concatenate([b, *got[3:]], axis=0)
        c = after(c, got)
        c_1, c_2, a_across, b_across, a_core = lax.optimization_barrier((swap(c, along[0]), swap(c, along[1]), swap(a, across[0]), swap(b, across[0]), swap(a, core)))
        b = doubled(b, b_across)
        b_across, b_core, c_3 = swap(b, across[1]), swap(b, core), swap(after(c, b), along[2])
        w_self, *saved1 = run_self_forward(halves, row, lengths, after(x, b), (a, a_across, a_core, swap(a_across, core)))
        b_across, c_3 = after((b_across, c_3), saved1[-1])
        ex, co = (jnp.concatenate([part[:, span] for part in (c, c_1, c_2, c_3)], axis=0) for span in (slice(0, 4), slice(4, 8)))
        b_across = after(b_across, ex)
        ex_across = swap(ex, across[0])
        w_cross = (b, b_across, b_core, swap(b_across, core))
        w_cross, vec, q2, k2, v2, *qkv2, unit1, kept1, scale1, low1 = run_cross_inputs(quarters, n, row, saved1[-1], x, mem, w_cross)
        ex_across = after(ex_across, unit1)
        co_across = swap(after(co, ex_across), across[0])
        ex_core, co_core, ex_last = swap(ex, core), swap(co, core), swap(ex_across, core)
        e2, r2, o2, kept_o2 = run_cross_forward(lengths, q2, k2, v2)
        saved2 = (*qkv2, e2, r2, kept_o2)
        co_across = after(co_across, o2)
        w_feed = ((ex, ex_across, ex_core, ex_last), (co, co_across, co_core, swap(co_across, core)))
        out, ds2, kept2, scale2, feed_keep, feed_send, dvec3 = run_feed(halves, reduced, n, row, o2, unit1, w_cross, cot, *w_feed, vec)
        feed_got = swap(feed_send, core)
        ds1, dk2, dv2, cross_keep, cross_send, dvec2 = run_cross_backward(reduced, row, n // 2, ds2, kept2, scale2, low1, mem, w_cross, vec, saved2)
        feed_got = after(feed_got, ds1)
        feed_out, feed = feed_keep[8:] + feed_got[8:], feed_keep[:8] + feed_got[:8]
        feed_got, cross_got = swap(feed_out, across[1]), swap(cross_send, core)
        part, dq, dk, dv, *others, dvec1 = run_self_backward(after(ds1, feed_out), kept1, scale1, x, w_cross, vec, saved1)
        feed_got, cross_got = after((feed_got, cross_got), dq)
        feed_out, feed = feed[4:] + feed_got[4:], feed[:4] + feed_got[:4]
        cross_out, cross = cross_keep[8:] + cross_got[8:], cross_keep[:8] + cross_got[:8]
        feed_got, cross_got = swap(feed_out, across[0]), swap(cross_out, across[1])
        keep, send = run_self_weights(reduced, row, n // 2, after((dq, dk, dv, *others), cross_out, feed_out), (dvec1, dvec2, dvec3))
        got = swap(send, core)
        dx, dmem = run_input_gradients(after(part, send), dq, dk, dv, w_self, dk2, dv2, w_cross)
        got = after(got, dx)
        out_part, total = keep[8:] + got[8:], keep[:8] + got[:8]
        feed_got, cross_got = after((feed_got, cross_got), got)
        feed = feed + feed_got
        feed_out, feed = feed[2:], feed[:2]
        got, feed_got = lax.optimization_barrier((swap(out_part, across[1]), swap(after(feed_out, out_part), line[1])))
        out_part = jnp.concatenate([total[4:] + got[4:], cross[4:] + cross_got[4:]], axis=1)
        total = jnp.concatenate([total[:4] + got[:4], cross[:4] + cross_got[:4]], axis=1)
        feed_out, feed = feed[1:] + feed_got[1:], feed[:1] + feed_got[:1]
        got, feed_got = lax.optimization_barrier((swap(out_part, across[0]), swap(after(feed_out, out_part), line[0])))
        out_part, total = total[2:] + got[2:], total[:2] + got[:2]
        feed = feed + feed_got
        feed = after(feed, out_part)
        got, feed_1, feed_2 = lax.optimization_barrier((swap(out_part, line[1]), swap(feed, across[0]), swap(feed, across[1])))
        out_part, total = total[1:] + got[1:], total[:1] + got[:1]
        got, feed_3 = lax.optimization_barrier((swap(out_part, line[0]), swap(after(feed_1, out_part), across[1])))
        total = total + got
        parts = after((feed, feed_1, feed_2, feed_3), total)
        feed_next = run_adam_feed(order, row, parts, (expand_weights, expand_first, expand_second), (contract_weights, contract_first, contract_second))
        got = lax.optimization_barrier(tuple(swap(total, route.among_dp(mask)) for mask in range(1, m)))
        got = after(got, feed_next[0])
        *stacked_next, vw, vm, vs = run_adam_stacked(holder, row, (total, *got), (stacked_weights, stacked_first, stacked_second), (scale_vectors, vector_first, vector_second))
        vector_next = (vw, vm, vs)
    else:
        row = jnp.array([0, 1, 0] + [0, 1, 2, 3] * 2, jnp.int32)
        expand_blocks = jnp.swapaxes(expand_weights.reshape(width, 4, WIDTH), 0, 1)
        vec_shard = lax.dynamic_update_slice(jnp.zeros((16, WIDTH), BF), scale_vectors.astype(BF), (0, here * width))
        all_low = lax.all_gather(stacked_weights.astype(BF), "fsdp", axis=1, tiled=True)
        vec_full = jnp.sum(lax.all_gather(vec_shard, "fsdp", axis=0).astype(F32), axis=0).astype(BF)
        vec_full = jnp.pad(vec_full, ((0, WIDTH - 16), (0, 0)))
        ex = lax.all_gather(expand_blocks.astype(BF), "fsdp", axis=1, tiled=True).reshape(4, 2, -1, WIDTH)
        co = lax.all_gather(contract_weights.astype(BF), "fsdp", axis=0, tiled=True).reshape(2, 4, -1, WIDTH)
        w_self = tuple(all_low[None, :3].reshape(1, 3, 2, -1, WIDTH)[:, :, core] for core in range(2))
        w_cross = jnp.concatenate([all_low[4:], all_low[3:4], vec_full[None]], axis=0).reshape(1, 6, 2, -1, WIDTH)
        w_feed = tuple(ex[None, :, core] for core in range(2)), tuple(co[None, core] for core in range(2))
        w_self, *saved1 = run_self_forward(0, row, lengths, x, w_self)
        w_cross, vec, q2, k2, v2, *qkv2, unit1, kept1, scale1, low1 = run_cross_inputs(0, 1, row, saved1[-1], x, mem, (w_cross[:, :, 0], w_cross[:, :, 1]))
        e2, r2, o2, kept_o2 = run_cross_forward(lengths, q2, k2, v2)
        saved2 = (*qkv2, e2, r2, kept_o2)
        out, ds2, kept2, scale2, feed_keep, feed_send, dvec3 = run_feed(0, 2, 2, row, o2, unit1, w_cross, cot, *w_feed, vec)
        dw_feed = jnp.stack([feed_keep, feed_send]).reshape(2, 8, WIDTH // 2, WIDTH)
        dex = jnp.swapaxes(dw_feed[:, :4], 0, 1).reshape(4, n, width, WIDTH)
        dco = dw_feed[:, 4:].reshape(n, 4, width, WIDTH)
        dw_feed = jnp.concatenate([jnp.swapaxes(dex, 0, 1), dco], axis=1)
        grad_feed = lax.psum(lax.psum_scatter(dw_feed, "fsdp", scatter_dimension=0, tiled=False), "dp")
        ds1, dk2, dv2, cross_keep, cross_send, dvec2 = run_cross_backward(2, row, 1, ds2, kept2, scale2, low1, mem, w_cross, vec, saved2)
        part, dq, dk, dv, *others, dvec1 = run_self_backward(ds1, kept1, scale1, x, w_cross, vec, saved1)
        keep, send = run_self_weights(2, row, 1, (dq, dk, dv, *others), (dvec1, dvec2, dvec3))
        dx, dmem = run_input_gradients(part, dq, dk, dv, w_self, dk2, dv2, w_cross)
        both, cross_both = jnp.stack([keep, send], axis=1), jnp.stack([cross_keep, cross_send], axis=1)
        rows = WIDTH // 2
        grad_vector = lax.psum(both[0, :, rows : rows + 9, :rows].astype(F32), BOTH)
        grad_vector = jnp.swapaxes(grad_vector, 0, 1).reshape(9, WIDTH)
        grad_vector = lax.dynamic_slice(grad_vector, (0, here * width), (9, width))
        both = jnp.concatenate([both[:, :, :rows], cross_both], axis=0).reshape(8, WIDTH, WIDTH)
        both = lax.psum(lax.psum_scatter(both, "fsdp", scatter_dimension=1, tiled=True), "dp")
        stacked_next = adam_update(stacked_weights, stacked_first, stacked_second, both.astype(F32))
        vector_next = adam_update(scale_vectors, vector_first, vector_second, grad_vector)
        feed_next = run_adam_feed(0, jnp.arange(4, dtype=jnp.int32), tuple(grad_feed.reshape(4, 1, 2 * width, WIDTH)), (expand_weights, expand_first, expand_second), (contract_weights, contract_first, contract_second))
    expand_next, contract_next = feed_next[:3], feed_next[3:]
    return (
        out.reshape(inputs.shape),
        dx.reshape(inputs.shape),
        dmem.reshape(inputs.shape),
        stacked_next[0],
        expand_next[0],
        contract_next[0],
        vector_next[0],
        stacked_next[1],
        stacked_next[2],
        expand_next[1],
        expand_next[2],
        contract_next[1],
        contract_next[2],
        vector_next[1],
        vector_next[2],
    )


def solution(mesh):
    tokens = P(None, ("dp", "fsdp"), None)
    pieces = P(None, ("dp", "fsdp"), None, None)
    stacked = P(None, "fsdp", None)
    rows = P("fsdp", None)
    columns = P(None, "fsdp")
    return jax.shard_map(
        per_device,
        mesh=mesh,
        in_specs=(tokens, tokens, tokens, pieces, stacked, rows, rows, columns) + (stacked, stacked, rows, rows, rows, rows, columns, columns),
        out_specs=(tokens, tokens, tokens, stacked, rows, rows, columns) + (stacked, stacked, rows, rows, rows, rows, columns, columns),
        check_vma=False,
    )
```

```python
import functools
import math

import jax
import jax.numpy as jnp
import numpy as np
from jax import lax
from jax.experimental import pallas as pl
from jax.experimental.pallas import tpu as pltpu
from jax.sharding import PartitionSpec as P

HEADS = 8
HEAD = 64
SLAB = 512
WIDTH = 512
PAIR = 2 * HEAD
STEP = 3
NORM_EPS = 1e-05
ADAM_EPS = 1e-08
LEARN_RATE = 0.2
FAR = -1e30
LOG2E = math.log2(math.e)
QSCALE = HEAD**-0.5 * LOG2E
TILE = 256
BF = jnp.bfloat16
F32 = jnp.float32
MIB = 1 << 20
FEED_MIB = 30
CROSS_MIB = 24
SELF_MIB = 40


def nn(a, b):
    return jnp.dot(a, b, preferred_element_type=F32)


def nt(a, b):
    return lax.dot_general(a, b, (((1,), (1,)), ((), ())), preferred_element_type=F32)


def tn(a, b):
    return lax.dot_general(a, b, (((0,), (0,)), ((), ())), preferred_element_type=F32)


def norm_forward(residual, eps=NORM_EPS):
    centred = residual - jnp.mean(residual, axis=-1, keepdims=True)
    spread = jnp.mean(centred * centred, axis=-1, keepdims=True)
    scale = lax.rsqrt(spread + eps)
    return centred * scale, scale


def norm_backward(upstream, unit, scale, gain):
    inner = upstream * gain
    first = jnp.mean(inner, axis=-1, keepdims=True)
    second = jnp.mean(inner * unit, axis=-1, keepdims=True)
    return scale * (inner - first - unit * second)


def rows_sum(values):
    return jnp.sum(values, axis=0, keepdims=True)


def first_lanes(rows):
    return lax.broadcasted_iota(jnp.int32, (rows, PAIR), 1) < HEAD


def attend_forward(q_ref, k_ref, v_ref, queries_in, keys_out, e_ref, o_ref, r_ref, causal, after=None):
    low = first_lanes(SLAB)
    ones = jnp.ones((SLAB, PAIR), BF)
    spans = ((0, TILE, TILE), (TILE, SLAB, SLAB)) if causal else ((0, SLAB, SLAB),)
    if causal:
        query_at = lax.broadcasted_iota(jnp.int32, (TILE, TILE), 0)
        key_at = lax.broadcasted_iota(jnp.int32, (TILE, TILE), 1)
        bias = jnp.where(key_at <= query_at, 0.0, FAR).astype(F32)
        blank = jnp.zeros((TILE, TILE), BF)

    def lanes(head):
        return slice(head // 2 * PAIR, (head // 2 + 1) * PAIR)

    def scores(head):
        left, right = q_ref[:, lanes(head)], k_ref[:, lanes(head)]
        if head % 2 == 0:
            left, right = jnp.where(low, left, queries_in), jnp.where(low, right, keys_out)
        else:
            left, right = jnp.where(low, queries_in, left), jnp.where(low, keys_out, right)
        return [nt(left[first:last], right[:depth]) for first, last, depth in spans]

    def powers(head, found):
        results = []
        for (first, last, depth), part in zip(spans, found):
            if causal:
                end = part[:, depth - TILE :] + bias
                part = end if depth == TILE else jnp.concatenate([part[:, : depth - TILE], end], axis=1)
            power = jnp.exp2(part - jnp.max(part, axis=1, keepdims=True)).astype(BF)
            e_ref[head, first:last, :depth] = power
            if depth < SLAB:
                e_ref[head, first:last, depth:] = blank
            results.append(power)
        if after is not None:
            after(head)
        return results

    def mixes(head, found):
        right = jnp.concatenate([v_ref[:, lanes(head)], ones], axis=1)
        results = []
        for (_, _, depth), power in zip(spans, found):
            mixed = nn(power, right[:depth])
            inverse = 1.0 / mixed[:, PAIR:]
            results.append((mixed[:, :PAIR] * inverse, inverse))
        return results

    def put(pair, even, odd):
        for (first, last, _), (mix_0, inverse_0), (mix_1, inverse_1) in zip(spans, even, odd):
            here = first_lanes(last - first)
            o_ref[first:last, pair * PAIR : (pair + 1) * PAIR] = jnp.where(here, mix_0, mix_1).astype(BF)
            r_ref[first:last, pair * PAIR : (pair + 1) * PAIR] = jnp.where(here, inverse_0, inverse_1).astype(BF)

    following = scores(0)
    earlier = None
    mixed = {}
    for head in range(HEADS):
        found = following
        if head + 1 < HEADS:
            following = scores(head + 1)
        now = powers(head, found)
        if earlier is not None:
            mixed[head - 1] = mixes(head - 1, earlier)
            if head % 2 == 0:
                put(head // 2 - 1, mixed[head - 2], mixed[head - 1])
        earlier = now
    mixed[HEADS - 1] = mixes(HEADS - 1, earlier)
    put(HEADS // 2 - 1, mixed[HEADS - 2], mixed[HEADS - 1])


def attend_backward(e_ref, r_ref, o_ref, q_ref, k_ref, v_ref, dm_ref, dq_ref, dkt_ref, dvt_ref):
    low = first_lanes(SLAB)
    lane = lax.broadcasted_iota(jnp.int32, (SLAB, PAIR), 1) % HEAD
    units = jnp.where(lane < 2, 1.0, 0.0).astype(BF)
    none = jnp.zeros((), BF)
    qt = q_ref[...].T
    for pair in range(HEADS // 2):
        lanes = slice(pair * PAIR, (pair + 1) * PAIR)
        mixed = (dm_ref[:, lanes] * r_ref[:, lanes].astype(F32)).astype(BF)
        weighed = mixed.astype(F32) * o_ref[:, lanes].astype(F32)
        keys, values = k_ref[:, lanes], v_ref[:, lanes]
        mixed_t = mixed.T
        dq = []
        for side in range(2):
            head = 2 * pair + side
            rows = slice(head * HEAD, (head + 1) * HEAD)
            mine = low if side == 0 else ~low
            centre = jnp.sum(jnp.where(mine, weighed, 0.0), axis=1, keepdims=True)
            high = centre.astype(BF)
            rest = (centre - high.astype(F32)).astype(BF)
            column = jnp.where(lane == 0, -high, jnp.where(lane == 1, -rest, none))
            grad = nt(jnp.where(mine, mixed, column), jnp.where(mine, values, units))
            power = e_ref[head]
            score = (power.astype(F32) * grad).astype(BF)
            dq.append(nn(score, keys))
            dkt_ref[rows, :] = (nn(qt[rows], score) * (1.0 / LOG2E)).astype(BF)
            dvt_ref[rows, :] = nn(mixed_t[side * HEAD : (side + 1) * HEAD], power).astype(BF)
        dq_ref[:, lanes] = (jnp.where(low, dq[0], dq[1]) * HEAD**-0.5).astype(BF)


def piece_columns(lengths_ref, slab, side):
    column = lax.broadcasted_iota(jnp.int32, (1, PAIR), 1) % HEAD
    opening = jnp.zeros((1, PAIR), jnp.int32)
    closing = jnp.zeros((1, PAIR), jnp.int32)
    total = jnp.int32(0)
    for piece in range(lengths_ref.shape[2]):
        following = total + lengths_ref[slab, side, piece]
        opening = jnp.where(column == piece, total, opening)
        closing = jnp.where(column == piece, following, closing)
        total = following
    place = lax.broadcasted_iota(jnp.int32, (SLAB, PAIR), 0)
    return jnp.where((opening <= place) & (place < closing), 1.0, 0.0).astype(BF)


def outside(columns):
    return jnp.where(columns > 0, 0.0, FAR).astype(BF)


def load_pieces(place_ref, first, pieces, w_s, sems):
    copies = []
    for blocks in pieces:
        rows = blocks.shape[2]
        for index in range(blocks.shape[0]):
            start = pl.multiple_of(place_ref[first + len(copies)] * rows, rows)
            copies.append(pltpu.make_async_copy(blocks.at[index], w_s.at[:, pl.ds(start, rows), :], sems.at[len(copies)]))
    for copy in copies:
        copy.start()
    for copy in copies:
        copy.wait()


def load_once(place_ref, first, pieces, w_s, sems):
    @pl.when(pl.program_id(0) == 0)
    def _():
        load_pieces(place_ref, first, pieces, w_s, sems)


def here(*refs):
    step = pl.program_id(0)
    return [ref.at[step if ref.shape[0] > 1 else 0] for ref in refs]


def self_forward(count, first, place_ref, lengths_ref, x_ref, *refs):
    pieces, (out_ref, q_ref, k_ref, v_ref, e_ref, r_ref, o_ref, w_ref, e_s, sems, e_sems, out_sem) = refs[:count], refs[count:]
    load_once(place_ref, first, pieces, w_ref, sems)
    pass_on = pltpu.make_async_copy(w_ref, out_ref, out_sem)
    x_ref, q_ref, k_ref, v_ref, r_ref, o_ref = here(x_ref, q_ref, k_ref, v_ref, r_ref, o_ref)
    step = pl.program_id(0)

    @pl.when(step == 0)
    def _():
        pass_on.start()

    def store(slab, head):
        return pltpu.make_async_copy(e_s.at[slab, head], e_ref.at[slab, head], e_sems.at[slab, head])

    x = x_ref[...]
    q_ref[...] = (nn(x, w_ref[0]) * QSCALE).astype(BF)
    k_ref[...] = nn(x, w_ref[1]).astype(BF)
    v_ref[...] = nn(x, w_ref[2]).astype(BF)
    columns = piece_columns(lengths_ref, pl.program_id(0), 0)
    attend_forward(q_ref, k_ref, v_ref, columns, outside(columns), e_s.at[step], o_ref, r_ref, True, lambda head: store(step, head).start())

    @pl.when(step == pl.num_programs(0) - 1)
    def _():
        pass_on.wait()
        for slab in range(e_s.shape[0]):
            for head in range(HEADS):
                store(slab, head).wait()


def cross_inputs(count, first, owners, place_ref, o1_ref, x_ref, mem_ref, *refs):
    pieces, refs = refs[:count], refs[count:]
    out_ref, vec_ref, q_ref, k_ref, v_ref, q_kept, k_kept, v_kept, unit1_ref, kept1_ref, scale1_ref, low1_ref, w_ref, sems, out_sem = refs
    load_once(place_ref, first, pieces, w_ref, sems)
    pass_on = pltpu.make_async_copy(w_ref, out_ref, out_sem)

    @pl.when(pl.program_id(0) == 0)
    def _():
        pass_on.start()
        rows = WIDTH // owners
        total = w_ref[5, 0:16, :].astype(F32)
        for owner in range(1, owners):
            total = total + w_ref[5, owner * rows : owner * rows + 16, :].astype(F32)
        vec_ref[...] = total

    o1_ref, x_ref, mem_ref, q_ref, k_ref, v_ref = here(o1_ref, x_ref, mem_ref, q_ref, k_ref, v_ref)
    q_kept, k_kept, v_kept = here(q_kept, k_kept, v_kept)
    unit1_ref, kept1_ref, scale1_ref, low1_ref = here(unit1_ref, kept1_ref, scale1_ref, low1_ref)
    residual = vec_ref[6:7, :] * x_ref[...].astype(F32) + nn(o1_ref[...], w_ref[4])
    unit, scale = norm_forward(residual)
    unit1_ref[...] = unit
    kept1_ref[...] = unit
    scale1_ref[...] = scale
    low = (unit * vec_ref[0:1, :] + vec_ref[3:4, :]).astype(BF)
    low1_ref[...] = low
    memory = mem_ref[...]
    for once, kept, value in ((k_ref, k_kept, nn(memory, w_ref[1])), (v_ref, v_kept, nn(memory, w_ref[2])), (q_ref, q_kept, nn(low, w_ref[0]) * QSCALE)):
        value = value.astype(BF)
        once[...] = value
        kept[...] = value

    @pl.when(pl.program_id(0) == pl.num_programs(0) - 1)
    def _():
        pass_on.wait()


def cross_forward(lengths_ref, q_ref, k_ref, v_ref, e_ref, r_ref, o_ref, kept_ref):
    slab = pl.program_id(0)
    q_ref, k_ref, v_ref, e_ref, r_ref, o_ref, kept_ref = here(q_ref, k_ref, v_ref, e_ref, r_ref, o_ref, kept_ref)
    queries_in, keys_out = piece_columns(lengths_ref, slab, 0), outside(piece_columns(lengths_ref, slab, 1))
    attend_forward(q_ref, k_ref, v_ref, queries_in, keys_out, e_ref, o_ref, r_ref, False)
    kept_ref[...] = o_ref[...]


CUBE = 0.044715
ROOT = math.sqrt(2.0 / math.pi)


def feed_copies(place_ref, begin, first, second, ex_s, co_s, sems):
    each = co_s.shape[1]
    results = [], []
    for side, pieces in enumerate((first, second)):
        for blocks in pieces:
            rows = blocks.shape[2]
            for index in range(blocks.shape[0]):
                number = len(results[side])
                start = place_ref[begin + number] * rows
                owner = start // each
                if side == 0:
                    goal = ex_s.at[:, pl.ds(pl.multiple_of(start, rows), rows), :]
                else:
                    goal = co_s.at[pl.ds(owner * 4, 4), pl.ds(pl.multiple_of(start - owner * each, rows), rows), :]
                results[side].append(pltpu.make_async_copy(blocks.at[index], goal, sems.at[side, number]))
    return results


def feed_both(count, begin, reduce_at, place_ref, o2_ref, unit1_ref, w_ref, cot_ref, vec_ref, *refs):
    pieces, refs = refs[: 2 * count], refs[2 * count :]
    (out_ref, ds_ref, unit_s, scale_ref, keep_ref, send_ref, dvec_ref,
     act_s, slope_s, branch_s, low_s, dbranch_s, cot_s, out_s, dex_s, dco_s, ex_s, co_s, sems, own_sems) = refs
    slabs = unit_s.shape[0]
    chunks = ex_s.shape[0]
    owners = co_s.shape[0] // 4
    first, second = feed_copies(place_ref, begin, pieces[:count], pieces[count:], ex_s, co_s, sems)
    cot_copy = pltpu.make_async_copy(cot_ref, cot_s, own_sems.at[0])
    out_copy = pltpu.make_async_copy(out_s, out_ref, own_sems.at[1])
    for copy in first + second + [cot_copy]:
        copy.start()

    def rows(slab):
        return slice(slab * SLAB, (slab + 1) * SLAB)

    def contract(part):
        return co_s[part * owners : (part + 1) * owners].reshape(WIDTH, WIDTH)

    def state(slab):
        return unit_s[slab] * vec_ref[1:2, :] + vec_ref[4:5, :]

    for slab in range(slabs):
        before = unit1_ref[slab] * vec_ref[0:1, :] + vec_ref[3:4, :]
        unit_s[slab], scale_ref[slab] = norm_forward(vec_ref[7:8, :] * before + nn(o2_ref[slab], w_ref[0]))
        low_s[rows(slab), :] = state(slab).astype(BF)
    for copy in first:
        copy.wait()
    following = nn(low_s[...], ex_s[0])
    for part in range(chunks):
        u = following
        if part + 1 < chunks:
            following = nn(low_s[...], ex_s[part + 1])
        square = u * u
        bend = jnp.tanh(u * (ROOT + (ROOT * CUBE) * square))
        half = 0.5 + 0.5 * bend
        act_s[part] = (u * half).astype(BF)
        slope_s[part] = half + (u * half) * (1.0 - bend) * (ROOT + (3.0 * ROOT * CUBE) * square)
        if part == 0:
            for copy in second:
                copy.wait()
            branch_s[...] = nn(act_s[part], contract(part))
        else:
            branch_s[...] += nn(act_s[part], contract(part))
    cot_copy.wait()
    for slab in range(slabs):
        now = state(slab)
        unit, scale = norm_forward(vec_ref[8:9, :] * now + branch_s[rows(slab), :])
        out_s[slab] = (unit * vec_ref[2:3, :] + vec_ref[5:6, :]).astype(BF)
        up = cot_s[slab].astype(F32)
        dres = norm_backward(up, unit, scale, vec_ref[2:3, :])
        sums = (rows_sum(up * unit), rows_sum(up), rows_sum(dres * now))
        for row, value in enumerate(sums):
            if slab == 0:
                dvec_ref[row : row + 1, :] = value
            else:
                dvec_ref[row : row + 1, :] += value
        branch_s[rows(slab), :] = dres * vec_ref[8:9, :]
        dbranch_s[rows(slab), :] = dres.astype(BF)
    out_copy.start()
    low_t = low_s[...].T
    for part in range(chunks):
        dco_s[part] = tn(act_s[part], dbranch_s[...]).astype(BF)
        dhid = (nt(dbranch_s[...], contract(part)) * slope_s[part]).astype(BF)
        dex_s[part] = nn(low_t, dhid).astype(BF)
        branch_s[...] += nt(dhid, ex_s[part])
    for slab in range(slabs):
        ds_ref[slab] = branch_s[rows(slab), :]
    put_feed(place_ref, reduce_at, dex_s, dco_s, keep_ref, send_ref)
    out_copy.wait()


def put_gradients(place_ref, begin, dw_s, keep_ref, send_ref, first):
    blocks = keep_ref.shape[0]
    owners = blocks // dw_s.shape[0]
    rows = WIDTH // (2 * owners)
    core = place_ref[begin]
    for matrix in range(dw_s.shape[0]):
        for owner in range(owners):
            at = begin + 1 + matrix * owners + owner
            start = pl.multiple_of((2 * owner + core) * rows, rows)
            keep_ref[place_ref[at], first : first + rows, :] = dw_s[matrix, pl.ds(start, rows), :]
            start = pl.multiple_of((2 * owner + 1 - core) * rows, rows)
            send_ref[place_ref[at + blocks], first : first + rows, :] = dw_s[matrix, pl.ds(start, rows), :]


def put_vectors(place_ref, begin, dvec_s, count, keep_ref, send_ref, first):
    blocks = keep_ref.shape[0]
    owners = blocks // count
    columns = WIDTH // (2 * owners)
    core = place_ref[begin]
    rows = slice(first, first + 16)
    blank = jnp.zeros((16, WIDTH), BF)
    for block in range(blocks):
        keep_ref[block, rows, :] = blank
        send_ref[block, rows, :] = blank
    for owner in range(owners):
        low = dvec_s[:, 2 * owner * columns : (2 * owner + 1) * columns]
        high = dvec_s[:, (2 * owner + 1) * columns : (2 * owner + 2) * columns]
        rest = jnp.zeros((16, WIDTH - columns), F32)
        own = jnp.where(core == 0, low, high)
        other = jnp.where(core == 0, high, low)
        at = begin + 1 + owner
        keep_ref[place_ref[at], rows, :] = jnp.concatenate([own, rest], axis=1).astype(BF)
        send_ref[place_ref[at + blocks], rows, :] = jnp.concatenate([other, rest], axis=1).astype(BF)


def put_feed(place_ref, begin, dex_s, dco_s, keep_ref, send_ref):
    blocks = keep_ref.shape[0]
    owners = blocks // 4
    each = keep_ref.shape[1] // 2
    core = place_ref[begin]
    for pair in range(4):
        for owner in range(owners):
            at = begin + 1 + pair * owners + owner
            for out_ref, on, block in ((keep_ref, core, place_ref[at]), (send_ref, 1 - core, place_ref[at + blocks])):
                shard = 2 * owner + on
                for side in range(2):
                    number = 2 * pair + side
                    rows = slice(side * each, (side + 1) * each)
                    if number < 4:
                        out_ref[block, rows, :] = dex_s[number, pl.ds(pl.multiple_of(shard * each, each), each), :]
                    else:
                        row = (shard * 4 + number - 4) * each
                        chunk = row // WIDTH
                        out_ref[block, rows, :] = dco_s[chunk, pl.ds(pl.multiple_of(row - chunk * WIDTH, each), each), :]


def fetcher(pairs, sems):
    step = pl.program_id(0)

    def copy(number, slab):
        return pltpu.make_async_copy(pairs[number][0].at[slab], pairs[number][1].at[slab], sems.at[number, slab])

    @pl.when(step == 0)
    def _():
        for slab in range(pairs[0][1].shape[0]):
            for number in range(len(pairs)):
                copy(number, slab).start()

    def wait(first, last):
        for number in range(first, last):
            copy(number, step).wait()

    return wait


def all_rows(ref):
    return ref[...].reshape(-1, WIDTH)


def cross_backward(begin, place_ref, ds2_ref, unit2_ref, scale2_ref, w_ref, vec_ref, q_ref, k_ref, v_ref, r_ref, o_ref, low1_ref, mem_ref, e_ref,
                   ds1_ref, dk_ref, dv_ref, keep_ref, send_ref, dvec_ref,
                   q_s, k_s, v_s, r_s, o_s, low1_s, mem_s, w_s, dm_s, dq_s, dk_s, dv_s, dbranch_s, dkt_s, dvt_s, dw_s, sems, out_sems, w_sems):
    step = pl.program_id(0)
    steps = pl.num_programs(0)
    w_copies = [pltpu.make_async_copy(w_ref.at[3], w_s.at[3], w_sems.at[0]), pltpu.make_async_copy(w_ref.at[0:3], w_s.at[0:3], w_sems.at[1])]

    @pl.when(step == 0)
    def _():
        w_copies[0].start()

    wait = fetcher([(q_ref, q_s), (k_ref, k_s), (v_ref, v_s), (r_ref, r_s), (o_ref, o_s), (low1_ref, low1_s), (mem_ref, mem_s)], sems)
    outward = [pltpu.make_async_copy(dk_s, dk_ref, out_sems.at[0]), pltpu.make_async_copy(dv_s, dv_ref, out_sems.at[1])]

    @pl.when(step == 0)
    def _():
        w_copies[1].start()
        dvec_ref[...] = jnp.zeros_like(dvec_ref)

    ds2_ref, unit2_ref, scale2_ref, ds1_ref = here(ds2_ref, unit2_ref, scale2_ref, ds1_ref)
    up = ds2_ref[...]
    unit = unit2_ref[...]
    dvec_ref[0:1, :] += rows_sum(up * unit)
    dvec_ref[1:2, :] += rows_sum(up)
    dres = norm_backward(up, unit, scale2_ref[...], vec_ref[1:2, :])
    dbranch = dres.astype(BF)
    dbranch_s[step] = dbranch

    @pl.when(step == 0)
    def _():
        w_copies[0].wait()

    dm_s[...] = nt(dbranch, w_s[3])
    ds1_ref[...] = dres * vec_ref[7:8, :]
    wait(0, 5)
    attend_backward(e_ref.at[step], r_s.at[step], o_s.at[step], q_s.at[step], k_s.at[step], v_s.at[step], dm_s, dq_s.at[step], dkt_s, dvt_s)
    wait(5, 7)
    dvec_ref[2:3, :] += rows_sum(dbranch_s[step].astype(F32) * low1_s[step].astype(F32))

    @pl.when(step == 0)
    def _():
        w_copies[1].wait()

    ds1_ref[...] += nt(dq_s[step], w_s[0])
    dk_s[step] = dkt_s[...].T
    dv_s[step] = dvt_s[...].T

    @pl.when(step == steps - 1)
    def _():
        for copy in outward:
            copy.start()
        dw_s[0] = tn(all_rows(low1_s), all_rows(dq_s)).astype(BF)
        memory_t = all_rows(mem_s).T
        dw_s[1] = nn(memory_t, all_rows(dk_s)).astype(BF)
        dw_s[2] = nn(memory_t, all_rows(dv_s)).astype(BF)
        dw_s[3] = tn(all_rows(o_s), all_rows(dbranch_s)).astype(BF)
        put_gradients(place_ref, begin, dw_s, keep_ref, send_ref, 0)
        for copy in outward:
            copy.wait()


def self_backward(ds1_ref, unit1_ref, scale1_ref, w3_ref, vec_ref, q_ref, k_ref, v_ref, r_ref, o_ref, x_ref, e_ref,
                  part_ref, dq_ref, dk_ref, dv_ref, dbranch_ref, o_s, x_s, dvec_ref, q_s, k_s, v_s, r_s, e_s, dm_s, dkt_s, dvt_s, sems):
    step = pl.program_id(0)
    wait = fetcher([(e_ref, e_s), (q_ref, q_s), (k_ref, k_s), (v_ref, v_s), (r_ref, r_s), (o_ref, o_s), (x_ref, x_s)], sems)

    @pl.when(step == 0)
    def _():
        dvec_ref[...] = jnp.zeros_like(dvec_ref)

    ds1_ref, unit1_ref, scale1_ref, part_ref, dq_ref, dk_ref, dv_ref, dbranch_ref = here(ds1_ref, unit1_ref, scale1_ref, part_ref, dq_ref, dk_ref, dv_ref, dbranch_ref)
    up = ds1_ref[...]
    unit = unit1_ref[...]
    dvec_ref[0:1, :] += rows_sum(up * unit)
    dvec_ref[1:2, :] += rows_sum(up)
    dres = norm_backward(up, unit, scale1_ref[...], vec_ref[0:1, :])
    dbranch = dres.astype(BF)
    dbranch_ref[...] = dbranch
    dm_s[...] = nt(dbranch, w3_ref[0])
    part_ref[...] = dres * vec_ref[6:7, :]
    wait(0, 6)
    attend_backward(e_s.at[step], r_s.at[step], o_s.at[step], q_s.at[step], k_s.at[step], v_s.at[step], dm_s, dq_ref, dkt_s, dvt_s)
    dk_ref[...] = dkt_s[...].T
    dv_ref[...] = dvt_s[...].T
    wait(6, 7)
    dvec_ref[2:3, :] += rows_sum(dbranch_ref[...].astype(F32) * x_s[step].astype(F32))


def self_weights(begin, place_ref, dq_ref, dk_ref, dv_ref, dbranch_ref, o_ref, x_ref, dvec1_ref, dvec2_ref, dvec3_ref, keep_ref, send_ref, dw_s, dvec_s):
    dvec_s[...] = jnp.zeros_like(dvec_s)
    for row in range(3):
        for number, ref in enumerate((dvec1_ref, dvec2_ref, dvec3_ref)):
            dvec_s[3 * row + number : 3 * row + number + 1, :] = ref[row : row + 1, :]
    x_t = all_rows(x_ref).T
    dw_s[0] = nn(x_t, all_rows(dq_ref)).astype(BF)
    dw_s[1] = nn(x_t, all_rows(dk_ref)).astype(BF)
    dw_s[2] = nn(x_t, all_rows(dv_ref)).astype(BF)
    dw_s[3] = tn(all_rows(o_ref), all_rows(dbranch_ref)).astype(BF)
    put_gradients(place_ref, begin, dw_s, keep_ref, send_ref, 0)
    put_vectors(place_ref, begin, dvec_s, dw_s.shape[0], keep_ref, send_ref, keep_ref.shape[1] - 16)


def input_gradients(part_ref, dq_ref, dk_ref, dv_ref, w_ref, dk2_ref, dv2_ref, w2_ref, dx_ref, dmem_ref):
    part_ref, dq_ref, dk_ref, dv_ref, dk2_ref, dv2_ref, dx_ref, dmem_ref = here(part_ref, dq_ref, dk_ref, dv_ref, dk2_ref, dv2_ref, dx_ref, dmem_ref)
    dx_ref[...] = part_ref[...] + nt(dq_ref[...], w_ref[0]) + nt(dk_ref[...], w_ref[1]) + nt(dv_ref[...], w_ref[2])
    dmem_ref[...] = nt(dk2_ref[...], w2_ref[1]) + nt(dv2_ref[...], w2_ref[2])


def cut_shards(at, place_ref, stacked_ref, expand_ref, contract_ref, vec_ref, a_ref, b_ref, c_ref, a_s, b_s, ex_s, co_s, vec_s, sems):
    rows = stacked_ref.shape[1]
    middle = pl.multiple_of(place_ref[at] * (rows // 2), rows // 2)
    half = pl.ds(middle, rows // 2)
    start = pl.multiple_of(place_ref[at + 1] * (rows // 4), rows // 4)
    quarter = pl.ds(start, rows // 4)
    copies = [
        pltpu.make_async_copy(stacked_ref.at[0:3, half, :], a_s, sems.at[0]),
        pltpu.make_async_copy(stacked_ref.at[3:8, quarter, :], b_s, sems.at[1]),
        pltpu.make_async_copy(vec_ref, vec_s, sems.at[2]),
        pltpu.make_async_copy(expand_ref.at[half, :], ex_s, sems.at[3]),
    ]
    copies += [
        pltpu.make_async_copy(contract_ref.at[pl.ds(pl.multiple_of(part * rows + middle, rows // 2), rows // 2), :], co_s.at[part], sems.at[4 + part])
        for part in range(4)
    ]
    for copy in copies:
        copy.start()
    for copy in copies:
        copy.wait()
    a_ref[0] = a_s[...].astype(BF)
    for index, matrix in enumerate((4, 5, 6, 7, 3)):
        b_ref[0, index] = b_s[matrix - 3].astype(BF)
    vec = jnp.concatenate([vec_s[...]] * (WIDTH // vec_ref.shape[1]), axis=1)
    owner = lax.broadcasted_iota(jnp.int32, vec.shape, 1) // vec_ref.shape[1]
    vec = jnp.where(owner == place_ref[at + 2], vec, 0.0)
    b_ref[0, 5] = jnp.concatenate([vec, jnp.zeros((rows // 4 - vec.shape[0], WIDTH), F32)], axis=0).astype(BF)
    for part in range(4):
        c_ref[0, part] = ex_s[:, part * WIDTH : (part + 1) * WIDTH].astype(BF)
        c_ref[0, 4 + part] = co_s[part].astype(BF)


def per_slab(*tail):
    return pl.BlockSpec((1,) + tail, lambda m: (m,) + (0,) * len(tail))


def fixed(*dims):
    return pl.BlockSpec(dims, lambda m: (0,) * len(dims), pipeline_mode=pl.Buffered(1))


def shape(dims, kind):
    return jax.ShapeDtypeStruct(tuple(dims), kind)


def options(mib):
    return pltpu.CompilerParams(dimension_semantics=("arbitrary",), vmem_limit_bytes=mib * MIB)


def estimate(microseconds):
    return pl.CostEstimate(flops=int(microseconds * 1e9), bytes_accessed=1 << 20, transcendentals=0)


SCALARS = pl.BlockSpec(memory_space=pltpu.SMEM)
ANYWHERE = pl.BlockSpec(memory_space=pl.ANY)
RESIDENT = pl.BlockSpec(memory_space=pltpu.VMEM)
ROWS = per_slab(SLAB, WIDTH)
SCALE = per_slab(SLAB, 1)


def near(*arrays):
    return tuple(pltpu.with_memory_space_constraint(array, pltpu.VMEM) for array in arrays)


def far(*arrays):
    return tuple(pltpu.with_memory_space_constraint(array, pltpu.HBM) for array in arrays)


def near_shape(dims, kind):
    return pltpu.VMEM(tuple(dims), kind)


def far_shape(dims, kind):
    return pltpu.HBM(tuple(dims), kind)


def slabs(g, kind, place=far_shape):
    return place((g, SLAB, WIDTH), kind)


def powers_shape(g, place):
    return place((g, HEADS, SLAB, SLAB), BF)


def run_cut_shards(at, place, stacked, expand, contract, vec):
    rows = stacked.shape[1]
    return pl.pallas_call(
        functools.partial(cut_shards, at),
        in_specs=[SCALARS] + [ANYWHERE] * 4,
        out_specs=[RESIDENT] * 3,
        out_shape=[shape((1, 3, rows // 2, WIDTH), BF), shape((1, 6, rows // 4, WIDTH), BF), shape((1, 8, rows // 2, WIDTH), BF)],
        scratch_shapes=[
            pltpu.VMEM((3, rows // 2, WIDTH), F32),
            pltpu.VMEM((5, rows // 4, WIDTH), F32),
            pltpu.VMEM((rows // 2, expand.shape[1]), F32),
            pltpu.VMEM((4, rows // 2, WIDTH), F32),
            pltpu.VMEM(vec.shape, F32),
            pltpu.SemaphoreType.DMA((8,)),
        ],
        compiler_params=pltpu.CompilerParams(vmem_limit_bytes=16 * MIB),
        name="cut_shards",
    )(place, *far(stacked, expand, contract, vec))


def run_self_forward(first, place, lengths, x, w):
    g = x.shape[0]
    return pl.pallas_call(
        functools.partial(self_forward, len(w), first),
        grid=(g,),
        in_specs=[SCALARS, SCALARS, ROWS] + [ANYWHERE] * len(w),
        out_specs=[ANYWHERE, ROWS, ROWS, ROWS, ANYWHERE, ROWS, RESIDENT],
        out_shape=[far_shape((3, WIDTH, WIDTH), BF)] + [slabs(g, BF)] * 3 + [powers_shape(g, far_shape), slabs(g, BF), slabs(g, BF, near_shape)],
        scratch_shapes=[pltpu.VMEM((3, WIDTH, WIDTH), BF), pltpu.VMEM((g, HEADS, SLAB, SLAB), BF), pltpu.SemaphoreType.DMA((sum(piece.shape[0] for piece in w),)), pltpu.SemaphoreType.DMA((g, HEADS)), pltpu.SemaphoreType.DMA],
        compiler_params=options(32),
        cost_estimate=estimate(12),
        name="self_forward",
    )(place, lengths, x, *w)


def run_cross_inputs(first, owners, place, o1, x, memory, w):
    g = memory.shape[0]
    return pl.pallas_call(
        functools.partial(cross_inputs, len(w), first, owners),
        grid=(g,),
        in_specs=[SCALARS, RESIDENT, ROWS, ROWS] + [ANYWHERE] * len(w),
        out_specs=[ANYWHERE, fixed(16, WIDTH), RESIDENT, RESIDENT, RESIDENT, ROWS, ROWS, ROWS, RESIDENT, ROWS, SCALE, ROWS],
        out_shape=[far_shape((6, WIDTH, WIDTH), BF), far_shape((16, WIDTH), F32)]
        + [slabs(g, BF, near_shape)] * 3
        + [slabs(g, BF)] * 3
        + [slabs(g, F32, near_shape), slabs(g, F32), far_shape((g, SLAB, 1), F32), slabs(g, BF)],
        scratch_shapes=[pltpu.VMEM((6, WIDTH, WIDTH), BF), pltpu.SemaphoreType.DMA((sum(piece.shape[0] for piece in w),)), pltpu.SemaphoreType.DMA],
        compiler_params=options(24),
        cost_estimate=estimate(7),
        name="cross_inputs",
    )(place, *near(o1), x, memory, *w)


def run_cross_forward(lengths, q, k, v):
    g = q.shape[0]
    return pl.pallas_call(
        cross_forward,
        grid=(g,),
        in_specs=[SCALARS] + [RESIDENT] * 3,
        out_specs=[RESIDENT, ROWS, RESIDENT, ROWS],
        out_shape=[powers_shape(g, near_shape), slabs(g, BF), slabs(g, BF, near_shape), slabs(g, BF)],
        compiler_params=options(24),
        cost_estimate=estimate(10),
        name="cross_forward",
    )(lengths, *near(q, k, v))


def run_feed(begin, reduce_at, owners, place, o2, unit1, w_cross, cot, first, second, vec):
    g = unit1.shape[0]
    rows = WIDTH // owners
    pieces = sum(piece.shape[0] for piece in first)
    dims = (2 * owners, 2 * rows, WIDTH)
    tokens = g * SLAB
    last = pl.BlockSpec((1, WIDTH, WIDTH), lambda m: (3, 0, 0))
    return pl.pallas_call(
        functools.partial(feed_both, len(first), begin, reduce_at),
        grid=(1,),
        in_specs=[SCALARS, RESIDENT, RESIDENT, last, ANYWHERE, fixed(16, WIDTH)] + [ANYWHERE] * (2 * len(first)),
        out_specs=[ANYWHERE, RESIDENT, RESIDENT, fixed(g, SLAB, 1), RESIDENT, RESIDENT, fixed(8, WIDTH)],
        out_shape=[slabs(g, BF), slabs(g, F32, near_shape), slabs(g, F32, near_shape), far_shape((g, SLAB, 1), F32)] + [near_shape(dims, BF)] * 2 + [far_shape((8, WIDTH), F32)],
        scratch_shapes=[
            pltpu.VMEM((4, tokens, WIDTH), BF),
            pltpu.VMEM((4, tokens, WIDTH), F32),
            pltpu.VMEM((tokens, WIDTH), F32),
            pltpu.VMEM((tokens, WIDTH), BF),
            pltpu.VMEM((tokens, WIDTH), BF),
            pltpu.VMEM((g, SLAB, WIDTH), BF),
            pltpu.VMEM((g, SLAB, WIDTH), BF),
            pltpu.VMEM((4, WIDTH, WIDTH), BF),
            pltpu.VMEM((4, WIDTH, WIDTH), BF),
            pltpu.VMEM((4, WIDTH, WIDTH), BF),
            pltpu.VMEM((4 * owners, rows, WIDTH), BF),
            pltpu.SemaphoreType.DMA((2, pieces)),
            pltpu.SemaphoreType.DMA((2,)),
        ],
        compiler_params=options(FEED_MIB),
        cost_estimate=estimate(24),
        name="feed_both",
    )(place, *near(o2, unit1), *far(w_cross), cot, *far(vec), *first, *second)


def slab_scratch(g, kinds):
    return [pltpu.VMEM((g, SLAB, WIDTH), kind) for kind in kinds]


def run_cross_backward(begin, place, owners, ds2, unit2, scale2, low1, memory, w, vec, saved):
    g = memory.shape[0]
    dims = (4 * owners, WIDTH // (2 * owners), WIDTH)
    q, k, v, e, r, o = saved
    return pl.pallas_call(
        functools.partial(cross_backward, begin),
        grid=(g,),
        in_specs=[SCALARS, RESIDENT, RESIDENT, SCALE, ANYWHERE, fixed(16, WIDTH)] + [ANYWHERE] * 7 + [RESIDENT],
        out_specs=[RESIDENT, ANYWHERE, ANYWHERE, RESIDENT, RESIDENT, fixed(8, WIDTH)],
        out_shape=[slabs(g, F32, near_shape), slabs(g, BF), slabs(g, BF), near_shape(dims, BF), near_shape(dims, BF), far_shape((8, WIDTH), F32)],
        scratch_shapes=slab_scratch(g, [BF] * 7)
        + [pltpu.VMEM((4, WIDTH, WIDTH), BF), pltpu.VMEM((SLAB, WIDTH), F32)]
        + slab_scratch(g, [BF] * 4)
        + [pltpu.VMEM((WIDTH, SLAB), BF)] * 2
        + [pltpu.VMEM((4, WIDTH, WIDTH), BF), pltpu.SemaphoreType.DMA((7, g)), pltpu.SemaphoreType.DMA((2,)), pltpu.SemaphoreType.DMA((2,))],
        compiler_params=options(CROSS_MIB),
        cost_estimate=estimate(19),
        name="cross_backward",
    )(place, *near(ds2, unit2), *far(scale2, w, vec, q, k, v, r, o, low1), memory, *near(e))


def run_self_backward(ds1, unit1, scale1, x, w_cross, vec, saved):
    g = x.shape[0]
    q, k, v, e, r, o = saved
    third = pl.BlockSpec((1, WIDTH, WIDTH), lambda m: (4, 0, 0))
    return pl.pallas_call(
        self_backward,
        grid=(g,),
        in_specs=[RESIDENT, ROWS, SCALE, third, fixed(16, WIDTH)] + [ANYWHERE] * 7,
        out_specs=[ROWS] + [RESIDENT] * 6 + [fixed(8, WIDTH)],
        out_shape=[slabs(g, F32)] + [slabs(g, BF, near_shape)] * 6 + [far_shape((8, WIDTH), F32)],
        scratch_shapes=slab_scratch(g, [BF] * 4)
        + [pltpu.VMEM((g, HEADS, SLAB, SLAB), BF), pltpu.VMEM((SLAB, WIDTH), F32)]
        + [pltpu.VMEM((WIDTH, SLAB), BF)] * 2
        + [pltpu.SemaphoreType.DMA((7, g))],
        compiler_params=options(SELF_MIB),
        cost_estimate=estimate(17),
        name="self_backward",
    )(*near(ds1), *far(unit1, scale1, w_cross, vec, q, k, v, r, o), x, *far(e))


def run_self_weights(begin, place, owners, grads, dvecs):
    dims = (4 * owners, WIDTH // (2 * owners) + 16, WIDTH)
    return pl.pallas_call(
        functools.partial(self_weights, begin),
        grid=(1,),
        in_specs=[SCALARS] + [RESIDENT] * 6 + [fixed(8, WIDTH)] * 3,
        out_specs=[RESIDENT] * 2,
        out_shape=[near_shape(dims, BF)] * 2,
        scratch_shapes=[pltpu.VMEM((4, WIDTH, WIDTH), BF), pltpu.VMEM((16, WIDTH), F32)],
        compiler_params=options(20),
        cost_estimate=estimate(4),
        name="self_weights",
    )(place, *near(*grads), *far(*dvecs))


def run_input_gradients(part, dq, dk, dv, w, dk2, dv2, w2):
    g = part.shape[0]
    return pl.pallas_call(
        input_gradients,
        grid=(g,),
        in_specs=[ROWS] + [RESIDENT] * 3 + [fixed(3, WIDTH, WIDTH), ROWS, ROWS, fixed(3, WIDTH, WIDTH)],
        out_specs=[ROWS, ROWS],
        out_shape=[slabs(g, F32), slabs(g, F32)],
        compiler_params=options(28),
        cost_estimate=estimate(6),
        name="input_gradients",
    )(*far(part), *near(dq, dk, dv), *far(w, dk2, dv2, w2))
def adam_update(weight, first_moment, second_moment, gradient):
    correction = 1.0 - 0.5**STEP
    first_next = 0.5 * first_moment + 0.5 * gradient
    second_next = 0.5 * second_moment + 0.5 * gradient * gradient
    weight_next = weight - LEARN_RATE * (first_next / correction) / (jnp.sqrt(second_next / correction) + ADAM_EPS)
    return (weight_next, first_next, second_next)


def picked(order, parts):
    value = parts[0]
    for number in range(1, len(parts)):
        value = jnp.where(order == number, parts[number], value)
    return value.astype(F32)


def adam_stacked(at, place_ref, part_0, part_1, part_2, part_3, w_ref, m_ref, s_ref, vw_ref, vm_ref, vs_ref, w_out, m_out, s_out, vw_out, vm_out, vs_out):
    rows = w_ref.shape[1]
    group = pl.program_id(0)
    parts = (part_0, part_1, part_2, part_3)

    def update(first):
        for matrix in range(4):
            grad = picked(place_ref[at + matrix], [part[0, first : first + rows, :] for part in parts])
            w_out[matrix], m_out[matrix], s_out[matrix] = adam_update(w_ref[matrix], m_ref[matrix], s_ref[matrix], grad)

    @pl.when(group == 0)
    def _():
        update(0)
        grad = picked(place_ref[at], [part[0, rows : rows + 16, :] for part in parts])
        vw_out[...], vm_out[...], vs_out[...] = adam_update(vw_ref[...], vm_ref[...], vs_ref[...], grad[: vw_ref.shape[0], : vw_ref.shape[1]])

    @pl.when(group == 1)
    def _():
        update(rows + 16)


def run_adam_stacked(at, place, parts, stacked, vectors):
    rows = stacked[0].shape[1]
    block = pl.BlockSpec((4, rows, WIDTH), lambda group: (group, 0, 0))
    vector = fixed(*vectors[0].shape)
    return pl.pallas_call(
        functools.partial(adam_stacked, at),
        grid=(2,),
        in_specs=[SCALARS] + [fixed(*part.shape) for part in parts] + [block] * 3 + [vector] * 3,
        out_specs=[block] * 3 + [vector] * 3,
        out_shape=[shape(a.shape, F32) for a in tuple(stacked) + tuple(vectors)],
        compiler_params=options(24),
        cost_estimate=estimate(4),
        name="adam_stacked",
    )(place, *parts, *stacked, *vectors)


def adam_feed(at, place_ref, part_0, part_1, part_2, part_3, *refs):
    rows = part_0.shape[1] // 2
    parts = (part_0, part_1, part_2, part_3)

    def grad(number):
        span = slice(number % 2 * rows, (number % 2 + 1) * rows)
        return picked(place_ref[at + number // 2], [part[0, span, :] for part in parts])

    for part in range(4):
        where = (slice(None), slice(part * WIDTH, (part + 1) * WIDTH))
        refs[6][where], refs[7][where], refs[8][where] = adam_update(*(ref[where] for ref in refs[0:3]), grad(part))
        where = (slice(part * rows, (part + 1) * rows), slice(None))
        refs[9][where], refs[10][where], refs[11][where] = adam_update(*(ref[where] for ref in refs[3:6]), grad(4 + part))


def run_adam_feed(at, place, parts, expand, contract):
    arrays = tuple(expand) + tuple(contract)
    whole = pl.BlockSpec(memory_space=pltpu.VMEM)
    return pl.pallas_call(
        functools.partial(adam_feed, at),
        in_specs=[SCALARS] + [whole] * 10,
        out_specs=[whole] * 6,
        out_shape=[shape(a.shape, F32) for a in arrays],
        compiler_params=pltpu.CompilerParams(vmem_limit_bytes=24 * MIB),
        cost_estimate=estimate(4),
        name="adam_feed",
    )(place, *parts, *arrays)


class Route:
    def __init__(self, m, n):
        self.m, self.n = m, n
        self.dp_bits = m.bit_length() - 1
        self.line_bits = n.bit_length() - 2
        self.line = n // 2

    def pairs(self, partner):
        return [(d * self.n + f, partner(d, f)) for d in range(self.m) for f in range(self.n)]

    def across_core(self):
        return self.pairs(lambda d, f: d * self.n + (f ^ 1))

    def along_line(self, mask):
        return self.pairs(lambda d, f: d * self.n + (f ^ (2 * mask)))

    def among_dp(self, mask):
        return self.pairs(lambda d, f: (d ^ mask) * self.n + f)

    def across_line(self, step):
        return self.pairs(lambda d, f: d * self.n + (f ^ (2 << (self.line_bits - 1 - step))))

    def across_dp(self, step):
        def partner(d, f):
            bit = step if f % 2 == 0 else self.dp_bits - 1 - step
            return (d ^ (1 << bit)) * self.n + f

        return self.pairs(partner)

    @staticmethod
    def spot(mask, bits, core):
        return mask if core == 0 else sum(((mask >> b) & 1) << (bits - 1 - b) for b in range(bits))

    def part(self, share, d, f):
        return sum(((d >> (bit if f % 2 == 0 else self.dp_bits - 1 - bit)) & 1) << bit for bit in range(share))

    def gather_row(self, share, d, f):
        z, c = divmod(f, 2)
        return [
            ((2 * (z ^ k) + who) << share) + (self.part(share, d, who) ^ step)
            for who in (c, 1 - c)
            for step in range(1 << share)
            for k in range(self.line)
        ]

    def reduce_row(self, d, f):
        z, c = divmod(f, 2)
        row = [c]
        for who in (c, 1 - c):
            line = [self.spot(owner ^ z, self.line_bits, 1) for owner in range(self.line)]
            row += [self.spot(j ^ d, self.dp_bits, who) * self.line + at for j in range(self.m) for at in line]
        return row + [self.spot(j ^ d, self.dp_bits, c) for j in range(self.m)] + [j ^ d for j in range(self.m)]

    def part_row(self, d, f):
        return [self.part(1, d, f), self.part(2, d, f), f]

    def tables(self):
        kinds = (functools.partial(self.gather_row, 1), functools.partial(self.gather_row, 2), self.reduce_row, self.part_row)
        rows = [[kind(d, f) for kind in kinds] for d in range(self.m) for f in range(self.n)]
        ends = np.cumsum([0] + [len(row) for row in rows[0]])
        return np.array([sum(row, []) for row in rows], np.int32), ends


BOTH = ("dp", "fsdp")


def after(values, *earlier):
    return lax.optimization_barrier((values,) + earlier)[0]


def doubled(blocks, got):
    return jnp.concatenate([blocks, got], axis=0)


def per_device(
    inputs,
    memory,
    cotangent,
    lengths,
    stacked_weights,
    expand_weights,
    contract_weights,
    scale_vectors,
    stacked_first,
    stacked_second,
    expand_first,
    expand_second,
    contract_first,
    contract_second,
    vector_first,
    vector_second,
):
    m, n = lax.axis_size("dp"), lax.axis_size("fsdp")
    width = WIDTH // n
    slabs = inputs.shape[0] * lengths.shape[1]
    x = inputs.reshape(slabs, SLAB, WIDTH)
    mem = memory.reshape(slabs, SLAB, WIDTH)
    cot = cotangent.reshape(slabs, SLAB, WIDTH)
    by_hand = m == 4 and width == 64 and n == 8
    here = lax.axis_index("fsdp")
    lengths = lengths.reshape(slabs, 2, -1)
    if by_hand:
        route = Route(m, n)
        table, ends = route.tables()
        row = lax.dynamic_index_in_dim(jnp.asarray(table), lax.axis_index("dp") * n + here, keepdims=False)
        halves, quarters, reduced, parts = (int(end) for end in ends[:4])
        order, holder = parts - 2 * m, parts - m

        def swap(blocks, pairs):
            return lax.ppermute(blocks, BOTH, pairs)

        along = [route.along_line(mask) for mask in range(1, n // 2)]
        line = [route.across_line(step) for step in range(route.line_bits)]
        across = [route.across_dp(step) for step in range(route.dp_bits)]
        core = route.across_core()
        a, b, c = run_cut_shards(parts, row, stacked_weights, expand_weights, contract_weights, scale_vectors)
        got = lax.optimization_barrier(tuple(swap(a, pairs) for pairs in along) + tuple(swap(b, pairs) for pairs in along))
        a, b = jnp.concatenate([a, *got[:3]], axis=0), jnp.concatenate([b, *got[3:]], axis=0)
        c = after(c, got)
        c_1, c_2, a_across, b_across, a_core = lax.optimization_barrier((swap(c, along[0]), swap(c, along[1]), swap(a, across[0]), swap(b, across[0]), swap(a, core)))
        b = doubled(b, b_across)
        b_across, b_core, c_3 = swap(b, across[1]), swap(b, core), swap(after(c, b), along[2])
        w_self, *saved1 = run_self_forward(halves, row, lengths, after(x, b), (a, a_across, a_core, swap(a_across, core)))
        b_across, c_3 = after((b_across, c_3), saved1[-1])
        ex, co = (jnp.concatenate([part[:, span] for part in (c, c_1, c_2, c_3)], axis=0) for span in (slice(0, 4), slice(4, 8)))
        b_across = after(b_across, ex)
        ex_across = swap(ex, across[0])
        w_cross = (b, b_across, b_core, swap(b_across, core))
        w_cross, vec, q2, k2, v2, *qkv2, unit1, kept1, scale1, low1 = run_cross_inputs(quarters, n, row, saved1[-1], x, mem, w_cross)
        ex_across = after(ex_across, unit1)
        co_across = swap(after(co, ex_across), across[0])
        ex_core, co_core, ex_last = swap(ex, core), swap(co, core), swap(ex_across, core)
        e2, r2, o2, kept_o2 = run_cross_forward(lengths, q2, k2, v2)
        saved2 = (*qkv2, e2, r2, kept_o2)
        co_across = after(co_across, o2)
        w_feed = ((ex, ex_across, ex_core, ex_last), (co, co_across, co_core, swap(co_across, core)))
        out, ds2, kept2, scale2, feed_keep, feed_send, dvec3 = run_feed(halves, reduced, n, row, o2, unit1, w_cross, cot, *w_feed, vec)
        feed_got = swap(feed_send, core)
        ds1, dk2, dv2, cross_keep, cross_send, dvec2 = run_cross_backward(reduced, row, n // 2, ds2, kept2, scale2, low1, mem, w_cross, vec, saved2)
        feed_got = after(feed_got, ds1)
        feed_out, feed = feed_keep[8:] + feed_got[8:], feed_keep[:8] + feed_got[:8]
        feed_got, cross_got = swap(feed_out, across[1]), swap(cross_send, core)
        part, dq, dk, dv, *others, dvec1 = run_self_backward(after(ds1, feed_out), kept1, scale1, x, w_cross, vec, saved1)
        feed_got, cross_got = after((feed_got, cross_got), dq)
        feed_out, feed = feed[4:] + feed_got[4:], feed[:4] + feed_got[:4]
        cross_out, cross = cross_keep[8:] + cross_got[8:], cross_keep[:8] + cross_got[:8]
        feed_got, cross_got = swap(feed_out, across[0]), swap(cross_out, across[1])
        keep, send = run_self_weights(reduced, row, n // 2, after((dq, dk, dv, *others), cross_out, feed_out), (dvec1, dvec2, dvec3))
        got = swap(send, core)
        dx, dmem = run_input_gradients(after(part, send), dq, dk, dv, w_self, dk2, dv2, w_cross)
        got = after(got, dx)
        out_part, total = keep[8:] + got[8:], keep[:8] + got[:8]
        feed_got, cross_got = after(feed_got, got), after(cross_got, got)
        feed = feed + feed_got
        feed_out, feed = feed[2:], feed[:2]
        got, feed_got = lax.optimization_barrier((swap(out_part, across[1]), swap(after(feed_out, out_part), line[1])))
        out_part = jnp.concatenate([total[4:] + got[4:], cross[4:] + cross_got[4:]], axis=1)
        total = jnp.concatenate([total[:4] + got[:4], cross[:4] + cross_got[:4]], axis=1)
        feed_out, feed = feed[1:] + feed_got[1:], feed[:1] + feed_got[:1]
        got, feed_got = lax.optimization_barrier((swap(out_part, across[0]), swap(after(feed_out, out_part), line[0])))
        out_part, total = total[2:] + got[2:], total[:2] + got[:2]
        feed = feed + feed_got
        feed = after(feed, out_part)
        got, feed_1, feed_2 = lax.optimization_barrier((swap(out_part, line[1]), swap(feed, across[0]), swap(feed, across[1])))
        out_part, total = total[1:] + got[1:], total[:1] + got[:1]
        got, feed_3 = lax.optimization_barrier((swap(out_part, line[0]), swap(after(feed_1, out_part), across[1])))
        total = total + got
        parts = after((feed, feed_1, feed_2, feed_3), total)
        feed_next = run_adam_feed(order, row, parts, (expand_weights, expand_first, expand_second), (contract_weights, contract_first, contract_second))
        got = lax.optimization_barrier(tuple(swap(total, route.among_dp(mask)) for mask in range(1, m)))
        got = after(got, feed_next[0])
        *stacked_next, vw, vm, vs = run_adam_stacked(holder, row, (total, *got), (stacked_weights, stacked_first, stacked_second), (scale_vectors, vector_first, vector_second))
        vector_next = (vw, vm, vs)
    else:
        row = jnp.array([0, 1, 0] + [0, 1, 2, 3] * 2, jnp.int32)
        expand_blocks = jnp.swapaxes(expand_weights.reshape(width, 4, WIDTH), 0, 1)
        vec_shard = lax.dynamic_update_slice(jnp.zeros((16, WIDTH), BF), scale_vectors.astype(BF), (0, here * width))
        all_low = lax.all_gather(stacked_weights.astype(BF), "fsdp", axis=1, tiled=True)
        vec_full = jnp.sum(lax.all_gather(vec_shard, "fsdp", axis=0).astype(F32), axis=0).astype(BF)
        vec_full = jnp.pad(vec_full, ((0, WIDTH - 16), (0, 0)))
        ex = lax.all_gather(expand_blocks.astype(BF), "fsdp", axis=1, tiled=True).reshape(4, 2, -1, WIDTH)
        co = lax.all_gather(contract_weights.astype(BF), "fsdp", axis=0, tiled=True).reshape(2, 4, -1, WIDTH)
        w_self = tuple(all_low[None, :3].reshape(1, 3, 2, -1, WIDTH)[:, :, core] for core in range(2))
        w_cross = jnp.concatenate([all_low[4:], all_low[3:4], vec_full[None]], axis=0).reshape(1, 6, 2, -1, WIDTH)
        w_feed = tuple(ex[None, :, core] for core in range(2)), tuple(co[None, core] for core in range(2))
        w_self, *saved1 = run_self_forward(0, row, lengths, x, w_self)
        w_cross, vec, q2, k2, v2, *qkv2, unit1, kept1, scale1, low1 = run_cross_inputs(0, 1, row, saved1[-1], x, mem, (w_cross[:, :, 0], w_cross[:, :, 1]))
        e2, r2, o2, kept_o2 = run_cross_forward(lengths, q2, k2, v2)
        saved2 = (*qkv2, e2, r2, kept_o2)
        out, ds2, kept2, scale2, feed_keep, feed_send, dvec3 = run_feed(0, 2, 2, row, o2, unit1, w_cross, cot, *w_feed, vec)
        dw_feed = jnp.stack([feed_keep, feed_send]).reshape(2, 8, WIDTH // 2, WIDTH)
        dex = jnp.swapaxes(dw_feed[:, :4], 0, 1).reshape(4, n, width, WIDTH)
        dco = dw_feed[:, 4:].reshape(n, 4, width, WIDTH)
        dw_feed = jnp.concatenate([jnp.swapaxes(dex, 0, 1), dco], axis=1)
        grad_feed = lax.psum(lax.psum_scatter(dw_feed, "fsdp", scatter_dimension=0, tiled=False), "dp")
        ds1, dk2, dv2, cross_keep, cross_send, dvec2 = run_cross_backward(2, row, 1, ds2, kept2, scale2, low1, mem, w_cross, vec, saved2)
        part, dq, dk, dv, *others, dvec1 = run_self_backward(ds1, kept1, scale1, x, w_cross, vec, saved1)
        keep, send = run_self_weights(2, row, 1, (dq, dk, dv, *others), (dvec1, dvec2, dvec3))
        dx, dmem = run_input_gradients(part, dq, dk, dv, w_self, dk2, dv2, w_cross)
        both, cross_both = jnp.stack([keep, send], axis=1), jnp.stack([cross_keep, cross_send], axis=1)
        rows = WIDTH // 2
        grad_vector = lax.psum(both[0, :, rows : rows + 9, :rows].astype(F32), BOTH)
        grad_vector = jnp.swapaxes(grad_vector, 0, 1).reshape(9, WIDTH)
        grad_vector = lax.dynamic_slice(grad_vector, (0, here * width), (9, width))
        both = jnp.concatenate([both[:, :, :rows], cross_both], axis=0).reshape(8, WIDTH, WIDTH)
        both = lax.psum(lax.psum_scatter(both, "fsdp", scatter_dimension=1, tiled=True), "dp")
        stacked_next = adam_update(stacked_weights, stacked_first, stacked_second, both.astype(F32))
        vector_next = adam_update(scale_vectors, vector_first, vector_second, grad_vector)
        feed_next = run_adam_feed(0, jnp.arange(4, dtype=jnp.int32), tuple(grad_feed.reshape(4, 1, 2 * width, WIDTH)), (expand_weights, expand_first, expand_second), (contract_weights, contract_first, contract_second))
    expand_next, contract_next = feed_next[:3], feed_next[3:]
    return (
        out.reshape(inputs.shape),
        dx.reshape(inputs.shape),
        dmem.reshape(inputs.shape),
        stacked_next[0],
        expand_next[0],
        contract_next[0],
        vector_next[0],
        stacked_next[1],
        stacked_next[2],
        expand_next[1],
        expand_next[2],
        contract_next[1],
        contract_next[2],
        vector_next[1],
        vector_next[2],
    )


def solution(mesh):
    tokens = P(None, ("dp", "fsdp"), None)
    pieces = P(None, ("dp", "fsdp"), None, None)
    stacked = P(None, "fsdp", None)
    rows = P("fsdp", None)
    columns = P(None, "fsdp")
    return jax.shard_map(
        per_device,
        mesh=mesh,
        in_specs=(tokens, tokens, tokens, pieces, stacked, rows, rows, columns) + (stacked, stacked, rows, rows, rows, rows, columns, columns),
        out_specs=(tokens, tokens, tokens, stacked, rows, rows, columns) + (stacked, stacked, rows, rows, rows, rows, columns, columns),
        check_vma=False,
    )
```
